32 devices in a mesh: dp: 8 (over z, x), chan: 4 (over y, core).
Axes of the slice: x: 2, y: 2, z: 4, core: 2. Of those that a mesh axis runs over, the one named last changes fastest.
Arguments:
- activations: bfloat16 [4, 6272, 1024], P(None, 'dp', 'chan'), may hold values from -6 to 6
- counts: int32 [4, 8], replicated, may hold values from 2 to 4, as said below
- weight_in: bfloat16 [1024, 256], P(None, 'chan'), may hold values from -0.1875 to 0.1875
- gain_in: bfloat16 [256], P('chan'), may hold values from 0.5 to 1.5
- shift_in: bfloat16 [256], P('chan'), may hold values from -1.5 to 1.5
- weight_mid: bfloat16 [3, 3, 128, 2, 256], P(None, None, None, None, 'chan'), may hold values from -0.1875 to 0.1875
- gain_mid: bfloat16 [2, 256], P(None, 'chan'), may hold values from 0.5 to 1.5
- shift_mid: bfloat16 [2, 256], P(None, 'chan'), may hold values from -1.5 to 1.5
- weight_squeeze: bfloat16 [256, 128], P('chan'), may hold values from -0.375 to 0.375
- gain_gate: bfloat16 [128], replicated, may hold values from 0.5 to 1.5
- shift_gate: bfloat16 [128], replicated, may hold values from -1.5 to 1.5
- weight_excite: bfloat16 [128, 2, 256], P(None, None, 'chan'), may hold values from -0.5 to 0.5
- shift_excite: bfloat16 [2, 256], P(None, 'chan'), may hold values from -2 to 2
- weight_out: bfloat16 [256, 1024], P(None, 'chan'), may hold values from -0.375 to 0.375
- gain_out: bfloat16 [1024], P('chan'), may hold values from 0.5 to 1.5
- shift_out: bfloat16 [1024], P('chan'), may hold values from -1.5 to 1.5
- cotangent: bfloat16 [4, 6272, 1024], P(None, 'dp', 'chan'), may hold values from -6 to 6
Outputs:
- result: bfloat16 [4, 6272, 1024], P(None, 'dp', 'chan')
- grad_activations: bfloat16 [4, 6272, 1024], P(None, 'dp', 'chan')
- grad_weight_in: float32 [1024, 256], P(None, 'chan')
- grad_gain_in: float32 [256], P('chan')
- grad_shift_in: float32 [256], P('chan')
- grad_weight_mid: float32 [3, 3, 128, 2, 256], P(None, None, None, None, 'chan')
- grad_gain_mid: float32 [2, 256], P(None, 'chan')
- grad_shift_mid: float32 [2, 256], P(None, 'chan')
- grad_weight_squeeze: float32 [256, 128], P('chan')
- grad_gain_gate: float32 [128], replicated
- grad_shift_gate: float32 [128], replicated
- grad_weight_excite: float32 [128, 2, 256], P(None, None, 'chan')
- grad_shift_excite: float32 [2, 256], P(None, 'chan')
- grad_weight_out: float32 [256, 1024], P(None, 'chan')
- grad_gain_out: float32 [1024], P('chan')
- grad_shift_out: float32 [1024], P('chan')
The draws below stay inside these ranges and needn't reach their ends.
Inputs may be any that keep to these rules, and one draw needn't show every extreme that they name: counts[m, d] is how many of the 4 slots of block d in micro-batch m hold real images, the first ones; the rest are padding. In every micro-batch some block is full.
All inputs are finite; a program needn't handle non-finite values.
Results may differ from the reference program's by a relative error of at most 0.013.
Values may be sent and summed in bfloat16 or wider, within the bound.
No kernel may reach another device: no remote copies, remote signals or barrier semaphores. Data moves between devices by JAX's collectives and lax.ppermute only.
A program may use at most 192 MiB of HBM per device.

```python
import jax
import jax.numpy as jnp
from jax import lax

CIN = 1024
WIDTH = 256
INTER = 128
SIDE = 14
NMB = 4
IMG_DEV = 4
GROUPS = 8
ROWS = 6272


def draw_counts(key, part):
    key = jax.random.fold_in(key, 7)
    first_key, second_key = jax.random.split(key)
    drawn = jax.random.randint(first_key, (NMB, GROUPS), IMG_DEV // 2, IMG_DEV + 1)
    fullest = jax.random.randint(second_key, (NMB, 1), 0, GROUPS)
    places = jnp.arange(GROUPS, dtype=jnp.int32)[None, :]
    return jnp.where(places == fullest, IMG_DEV, drawn).astype(jnp.int32)


def block_levels(stream_key, shape, cuts, least, largest):
    def one(dim, parts):
        heights = jax.random.uniform(jax.random.fold_in(jax.random.fold_in(stream_key, 6), dim), (parts,), jnp.float32, least / len(cuts), largest / len(cuts))
        return jnp.repeat(jnp.exp(heights), shape[dim] // parts).reshape((-1,) + (1,) * (len(shape) - dim - 1))

    level = one(*cuts[0])
    for cut in cuts[1:]:
        level = level * one(*cut)
    return level


def gaussian(rng, shape, deviation, reach, cuts=(), kind=jnp.bfloat16):
    factor_of = block_levels(rng, shape, cuts, -0.22, 0.18) if cuts else 1.0
    values = jax.random.normal(rng, shape, jnp.float32) * deviation * factor_of
    return jnp.minimum(jnp.maximum(values, -reach), reach).astype(kind)


def setup_inputs(seed: int = 0) -> dict:
    arg_keys = jax.random.split(jax.random.key(seed), 18)
    activations = gaussian(arg_keys[0], (NMB, ROWS, CIN), 1.0, 6.0, ((1, 8), (2, 4)))
    counts = draw_counts(jax.random.fold_in(arg_keys[17], 71), 0)
    weight_in = gaussian(arg_keys[2], (CIN, WIDTH), CIN ** -0.5, 0.1875, ((1, 4),))
    gain_in = jnp.clip(1.0 + 0.1 * jax.random.normal(arg_keys[3], (WIDTH,), jnp.float32), 0.5, 1.5).astype(jnp.bfloat16)
    shift_in = gaussian(arg_keys[4], (WIDTH,), 0.3, 1.5, ((0, 4),))
    weight_mid = gaussian(arg_keys[5], (3, 3, WIDTH // 2, 2, WIDTH), (9 * WIDTH // 2) ** -0.5, 0.1875, ((4, 4),))
    gain_mid = jnp.clip(1.0 + 0.1 * jax.random.normal(arg_keys[6], (2, WIDTH), jnp.float32), 0.5, 1.5).astype(jnp.bfloat16)
    shift_mid = gaussian(arg_keys[7], (2, WIDTH), 0.3, 1.5, ((1, 4),))
    weight_squeeze = gaussian(arg_keys[8], (WIDTH, INTER), WIDTH ** -0.5, 0.375, ((0, 4),))
    gain_gate = jnp.clip(1.0 + 0.1 * jax.random.normal(arg_keys[9], (INTER,), jnp.float32), 0.5, 1.5).astype(jnp.bfloat16)
    shift_gate = gaussian(arg_keys[10], (INTER,), 0.3, 1.5)
    weight_excite = gaussian(arg_keys[11], (INTER, 2, WIDTH), INTER ** -0.5, 0.5, ((2, 4),))
    shift_excite = gaussian(arg_keys[12], (2, WIDTH), 0.5, 2.0, ((1, 4),))
    weight_out = gaussian(arg_keys[13], (WIDTH, CIN), WIDTH ** -0.5, 0.375, ((1, 4),))
    gain_out = jnp.clip(1.0 + 0.1 * jax.random.normal(arg_keys[14], (CIN,), jnp.float32), 0.5, 1.5).astype(jnp.bfloat16)
    shift_out = gaussian(arg_keys[15], (CIN,), 0.3, 1.5, ((0, 4),))
    cotangent = gaussian(arg_keys[16], (NMB, ROWS, CIN), 1.0, 6.0, ((1, 8), (2, 4)))
    return {"activations": activations, "counts": counts, "weight_in": weight_in, "gain_in": gain_in, "shift_in": shift_in, "weight_mid": weight_mid, "gain_mid": gain_mid, "shift_mid": shift_mid, "weight_squeeze": weight_squeeze, "gain_gate": gain_gate, "shift_gate": shift_gate, "weight_excite": weight_excite, "shift_excite": shift_excite, "weight_out": weight_out, "gain_out": gain_out, "shift_out": shift_out, "cotangent": cotangent}


epsilon = 1e-05
highest = lax.Precision.HIGHEST

@jax.custom_vjp
def low(v):
    return lax.optimization_barrier(v.astype(jnp.bfloat16)).astype(jnp.float32)

@jax.custom_vjp
def low_back(v):
    return v

def low_keep(v):
    return (low(v), None)

def low_pass(kept, grad):
    return (grad,)

def back_keep(v):
    return (v, None)

def back_low(kept, grad):
    return (low(grad),)
low.defvjp(low_keep, low_pass)
low_back.defvjp(back_keep, back_low)

def batch_norm(values_in, weights_row, total, gain, shift):
    center = lax.optimization_barrier(jnp.sum(weights_row * values_in, axis=0)) / total
    second_sum = lax.optimization_barrier(jnp.sum(weights_row * values_in * values_in, axis=0)) / total
    scaled = lax.rsqrt(second_sum - center * center + epsilon)
    return (values_in - center) * scaled * gain + shift

def block_forward(inputs, mask_image, total_image, params):
    weight_in, gain_in, shift_in, weight_mid, gain_mid, shift_mid, weight_squeeze, gain_gate, shift_gate, weight_excite, shift_excite, weight_out, gain_out, shift_out = params
    pixels = SIDE * SIDE
    images = mask_image.shape[0]
    row_count = images * pixels
    mask_rows = jnp.repeat(mask_image, pixels)[:, None]
    pixel_total = total_image * pixels
    pre_in = low_back(jnp.dot(inputs, weight_in, precision=highest))
    hidden = low(jax.nn.silu(batch_norm(pre_in, mask_rows, pixel_total, gain_in, shift_in)))
    hidden_grid = hidden.reshape(images, SIDE, SIDE, WIDTH)
    kernel = weight_mid.reshape(3, 3, WIDTH // 2, 2 * WIDTH)
    pre_mid = lax.conv_general_dilated(hidden_grid, kernel, (1, 1), ((1, 1), (1, 1)), dimension_numbers=('NHWC', 'HWIO', 'NHWC'), feature_group_count=2, precision=highest)
    pre_mid = low_back(pre_mid.reshape(row_count, 2 * WIDTH))
    branches = jax.nn.silu(batch_norm(pre_mid, mask_rows, pixel_total, gain_mid.reshape(-1), shift_mid.reshape(-1)))
    branches = branches.reshape(images, pixels, 2, WIDTH)
    pooled = lax.optimization_barrier(jnp.sum(branches, axis=(1, 2))) / pixels
    squeeze = jnp.dot(pooled, weight_squeeze, precision=highest)
    gate = jax.nn.silu(batch_norm(squeeze, mask_image[:, None], total_image, gain_gate, shift_gate))
    logits = jnp.dot(gate, weight_excite.reshape(INTER, 2 * WIDTH), precision=highest).reshape(images, 2, WIDTH)
    attention = jax.nn.softmax(logits + shift_excite, axis=1)
    weighted = low(lax.optimization_barrier(jnp.sum(attention[:, None] * branches, axis=2)).reshape(row_count, WIDTH))
    pre_out = low_back(jnp.dot(weighted, weight_out, precision=highest))
    summed = inputs + batch_norm(pre_out, mask_rows, pixel_total, gain_out, shift_out)
    return mask_rows * jax.nn.silu(summed)

def reference(activations, counts, weight_in, gain_in, shift_in, weight_mid, gain_mid, shift_mid, weight_squeeze, gain_gate, shift_gate, weight_excite, shift_excite, weight_out, gain_out, shift_out, cotangent):
    params = tuple((member.astype(jnp.float32) for member in (weight_in, gain_in, shift_in, weight_mid, gain_mid, shift_mid, weight_squeeze, gain_gate, shift_gate, weight_excite, shift_excite, weight_out, gain_out, shift_out)))

    def one_batch(running, pieces):
        inputs, upstream, count_row = pieces
        slot_ids = jnp.arange(IMG_DEV, dtype=jnp.int32)
        mask_image = (slot_ids[None, :] < count_row[:, None]).astype(jnp.float32).reshape(-1)
        total_image = jnp.sum(count_row).astype(jnp.float32)

        def forward(inputs_wide, weights):
            return block_forward(inputs_wide, mask_image, total_image, weights)
        output, pullback = jax.vjp(forward, inputs.astype(jnp.float32), params)
        grad_inputs, grad_params = pullback(upstream.astype(jnp.float32))
        running = jax.tree.map(jnp.add, running, grad_params)
        return (running, (output.astype(jnp.bfloat16), grad_inputs.astype(jnp.bfloat16)))
    initial = jax.tree.map(jnp.zeros_like, params)
    totals, (results, input_grads) = lax.scan(one_batch, initial, (activations, cotangent, counts))
    return (results, input_grads, totals[0], totals[1], totals[2], totals[3], totals[4], totals[5], totals[6], totals[7], totals[8], totals[9], totals[10], totals[11], totals[12], totals[13])
```

```python
import functools

import jax
import jax.numpy as jnp
from jax import lax
from jax.experimental import pallas as pl
from jax.experimental.pallas import tpu as pltpu
from jax.sharding import PartitionSpec as P

SIDE = 14
PIXELS = SIDE * SIDE
WIDE = 16
PADDED = SIDE * WIDE
STRIDE = PADDED + WIDE
CHUNK = 16
UNROLL = 2
EPSILON = 1e-05
HIGHEST = lax.Precision.HIGHEST
F32 = jnp.float32
BF16 = jnp.bfloat16


def dot_nn(left, right):
    return lax.dot_general(left, right, (((1,), (0,)), ((), ())), preferred_element_type=F32)


def dot_nt(left, right, precision=None):
    return lax.dot_general(
        left, right, (((1,), (1,)), ((), ())), preferred_element_type=F32, precision=precision
    )


def dot_tn(left, right):
    return lax.dot_general(left, right, (((0,), (0,)), ((), ())), preferred_element_type=F32)


def logistic(value):
    return 0.5 + 0.5 * jnp.tanh(0.5 * value)


def silu(value):
    return value * logistic(value)


def slope(value):
    share = logistic(value)
    return share * (1.0 + value * (1.0 - share))


def moments(first, second, total):
    center = first / total
    return center, lax.rsqrt(second / total - center * center + EPSILON)


def fold(value):
    return jnp.sum(value.reshape(-1, 8, value.shape[-1]), axis=0)


def total_of(value):
    return jnp.sum(value, axis=0, keepdims=True)


def columns_real(rows):
    spot = lax.broadcasted_iota(jnp.int32, (rows, 1), 0)
    return (lax.rem(spot, WIDE) < SIDE).astype(F32)


def real_image(count_ref, image):
    return jnp.where(count_ref[0] > image, 1.0, 0.0).astype(F32)


def spread_map_rows(flat_ref, wide_ref):
    for line in range(flat_ref.shape[0] // SIDE):
        wide_ref[line * WIDE : line * WIDE + SIDE, :] = flat_ref[line * SIDE : (line + 1) * SIDE, :]
        wide_ref[line * WIDE + SIDE : (line + 1) * WIDE, :] = jnp.zeros(
            (WIDE - SIDE, wide_ref.shape[1]), wide_ref.dtype
        )


def pack_map_rows(wide_ref, flat_ref):
    for line in range(flat_ref.shape[0] // SIDE):
        flat_ref[line * SIDE : (line + 1) * SIDE, :] = wide_ref[line * WIDE : line * WIDE + SIDE, :]


def clear_gaps(taps_ref, images):
    for gap in range(images + 1):
        taps_ref[:, gap * STRIDE : gap * STRIDE + WIDE, :] = jnp.zeros(
            (3, WIDE, taps_ref.shape[2]), taps_ref.dtype
        )


def store_taps(taps_ref, at, value):
    here = pl.ds(pl.multiple_of(at, WIDE), WIDE)
    taps_ref[0, here, :] = pltpu.roll(value, 1, 0).astype(taps_ref.dtype)
    taps_ref[1, here, :] = value.astype(taps_ref.dtype)
    taps_ref[2, here, :] = pltpu.roll(value, WIDE - 1, 0).astype(taps_ref.dtype)


def call(body, outs, scratch, flops, *args, smem=1):
    specs = [pl.BlockSpec(memory_space=pltpu.SMEM)] * smem + [
        pl.BlockSpec(memory_space=pltpu.VMEM)
    ] * (len(args) - smem)
    moved = sum(a.size * a.dtype.itemsize for a in args) + sum(
        o.size * o.dtype.itemsize for o in outs
    )
    return pl.pallas_call(
        body,
        out_shape=outs,
        in_specs=specs,
        out_specs=[pl.BlockSpec(memory_space=pltpu.VMEM)] * len(outs),
        scratch_shapes=scratch,
        compiler_params=pltpu.CompilerParams(vmem_limit_bytes=50 * 2**20),
        cost_estimate=pl.CostEstimate(flops=flops, bytes_accessed=moved, transcendentals=0),
        name=body.func.__name__ if isinstance(body, functools.partial) else body.__name__,
    )(*args)


def shape(dims, kind=F32):
    return jax.ShapeDtypeStruct(dims, kind)


def reduce_in(count_ref, x_ref, w_ref, pre_ref, msg_ref, flat_ref):
    parts = [dot_nn(x_ref[k], w_ref[k]) for k in range(x_ref.shape[0])]
    flat_ref[...] = functools.reduce(jnp.add, parts)
    spread_map_rows(flat_ref, pre_ref)
    first = jnp.zeros((1, pre_ref.shape[1]), F32)
    second = jnp.zeros((1, pre_ref.shape[1]), F32)
    for image in range(pre_ref.shape[0] // PADDED):
        real = real_image(count_ref, image)
        value = pre_ref[image * PADDED : (image + 1) * PADDED, :]
        first = first + real * total_of(value)
        second = second + real * total_of(value * value)
    sums = jnp.concatenate([first, second], axis=0)
    msg_ref[...] = jnp.broadcast_to(sums[None], msg_ref.shape)


def conv_mid(
    count_ref, total_ref, pre_ref, sums_ref, affine_ref, w_ref, taps_ref, mid_ref, msg_ref
):
    images = pre_ref.shape[0] // PADDED
    total = total_ref[0] * PIXELS
    sums = jnp.sum(sums_ref[...], axis=0)
    center, scale = moments(sums[0:1], sums[1:2], total)
    gain = affine_ref[0:1, :] * scale
    shift = affine_ref[1:2, :]
    clear_gaps(taps_ref, images)
    keep = columns_real(WIDE)
    for image in range(images):

        def normalize(step, carry, image=image):
            rows = pl.multiple_of(step * WIDE, WIDE)
            value = pre_ref[pl.ds(image * PADDED + rows, WIDE), :]
            value = silu((value - center) * gain + shift) * keep
            store_taps(taps_ref, image * STRIDE + WIDE + rows, value)
            return carry

        lax.fori_loop(0, SIDE, normalize, 0, unroll=UNROLL)
    half = pre_ref.shape[1] // 2
    width = pre_ref.shape[1]
    keep = columns_real(PADDED)
    firsts = [jnp.zeros((1, width), F32) for _ in range(2)]
    seconds = [jnp.zeros((1, width), F32) for _ in range(2)]
    for image in range(images):
        real = real_image(count_ref, image)
        for r in range(2):
            left = jnp.concatenate(
                [
                    taps_ref[
                        b,
                        image * STRIDE + a * WIDE : image * STRIDE + a * WIDE + PADDED,
                        r * half : (r + 1) * half,
                    ]
                    for a in range(3)
                    for b in range(3)
                ],
                axis=1,
            )
            value = dot_nn(left, w_ref[r])
            mid_ref[image * PADDED : (image + 1) * PADDED, r * width : (r + 1) * width] = value
            held = value * keep
            firsts[r] = firsts[r] + real * total_of(held)
            seconds[r] = seconds[r] + real * total_of(held * held)
    sums = jnp.concatenate(
        [jnp.concatenate(firsts, axis=1), jnp.concatenate(seconds, axis=1)], axis=0
    )
    msg_ref[...] = jnp.broadcast_to(sums[None], msg_ref.shape)


def mid_norm(total_ref, sums_ref, affine_ref):
    sums = jnp.sum(sums_ref[...], axis=0)
    center, scale = moments(sums[0:1], sums[1:2], total_ref[0] * PIXELS)
    return center, scale, affine_ref[0:1, :], affine_ref[1:2, :]


def pool(count_ref, total_ref, mid_ref, sums_ref, affine_ref, squeeze_ref, pooled_ref, msg_ref):
    images = mid_ref.shape[0] // PADDED
    width = mid_ref.shape[1] // 2
    center, scale, gain, shift = mid_norm(total_ref, sums_ref, affine_ref)
    keep = columns_real(CHUNK)
    for image in range(images):

        def gather(step, carry, image=image):
            active, rise, lean = carry
            at = pl.multiple_of(image * PADDED + step * CHUNK, CHUNK)
            normed = (mid_ref[pl.ds(at, CHUNK), :] - center) * scale
            value = normed * gain + shift
            share = logistic(value)
            active = active + fold(value * share * keep)
            inclined = share * (1.0 + value * (1.0 - share)) * keep
            return active, rise + fold(inclined), lean + fold(inclined * normed)

        nothing = jnp.zeros((8, 2 * width), F32)
        active, rise, lean = lax.fori_loop(
            0, PADDED // CHUNK, gather, (nothing, nothing, nothing), unroll=UNROLL
        )
        active = total_of(active)
        pooled_ref[image : image + 1, :] = (active[:, :width] + active[:, width:]) / PIXELS
        rise, lean = total_of(rise), total_of(lean)
        lanes = msg_ref.shape[2]
        for t, row in enumerate((rise, lean)):
            for q in range(2 * width // lanes):
                at = images + (t * images + image) * (2 * width // lanes) + q
                msg_ref[:, at : at + 1, :] = jnp.broadcast_to(
                    row[:, q * lanes : (q + 1) * lanes][None], (msg_ref.shape[0], 1, lanes)
                )
    squeezed = lax.dot_general(
        pooled_ref[...],
        squeeze_ref[...].astype(F32),
        (((1,), (0,)), ((), ())),
        preferred_element_type=F32,
        precision=HIGHEST,
    )
    msg_ref[:, 0:images, :] = jnp.broadcast_to(
        squeezed[None], (msg_ref.shape[0],) + squeezed.shape
    )
    real = [real_image(count_ref, image) * pooled_ref[image : image + 1, :] for image in range(images)]
    real = functools.reduce(jnp.add, real)
    for q in range(width // lanes):
        at = images + 2 * images * (2 * width // lanes) + q
        msg_ref[:, at : at + 1, :] = jnp.broadcast_to(
            real[:, q * lanes : (q + 1) * lanes][None], (msg_ref.shape[0], 1, lanes)
        )


def gate_norm(total_ref, pooled_ref, wall_ref):
    images = wall_ref.shape[1]
    rows = pooled_ref[:, 0:images, :]
    wall = wall_ref[...]
    first = jnp.sum(jnp.sum(wall * rows, axis=0), axis=0, keepdims=True)
    second = jnp.sum(jnp.sum(wall * rows * rows, axis=0), axis=0, keepdims=True)
    return moments(first, second, total_ref[0])


def attend(
    count_ref,
    total_ref,
    pooled_ref,
    wall_ref,
    gate_affine_ref,
    excite_ref,
    bias_ref,
    mid_ref,
    mid_sums_ref,
    mid_affine_ref,
    w_out_ref,
    gate_ref,
    attention_ref,
    weighted_ref,
    out_ref,
    msg_ref,
    wide_ref,
    flat_ref,
):
    images = mid_ref.shape[0] // PADDED
    width = mid_ref.shape[1] // 2
    center, scale = gate_norm(total_ref, pooled_ref, wall_ref)
    own = pooled_ref[count_ref[1], 0:images, :]
    normed = (own - center) * scale
    gate_pre = normed * gate_affine_ref[0:1, :] + gate_affine_ref[1:2, :]
    gate = silu(gate_pre)
    gate_ref[0] = gate
    gate_ref[1] = slope(gate_pre)
    logits = (
        lax.dot_general(
            gate,
            excite_ref[...].astype(F32),
            (((1,), (0,)), ((), ())),
            preferred_element_type=F32,
            precision=HIGHEST,
        )
        + bias_ref[...]
    )
    lean = 0.5 * jnp.tanh(0.5 * (logits[:, :width] - logits[:, width:]))
    attention_ref[:, :width] = 0.5 + lean
    attention_ref[:, width:] = 0.5 - lean
    center, scale, gain, shift = mid_norm(total_ref, mid_sums_ref, mid_affine_ref)
    for image in range(images):
        share = attention_ref[image : image + 1, :]

        def weigh(step, carry, image=image, share=share):
            at = pl.multiple_of(image * PADDED + step * CHUNK, CHUNK)
            normed = (mid_ref[pl.ds(at, CHUNK), :] - center) * scale
            value = share * silu(normed * gain + shift)
            wide_ref[pl.ds(at, CHUNK), :] = value[:, :width] + value[:, width:]
            return carry

        lax.fori_loop(0, PADDED // CHUNK, weigh, 0, unroll=UNROLL)
    pack_map_rows(wide_ref, flat_ref)
    weighted_ref[...] = flat_ref[...].astype(BF16)
    spot = lax.broadcasted_iota(jnp.int32, (flat_ref.shape[0], 1), 0)
    real = (spot < count_ref[0] * PIXELS).astype(F32)
    blocks = w_out_ref.shape[0]
    for k in range(blocks):
        value = dot_nn(weighted_ref[...], w_out_ref[k])
        out_ref[k] = value
        held = value * real
        for t, row in enumerate((total_of(held), total_of(held * value))):
            msg_ref[:, t * blocks + k : t * blocks + k + 1, :] = jnp.broadcast_to(
                row[None], (msg_ref.shape[0], 1, row.shape[1])
            )


def finish(
    count_ref, total_ref, out_ref, sums_ref, affine_ref, x_ref, cot_ref, result_ref, grad_ref, msg_ref
):
    blocks, rows, lanes = out_ref.shape
    sums = jnp.sum(sums_ref[...], axis=0)
    center, scale = moments(sums[:blocks], sums[blocks:], total_ref[0] * PIXELS)
    limit = count_ref[0] * PIXELS
    for k in range(blocks):
        mu, r = center[k : k + 1], scale[k : k + 1]
        gain, shift = affine_ref[0, k : k + 1, :], affine_ref[1, k : k + 1, :]

        def chunk(step, carry, k=k, mu=mu, r=r, gain=gain, shift=shift):
            first, second = carry
            at = pl.multiple_of(step * CHUNK, CHUNK)
            here = pl.ds(at, CHUNK)
            spot = lax.broadcasted_iota(jnp.int32, (CHUNK, 1), 0) + at
            real = (spot < limit).astype(F32)
            normed = (out_ref[k, here, :] - mu) * r
            summed = x_ref[k, here, :].astype(F32) + (normed * gain + shift)
            share = logistic(summed) * real
            result_ref[k, here, :] = (summed * share).astype(BF16)
            upstream = cot_ref[k, here, :].astype(F32)
            grad = upstream * share * (1.0 + summed * (1.0 - share))
            grad_ref[k, here, :] = grad
            return first + fold(grad), second + fold(grad * normed)

        nothing = jnp.zeros((8, lanes), F32)
        first, second = lax.fori_loop(
            0, rows // CHUNK, chunk, (nothing, nothing), unroll=UNROLL
        )
        for t, row in enumerate((total_of(first), total_of(second))):
            msg_ref[:, t * blocks + k : t * blocks + k + 1, :] = jnp.broadcast_to(
                row[None], (msg_ref.shape[0], 1, lanes)
            )


def back_out(
    count_ref,
    total_ref,
    grad_ref,
    out_ref,
    sums_ref,
    back_ref,
    affine_ref,
    w_out_ref,
    mid_ref,
    mid_sums_ref,
    mid_affine_ref,
    attention_ref,
    gate_ref,
    excite_ref,
    low_ref,
    gw_ref,
    logits_ref,
    msg_ref,
    flat_ref,
):
    blocks, rows, lanes = out_ref.shape
    images = attention_ref.shape[0]
    width = attention_ref.shape[1] // 2
    total = total_ref[0] * PIXELS
    sums = jnp.sum(sums_ref[...], axis=0)
    center, scale = moments(sums[:blocks], sums[blocks:], total)
    back = jnp.sum(back_ref[...], axis=0) / total
    limit = count_ref[0] * PIXELS
    for k in range(blocks):
        mu, r = center[k : k + 1], scale[k : k + 1]
        gain = affine_ref[0, k : k + 1, :] * r
        first, second = back[k : k + 1], back[blocks + k : blocks + k + 1]

        def chunk(step, carry, k=k, mu=mu, r=r, gain=gain, first=first, second=second):
            at = pl.multiple_of(step * CHUNK, CHUNK)
            here = pl.ds(at, CHUNK)
            spot = lax.broadcasted_iota(jnp.int32, (CHUNK, 1), 0) + at
            real = (spot < limit).astype(F32)
            normed = (out_ref[k, here, :] - mu) * r
            value = gain * (grad_ref[k, here, :] - real * (first + normed * second))
            low_ref[k, here, :] = value.astype(BF16)
            return carry

        lax.fori_loop(0, rows // CHUNK, chunk, 0, unroll=UNROLL)
    parts = [dot_nt(low_ref[k], w_out_ref[k]) for k in range(blocks)]
    flat_ref[...] = functools.reduce(jnp.add, parts)
    spread_map_rows(flat_ref, gw_ref)
    center, scale, gain, shift = mid_norm(total_ref, mid_sums_ref, mid_affine_ref)
    rises, leans, attended = [], [], []
    for image in range(images):

        def gather(step, carry, image=image):
            attended, rise, lean = carry
            at = pl.multiple_of(image * PADDED + step * CHUNK, CHUNK)
            normed = (mid_ref[pl.ds(at, CHUNK), :] - center) * scale
            value = normed * gain + shift
            share = logistic(value)
            grad = gw_ref[pl.ds(at, CHUNK), :]
            grad = jnp.concatenate([grad, grad], axis=1)
            active = grad * share
            attended = attended + fold(active * value)
            inclined = active * (1.0 + value * (1.0 - share))
            return attended, rise + fold(inclined), lean + fold(inclined * normed)

        nothing = jnp.zeros((8, 2 * width), F32)
        parts = lax.fori_loop(
            0, PADDED // CHUNK, gather, (nothing, nothing, nothing), unroll=UNROLL
        )
        share = attention_ref[image : image + 1, :]
        attended.append(total_of(parts[0]))
        rises.append(share * total_of(parts[1]))
        leans.append(share * total_of(parts[2]))
    grad = jnp.concatenate(attended, axis=0)
    attention = attention_ref[...]
    inner = attention * grad
    inner = inner[:, :width] + inner[:, width:]
    logits = attention * (grad - jnp.concatenate([inner, inner], axis=1))
    logits_ref[...] = logits
    gate = dot_nt(logits, excite_ref[...].astype(F32), HIGHEST) * gate_ref[1]
    pack = msg_ref.shape[2]
    msg_ref[:, 0:images, :] = jnp.broadcast_to(gate[None], (msg_ref.shape[0],) + gate.shape)
    for t, row in enumerate((functools.reduce(jnp.add, rises), functools.reduce(jnp.add, leans))):
        for q in range(2 * width // pack):
            at = images + t * (2 * width // pack) + q
            msg_ref[:, at : at + 1, :] = jnp.broadcast_to(
                row[:, q * pack : (q + 1) * pack][None], (msg_ref.shape[0], 1, pack)
            )


def back_mid(
    count_ref,
    total_ref,
    back_ref,
    pooled_ref,
    wall_ref,
    gate_affine_ref,
    squeeze_ref,
    attention_ref,
    gw_ref,
    mid_ref,
    mid_sums_ref,
    mid_affine_ref,
    pre_ref,
    sums_ref,
    affine_ref,
    w_ref,
    low_ref,
    grad_ref,
    gate_ref,
    vector_ref,
    msg_ref,
    taps_ref,
):
    images = attention_ref.shape[0]
    width = attention_ref.shape[1] // 2
    groups = wall_ref.shape[0]
    lanes = wall_ref.shape[2]
    pieces = 2 * width // lanes
    total = total_ref[0] * PIXELS
    center, scale = gate_norm(total_ref, pooled_ref, wall_ref)
    gain = gate_affine_ref[0:1, :] * scale
    wall = wall_ref[...]
    normed = (pooled_ref[:, 0:images, :] - center) * scale
    grads = back_ref[:, 0:images, :]
    first = jnp.sum(jnp.sum(wall * grads, axis=0), axis=0, keepdims=True)
    second = jnp.sum(jnp.sum(wall * grads * normed, axis=0), axis=0, keepdims=True)
    vector_ref[0:1, 0:lanes] = second
    vector_ref[0:1, lanes : 2 * lanes] = first
    squeezed = gain * (grads - wall * (first + normed * second) / total_ref[0])
    gate_ref[...] = squeezed
    gate_rows = jnp.concatenate([gate_ref[g] for g in range(groups)], axis=0)
    pooled_grad = dot_nt(gate_rows, squeeze_ref[...].astype(F32), HIGHEST) / PIXELS
    back = []
    for t in range(2):
        row = [
            jnp.sum(back_ref[:, images + t * pieces + q, :], axis=0, keepdims=True)
            for q in range(pieces)
        ]
        for g in range(groups):
            for image in range(images):
                grad = pooled_grad[g * images + image : g * images + image + 1, :]
                for q in range(pieces):
                    at = images + (t * images + image) * pieces + q
                    place = (q * lanes) % width
                    row[q] = row[q] + pooled_ref[g, at : at + 1, :] * grad[:, place : place + lanes]
        back.append(jnp.concatenate(row, axis=1))
    vector_ref[1:2, :] = back[1]
    vector_ref[2:3, :] = back[0]
    first, second = back[0] / total, back[1] / total
    center, scale, gain, shift = mid_norm(total_ref, mid_sums_ref, mid_affine_ref)
    gained = gain * scale
    clear_gaps(taps_ref, images)
    keep = columns_real(WIDE)
    own = dot_nt(gate_ref[count_ref[1]], squeeze_ref[...].astype(F32), HIGHEST) / PIXELS
    own = jnp.concatenate([own, own], axis=1)
    for image in range(images):
        share = attention_ref[image : image + 1, :]
        offset = own[image : image + 1, :]
        real = real_image(count_ref, image)
        lead, lag = real * first, real * second

        def chunk(step, carry, image=image, share=share, offset=offset, lead=lead, lag=lag):
            rows = pl.multiple_of(step * WIDE, WIDE)
            here = pl.ds(image * PADDED + rows, WIDE)
            normed = (mid_ref[here, :] - center) * scale
            grad = gw_ref[here, :]
            grad = jnp.concatenate([grad, grad], axis=1)
            grad = (share * grad + offset) * slope(normed * gain + shift)
            value = gained * (grad - (lead + normed * lag)) * keep
            store_taps(taps_ref, image * STRIDE + WIDE + rows, value)
            return carry

        lax.fori_loop(0, SIDE, chunk, 0, unroll=UNROLL)
    low_ref[...] = taps_ref[1]
    sums = jnp.sum(sums_ref[...], axis=0)
    center, scale = moments(sums[0:1], sums[1:2], total)
    gain, shift = affine_ref[0:1, :], affine_ref[1:2, :]
    half = width // 2
    keep = columns_real(PADDED)
    firsts = [jnp.zeros((1, half), F32) for _ in range(2)]
    seconds = [jnp.zeros((1, half), F32) for _ in range(2)]
    for image in range(images):
        real = real_image(count_ref, image)
        here = slice(image * PADDED, (image + 1) * PADDED)
        for r in range(2):
            left = jnp.concatenate(
                [
                    taps_ref[
                        2 - b,
                        image * STRIDE + (2 - a) * WIDE : image * STRIDE + (2 - a) * WIDE + PADDED,
                        r * width : (r + 1) * width,
                    ]
                    for a in range(3)
                    for b in range(3)
                ],
                axis=1,
            )
            lane = slice(r * half, (r + 1) * half)
            normed = (pre_ref[here, lane] - center[:, lane]) * scale[:, lane]
            value = dot_nn(left, w_ref[r]) * slope(normed * gain[:, lane] + shift[:, lane])
            value = value * (keep * real)
            grad_ref[here, lane] = value
            firsts[r] = firsts[r] + total_of(value)
            seconds[r] = seconds[r] + total_of(value * normed)
    sums = jnp.concatenate(
        [jnp.concatenate(firsts, axis=1), jnp.concatenate(seconds, axis=1)], axis=0
    )
    msg_ref[...] = jnp.broadcast_to(sums[None], msg_ref.shape)


def weight_mid_term(taps_ref, low_ref, out_ref):
    half = taps_ref.shape[2] // 2
    width = low_ref.shape[1] // 2
    rows = low_ref.shape[0] - 2 * WIDE
    for r in range(2):
        right = low_ref[WIDE : WIDE + rows, r * width : (r + 1) * width]
        for a in range(3):
            for b in range(3):
                left = taps_ref[b, a * WIDE : a * WIDE + rows, r * half : (r + 1) * half]
                at = (3 * a + b) * half
                out_ref[r, at : at + half, :] = dot_tn(left, right)


def back_in(
    count_ref,
    total_ref,
    grad_ref,
    pre_ref,
    sums_ref,
    back_ref,
    affine_ref,
    w_ref,
    summed_ref,
    low_ref,
    result_ref,
    vector_ref,
    flat_ref,
):
    images = pre_ref.shape[0] // PADDED
    total = total_ref[0] * PIXELS
    sums = jnp.sum(sums_ref[...], axis=0)
    center, scale = moments(sums[0:1], sums[1:2], total)
    back = jnp.sum(back_ref[...], axis=0)
    vector_ref[0:1, :] = back[1:2]
    vector_ref[1:2, :] = back[0:1]
    first, second = back[0:1] / total, back[1:2] / total
    gain = affine_ref[0:1, :] * scale
    for image in range(images):
        real = real_image(count_ref, image)
        lead, lag = real * first, real * second
        for line in range(SIDE):
            at = image * PADDED + line * WIDE
            normed = (pre_ref[at : at + WIDE, :] - center) * scale
            value = gain * (grad_ref[at : at + WIDE, :] - (lead + normed * lag))
            at = image * PIXELS + line * SIDE
            flat_ref[at : at + SIDE, :] = value[:SIDE]
    low_ref[...] = flat_ref[...].astype(BF16)
    for k in range(w_ref.shape[0]):
        result_ref[k] = (dot_nt(low_ref[...], w_ref[k]) + summed_ref[k]).astype(BF16)


def stack_lanes(value):
    rows = value.shape[-2] // 2
    return jnp.concatenate([value[..., :rows, :], value[..., rows:, :]], axis=-1)


def unstack_lanes(value):
    lanes = value.shape[-1] // 2
    return jnp.concatenate([value[..., :lanes], value[..., lanes:]], axis=-2)


def per_device(
    activations,
    counts,
    weight_in,
    gain_in,
    shift_in,
    weight_mid,
    gain_mid,
    shift_mid,
    weight_squeeze,
    gain_gate,
    shift_gate,
    weight_excite,
    shift_excite,
    weight_out,
    gain_out,
    shift_out,
    cotangent,
    *,
    groups,
    parts,
):
    batches, rows, lanes = activations.shape
    images = rows // PIXELS
    own = weight_in.shape[1]
    width = own * parts
    inter = gain_gate.shape[0]
    wide_rows = images * PADDED
    gap_rows = WIDE + images * STRIDE
    batch = lax.axis_index("chan")
    group = lax.axis_index("dp")

    def over_chan(tensor):
        return lax.all_to_all(tensor, "chan", 0, 0, tiled=False)

    def over_groups(tensor):
        return lax.all_to_all(tensor, "dp", 0, 0, tiled=False)

    x = over_chan(activations)
    cot = over_chan(cotangent)
    count_row = lax.dynamic_index_in_dim(counts, batch, keepdims=False)
    own_count = lax.dynamic_index_in_dim(count_row, group, keepdims=False)
    count = jnp.stack([own_count, group]).astype(jnp.int32)
    total = jnp.sum(count_row).astype(F32).reshape(1)
    slots = jnp.arange(images, dtype=jnp.int32)
    wall = (slots[None, :] < count_row[:, None]).astype(F32)
    wall = jnp.broadcast_to(wall[:, :, None], (groups, images, inter))

    small = jnp.concatenate(
        [
            jnp.concatenate([gain_in, shift_in])[None],
            gain_mid.reshape(1, 2 * own),
            shift_mid.reshape(1, 2 * own),
            shift_excite.reshape(1, 2 * own),
            gain_out.reshape(-1, 2 * own),
            shift_out.reshape(-1, 2 * own),
        ]
    )
    small = jnp.pad(small, ((0, 16 - small.shape[0]), (0, 0)))
    blocks = [
        small,
        stack_lanes(weight_in),
        weight_mid.reshape(-1, 2 * own),
        stack_lanes(weight_squeeze.reshape(-1, 64)),
        weight_excite.reshape(inter, 2 * own),
        jnp.concatenate([weight_out[:, :128], weight_out[:, 128:]]),
    ]
    sizes = [b.shape[0] for b in blocks]
    packed = lax.all_gather(jnp.concatenate(blocks), "chan")
    pieces = []
    at = 0
    for size in sizes:
        pieces.append(packed[:, at : at + size])
        at += size
    small = pieces[0].astype(F32)
    in_affine = jnp.stack([small[:, 0, :own].reshape(-1), small[:, 0, own:].reshape(-1)])

    def halves(value):
        return value.reshape(parts, 2, own).transpose(1, 0, 2).reshape(1, 2 * width)

    mid_affine = jnp.concatenate([halves(small[:, 1]), halves(small[:, 2])])
    bias = halves(small[:, 3])
    outs = lanes // (2 * own)
    out_affine = jnp.stack(
        [small[:, 4 : 4 + outs].reshape(parts, lanes), small[:, 4 + outs : 4 + 2 * outs].reshape(parts, lanes)]
    )
    w_in = unstack_lanes(pieces[1]).transpose(1, 0, 2).reshape(parts, lanes, width)
    w_mid = pieces[2].reshape(parts, -1, 2, own).transpose(2, 1, 0, 3).reshape(2, -1, width)
    w_mid_back = (
        w_mid.reshape(2, 9, width // 2, width).transpose(0, 1, 3, 2).reshape(2, 9 * width, width // 2)
    )
    squeeze = unstack_lanes(pieces[3]).reshape(width, inter)
    excite = pieces[4].reshape(parts, inter, 2, own).transpose(1, 2, 0, 3).reshape(inter, 2 * width)
    w_out = jnp.concatenate(
        [pieces[5][:, :width], pieces[5][:, width:]], axis=-1
    )
    gate_affine = jnp.stack([gain_gate, shift_gate]).astype(F32)

    product = 2 * rows * lanes * parts * width
    pre_in, msg = call(
        reduce_in,
        [shape((wide_rows, width)), shape((groups, 2, width))],
        [pltpu.VMEM((rows, width), F32)],
        product,
        count,
        x,
        w_in,
    )
    in_sums = over_groups(msg)
    conv = 2 * wide_rows * 9 * width * width
    taps, mid, msg = call(
        conv_mid,
        [
            shape((3, gap_rows, width), BF16),
            shape((wide_rows, 2 * width)),
            shape((groups, 2, 2 * width)),
        ],
        [],
        conv,
        count,
        total,
        pre_in,
        in_sums,
        in_affine,
        w_mid,
        smem=2,
    )
    mid_sums = over_groups(msg)
    inclines = 2 * images * 2 * width // inter
    message = -(-(images + inclines + width // inter) // 8) * 8
    pooled, msg = call(
        pool,
        [shape((images, width)), shape((groups, message, inter))],
        [],
        0,
        count,
        total,
        mid,
        mid_sums,
        mid_affine,
        squeeze,
        smem=2,
    )
    gathered = over_groups(msg)
    gate, attention, weighted, out, msg = call(
        attend,
        [
            shape((2, images, inter)),
            shape((images, 2 * width)),
            shape((rows, width), BF16),
            shape((parts, rows, lanes)),
            shape((groups, 2 * parts, lanes)),
        ],
        [pltpu.VMEM((wide_rows, width), F32), pltpu.VMEM((rows, width), F32)],
        product,
        count,
        total,
        gathered,
        wall,
        gate_affine,
        excite,
        bias,
        mid,
        mid_sums,
        mid_affine,
        w_out,
        smem=2,
    )
    out_sums = over_groups(msg)
    result, grad, msg = call(
        finish,
        [
            shape((parts, rows, lanes), BF16),
            shape((parts, rows, lanes)),
            shape((groups, 2 * parts, lanes)),
        ],
        [],
        0,
        count,
        total,
        out,
        out_sums,
        out_affine,
        x,
        cot,
        smem=2,
    )
    out_back = over_groups(msg)
    result = over_chan(result)

    message = -(-(images + 2 * 2 * width // inter) // 8) * 8
    low_out, grad_weighted, grad_logits, msg = call(
        back_out,
        [
            shape((parts, rows, lanes), BF16),
            shape((wide_rows, width)),
            shape((images, 2 * width)),
            shape((groups, message, inter)),
        ],
        [pltpu.VMEM((rows, width), F32)],
        product,
        count,
        total,
        grad,
        out,
        out_sums,
        out_back,
        out_affine,
        w_out,
        mid,
        mid_sums,
        mid_affine,
        attention,
        gate,
        excite,
        smem=2,
    )
    mid_back = over_groups(msg)
    low_mid, grad_hidden, grad_squeeze, vectors, msg = call(
        back_mid,
        [
            shape((gap_rows, 2 * width), BF16),
            shape((wide_rows, width)),
            shape((groups, images, inter)),
            shape((8, 2 * width)),
            shape((groups, 2, width)),
        ],
        [pltpu.VMEM((3, gap_rows, 2 * width), BF16)],
        conv,
        count,
        total,
        mid_back,
        gathered,
        wall,
        gate_affine,
        squeeze,
        attention,
        grad_weighted,
        mid,
        mid_sums,
        mid_affine,
        pre_in,
        in_sums,
        in_affine,
        w_mid_back,
        smem=2,
    )
    in_back = over_groups(msg)
    low_in, grad_x, in_vectors = call(
        back_in,
        [
            shape((rows, width), BF16),
            shape((parts, rows, lanes), BF16),
            shape((8, width)),
        ],
        [pltpu.VMEM((rows, width), F32)],
        product,
        count,
        total,
        grad_hidden,
        pre_in,
        in_sums,
        in_back,
        in_affine,
        w_in,
        grad,
        smem=2,
    )
    grad_x = over_chan(grad_x)

    term_in = jnp.einsum("krc,ro->kco", x, low_in, preferred_element_type=F32)
    term_in = term_in.reshape(parts * lanes, parts, own).transpose(1, 0, 2)
    (term_mid,) = call(
        weight_mid_term, [shape((2, 9 * width // 2, width))], [], conv, taps, low_mid, smem=0
    )
    term_mid = term_mid.reshape(2, -1, parts, own).transpose(2, 1, 0, 3).reshape(parts, -1, 2 * own)
    term_out = jnp.einsum("rc,kro->kco", weighted, low_out, preferred_element_type=F32)
    own_squeeze = lax.dynamic_index_in_dim(grad_squeeze, group, keepdims=False)
    mean = jnp.sum(gathered[:, images + inclines : images + inclines + width // inter], axis=0)
    mean = mean.reshape(1, width) / total
    term_squeeze = jnp.einsum("bc,bk->ck", pooled - mean, own_squeeze, precision=HIGHEST)
    term_excite = jnp.einsum("bk,bo->ko", gate[0], grad_logits, precision=HIGHEST)
    term_excite = term_excite.reshape(inter, 2, parts, own).transpose(2, 0, 1, 3)
    term_bias = jnp.sum(grad_logits, axis=0).reshape(1, 2, parts, own).transpose(2, 0, 1, 3)
    out_vectors = jnp.sum(out_back, axis=0).reshape(2, parts, lanes)

    def piece(row):
        return row.reshape(2, parts, own).transpose(1, 0, 2).reshape(parts, 1, 2 * own)

    everyone = jnp.broadcast_to(vectors[0, : 2 * inter].reshape(1, 2, inter), (parts, 2, inter))
    batch_sums = jnp.concatenate(
        [
            piece(in_vectors[:2].reshape(-1)),
            piece(vectors[1]),
            piece(vectors[2]),
            everyone,
            out_vectors[1].reshape(parts, -1, 2 * own),
            out_vectors[0].reshape(parts, -1, 2 * own),
        ],
        axis=1,
    )
    terms = [
        stack_lanes(term_in),
        term_mid,
        stack_lanes(term_squeeze.reshape(parts, -1, 64)),
        term_excite.reshape(parts, inter, 2 * own),
        jnp.concatenate([term_out[..., :128], term_out[..., 128:]], axis=1),
        term_bias.reshape(parts, 1, 2 * own),
        batch_sums / groups,
    ]
    sizes = [t.shape[1] for t in terms]
    terms = jnp.concatenate(terms, axis=1)
    count_rows = terms.shape[1]
    whole = -(-count_rows // (16 * groups)) * 16 * groups
    terms = jnp.pad(terms, ((0, 0), (0, whole - count_rows), (0, 0)))
    terms = jnp.sum(over_chan(terms.astype(BF16)).astype(F32), axis=0)
    terms = terms.reshape(groups, whole // groups, 2 * own).astype(BF16)
    terms = jnp.sum(over_groups(terms).astype(F32), axis=0).astype(BF16)
    terms = over_groups(jnp.broadcast_to(terms[None], (groups,) + terms.shape))
    terms = terms.reshape(whole, 2 * own).astype(F32)
    pieces = []
    at = 0
    for size in sizes:
        pieces.append(terms[at : at + size])
        at += size
    sums = pieces[6]
    return (
        result,
        grad_x,
        unstack_lanes(pieces[0]),
        sums[0, :own],
        sums[0, own:],
        pieces[1].reshape(weight_mid.shape),
        sums[1].reshape(2, own),
        sums[2].reshape(2, own),
        unstack_lanes(pieces[2]).reshape(weight_squeeze.shape),
        sums[3],
        sums[4],
        pieces[3].reshape(weight_excite.shape),
        pieces[5].reshape(2, own),
        jnp.concatenate([pieces[4][:width], pieces[4][width:]], axis=1),
        sums[5 : 5 + outs].reshape(-1),
        sums[5 + outs : 5 + 2 * outs].reshape(-1),
    )


def solution(mesh):
    placed = (
        P(None, "dp", "chan"),
        P(),
        P(None, "chan"),
        P("chan"),
        P("chan"),
        P(None, None, None, None, "chan"),
        P(None, "chan"),
        P(None, "chan"),
        P("chan", None),
        P(),
        P(),
        P(None, None, "chan"),
        P(None, "chan"),
        P(None, "chan"),
        P("chan"),
        P("chan"),
        P(None, "dp", "chan"),
    )
    return jax.shard_map(
        functools.partial(per_device, groups=mesh.shape["dp"], parts=mesh.shape["chan"]),
        mesh=mesh,
        in_specs=placed,
        out_specs=placed[:1] + placed[:1] + placed[2:16],
        check_vma=False,
    )
```

```python
import functools

import jax
import jax.numpy as jnp
from jax import lax
from jax.experimental import pallas as pl
from jax.experimental.pallas import tpu as pltpu
from jax.sharding import PartitionSpec as P

SIDE = 14
PIXELS = SIDE * SIDE
WIDE = 16
PADDED = SIDE * WIDE
STRIDE = PADDED + WIDE
CHUNK = 16
UNROLL = 2
VMEM_LIMIT = 24 * 2**20
SLOTS = (0, 1, 2, 3)
ORDER = (0, 2, 1, 3)
EPSILON = 1e-05
HIGHEST = lax.Precision.HIGHEST
F32 = jnp.float32
BF16 = jnp.bfloat16


def dot_nn(left, right, precision=None):
    return lax.dot_general(
        left, right, (((1,), (0,)), ((), ())), preferred_element_type=F32, precision=precision
    )


def dot_nt(left, right, precision=None):
    return lax.dot_general(
        left, right, (((1,), (1,)), ((), ())), preferred_element_type=F32, precision=precision
    )


def dot_tn(left, right, precision=None):
    return lax.dot_general(
        left, right, (((0,), (0,)), ((), ())), preferred_element_type=F32, precision=precision
    )


def logistic(value):
    return 0.5 + 0.5 * jnp.tanh(0.5 * value)


def silu(value):
    return value * logistic(value)


def slope(value):
    share = logistic(value)
    return share * (1.0 + value * (1.0 - share))


def moments(first, second, total):
    center = first / total
    return center, lax.rsqrt(second / total - center * center + EPSILON)


def fold(value):
    return jnp.sum(value.reshape(-1, 8, value.shape[-1]), axis=0)


def total_of(value):
    return jnp.sum(value, axis=0, keepdims=True)


def columns_real(rows):
    spot = lax.broadcasted_iota(jnp.int32, (rows, 1), 0)
    return (lax.rem(spot, WIDE) < SIDE).astype(F32)


def summed_over(refs):
    values = [ref[...] for ref in refs]
    while len(values) > 1:
        values = [left + right for left, right in zip(values[::2], values[1::2])]
    return values[0]


def slot_rows(refs, size, first, count, skip=0):
    return jnp.concatenate(
        [
            ref[at + first : at + first + count, :]
            for ref in refs
            for at in range(skip, ref.shape[0], size)
        ],
        axis=0,
    )


class Place:
    def __init__(self, counts_ref):
        group = lax.axis_index("dp")
        self.chan = lax.axis_index("chan")
        self.parity, self.depth, self.core = group & 1, group >> 1, self.chan & 1
        self.batch = (self.chan & 2) | self.parity
        self.counts = counts_ref
        self.groups = counts_ref.shape[1]

    def images(self, depth, core):
        return self.counts[self.batch, 2 * depth + core]

    def real(self, image):
        return jnp.where(self.images(self.depth, self.core) > image, 1.0, 0.0).astype(F32)

    def total(self):
        every = [self.counts[self.batch, g] for g in range(self.groups)]
        return functools.reduce(jnp.add, every).astype(F32)


def spread_map_rows(flat_ref, wide_ref):
    for line in range(flat_ref.shape[0] // SIDE):
        wide_ref[line * WIDE : line * WIDE + SIDE, :] = flat_ref[line * SIDE : (line + 1) * SIDE, :]
        wide_ref[line * WIDE + SIDE : (line + 1) * WIDE, :] = jnp.zeros(
            (WIDE - SIDE, wide_ref.shape[1]), wide_ref.dtype
        )


def pack_map_rows(wide_ref, flat_ref):
    for line in range(flat_ref.shape[0] // SIDE):
        flat_ref[line * SIDE : (line + 1) * SIDE, :] = wide_ref[line * WIDE : line * WIDE + SIDE, :]


def clear_gaps(taps_ref, images):
    for gap in range(images + 1):
        taps_ref[:, gap * STRIDE : gap * STRIDE + WIDE, :] = jnp.zeros(
            (3, WIDE, taps_ref.shape[2]), taps_ref.dtype
        )


def store_taps(taps_ref, at, value):
    here = pl.ds(pl.multiple_of(at, WIDE), WIDE)
    taps_ref[0, here, :] = pltpu.roll(value, 1, 0).astype(taps_ref.dtype)
    taps_ref[1, here, :] = value.astype(taps_ref.dtype)
    taps_ref[2, here, :] = pltpu.roll(value, WIDE - 1, 0).astype(taps_ref.dtype)


def call(body, outs, scratch, flops, *args, smem=1):
    specs = tuple(
        pl.BlockSpec(memory_space=pltpu.SMEM)
        if place < smem
        else jax.tree.map(lambda _: pl.BlockSpec(memory_space=pltpu.VMEM), arg)
        for place, arg in enumerate(args)
    )
    moved = sum(a.size * a.dtype.itemsize for a in jax.tree.leaves((args, outs)))
    return pl.pallas_call(
        body,
        out_shape=outs,
        in_specs=specs,
        out_specs=[pl.BlockSpec(memory_space=pltpu.VMEM)] * len(outs),
        scratch_shapes=scratch,
        compiler_params=pltpu.CompilerParams(vmem_limit_bytes=VMEM_LIMIT),
        cost_estimate=pl.CostEstimate(flops=flops, bytes_accessed=moved, transcendentals=0),
        name=getattr(body, "func", body).__name__,
    )(*args)


def shape(dims, kind=F32):
    return jax.ShapeDtypeStruct(dims, kind)


def reduce_in(
    counts_ref,
    x0,
    x1,
    x2,
    x3,
    a0,
    a1,
    a2,
    a3,
    pre_ref,
    msg_ref,
    w_ref,
    in_affine_ref,
    mid_affine_ref,
    bias_ref,
    out_affine_ref,
    wall_ref,
    flat_ref,
    small_ref,
):
    place = Place(counts_ref)
    images = wall_ref.shape[0] // place.groups
    spot = lax.broadcasted_iota(jnp.int32, wall_ref.shape, 0)
    real = jnp.zeros(wall_ref.shape, jnp.int32)
    for slot in range(place.groups):
        number = place.images(place.depth ^ (slot >> 1), place.core ^ (slot & 1))
        here = (spot >= slot * images) & (spot < slot * images + number)
        real = jnp.where(here, 1, real)
    wall_ref[...] = real.astype(F32)
    chan, batch = place.chan, place.batch
    own = w_ref.shape[1] // len(SLOTS)
    half = w_ref.shape[2] // 2
    weights = 2 * w_ref.shape[0] * own
    for s, piece in enumerate((a0, a1, a2, a3)):
        here = pl.ds(pl.multiple_of((chan ^ s) * own, own), own)
        for block in range(2 * w_ref.shape[0]):
            lane = slice((block % 2) * half, (block % 2 + 1) * half)
            w_ref[block // 2, here, lane] = piece[block * own : (block + 1) * own, :]
        small = piece[weights:, :].astype(F32)
        small_ref[chan ^ s] = small
        for t in range(2):
            out_affine_ref[t, chan ^ s, :, :half] = small[4 + 2 * t : 5 + 2 * t, :]
            out_affine_ref[t, chan ^ s, :, half:] = small[5 + 2 * t : 6 + 2 * t, :]
    width = own * len(SLOTS)
    for k in range(len(SLOTS)):
        here = slice(k * own, (k + 1) * own)
        there = slice(width + k * own, width + (k + 1) * own)
        in_affine_ref[0:1, here] = small_ref[k, 0:1, :own]
        in_affine_ref[1:2, here] = small_ref[k, 0:1, own:]
        for t in range(2):
            mid_affine_ref[t : t + 1, here] = small_ref[k, 1 + t : 2 + t, :own]
            mid_affine_ref[t : t + 1, there] = small_ref[k, 1 + t : 2 + t, own:]
        bias_ref[0:1, here] = small_ref[k, 3:4, :own]
        bias_ref[0:1, there] = small_ref[k, 3:4, own:]
    parts = [dot_nt(x[...], w_ref[batch ^ s]) for s, x in enumerate((x0, x1, x2, x3))]
    flat_ref[...] = functools.reduce(jnp.add, parts)
    spread_map_rows(flat_ref, pre_ref)
    first = jnp.zeros((1, pre_ref.shape[1]), F32)
    second = jnp.zeros((1, pre_ref.shape[1]), F32)
    for image in range(pre_ref.shape[0] // PADDED):
        real = place.real(image)
        value = pre_ref[image * PADDED : (image + 1) * PADDED, :]
        first = first + real * total_of(value)
        second = second + real * total_of(value * value)
    msg_ref[...] = jnp.concatenate([first, second], axis=0)


def place_mid(counts_ref, b0, b1, b2, b3, w_ref, w_back_ref):
    place = Place(counts_ref)
    width, lanes = w_ref.shape[1], b0.shape[1]
    own = width // len(SLOTS)
    for s, piece in enumerate((b0, b1, b2, b3)):
        at = pl.multiple_of((place.chan ^ s) * own, own)
        for tap in range(9):
            for r in range(2):
                block = piece[(2 * tap + r) * own : (2 * tap + r + 1) * own, :]
                w_ref[r, pl.ds(at, own), tap * lanes : (tap + 1) * lanes] = block
                w_back_ref[r, pl.ds(tap * width + at, own), :] = block


def place_rest(counts_ref, b0, b1, b2, b3, excite_ref, squeeze_ref, w_out_ref):
    place = Place(counts_ref)
    width, lanes = squeeze_ref.shape
    own = width // len(SLOTS)
    for s, piece in enumerate((b0, b1, b2, b3)):
        at = pl.multiple_of((place.chan ^ s) * own, own)
        for r in range(2):
            excite_ref[pl.ds(r * width + at, own), :] = piece[r * own : (r + 1) * own, :]
        squeeze_ref[pl.ds(at, own), :] = piece[2 * own : 3 * own, :]
        row = 3 * own
        w_out_ref[place.chan ^ s, :, :lanes] = piece[row : row + width, :]
        w_out_ref[place.chan ^ s, :, lanes:] = piece[row + width : row + 2 * width, :]


def conv_mid(
    counts_ref,
    pre_ref,
    sums_refs,
    affine_ref,
    w_ref,
    taps_ref,
    mid_ref,
    msg_ref,
):
    place = Place(counts_ref)
    images = pre_ref.shape[0] // PADDED
    total = place.total() * PIXELS
    sums = summed_over(sums_refs)
    center, scale = moments(sums[0:1], sums[1:2], total)
    gain = affine_ref[0:1, :] * scale
    shift = affine_ref[1:2, :]
    clear_gaps(taps_ref, images)
    keep = columns_real(WIDE)
    for image in range(images):

        def normalize(step, carry, image=image):
            rows = pl.multiple_of(step * WIDE, WIDE)
            value = pre_ref[pl.ds(image * PADDED + rows, WIDE), :]
            value = silu((value - center) * gain + shift) * keep
            store_taps(taps_ref, image * STRIDE + WIDE + rows, value)
            return carry

        lax.fori_loop(0, SIDE, normalize, 0, unroll=UNROLL)
    half = pre_ref.shape[1] // 2
    width = pre_ref.shape[1]
    keep = columns_real(PADDED)
    firsts = [jnp.zeros((1, width), F32) for _ in range(2)]
    seconds = [jnp.zeros((1, width), F32) for _ in range(2)]
    for image in range(images):
        real = place.real(image)
        for r in range(2):
            left = jnp.concatenate(
                [
                    taps_ref[
                        b,
                        image * STRIDE + a * WIDE : image * STRIDE + a * WIDE + PADDED,
                        r * half : (r + 1) * half,
                    ]
                    for a in range(3)
                    for b in range(3)
                ],
                axis=1,
            )
            value = dot_nt(left, w_ref[r])
            mid_ref[image * PADDED : (image + 1) * PADDED, r * width : (r + 1) * width] = value
            held = value * keep
            firsts[r] = firsts[r] + real * total_of(held)
            seconds[r] = seconds[r] + real * total_of(held * held)
    sums = jnp.concatenate(
        [jnp.concatenate(firsts, axis=1), jnp.concatenate(seconds, axis=1)], axis=0
    )
    msg_ref[...] = sums


def mid_norm(
    place,
    sums_refs,
    affine_ref,
):
    sums = summed_over(sums_refs)
    center, scale = moments(sums[0:1], sums[1:2], place.total() * PIXELS)
    return center, scale, affine_ref[0:1, :], affine_ref[1:2, :]


def pool(
    counts_ref,
    mid_ref,
    sums_refs,
    affine_ref,
    squeeze_ref,
    pooled_ref,
    msg_ref,
    incline_ref,
):
    place = Place(counts_ref)
    images = mid_ref.shape[0] // PADDED
    width = mid_ref.shape[1] // 2
    lanes = msg_ref.shape[1]
    center, scale, gain, shift = mid_norm(place, sums_refs, affine_ref)
    keep = columns_real(CHUNK)
    inclines = [[], []]
    for image in range(images):

        def gather(step, carry, image=image):
            active, rise, lean = carry
            at = pl.multiple_of(image * PADDED + step * CHUNK, CHUNK)
            normed = (mid_ref[pl.ds(at, CHUNK), :] - center) * scale
            value = normed * gain + shift
            share = logistic(value)
            active = active + fold(value * share * keep)
            inclined = share * (1.0 + value * (1.0 - share)) * keep
            return active, rise + fold(inclined), lean + fold(inclined * normed)

        nothing = jnp.zeros((8, 2 * width), F32)
        active, rise, lean = lax.fori_loop(
            0, PADDED // CHUNK, gather, (nothing, nothing, nothing), unroll=UNROLL
        )
        active = total_of(active)
        pooled_ref[image : image + 1, :] = (active[:, :width] + active[:, width:]) / PIXELS
        inclines[0].append(total_of(rise))
        inclines[1].append(total_of(lean))
    incline_ref[...] = jnp.concatenate(inclines[0] + inclines[1], axis=0)
    msg_ref[...] = jnp.zeros_like(msg_ref)
    msg_ref[0:images, :] = dot_nn(pooled_ref[...], squeeze_ref[...].astype(F32), HIGHEST)
    real = [place.real(image) * pooled_ref[image : image + 1, :] for image in range(images)]
    real = functools.reduce(jnp.add, real)
    for q in range(width // lanes):
        msg_ref[images + q : images + q + 1, :] = real[:, q * lanes : (q + 1) * lanes]


def gate_norm(
    place,
    rows,
    wall,
):
    return moments(total_of(wall * rows), total_of(wall * rows * rows), place.total())


def attend(
    counts_ref,
    gathered_refs,
    wall_ref,
    gate_affine_ref,
    excite_ref,
    bias_ref,
    mid_ref,
    mid_sums_refs,
    mid_affine_ref,
    w_out_ref,
    gate_ref,
    attention_ref,
    weighted_ref,
    out_ref,
    msg_ref,
    wide_ref,
    flat_ref,
):
    place = Place(counts_ref)
    images = mid_ref.shape[0] // PADDED
    width = mid_ref.shape[1] // 2
    rows = slot_rows(gathered_refs, 8, 0, images)
    center, scale = gate_norm(place, rows, wall_ref[...])
    normed = (rows[0:images] - center) * scale
    gate_pre = normed * gate_affine_ref[0:1, :] + gate_affine_ref[1:2, :]
    gate = silu(gate_pre)
    gate_ref[0] = gate
    gate_ref[1] = slope(gate_pre)
    logits = (
        dot_nt(gate, excite_ref[...].astype(F32), HIGHEST) + bias_ref[...]
    )
    lean = 0.5 * jnp.tanh(0.5 * (logits[:, :width] - logits[:, width:]))
    attention_ref[:, :width] = 0.5 + lean
    attention_ref[:, width:] = 0.5 - lean
    center, scale, gain, shift = mid_norm(place, mid_sums_refs, mid_affine_ref)
    for image in range(images):
        share = attention_ref[image : image + 1, :]

        def weigh(step, carry, image=image, share=share):
            at = pl.multiple_of(image * PADDED + step * CHUNK, CHUNK)
            normed = (mid_ref[pl.ds(at, CHUNK), :] - center) * scale
            value = share * silu(normed * gain + shift)
            wide_ref[pl.ds(at, CHUNK), :] = value[:, :width] + value[:, width:]
            return carry

        lax.fori_loop(0, PADDED // CHUNK, weigh, 0, unroll=UNROLL)
    pack_map_rows(wide_ref, flat_ref)
    weighted_ref[...] = flat_ref[...].astype(BF16)
    spot = lax.broadcasted_iota(jnp.int32, (flat_ref.shape[0], 1), 0)
    real = (spot < place.images(place.depth, place.core) * PIXELS).astype(F32)
    blocks = w_out_ref.shape[0]
    for k in range(blocks):
        value = dot_nn(weighted_ref[...], w_out_ref[place.batch ^ k])
        out_ref[k] = value
        held = value * real
        for t, row in enumerate((total_of(held), total_of(held * value))):
            msg_ref[t * blocks + k : t * blocks + k + 1, :] = row


def finish(
    counts_ref,
    out_ref,
    sums_refs,
    affine_ref,
    x0,
    x1,
    x2,
    x3,
    c0,
    c1,
    c2,
    c3,
    r0,
    r1,
    r2,
    r3,
    grad_ref,
    msg_ref,
):
    place = Place(counts_ref)
    blocks, rows, lanes = out_ref.shape
    sums = summed_over(sums_refs)
    center, scale = moments(sums[:blocks], sums[blocks:], place.total() * PIXELS)
    limit = place.images(place.depth, place.core) * PIXELS
    for k in range(blocks):
        mu, r = center[k : k + 1], scale[k : k + 1]
        block = place.batch ^ k
        gain, shift = affine_ref[0, block], affine_ref[1, block]
        x_ref, cot_ref, result_ref = (x0, x1, x2, x3)[k], (c0, c1, c2, c3)[k], (r0, r1, r2, r3)[k]

        def chunk(
            step, carry, k=k, mu=mu, r=r, gain=gain, shift=shift,
            x_ref=x_ref, cot_ref=cot_ref, result_ref=result_ref,
        ):
            first, second = carry
            at = pl.multiple_of(step * CHUNK, CHUNK)
            here = pl.ds(at, CHUNK)
            spot = lax.broadcasted_iota(jnp.int32, (CHUNK, 1), 0) + at
            real = (spot < limit).astype(F32)
            normed = (out_ref[k, here, :] - mu) * r
            summed = x_ref[here, :].astype(F32) + (normed * gain + shift)
            share = logistic(summed) * real
            result_ref[here, :] = (summed * share).astype(BF16)
            upstream = cot_ref[here, :].astype(F32)
            grad = upstream * share * (1.0 + summed * (1.0 - share))
            grad_ref[k, here, :] = grad
            return first + fold(grad), second + fold(grad * normed)

        nothing = jnp.zeros((8, lanes), F32)
        first, second = lax.fori_loop(
            0, rows // CHUNK, chunk, (nothing, nothing), unroll=UNROLL
        )
        for t, row in enumerate((total_of(first), total_of(second))):
            msg_ref[t * blocks + k : t * blocks + k + 1, :] = row


def back_out(
    counts_ref,
    grad_ref,
    out_ref,
    sums_refs,
    back_refs,
    affine_ref,
    w_out_ref,
    mid_ref,
    mid_sums_refs,
    mid_affine_ref,
    attention_ref,
    gate_ref,
    excite_ref,
    low_ref,
    gw_ref,
    logits_ref,
    msg_ref,
    flat_ref,
):
    place = Place(counts_ref)
    blocks, rows, lanes = out_ref.shape
    images = attention_ref.shape[0]
    width = attention_ref.shape[1] // 2
    total = place.total() * PIXELS
    sums = summed_over(sums_refs)
    center, scale = moments(sums[:blocks], sums[blocks:], total)
    back = summed_over(back_refs) / total
    limit = place.images(place.depth, place.core) * PIXELS
    for k in range(blocks):
        mu, r = center[k : k + 1], scale[k : k + 1]
        gain = affine_ref[0, place.batch ^ k] * r
        first, second = back[k : k + 1], back[blocks + k : blocks + k + 1]

        def chunk(step, carry, k=k, mu=mu, r=r, gain=gain, first=first, second=second):
            at = pl.multiple_of(step * CHUNK, CHUNK)
            here = pl.ds(at, CHUNK)
            spot = lax.broadcasted_iota(jnp.int32, (CHUNK, 1), 0) + at
            real = (spot < limit).astype(F32)
            normed = (out_ref[k, here, :] - mu) * r
            value = gain * (grad_ref[k, here, :] - real * (first + normed * second))
            low_ref[k, here, :] = value.astype(BF16)
            return carry

        lax.fori_loop(0, rows // CHUNK, chunk, 0, unroll=UNROLL)
    parts = [dot_nt(low_ref[k], w_out_ref[place.batch ^ k]) for k in range(blocks)]
    flat_ref[...] = functools.reduce(jnp.add, parts)
    spread_map_rows(flat_ref, gw_ref)
    center, scale, gain, shift = mid_norm(place, mid_sums_refs, mid_affine_ref)
    rises, leans, attended = [], [], []
    for image in range(images):

        def gather(step, carry, image=image):
            attended, rise, lean = carry
            at = pl.multiple_of(image * PADDED + step * CHUNK, CHUNK)
            normed = (mid_ref[pl.ds(at, CHUNK), :] - center) * scale
            value = normed * gain + shift
            share = logistic(value)
            grad = gw_ref[pl.ds(at, CHUNK), :]
            grad = jnp.concatenate([grad, grad], axis=1)
            active = grad * share
            attended = attended + fold(active * value)
            inclined = active * (1.0 + value * (1.0 - share))
            return attended, rise + fold(inclined), lean + fold(inclined * normed)

        nothing = jnp.zeros((8, 2 * width), F32)
        parts = lax.fori_loop(
            0, PADDED // CHUNK, gather, (nothing, nothing, nothing), unroll=UNROLL
        )
        share = attention_ref[image : image + 1, :]
        attended.append(total_of(parts[0]))
        rises.append(share * total_of(parts[1]))
        leans.append(share * total_of(parts[2]))
    grad = jnp.concatenate(attended, axis=0)
    attention = attention_ref[...]
    inner = attention * grad
    inner = inner[:, :width] + inner[:, width:]
    logits = attention * (grad - jnp.concatenate([inner, inner], axis=1))
    logits_ref[...] = logits
    gate = dot_nn(logits, excite_ref[...].astype(F32), HIGHEST) * gate_ref[1]
    pack = msg_ref.shape[1]
    pieces = 2 * width // pack
    for t, row in enumerate((functools.reduce(jnp.add, rises), functools.reduce(jnp.add, leans))):
        for q in range(pieces):
            msg_ref[t * pieces + q : t * pieces + q + 1, :] = row[:, q * pack : (q + 1) * pack]
    msg_ref[2 * pieces : 2 * pieces + images, :] = gate


def back_mid(
    counts_ref,
    back_refs,
    gathered_refs,
    incline_refs,
    wall_ref,
    gate_affine_ref,
    squeeze_ref,
    attention_ref,
    gw_ref,
    mid_ref,
    mid_sums_refs,
    mid_affine_ref,
    pre_ref,
    sums_refs,
    affine_ref,
    w_ref,
    low_ref,
    grad_ref,
    gate_ref,
    vector_ref,
    msg_ref,
    taps_ref,
):
    place = Place(counts_ref)
    images = attention_ref.shape[0]
    width = attention_ref.shape[1] // 2
    lanes = wall_ref.shape[1]
    pieces = 2 * width // lanes
    total = place.total() * PIXELS
    wall = wall_ref[...]
    rows = slot_rows(gathered_refs, 8, 0, images)
    center, scale = gate_norm(place, rows, wall)
    gain = gate_affine_ref[0:1, :] * scale
    normed = (rows - center) * scale
    grads = slot_rows(back_refs, images, 0, images, 2 * pieces)
    first, second = total_of(wall * grads), total_of(wall * grads * normed)
    vector_ref[0:1, 0:lanes] = second
    vector_ref[0:1, lanes : 2 * lanes] = first
    squeezed = gain * (grads - wall * (first + normed * second) / place.total())
    gate_ref[...] = squeezed[0:images]
    pooled_grad = dot_nt(squeezed, squeeze_ref[...].astype(F32), HIGHEST) / PIXELS
    pooled_grad = jnp.concatenate([pooled_grad, pooled_grad], axis=1)
    slot = 0
    terms = jnp.zeros((2 * images, 2 * width), F32)
    for ref in incline_refs:
        inclines = ref[...]
        for at in range(0, inclines.shape[0], 2 * images):
            grad = pooled_grad[slot * images : (slot + 1) * images, :]
            terms = terms + inclines[at : at + 2 * images] * jnp.concatenate([grad, grad], axis=0)
            slot += 1
    sums = functools.reduce(jnp.add, [ref[0 : 2 * pieces, :] for ref in back_refs])
    back = []
    for t in range(2):
        row = [sums[t * pieces + q : t * pieces + q + 1, :] for q in range(pieces)]
        back.append(
            jnp.concatenate(row, axis=1) + total_of(terms[t * images : (t + 1) * images])
        )
    vector_ref[1:2, :] = back[1]
    vector_ref[2:3, :] = back[0]
    own = pooled_grad[0:images]
    first, second = back[0] / total, back[1] / total
    center, scale, gain, shift = mid_norm(place, mid_sums_refs, mid_affine_ref)
    gained = gain * scale
    clear_gaps(taps_ref, images)
    keep = columns_real(WIDE)
    for image in range(images):
        share = attention_ref[image : image + 1, :]
        offset = own[image : image + 1, :]
        real = place.real(image)
        lead, lag = real * first, real * second

        def chunk(step, carry, image=image, share=share, offset=offset, lead=lead, lag=lag):
            rows = pl.multiple_of(step * WIDE, WIDE)
            here = pl.ds(image * PADDED + rows, WIDE)
            normed = (mid_ref[here, :] - center) * scale
            grad = gw_ref[here, :]
            grad = jnp.concatenate([grad, grad], axis=1)
            grad = (share * grad + offset) * slope(normed * gain + shift)
            value = gained * (grad - (lead + normed * lag)) * keep
            store_taps(taps_ref, image * STRIDE + WIDE + rows, value)
            return carry

        lax.fori_loop(0, SIDE, chunk, 0, unroll=UNROLL)
    low_ref[...] = taps_ref[1]
    sums = summed_over(sums_refs)
    center, scale = moments(sums[0:1], sums[1:2], total)
    gain, shift = affine_ref[0:1, :], affine_ref[1:2, :]
    half = width // 2
    keep = columns_real(PADDED)
    firsts = [jnp.zeros((1, half), F32) for _ in range(2)]
    seconds = [jnp.zeros((1, half), F32) for _ in range(2)]
    for image in range(images):
        real = place.real(image)
        here = slice(image * PADDED, (image + 1) * PADDED)
        for r in range(2):
            left = jnp.concatenate(
                [
                    taps_ref[
                        2 - b,
                        image * STRIDE + (2 - a) * WIDE : image * STRIDE + (2 - a) * WIDE + PADDED,
                        r * width : (r + 1) * width,
                    ]
                    for a in range(3)
                    for b in range(3)
                ],
                axis=1,
            )
            lane = slice(r * half, (r + 1) * half)
            normed = (pre_ref[here, lane] - center[:, lane]) * scale[:, lane]
            value = dot_nn(left, w_ref[r]) * slope(normed * gain[:, lane] + shift[:, lane])
            value = value * (keep * real)
            grad_ref[here, lane] = value
            firsts[r] = firsts[r] + total_of(value)
            seconds[r] = seconds[r] + total_of(value * normed)
    sums = jnp.concatenate(
        [jnp.concatenate(firsts, axis=1), jnp.concatenate(seconds, axis=1)], axis=0
    )
    msg_ref[...] = sums


def sort_pieces(
    place,
    source_ref,
    keep_ref,
    send_ref,
    row,
):
    for turn, s in enumerate(ORDER):
        target = keep_ref if turn < 2 else send_ref
        rows = source_ref.shape[1]
        target[turn % 2, row : row + rows, :] = source_ref[place.chan ^ s].astype(BF16)


def weight_out_term(
    counts_ref,
    weighted_ref,
    low_ref,
    gate_ref,
    logits_ref,
    keep_ref,
    send_ref,
    wide_ref,
    small_ref,
):
    place = Place(counts_ref)
    width = weighted_ref.shape[1]
    lanes = keep_ref.shape[2]
    own = width // len(SLOTS)
    for turn, s in enumerate(ORDER):
        target = keep_ref if turn < 2 else send_ref
        held = place.batch ^ place.chan ^ s
        term = dot_tn(weighted_ref[...], low_ref[held]).astype(BF16)
        target[turn % 2, 0:width, :] = term[:, :lanes]
        target[turn % 2, width : 2 * width, :] = term[:, lanes:]
    wide_ref[...] = dot_tn(logits_ref[...], gate_ref[0], HIGHEST)
    for turn, s in enumerate(ORDER):
        target = keep_ref if turn < 2 else send_ref
        for r in range(2):
            at = pl.multiple_of(r * width + (place.chan ^ s) * own, own)
            row = 2 * width + r * own
            target[turn % 2, row : row + own, :] = wide_ref[pl.ds(at, own), :].astype(BF16)
    small_ref[...] = jnp.zeros_like(small_ref)
    bias = total_of(logits_ref[...])
    for k in range(len(SLOTS)):
        small_ref[k, 0:1, :own] = bias[:, k * own : (k + 1) * own]
        small_ref[k, 0:1, own:] = bias[:, width + k * own : width + (k + 1) * own]
    sort_pieces(place, small_ref, keep_ref, send_ref, 2 * width + 2 * own)


def weight_mid_term(
    counts_ref,
    taps_ref,
    low_ref,
    pooled_ref,
    gathered_refs,
    squeezed_ref,
    keep_ref,
    send_ref,
    wide_ref,
    narrow_ref,
):
    place = Place(counts_ref)
    half = taps_ref.shape[2] // 2
    width = low_ref.shape[1] // 2
    own = width // len(SLOTS)
    rows = low_ref.shape[0] - 2 * WIDE
    for r in range(2):
        right = jnp.concatenate(
            [
                taps_ref[b, a * WIDE : a * WIDE + rows, r * half : (r + 1) * half]
                for a in range(3)
                for b in range(3)
            ],
            axis=1,
        )
        wide_ref[...] = dot_tn(low_ref[WIDE : WIDE + rows, r * width : (r + 1) * width], right)
        for turn, s in enumerate(ORDER):
            target = keep_ref if turn < 2 else send_ref
            here = pl.ds(pl.multiple_of((place.chan ^ s) * own, own), own)
            for tap in range(9):
                row = (2 * tap + r) * own
                target[turn % 2, row : row + own, :] = wide_ref[
                    here, tap * half : (tap + 1) * half
                ].astype(BF16)
    images, lanes = pooled_ref.shape[0], squeezed_ref.shape[1]
    mean = [
        total_of(slot_rows(gathered_refs, 8, images + q, 1)) for q in range(width // lanes)
    ]
    mean = jnp.concatenate(mean, axis=1) / place.total()
    narrow_ref[...] = dot_tn(pooled_ref[...] - mean, squeezed_ref[...], HIGHEST)
    for turn, s in enumerate(ORDER):
        target = keep_ref if turn < 2 else send_ref
        here = pl.ds(pl.multiple_of((place.chan ^ s) * own, own), own)
        target[turn % 2, 18 * own : 19 * own, :] = narrow_ref[here, :].astype(BF16)


def back_in(
    share,
    counts_ref,
    grad_ref,
    pre_ref,
    sums_refs,
    back_refs,
    affine_ref,
    x0,
    x1,
    x2,
    x3,
    vector_ref,
    out_back_refs,
    low_ref,
    keep_ref,
    send_ref,
    flat_ref,
    wide_ref,
    small_ref,
):
    place = Place(counts_ref)
    images = pre_ref.shape[0] // PADDED
    width = pre_ref.shape[1]
    own = width // len(SLOTS)
    chan, batch = place.chan, place.batch
    total = place.total() * PIXELS
    sums = summed_over(sums_refs)
    center, scale = moments(sums[0:1], sums[1:2], total)
    back = summed_over(back_refs)
    first, second = back[0:1] / total, back[1:2] / total
    gain = affine_ref[0:1, :] * scale
    for image in range(images):
        real = place.real(image)
        lead, lag = real * first, real * second
        for line in range(SIDE):
            at = image * PADDED + line * WIDE
            normed = (pre_ref[at : at + WIDE, :] - center) * scale
            value = gain * (grad_ref[at : at + WIDE, :] - (lead + normed * lag))
            at = image * PIXELS + line * SIDE
            flat_ref[at : at + SIDE, :] = value[:SIDE]
    low_ref[...] = flat_ref[...].astype(BF16)
    lanes = keep_ref.shape[2]
    for k, x in enumerate((x0, x1, x2, x3)):
        wide_ref[...] = dot_tn(low_ref[...], x[...])
        for turn, s in enumerate(ORDER):
            target = keep_ref if turn < 2 else send_ref
            here = pl.ds(pl.multiple_of((chan ^ s) * own, own), own)
            for part in range(wide_ref.shape[1] // lanes):
                at = pl.multiple_of(((batch ^ k) * (wide_ref.shape[1] // lanes) + part) * own, own)
                target[turn % 2, pl.ds(at, own), :] = wide_ref[
                    here, part * lanes : (part + 1) * lanes
                ].astype(BF16)
    small_ref[...] = jnp.zeros_like(small_ref)
    outs = summed_over(out_back_refs)
    for k in range(len(SLOTS)):
        here = slice(k * own, (k + 1) * own)
        there = slice(width + k * own, width + (k + 1) * own)
        small_ref[k, 0:1, :own] = back[1:2, here]
        small_ref[k, 0:1, own:] = back[0:1, here]
        for t in range(2):
            small_ref[k, 1 + t : 2 + t, :own] = vector_ref[1 + t : 2 + t, here]
            small_ref[k, 1 + t : 2 + t, own:] = vector_ref[1 + t : 2 + t, there]
        small_ref[k, 3:4, :] = vector_ref[0:1, 0:lanes]
        small_ref[k, 4:5, :] = vector_ref[0:1, lanes : 2 * lanes]
    for s in SLOTS:
        for t in range(2):
            row = outs[(1 - t) * len(SLOTS) + s : (1 - t) * len(SLOTS) + s + 1, :]
            small_ref[batch ^ s, 5 + 2 * t : 6 + 2 * t, :] = row[:, :lanes]
            small_ref[batch ^ s, 6 + 2 * t : 7 + 2 * t, :] = row[:, lanes:]
    small_ref[...] = small_ref[...] * share
    sort_pieces(place, small_ref, keep_ref, send_ref, keep_ref.shape[1] - small_ref.shape[1])


def grad_input(
    counts_ref,
    low_ref,
    w_ref,
    summed_ref,
    g0,
    g1,
    g2,
    g3,
):
    place = Place(counts_ref)
    for s, target in enumerate((g0, g1, g2, g3)):
        target[...] = (dot_nn(low_ref[...], w_ref[place.batch ^ s]) + summed_ref[s]).astype(BF16)


def add_groups(terms_ref, sum_ref):
    value = jnp.sum(terms_ref[...].astype(F32), axis=0).astype(BF16)
    sum_ref[...] = jnp.broadcast_to(value[None], sum_ref.shape)


def added(left_ref, right_ref):
    return left_ref[...].astype(F32) + right_ref[...].astype(F32)


def add_core(keep_ref, arrived_ref, kept_ref, send_ref):
    value = added(keep_ref, arrived_ref).astype(BF16)
    kept_ref[...] = value[0]
    send_ref[...] = value[1]


def add_chip(counts_ref, keep_refs, arrived_refs, kept_ref, send_ref, whole_ref):
    place = Place(counts_ref)
    at = 0
    for keep_ref, arrived_ref in zip(keep_refs, arrived_refs):
        whole_ref[at : at + keep_ref.shape[0], :] = added(keep_ref, arrived_ref)
        at += keep_ref.shape[0]
    if at < whole_ref.shape[0]:
        whole_ref[at:, :] = jnp.zeros((whole_ref.shape[0] - at, whole_ref.shape[1]), F32)
    rows = kept_ref.shape[0]
    own = place.parity
    kept_ref[...] = whole_ref[pl.ds(pl.multiple_of(own * rows, 16), rows), :]
    send_ref[...] = whole_ref[pl.ds(pl.multiple_of((1 - own) * rows, 16), rows), :].astype(BF16)


def add_parity(
    counts_ref,
    keep_ref,
    arrived_ref,
    kept_ref,
    s1,
    s2,
    s3,
    whole_ref,
):
    place = Place(counts_ref)
    whole_ref[...] = added(keep_ref, arrived_ref)
    rows = kept_ref.shape[0]
    for t, target in enumerate((kept_ref, s1, s2, s3)):
        at = pl.multiple_of((place.depth ^ t) * rows, 16)
        target[...] = whole_ref[pl.ds(at, rows), :].astype(target.dtype)


def add_depth(keep_ref, arrived_refs, sum_ref):
    value = keep_ref[...]
    for ref in arrived_refs:
        value = value + ref[...].astype(F32)
    sum_ref[...] = value.astype(BF16)


def join_depth(
    counts_ref,
    piece_refs,
    whole_ref,
):
    place = Place(counts_ref)
    rows = piece_refs[0].shape[0]
    for t, ref in enumerate(piece_refs):
        whole_ref[pl.ds(pl.multiple_of((place.depth ^ t) * rows, 16), rows), :] = ref[...]


def join_parity(
    place,
    half_refs,
    whole_ref,
):
    rows = half_refs[0].shape[0]
    for t, ref in enumerate(half_refs):
        at = pl.multiple_of((place.parity ^ t) * rows, 16)
        whole_ref[pl.ds(at, rows), :] = ref[...].astype(F32)


def unpack(
    counts_ref,
    half_refs,
    in_ref,
    mid_ref,
    squeeze_ref,
    excite_ref,
    bias_ref,
    out_ref,
    small_ref,
    whole_ref,
):
    join_parity(Place(counts_ref), half_refs, whole_ref)
    own, lanes = squeeze_ref.shape
    width = out_ref.shape[0]
    out_ref[:, :lanes] = whole_ref[0:width, :]
    out_ref[:, lanes:] = whole_ref[width : 2 * width, :]
    row = 2 * width
    for target in (excite_ref, bias_ref, mid_ref, squeeze_ref):
        target[...] = whole_ref[row : row + target.shape[0], :]
        row += target.shape[0]
    for block in range(in_ref.shape[1] // lanes):
        in_ref[:, block * lanes : (block + 1) * lanes] = whole_ref[row : row + own, :]
        row += own
    small_ref[...] = whole_ref[row : row + small_ref.shape[0], :]


def per_device(
    activations,
    counts,
    weight_in,
    gain_in,
    shift_in,
    weight_mid,
    gain_mid,
    shift_mid,
    weight_squeeze,
    gain_gate,
    shift_gate,
    weight_excite,
    shift_excite,
    weight_out,
    gain_out,
    shift_out,
    cotangent,
    *,
    groups,
    parts,
):
    batches, rows, lanes = activations.shape
    images = rows // PIXELS
    own = weight_in.shape[1]
    width = own * parts
    inter = gain_gate.shape[0]
    wide_rows = images * PADDED
    gap_rows = WIDE + images * STRIDE
    chan, group = lax.axis_index("chan"), lax.axis_index("dp")
    depth = groups // 2

    def permute(tensor, to):
        pairs = []
        for index in range(groups * parts):
            z, x, y, c = index // parts // 2, index // parts % 2, index % parts // 2, index % 2
            z, x, y, c = to(z, x, y, c)
            pairs.append((index, (2 * z + x) * parts + 2 * y + c))
        return lax.ppermute(tensor, ("dp", "chan"), pairs)

    def home(tensor, s):
        return permute(tensor, lambda z, x, y, c: (z, c ^ (s & 1), y ^ (s >> 1), x))

    def away(tensor, s):
        return permute(tensor, lambda z, x, y, c: (z, c, y ^ (s >> 1), x ^ (s & 1)))

    def core(tensor):
        return permute(tensor, lambda z, x, y, c: (z, x, y, c ^ 1))

    def across(tensor):
        return permute(tensor, lambda z, x, y, c: (z, x, y ^ 1, c))

    def parity(tensor):
        return permute(tensor, lambda z, x, y, c: (z, x ^ 1, y, c))

    def along(tensor, t):
        return permute(tensor, lambda z, x, y, c: (z ^ t, x, y, c))

    def after(tensor, *others):
        return lax.optimization_barrier((tensor,) + others)[0]

    def after_all(tensors, *others):
        return lax.optimization_barrier(tuple(tensors) + others)[: len(tensors)]

    def exchange(total, gather):
        def merge(mine, other):
            cut = 0 if total is None else total
            joined = [mine[:cut] + other[:cut]] if cut else []
            if gather:
                joined += [mine[cut : cut + gather], other[cut : cut + gather]]
            return jnp.concatenate(joined) if len(joined) > 1 else joined[0]

        def run(mine):
            nonlocal gather
            mine = merge(mine, core(mine))
            gather = 2 * gather
            if depth <= 4:
                return (mine,) + tuple(along(mine, t) for t in range(1, depth))
            step = 1
            while step < depth:
                mine = merge(mine, along(mine, step))
                gather, step = 2 * gather, 2 * step
            return (mine,)

        return run

    def add_over_chan(keep, send):
        rows = keep.shape[1]
        keep, send = call(
            add_core, [shape((rows, 2 * own), BF16)] * 2, [], 0, keep, core(send), smem=0
        )
        return keep, across(send)

    def add_over_dp(keep, arrived):
        rows = sum(k.shape[0] for k in keep)
        if groups != 8:
            whole = -(-rows // (16 * groups)) * 16 * groups
            terms = jnp.concatenate(keep).astype(F32) + jnp.concatenate(arrived).astype(F32)
            terms = jnp.pad(terms.astype(BF16), ((0, whole - rows), (0, 0)))
            terms = lax.all_to_all(terms.reshape(groups, whole // groups, -1), "dp", 0, 0)
            (terms,) = call(add_groups, [shape(terms.shape, BF16)], [], 0, terms, smem=0)
            terms = lax.all_to_all(terms, "dp", 0, 0).reshape(2, whole // 2, -1)
            swap = group % 2 == 1
            return (
                jnp.where(swap, terms[1], terms[0]),
                jnp.where(swap, terms[0], terms[1]),
            )
        piece = -(-rows // (16 * groups)) * 16
        half = piece * depth
        keep, send = call(
            add_chip,
            [shape((half, 2 * own)), shape((half, 2 * own), BF16)],
            [pltpu.VMEM((2 * half, 2 * own), F32)],
            0,
            counts,
            keep,
            arrived,
        )
        keep, *send = call(
            add_parity,
            [shape((piece, 2 * own))] + [shape((piece, 2 * own), BF16)] * (depth - 1),
            [pltpu.VMEM((half, 2 * own), F32)],
            0,
            counts,
            keep,
            parity(send),
        )
        arrived = tuple(along(send[t - 1], t) for t in range(1, depth))
        (mine,) = call(add_depth, [shape((piece, 2 * own), BF16)], [], 0, keep, arrived, smem=0)
        pieces = (mine,) + tuple(along(mine, t) for t in range(1, depth))
        (mine,) = call(join_depth, [shape((half, 2 * own), BF16)], [], 0, counts, pieces)
        return mine, parity(mine)

    def send_home(tensor):
        pieces = [lax.dynamic_index_in_dim(tensor, chan ^ s, 0, keepdims=False) for s in SLOTS]
        return tuple(home(piece, s) for s, piece in enumerate(pieces))

    x = send_home(activations)
    small = jnp.concatenate(
        [
            jnp.concatenate([gain_in, shift_in])[None],
            gain_mid.reshape(1, 2 * own),
            shift_mid.reshape(1, 2 * own),
            shift_excite.reshape(1, 2 * own),
            gain_out.reshape(-1, 2 * own),
            shift_out.reshape(-1, 2 * own),
            jnp.zeros((8, 2 * own), BF16),
        ]
    )

    def lane_blocks(tensor):
        return [tensor[:, at : at + 2 * own] for at in range(0, tensor.shape[1], 2 * own)]

    first = jnp.concatenate(lane_blocks(weight_in.T) + [small])
    second = weight_mid.transpose(0, 1, 3, 4, 2).reshape(-1, 2 * own)
    third = jnp.concatenate(
        [weight_excite.transpose(1, 2, 0).reshape(-1, inter), weight_squeeze]
        + lane_blocks(weight_out)
    )

    def gather_slots(tensor, *others):
        near, other = core(tensor), across(tensor)
        other = after(other, near, *others)
        return tensor, near, other, core(other)

    first = gather_slots(first, x[0], x[1])
    second = gather_slots(after(second, x[2], x[3], first[2]))
    third = gather_slots(after(third, second[2]))
    gate_affine = jnp.stack([gain_gate, shift_gate]).astype(F32)

    product = 2 * rows * lanes * parts * width
    pre_in, msg, w_in, in_affine, mid_affine, bias, out_affine, wall = call(
        reduce_in,
        [
            shape((wide_rows, width)),
            shape((2, width)),
            shape((parts, width, lanes), BF16),
            shape((2, width)),
            shape((2, 2 * width)),
            shape((1, 2 * width)),
            shape((2, parts, 1, lanes)),
            shape((groups * images, inter)),
        ],
        [pltpu.VMEM((rows, width), F32), pltpu.VMEM((parts, 16, 2 * own), F32)],
        product,
        counts,
        *x,
        *first,
    )
    in_sums = exchange(2, 0)(msg)
    w_mid, w_mid_back = call(
        place_mid,
        [shape((2, width, 9 * inter), BF16), shape((2, 9 * width, inter), BF16)],
        [],
        0,
        counts,
        *second,
    )
    excite, squeeze, w_out = call(
        place_rest,
        [
            shape((2 * width, inter), BF16),
            shape((width, inter), BF16),
            shape((parts, width, lanes), BF16),
        ],
        [],
        0,
        counts,
        *third,
    )
    cot = send_home(after(cotangent, third[2]))
    conv = 2 * wide_rows * 9 * width * width
    taps, mid, msg = call(
        conv_mid,
        [
            shape((3, gap_rows, width), BF16),
            shape((wide_rows, 2 * width)),
            shape((2, 2 * width)),
        ],
        [],
        conv,
        counts,
        pre_in,
        in_sums,
        in_affine,
        w_mid,
    )
    mid_sums = exchange(2, 0)(msg)
    pooled, msg, inclines = call(
        pool,
        [shape((images, width)), shape((8, inter)), shape((2 * images, 2 * width))],
        [],
        0,
        counts,
        mid,
        mid_sums,
        mid_affine,
        squeeze,
    )
    gathered = exchange(None, 8)(msg)
    inclines = exchange(None, 2 * images)(inclines)
    gate, attention, weighted, out, msg = call(
        attend,
        [
            shape((2, images, inter)),
            shape((images, 2 * width)),
            shape((rows, width), BF16),
            shape((parts, rows, lanes)),
            shape((2 * parts, lanes)),
        ],
        [pltpu.VMEM((wide_rows, width), F32), pltpu.VMEM((rows, width), F32)],
        product,
        counts,
        gathered,
        wall,
        gate_affine,
        excite,
        bias,
        mid,
        mid_sums,
        mid_affine,
        w_out,
    )
    out_sums = exchange(2 * parts, 0)(msg)
    *result, grad, msg = call(
        finish,
        [shape((rows, lanes), BF16)] * parts
        + [shape((parts, rows, lanes)), shape((2 * parts, lanes))],
        [],
        0,
        counts,
        out,
        out_sums,
        out_affine,
        *x,
        *cot,
    )
    out_back = exchange(2 * parts, 0)(msg)

    def settle(pieces, *others):
        pieces = after_all([away(piece, s) for s, piece in enumerate(pieces)], *others)
        settled = jnp.zeros((batches, rows, lanes), BF16)
        for s, piece in enumerate(pieces):
            settled = lax.dynamic_update_index_in_dim(settled, piece, chan ^ s, 0)
        return settled

    result = settle(result)

    sums_rows = 2 * 2 * width // inter
    low_out, grad_weighted, grad_logits, msg = call(
        back_out,
        [
            shape((parts, rows, lanes), BF16),
            shape((wide_rows, width)),
            shape((images, 2 * width)),
            shape((sums_rows + images, inter)),
        ],
        [pltpu.VMEM((rows, width), F32)],
        product,
        counts,
        grad,
        out,
        out_sums,
        out_back,
        out_affine,
        w_out,
        mid,
        mid_sums,
        mid_affine,
        attention,
        gate,
        excite,
    )
    mid_back = exchange(sums_rows, images)(msg)
    term_rows = 2 * width + 2 * own + 16
    keep, send = call(
        weight_out_term,
        [shape((2, term_rows, 2 * own), BF16)] * 2,
        [pltpu.VMEM((2 * width, inter), F32), pltpu.VMEM((parts, 16, 2 * own), F32)],
        product,
        counts,
        after(weighted, mid_back[0]),
        low_out,
        gate,
        grad_logits,
    )
    mid_back = after_all(mid_back, keep)
    out_keep, out_arrived = add_over_chan(keep, send)
    low_mid, grad_hidden, grad_squeeze, vectors, msg = call(
        back_mid,
        [
            shape((gap_rows, 2 * width), BF16),
            shape((wide_rows, width)),
            shape((images, inter)),
            shape((8, 2 * width)),
            shape((2, width)),
        ],
        [pltpu.VMEM((3, gap_rows, 2 * width), BF16)],
        conv,
        counts,
        mid_back,
        gathered,
        inclines,
        wall,
        gate_affine,
        squeeze,
        attention,
        grad_weighted,
        mid,
        mid_sums,
        mid_affine,
        pre_in,
        in_sums,
        in_affine,
        w_mid_back,
    )
    in_back = exchange(2, 0)(msg)
    keep, send = call(
        weight_mid_term,
        [shape((2, 19 * own, 2 * own), BF16)] * 2,
        [pltpu.VMEM((width, 9 * inter), F32), pltpu.VMEM((width, inter), F32)],
        conv,
        counts,
        after(taps, in_back[0]),
        low_mid,
        pooled,
        gathered,
        grad_squeeze,
    )
    in_back = after_all(in_back, keep)
    mid_keep, mid_arrived = add_over_chan(keep, send)
    in_rows = parts * lanes // (2 * own) * own
    low_in, keep, send = call(
        functools.partial(back_in, 1.0 / groups),
        [shape((rows, width), BF16)] + [shape((2, in_rows + 16, 2 * own), BF16)] * 2,
        [
            pltpu.VMEM((rows, width), F32),
            pltpu.VMEM((width, lanes), F32),
            pltpu.VMEM((parts, 16, 2 * own), F32),
        ],
        product,
        counts,
        grad_hidden,
        pre_in,
        in_sums,
        in_back,
        in_affine,
        *x,
        vectors,
        out_back,
    )
    in_keep, in_arrived = add_over_chan(keep, send)
    low_in = after(low_in, in_arrived)
    grad_x = call(
        grad_input, [shape((rows, lanes), BF16)] * parts, [], product, counts, low_in, w_in, grad
    )
    halves = add_over_dp((out_keep, mid_keep, in_keep), (out_arrived, mid_arrived, in_arrived))
    g_in, g_mid, g_squeeze, g_excite, g_bias, g_out, sums = call(
        unpack,
        [
            shape((own, parts * lanes)),
            shape((18 * own, inter)),
            shape((own, inter)),
            shape((2 * own, inter)),
            shape((16, 2 * own)),
            shape((width, lanes)),
            shape((16, 2 * own)),
        ],
        [pltpu.VMEM((2 * halves[0].shape[0], 2 * own), F32)],
        0,
        counts,
        halves,
    )
    grad_x = settle(grad_x, g_in)
    outs = lanes // (2 * own)
    return (
        result,
        grad_x,
        g_in.T,
        sums[0, :own],
        sums[0, own:],
        g_mid.reshape(3, 3, 2, own, inter).transpose(0, 1, 4, 2, 3),
        sums[1].reshape(2, own),
        sums[2].reshape(2, own),
        g_squeeze,
        sums[3],
        sums[4],
        g_excite.reshape(2, own, inter).transpose(2, 0, 1),
        g_bias[0].reshape(2, own),
        g_out,
        sums[5 : 5 + outs].reshape(-1),
        sums[5 + outs : 5 + 2 * outs].reshape(-1),
    )


def solution(mesh):
    placed = (
        P(None, "dp", "chan"),
        P(),
        P(None, "chan"),
        P("chan"),
        P("chan"),
        P(None, None, None, None, "chan"),
        P(None, "chan"),
        P(None, "chan"),
        P("chan", None),
        P(),
        P(),
        P(None, None, "chan"),
        P(None, "chan"),
        P(None, "chan"),
        P("chan"),
        P("chan"),
        P(None, "dp", "chan"),
    )
    return jax.shard_map(
        functools.partial(per_device, groups=mesh.shape["dp"], parts=mesh.shape["chan"]),
        mesh=mesh,
        in_specs=placed,
        out_specs=placed[:1] + placed[:1] + placed[2:16],
        check_vma=False,
    )
```

```python
import functools

import jax
import jax.numpy as jnp
from jax import lax
from jax.experimental import pallas as pl
from jax.experimental.pallas import tpu as pltpu
from jax.sharding import PartitionSpec as P

SIDE = 14
PIXELS = SIDE * SIDE
WIDE = 16
PADDED = SIDE * WIDE
STRIDE = PADDED + WIDE
CHUNK = 16
UNROLL = 2
VMEM_LIMIT = 24 * 2**20
SLOTS = (0, 1, 2, 3)
GATHERED = 40
ORDER = (0, 2, 1, 3)
EPSILON = 1e-05
HIGHEST = lax.Precision.HIGHEST
F32 = jnp.float32
BF16 = jnp.bfloat16


def dot_nn(left, right, precision=None):
    return lax.dot_general(
        left, right, (((1,), (0,)), ((), ())), preferred_element_type=F32, precision=precision
    )


def dot_nt(left, right, precision=None):
    return lax.dot_general(
        left, right, (((1,), (1,)), ((), ())), preferred_element_type=F32, precision=precision
    )


def dot_tn(left, right, precision=None):
    return lax.dot_general(
        left, right, (((0,), (0,)), ((), ())), preferred_element_type=F32, precision=precision
    )


def logistic(value):
    return 0.5 + 0.5 * jnp.tanh(0.5 * value)


def silu(value):
    return value * logistic(value)


def slope(value):
    share = logistic(value)
    return share * (1.0 + value * (1.0 - share))


def moments(first, second, total):
    center = first / total
    return center, lax.rsqrt(second / total - center * center + EPSILON)


def fold(value):
    return jnp.sum(value.reshape(-1, 8, value.shape[-1]), axis=0)


def total_of(value):
    return jnp.sum(value, axis=0, keepdims=True)


def columns_real(rows):
    spot = lax.broadcasted_iota(jnp.int32, (rows, 1), 0)
    return (lax.rem(spot, WIDE) < SIDE).astype(F32)


def summed_over(refs):
    values = [ref[...] for ref in refs]
    while len(values) > 1:
        values = [left + right for left, right in zip(values[::2], values[1::2])]
    return values[0]


def slot_rows(refs, size, first, count, skip=0):
    return jnp.concatenate(
        [
            ref[at + first : at + first + count, :]
            for ref in refs
            for at in range(skip, ref.shape[0], size)
        ],
        axis=0,
    )


class Place:
    def __init__(self, counts_ref):
        group = lax.axis_index("dp")
        self.chan = lax.axis_index("chan")
        self.parity, self.depth, self.core = group & 1, group >> 1, self.chan & 1
        self.batch = (self.chan & 2) | self.parity
        self.counts = counts_ref
        self.groups = counts_ref.shape[1]

    def images(self, depth, core):
        return self.counts[self.batch, 2 * depth + core]

    def real(self, image):
        return jnp.where(self.images(self.depth, self.core) > image, 1.0, 0.0).astype(F32)

    def total(self):
        every = [self.counts[self.batch, g] for g in range(self.groups)]
        return functools.reduce(jnp.add, every).astype(F32)


def spread_map_rows(flat_ref, wide_ref):
    for line in range(flat_ref.shape[0] // SIDE):
        wide_ref[line * WIDE : line * WIDE + SIDE, :] = flat_ref[line * SIDE : (line + 1) * SIDE, :]
        wide_ref[line * WIDE + SIDE : (line + 1) * WIDE, :] = jnp.zeros(
            (WIDE - SIDE, wide_ref.shape[1]), wide_ref.dtype
        )


def pack_map_rows(wide_ref, flat_ref):
    for line in range(flat_ref.shape[0] // SIDE):
        flat_ref[line * SIDE : (line + 1) * SIDE, :] = wide_ref[line * WIDE : line * WIDE + SIDE, :]


def clear_gaps(taps_ref, images):
    for gap in range(images + 1):
        taps_ref[:, gap * STRIDE : gap * STRIDE + WIDE, :] = jnp.zeros(
            (3, WIDE, taps_ref.shape[2]), taps_ref.dtype
        )


def store_taps(taps_ref, at, value):
    here = pl.ds(pl.multiple_of(at, WIDE), WIDE)
    taps_ref[0, here, :] = pltpu.roll(value, 1, 0).astype(taps_ref.dtype)
    taps_ref[1, here, :] = value.astype(taps_ref.dtype)
    taps_ref[2, here, :] = pltpu.roll(value, WIDE - 1, 0).astype(taps_ref.dtype)


def call(body, outs, scratch, flops, *args, smem=1):
    specs = tuple(
        pl.BlockSpec(memory_space=pltpu.SMEM)
        if place < smem
        else jax.tree.map(lambda _: pl.BlockSpec(memory_space=pltpu.VMEM), arg)
        for place, arg in enumerate(args)
    )
    moved = sum(a.size * a.dtype.itemsize for a in jax.tree.leaves((args, outs)))
    return pl.pallas_call(
        body,
        out_shape=outs,
        in_specs=specs,
        out_specs=[pl.BlockSpec(memory_space=pltpu.VMEM)] * len(outs),
        scratch_shapes=scratch,
        compiler_params=pltpu.CompilerParams(vmem_limit_bytes=VMEM_LIMIT),
        cost_estimate=pl.CostEstimate(flops=flops, bytes_accessed=moved, transcendentals=0),
        name=getattr(body, "func", body).__name__,
    )(*args)


def shape(dims, kind=F32):
    return jax.ShapeDtypeStruct(dims, kind)


def slot_refs(even_ref, odd_ref, across_ref):
    return even_ref.at[0], odd_ref.at[0], across_ref.at[0], across_ref.at[1]


def reduce_in(
    counts_ref, x0, x1, x2, x3, a0, a1, a2, a3, pre_ref, msg_ref, w_ref, wall_ref, flat_ref
):
    place = Place(counts_ref)
    images = wall_ref.shape[0] // place.groups
    spot = lax.broadcasted_iota(jnp.int32, wall_ref.shape, 0)
    real = jnp.zeros(wall_ref.shape, jnp.int32)
    for slot in range(place.groups):
        number = place.images(place.depth ^ (slot >> 1), place.core ^ (slot & 1))
        here = (spot >= slot * images) & (spot < slot * images + number)
        real = jnp.where(here, 1, real)
    wall_ref[...] = real.astype(F32)
    own = w_ref.shape[1] // len(SLOTS)
    lanes = w_ref.shape[2]
    for s, piece in enumerate((a0, a1, a2, a3)):
        here = pl.ds(pl.multiple_of((place.chan ^ s) * own, own), own)
        for block in range(w_ref.shape[0]):
            w_ref[block, here, :] = piece[:, block * lanes : (block + 1) * lanes]
    parts = [dot_nt(x[...], w_ref[place.batch ^ s]) for s, x in enumerate((x0, x1, x2, x3))]
    flat_ref[...] = functools.reduce(jnp.add, parts)
    spread_map_rows(flat_ref, pre_ref)
    first = jnp.zeros((1, pre_ref.shape[1]), F32)
    second = jnp.zeros((1, pre_ref.shape[1]), F32)
    for image in range(pre_ref.shape[0] // PADDED):
        real = place.real(image)
        value = pre_ref[image * PADDED : (image + 1) * PADDED, :]
        first = first + real * total_of(value)
        second = second + real * total_of(value * value)
    msg_ref[...] = jnp.concatenate([first, second], axis=0)


def place_mid(
    counts_ref,
    b0,
    b1,
    b2,
    b3,
    w_ref,
    w_back_ref,
    squeeze_ref,
    in_affine_ref,
    mid_affine_ref,
    bias_ref,
    out_affine_ref,
    small_ref,
):
    place = Place(counts_ref)
    width, lanes = w_ref.shape[1], b0.shape[1]
    own = width // len(SLOTS)
    for s, piece in enumerate((b0, b1, b2, b3)):
        at = pl.multiple_of((place.chan ^ s) * own, own)
        for tap in range(9):
            for r in range(2):
                block = piece[(2 * tap + r) * own : (2 * tap + r + 1) * own, :]
                w_ref[r, pl.ds(at, own), tap * lanes : (tap + 1) * lanes] = block
                w_back_ref[r, pl.ds(tap * width + at, own), :] = block
        squeeze_ref[pl.ds(at, own), :] = piece[18 * own : 19 * own, :]
        small = piece[19 * own : 19 * own + 16, :].astype(F32)
        small_ref[place.chan ^ s] = small
        for t in range(2):
            out_affine_ref[t, place.chan ^ s, :, :lanes] = small[4 + 2 * t : 5 + 2 * t, :]
            out_affine_ref[t, place.chan ^ s, :, lanes:] = small[5 + 2 * t : 6 + 2 * t, :]
    for k in range(len(SLOTS)):
        here = slice(k * own, (k + 1) * own)
        there = slice(width + k * own, width + (k + 1) * own)
        in_affine_ref[0:1, here] = small_ref[k, 0:1, :own]
        in_affine_ref[1:2, here] = small_ref[k, 0:1, own:]
        for t in range(2):
            mid_affine_ref[t : t + 1, here] = small_ref[k, 1 + t : 2 + t, :own]
            mid_affine_ref[t : t + 1, there] = small_ref[k, 1 + t : 2 + t, own:]
        bias_ref[0:1, here] = small_ref[k, 3:4, :own]
        bias_ref[0:1, there] = small_ref[k, 3:4, own:]


def place_rest(counts_ref, b0, b1, b2, b3, excite_ref, w_out_ref):
    place = Place(counts_ref)
    width, lanes = w_out_ref.shape[1], b0.shape[1]
    own = width // len(SLOTS)
    for s, piece in enumerate((b0, b1, b2, b3)):
        row = 19 * own + 16
        for r in range(2):
            at = pl.multiple_of(r * width + (place.chan ^ s) * own, own)
            excite_ref[pl.ds(at, own), :] = piece[row : row + own, :]
            row += own
        w_out_ref[place.chan ^ s, :, :lanes] = piece[row : row + width, :]
        w_out_ref[place.chan ^ s, :, lanes:] = piece[row + width : row + 2 * width, :]


def conv_mid(
    counts_ref,
    pre_ref,
    sums_refs,
    affine_ref,
    w_ref,
    taps_ref,
    mid_ref,
    msg_ref,
):
    place = Place(counts_ref)
    images = pre_ref.shape[0] // PADDED
    total = place.total() * PIXELS
    sums = summed_over(sums_refs)
    center, scale = moments(sums[0:1], sums[1:2], total)
    gain = affine_ref[0:1, :] * scale
    shift = affine_ref[1:2, :]
    clear_gaps(taps_ref, images)
    keep = columns_real(WIDE)
    for image in range(images):

        def normalize(step, carry, image=image):
            rows = pl.multiple_of(step * WIDE, WIDE)
            value = pre_ref[pl.ds(image * PADDED + rows, WIDE), :]
            value = silu((value - center) * gain + shift) * keep
            store_taps(taps_ref, image * STRIDE + WIDE + rows, value)
            return carry

        lax.fori_loop(0, SIDE, normalize, 0, unroll=UNROLL)
    half = pre_ref.shape[1] // 2
    width = pre_ref.shape[1]
    keep = columns_real(PADDED)
    firsts = [jnp.zeros((1, width), F32) for _ in range(2)]
    seconds = [jnp.zeros((1, width), F32) for _ in range(2)]
    for image in range(images):
        real = place.real(image)
        for r in range(2):
            left = jnp.concatenate(
                [
                    taps_ref[
                        b,
                        image * STRIDE + a * WIDE : image * STRIDE + a * WIDE + PADDED,
                        r * half : (r + 1) * half,
                    ]
                    for a in range(3)
                    for b in range(3)
                ],
                axis=1,
            )
            value = dot_nt(left, w_ref[r])
            mid_ref[image * PADDED : (image + 1) * PADDED, r * width : (r + 1) * width] = value
            held = value * keep
            firsts[r] = firsts[r] + real * total_of(held)
            seconds[r] = seconds[r] + real * total_of(held * held)
    sums = jnp.concatenate(
        [jnp.concatenate(firsts, axis=1), jnp.concatenate(seconds, axis=1)], axis=0
    )
    msg_ref[...] = sums


def mid_norm(
    place,
    sums_refs,
    affine_ref,
):
    sums = summed_over(sums_refs)
    center, scale = moments(sums[0:1], sums[1:2], place.total() * PIXELS)
    return center, scale, affine_ref[0:1, :], affine_ref[1:2, :]


def pool(
    counts_ref,
    mid_ref,
    sums_refs,
    affine_ref,
    squeeze_ref,
    pooled_ref,
    msg_ref,
):
    place = Place(counts_ref)
    images = mid_ref.shape[0] // PADDED
    width = mid_ref.shape[1] // 2
    lanes = msg_ref.shape[1]
    center, scale, gain, shift = mid_norm(place, sums_refs, affine_ref)
    keep = columns_real(CHUNK)
    inclines = [[], []]
    for image in range(images):

        def gather(step, carry, image=image):
            active, rise, lean = carry
            at = pl.multiple_of(image * PADDED + step * CHUNK, CHUNK)
            normed = (mid_ref[pl.ds(at, CHUNK), :] - center) * scale
            value = normed * gain + shift
            share = logistic(value)
            active = active + fold(value * share * keep)
            inclined = share * (1.0 + value * (1.0 - share)) * keep
            return active, rise + fold(inclined), lean + fold(inclined * normed)

        nothing = jnp.zeros((8, 2 * width), F32)
        active, rise, lean = lax.fori_loop(
            0, PADDED // CHUNK, gather, (nothing, nothing, nothing), unroll=UNROLL
        )
        active = total_of(active)
        pooled_ref[image : image + 1, :] = (active[:, :width] + active[:, width:]) / PIXELS
        inclines[0].append(total_of(rise))
        inclines[1].append(total_of(lean))
    inclined = jnp.concatenate(inclines[0] + inclines[1], axis=0)
    msg_ref[...] = jnp.zeros_like(msg_ref)
    for q in range(2 * width // lanes):
        row = 8 + q * 2 * images
        msg_ref[row : row + 2 * images, :] = inclined[:, q * lanes : (q + 1) * lanes]
    msg_ref[0:images, :] = dot_nn(pooled_ref[...], squeeze_ref[...].astype(F32), HIGHEST)
    real = [place.real(image) * pooled_ref[image : image + 1, :] for image in range(images)]
    real = functools.reduce(jnp.add, real)
    for q in range(width // lanes):
        msg_ref[images + q : images + q + 1, :] = real[:, q * lanes : (q + 1) * lanes]


def gate_norm(
    place,
    rows,
    wall,
):
    return moments(total_of(wall * rows), total_of(wall * rows * rows), place.total())


def attend(
    counts_ref,
    gathered_refs,
    wall_ref,
    gate_affine_ref,
    excite_ref,
    bias_ref,
    mid_ref,
    mid_sums_refs,
    mid_affine_ref,
    w_out_ref,
    gate_ref,
    attention_ref,
    weighted_ref,
    out_ref,
    msg_ref,
    wide_ref,
    flat_ref,
):
    place = Place(counts_ref)
    images = mid_ref.shape[0] // PADDED
    width = mid_ref.shape[1] // 2
    rows = slot_rows(gathered_refs, GATHERED, 0, images)
    center, scale = gate_norm(place, rows, wall_ref[...])
    normed = (rows[0:images] - center) * scale
    gate_pre = normed * gate_affine_ref[0:1, :] + gate_affine_ref[1:2, :]
    gate = silu(gate_pre)
    gate_ref[0] = gate
    gate_ref[1] = slope(gate_pre)
    logits = (
        dot_nt(gate, excite_ref[...].astype(F32), HIGHEST) + bias_ref[...]
    )
    lean = 0.5 * jnp.tanh(0.5 * (logits[:, :width] - logits[:, width:]))
    attention_ref[:, :width] = 0.5 + lean
    attention_ref[:, width:] = 0.5 - lean
    center, scale, gain, shift = mid_norm(place, mid_sums_refs, mid_affine_ref)
    for image in range(images):
        share = attention_ref[image : image + 1, :]

        def weigh(step, carry, image=image, share=share):
            at = pl.multiple_of(image * PADDED + step * CHUNK, CHUNK)
            normed = (mid_ref[pl.ds(at, CHUNK), :] - center) * scale
            value = share * silu(normed * gain + shift)
            wide_ref[pl.ds(at, CHUNK), :] = value[:, :width] + value[:, width:]
            return carry

        lax.fori_loop(0, PADDED // CHUNK, weigh, 0, unroll=UNROLL)
    pack_map_rows(wide_ref, flat_ref)
    weighted_ref[...] = flat_ref[...].astype(BF16)
    spot = lax.broadcasted_iota(jnp.int32, (flat_ref.shape[0], 1), 0)
    real = (spot < place.images(place.depth, place.core) * PIXELS).astype(F32)
    blocks = w_out_ref.shape[0]
    for k in range(blocks):
        value = dot_nn(weighted_ref[...], w_out_ref[place.batch ^ k])
        out_ref[k] = value
        held = value * real
        for t, row in enumerate((total_of(held), total_of(held * value))):
            msg_ref[t * blocks + k : t * blocks + k + 1, :] = row


def finish(
    counts_ref,
    out_ref,
    sums_refs,
    affine_ref,
    x_refs,
    cot_even_ref,
    cot_odd_ref,
    cot_across_ref,
    even_ref,
    odd_ref,
    grad_ref,
    msg_ref,
):
    place = Place(counts_ref)
    cot_refs = slot_refs(cot_even_ref, cot_odd_ref, cot_across_ref)
    blocks, rows, lanes = out_ref.shape
    sums = summed_over(sums_refs)
    center, scale = moments(sums[:blocks], sums[blocks:], place.total() * PIXELS)
    limit = place.images(place.depth, place.core) * PIXELS
    for k in range(blocks):
        mu, r = center[k : k + 1], scale[k : k + 1]
        block = place.batch ^ k
        gain, shift = affine_ref[0, block], affine_ref[1, block]
        x_ref, cot_ref, summed_ref = x_refs[k], cot_refs[k], (even_ref, odd_ref)[k & 1].at[k >> 1]

        def chunk(
            step, carry, k=k, mu=mu, r=r, gain=gain, shift=shift,
            x_ref=x_ref, cot_ref=cot_ref, summed_ref=summed_ref,
        ):
            first, second = carry
            at = pl.multiple_of(step * CHUNK, CHUNK)
            here = pl.ds(at, CHUNK)
            spot = lax.broadcasted_iota(jnp.int32, (CHUNK, 1), 0) + at
            real = (spot < limit).astype(F32)
            normed = (out_ref[k, here, :] - mu) * r
            summed = x_ref[here, :].astype(F32) + (normed * gain + shift)
            summed_ref[here, :] = summed.astype(BF16)
            share = logistic(summed)
            grad = cot_ref[here, :].astype(F32) * real * (share * (1.0 + summed * (1.0 - share)))
            grad_ref[k, here, :] = grad
            return first + fold(grad), second + fold(grad * normed)

        nothing = jnp.zeros((8, lanes), F32)
        first, second = lax.fori_loop(
            0, rows // CHUNK, chunk, (nothing, nothing), unroll=UNROLL
        )
        for t, row in enumerate((total_of(first), total_of(second))):
            msg_ref[t * blocks + k : t * blocks + k + 1, :] = row


def finish_owned(counts_ref, even_ref, odd_ref, across_ref, cot_ref, result_ref, grad_ref):
    chan, group = lax.axis_index("chan"), lax.axis_index("dp")
    pieces = slot_refs(even_ref, odd_ref, across_ref)
    rows = cot_ref.shape[1]
    for s, piece in enumerate(pieces):
        batch = chan ^ s
        limit = counts_ref[batch, group] * PIXELS

        def chunk(step, carry, piece=piece, batch=batch, limit=limit):
            at = pl.multiple_of(step * CHUNK, CHUNK)
            here = pl.ds(at, CHUNK)
            spot = lax.broadcasted_iota(jnp.int32, (CHUNK, 1), 0) + at
            real = (spot < limit).astype(F32)
            summed = piece[here, :].astype(F32)
            share = logistic(summed)
            held = share * real
            result_ref[batch, here, :] = (summed * held).astype(BF16)
            grad = cot_ref[batch, here, :].astype(F32) * (held * (1.0 + summed * (1.0 - share)))
            grad_ref[batch, here, :] = grad.astype(BF16)
            return carry

        lax.fori_loop(0, rows // CHUNK, chunk, 0, unroll=UNROLL)


def back_out(
    counts_ref,
    grad_ref,
    out_ref,
    sums_refs,
    back_refs,
    affine_ref,
    w_out_ref,
    mid_ref,
    mid_sums_refs,
    mid_affine_ref,
    attention_ref,
    gate_ref,
    excite_ref,
    low_ref,
    gw_ref,
    logits_ref,
    msg_ref,
    flat_ref,
):
    place = Place(counts_ref)
    blocks, rows, lanes = out_ref.shape
    images = attention_ref.shape[0]
    width = attention_ref.shape[1] // 2
    total = place.total() * PIXELS
    sums = summed_over(sums_refs)
    center, scale = moments(sums[:blocks], sums[blocks:], total)
    back = summed_over(back_refs) / total
    limit = place.images(place.depth, place.core) * PIXELS
    for k in range(blocks):
        mu, r = center[k : k + 1], scale[k : k + 1]
        gain = affine_ref[0, place.batch ^ k] * r
        first, second = back[k : k + 1], back[blocks + k : blocks + k + 1]

        def chunk(step, carry, k=k, mu=mu, r=r, gain=gain, first=first, second=second):
            at = pl.multiple_of(step * CHUNK, CHUNK)
            here = pl.ds(at, CHUNK)
            spot = lax.broadcasted_iota(jnp.int32, (CHUNK, 1), 0) + at
            real = (spot < limit).astype(F32)
            normed = (out_ref[k, here, :] - mu) * r
            value = gain * (grad_ref[k, here, :] - real * (first + normed * second))
            low_ref[k, here, :] = value.astype(BF16)
            return carry

        lax.fori_loop(0, rows // CHUNK, chunk, 0, unroll=UNROLL)
    parts = [dot_nt(low_ref[k], w_out_ref[place.batch ^ k]) for k in range(blocks)]
    flat_ref[...] = functools.reduce(jnp.add, parts)
    spread_map_rows(flat_ref, gw_ref)
    center, scale, gain, shift = mid_norm(place, mid_sums_refs, mid_affine_ref)
    rises, leans, attended = [], [], []
    for image in range(images):

        def gather(step, carry, image=image):
            attended, rise, lean = carry
            at = pl.multiple_of(image * PADDED + step * CHUNK, CHUNK)
            normed = (mid_ref[pl.ds(at, CHUNK), :] - center) * scale
            value = normed * gain + shift
            share = logistic(value)
            grad = gw_ref[pl.ds(at, CHUNK), :]
            grad = jnp.concatenate([grad, grad], axis=1)
            active = grad * share
            attended = attended + fold(active * value)
            inclined = active * (1.0 + value * (1.0 - share))
            return attended, rise + fold(inclined), lean + fold(inclined * normed)

        nothing = jnp.zeros((8, 2 * width), F32)
        parts = lax.fori_loop(
            0, PADDED // CHUNK, gather, (nothing, nothing, nothing), unroll=UNROLL
        )
        share = attention_ref[image : image + 1, :]
        attended.append(total_of(parts[0]))
        rises.append(share * total_of(parts[1]))
        leans.append(share * total_of(parts[2]))
    grad = jnp.concatenate(attended, axis=0)
    attention = attention_ref[...]
    inner = attention * grad
    inner = inner[:, :width] + inner[:, width:]
    logits = attention * (grad - jnp.concatenate([inner, inner], axis=1))
    logits_ref[...] = logits
    gate = dot_nn(logits, excite_ref[...].astype(F32), HIGHEST) * gate_ref[1]
    pack = msg_ref.shape[1]
    pieces = 2 * width // pack
    for t, row in enumerate((functools.reduce(jnp.add, rises), functools.reduce(jnp.add, leans))):
        for q in range(pieces):
            msg_ref[t * pieces + q : t * pieces + q + 1, :] = row[:, q * pack : (q + 1) * pack]
    msg_ref[2 * pieces : 2 * pieces + images, :] = gate


def back_mid(
    counts_ref,
    back_refs,
    gathered_refs,
    wall_ref,
    gate_affine_ref,
    squeeze_ref,
    attention_ref,
    gw_ref,
    mid_ref,
    mid_sums_refs,
    mid_affine_ref,
    pre_ref,
    sums_refs,
    affine_ref,
    w_ref,
    low_ref,
    grad_ref,
    gate_ref,
    vector_ref,
    msg_ref,
    taps_ref,
):
    place = Place(counts_ref)
    images = attention_ref.shape[0]
    width = attention_ref.shape[1] // 2
    lanes = wall_ref.shape[1]
    pieces = 2 * width // lanes
    total = place.total() * PIXELS
    wall = wall_ref[...]
    rows = slot_rows(gathered_refs, GATHERED, 0, images)
    center, scale = gate_norm(place, rows, wall)
    gain = gate_affine_ref[0:1, :] * scale
    normed = (rows - center) * scale
    grads = slot_rows(back_refs, images, 0, images, 2 * pieces)
    first, second = total_of(wall * grads), total_of(wall * grads * normed)
    vector_ref[0:1, 0:lanes] = second
    vector_ref[0:1, lanes : 2 * lanes] = first
    squeezed = gain * (grads - wall * (first + normed * second) / place.total())
    gate_ref[...] = squeezed[0:images]
    pooled_grad = dot_nt(squeezed, squeeze_ref[...].astype(F32), HIGHEST) / PIXELS
    pooled_grad = jnp.concatenate([pooled_grad, pooled_grad], axis=1)
    slot = 0
    terms = jnp.zeros((2 * images, 2 * width), F32)
    for ref in gathered_refs:
        for at in range(8, ref.shape[0], GATHERED):
            inclines = [
                ref[at + q * 2 * images : at + (q + 1) * 2 * images, :] for q in range(pieces)
            ]
            grad = pooled_grad[slot * images : (slot + 1) * images, :]
            grad = jnp.concatenate([grad, grad], axis=0)
            terms = terms + jnp.concatenate(inclines, axis=1) * grad
            slot += 1
    sums = functools.reduce(jnp.add, [ref[0 : 2 * pieces, :] for ref in back_refs])
    back = []
    for t in range(2):
        row = [sums[t * pieces + q : t * pieces + q + 1, :] for q in range(pieces)]
        back.append(
            jnp.concatenate(row, axis=1) + total_of(terms[t * images : (t + 1) * images])
        )
    vector_ref[1:2, :] = back[1]
    vector_ref[2:3, :] = back[0]
    own = pooled_grad[0:images]
    first, second = back[0] / total, back[1] / total
    center, scale, gain, shift = mid_norm(place, mid_sums_refs, mid_affine_ref)
    gained = gain * scale
    clear_gaps(taps_ref, images)
    keep = columns_real(WIDE)
    for image in range(images):
        share = attention_ref[image : image + 1, :]
        offset = own[image : image + 1, :]
        real = place.real(image)
        lead, lag = real * first, real * second

        def chunk(step, carry, image=image, share=share, offset=offset, lead=lead, lag=lag):
            rows = pl.multiple_of(step * WIDE, WIDE)
            here = pl.ds(image * PADDED + rows, WIDE)
            normed = (mid_ref[here, :] - center) * scale
            grad = gw_ref[here, :]
            grad = jnp.concatenate([grad, grad], axis=1)
            grad = (share * grad + offset) * slope(normed * gain + shift)
            value = gained * (grad - (lead + normed * lag)) * keep
            store_taps(taps_ref, image * STRIDE + WIDE + rows, value)
            return carry

        lax.fori_loop(0, SIDE, chunk, 0, unroll=UNROLL)
    low_ref[...] = taps_ref[1]
    sums = summed_over(sums_refs)
    center, scale = moments(sums[0:1], sums[1:2], total)
    gain, shift = affine_ref[0:1, :], affine_ref[1:2, :]
    half = width // 2
    keep = columns_real(PADDED)
    firsts = [jnp.zeros((1, half), F32) for _ in range(2)]
    seconds = [jnp.zeros((1, half), F32) for _ in range(2)]
    for image in range(images):
        real = place.real(image)
        here = slice(image * PADDED, (image + 1) * PADDED)
        for r in range(2):
            left = jnp.concatenate(
                [
                    taps_ref[
                        2 - b,
                        image * STRIDE + (2 - a) * WIDE : image * STRIDE + (2 - a) * WIDE + PADDED,
                        r * width : (r + 1) * width,
                    ]
                    for a in range(3)
                    for b in range(3)
                ],
                axis=1,
            )
            lane = slice(r * half, (r + 1) * half)
            normed = (pre_ref[here, lane] - center[:, lane]) * scale[:, lane]
            value = dot_nn(left, w_ref[r]) * slope(normed * gain[:, lane] + shift[:, lane])
            value = value * (keep * real)
            grad_ref[here, lane] = value
            firsts[r] = firsts[r] + total_of(value)
            seconds[r] = seconds[r] + total_of(value * normed)
    sums = jnp.concatenate(
        [jnp.concatenate(firsts, axis=1), jnp.concatenate(seconds, axis=1)], axis=0
    )
    msg_ref[...] = sums


def sort_pieces(
    place,
    source_ref,
    keep_ref,
    send_ref,
    row,
):
    for turn, s in enumerate(ORDER):
        target = keep_ref if turn < 2 else send_ref
        rows = source_ref.shape[1]
        target[turn % 2, row : row + rows, :] = source_ref[place.chan ^ s].astype(BF16)


def weight_out_term(
    counts_ref,
    weighted_ref,
    low_ref,
    gate_ref,
    logits_ref,
    keep_ref,
    send_ref,
    wide_ref,
    small_ref,
):
    place = Place(counts_ref)
    width = weighted_ref.shape[1]
    lanes = keep_ref.shape[2]
    own = width // len(SLOTS)
    for turn, s in enumerate(ORDER):
        target = keep_ref if turn < 2 else send_ref
        held = place.batch ^ place.chan ^ s
        term = dot_tn(weighted_ref[...], low_ref[held]).astype(BF16)
        target[turn % 2, 0:width, :] = term[:, :lanes]
        target[turn % 2, width : 2 * width, :] = term[:, lanes:]
    wide_ref[...] = dot_tn(logits_ref[...], gate_ref[0], HIGHEST)
    for turn, s in enumerate(ORDER):
        target = keep_ref if turn < 2 else send_ref
        for r in range(2):
            at = pl.multiple_of(r * width + (place.chan ^ s) * own, own)
            row = 2 * width + r * own
            target[turn % 2, row : row + own, :] = wide_ref[pl.ds(at, own), :].astype(BF16)
    small_ref[...] = jnp.zeros_like(small_ref)
    bias = total_of(logits_ref[...])
    for k in range(len(SLOTS)):
        small_ref[k, 0:1, :own] = bias[:, k * own : (k + 1) * own]
        small_ref[k, 0:1, own:] = bias[:, width + k * own : width + (k + 1) * own]
    sort_pieces(place, small_ref, keep_ref, send_ref, 2 * width + 2 * own)


def weight_mid_term(
    counts_ref,
    taps_ref,
    low_ref,
    keep_ref,
    send_ref,
    wide_ref,
):
    place = Place(counts_ref)
    half = taps_ref.shape[2] // 2
    width = low_ref.shape[1] // 2
    own = width // len(SLOTS)
    rows = low_ref.shape[0] - 2 * WIDE
    for r in range(2):
        right = jnp.concatenate(
            [
                taps_ref[b, a * WIDE : a * WIDE + rows, r * half : (r + 1) * half]
                for a in range(3)
                for b in range(3)
            ],
            axis=1,
        )
        wide_ref[...] = dot_tn(low_ref[WIDE : WIDE + rows, r * width : (r + 1) * width], right)
        for turn, s in enumerate(ORDER):
            target = keep_ref if turn < 2 else send_ref
            here = pl.ds(pl.multiple_of((place.chan ^ s) * own, own), own)
            for tap in range(9):
                row = (2 * tap + r) * own
                target[turn % 2, row : row + own, :] = wide_ref[
                    here, tap * half : (tap + 1) * half
                ].astype(BF16)


def back_in(
    share,
    counts_ref,
    grad_ref,
    pre_ref,
    sums_refs,
    back_refs,
    affine_ref,
    x0,
    x1,
    x2,
    x3,
    vector_ref,
    out_back_refs,
    pooled_ref,
    gathered_refs,
    squeezed_ref,
    low_ref,
    keep_ref,
    send_ref,
    flat_ref,
    wide_ref,
    narrow_ref,
    small_ref,
):
    place = Place(counts_ref)
    images = pre_ref.shape[0] // PADDED
    width = pre_ref.shape[1]
    own = width // len(SLOTS)
    chan, batch = place.chan, place.batch
    total = place.total() * PIXELS
    sums = summed_over(sums_refs)
    center, scale = moments(sums[0:1], sums[1:2], total)
    back = summed_over(back_refs)
    first, second = back[0:1] / total, back[1:2] / total
    gain = affine_ref[0:1, :] * scale
    for image in range(images):
        real = place.real(image)
        lead, lag = real * first, real * second
        for line in range(SIDE):
            at = image * PADDED + line * WIDE
            normed = (pre_ref[at : at + WIDE, :] - center) * scale
            value = gain * (grad_ref[at : at + WIDE, :] - (lead + normed * lag))
            at = image * PIXELS + line * SIDE
            flat_ref[at : at + SIDE, :] = value[:SIDE]
    low_ref[...] = flat_ref[...].astype(BF16)
    lanes = keep_ref.shape[2]
    for k, x in enumerate((x0, x1, x2, x3)):
        wide_ref[...] = dot_tn(low_ref[...], x[...])
        for turn, s in enumerate(ORDER):
            target = keep_ref if turn < 2 else send_ref
            here = pl.ds(pl.multiple_of((chan ^ s) * own, own), own)
            for part in range(wide_ref.shape[1] // lanes):
                at = pl.multiple_of(((batch ^ k) * (wide_ref.shape[1] // lanes) + part) * own, own)
                target[turn % 2, pl.ds(at, own), :] = wide_ref[
                    here, part * lanes : (part + 1) * lanes
                ].astype(BF16)
    mean = [
        total_of(slot_rows(gathered_refs, GATHERED, images + q, 1)) for q in range(width // lanes)
    ]
    mean = jnp.concatenate(mean, axis=1) / place.total()
    narrow_ref[...] = dot_tn(pooled_ref[...] - mean, squeezed_ref[...], HIGHEST)
    row = keep_ref.shape[1] - small_ref.shape[1] - own
    for turn, s in enumerate(ORDER):
        target = keep_ref if turn < 2 else send_ref
        here = pl.ds(pl.multiple_of((chan ^ s) * own, own), own)
        target[turn % 2, row : row + own, :] = narrow_ref[here, :].astype(BF16)
    small_ref[...] = jnp.zeros_like(small_ref)
    outs = summed_over(out_back_refs)
    for k in range(len(SLOTS)):
        here = slice(k * own, (k + 1) * own)
        there = slice(width + k * own, width + (k + 1) * own)
        small_ref[k, 0:1, :own] = back[1:2, here]
        small_ref[k, 0:1, own:] = back[0:1, here]
        for t in range(2):
            small_ref[k, 1 + t : 2 + t, :own] = vector_ref[1 + t : 2 + t, here]
            small_ref[k, 1 + t : 2 + t, own:] = vector_ref[1 + t : 2 + t, there]
        small_ref[k, 3:4, :] = vector_ref[0:1, 0:lanes]
        small_ref[k, 4:5, :] = vector_ref[0:1, lanes : 2 * lanes]
    for s in SLOTS:
        for t in range(2):
            row = outs[(1 - t) * len(SLOTS) + s : (1 - t) * len(SLOTS) + s + 1, :]
            small_ref[batch ^ s, 5 + 2 * t : 6 + 2 * t, :] = row[:, :lanes]
            small_ref[batch ^ s, 6 + 2 * t : 7 + 2 * t, :] = row[:, lanes:]
    small_ref[...] = small_ref[...] * share
    sort_pieces(place, small_ref, keep_ref, send_ref, keep_ref.shape[1] - small_ref.shape[1])


def grad_owned(low_refs, w_ref, summed_ref, result_ref):
    chan = lax.axis_index("chan")
    for s, low_ref in enumerate(low_refs):
        value = dot_nn(low_ref[...], w_ref[chan]) + summed_ref[chan ^ s].astype(F32)
        result_ref[chan ^ s] = value.astype(BF16)


def add_groups(terms_ref, sum_ref):
    value = jnp.sum(terms_ref[...].astype(F32), axis=0).astype(BF16)
    sum_ref[...] = jnp.broadcast_to(value[None], sum_ref.shape)


def added(left_ref, right_ref):
    return left_ref[...].astype(F32) + right_ref[...].astype(F32)


def add_core(keep_refs, arrived_refs, kept_ref, send_ref):
    at = 0
    for keep_ref, arrived_ref in zip(keep_refs, arrived_refs):
        value = added(keep_ref, arrived_ref).astype(BF16)
        rows = keep_ref.shape[1]
        kept_ref[at : at + rows, :] = value[0]
        send_ref[at : at + rows, :] = value[1]
        at += rows
    if at < kept_ref.shape[0]:
        for ref in (kept_ref, send_ref):
            ref[at:, :] = jnp.zeros((kept_ref.shape[0] - at, ref.shape[1]), BF16)


def split_rows(parity, whole_ref, kept_ref, send_ref):
    rows = kept_ref.shape[-2]
    mine = pl.ds(pl.multiple_of(parity * rows, 16), rows)
    other = pl.ds(pl.multiple_of((1 - parity) * rows, 16), rows)
    if whole_ref.ndim == 2:
        kept_ref[...] = whole_ref[mine, :]
        send_ref[...] = whole_ref[other, :].astype(BF16)
    else:
        kept_ref[...] = whole_ref[:, mine, :]
        send_ref[...] = whole_ref[:, other, :].astype(BF16)


def add_core_first(counts_ref, keep_ref, arrived_ref, kept_ref, send_ref, whole_ref):
    whole_ref[...] = added(keep_ref, arrived_ref)
    split_rows(Place(counts_ref).parity, whole_ref, kept_ref, send_ref)


def add_parity_first(keep_ref, arrived_ref, kept_ref, send_ref):
    value = added(keep_ref, arrived_ref)
    kept_ref[...] = value[0]
    send_ref[...] = value[1].astype(BF16)


def add_chip(counts_ref, keep_ref, arrived_ref, kept_ref, send_ref, whole_ref):
    whole_ref[...] = added(keep_ref, arrived_ref)
    split_rows(Place(counts_ref).parity, whole_ref, kept_ref, send_ref)


def add_last(counts_ref, keep_refs, arrived_refs, kept_ref, s1, s2, s3, whole_refs):
    place = Place(counts_ref)
    at = 0
    for keep_ref, arrived_ref, whole_ref in zip(keep_refs, arrived_refs, whole_refs):
        whole_ref[...] = added(keep_ref, arrived_ref)
        rows = keep_ref.shape[0] // len(SLOTS)
        for t, target in enumerate((kept_ref, s1, s2, s3)):
            here = pl.ds(pl.multiple_of((place.depth ^ t) * rows, 16), rows)
            target[at : at + rows, :] = whole_ref[here, :].astype(target.dtype)
        at += rows


def add_depth(keep_ref, arrived_refs, sum_ref):
    value = keep_ref[...]
    for ref in arrived_refs:
        value = value + ref[...].astype(F32)
    sum_ref[...] = value.astype(BF16)


def join_depth(
    counts_ref,
    piece_refs,
    whole_ref,
):
    place = Place(counts_ref)
    rows = piece_refs[0].shape[0]
    for t, ref in enumerate(piece_refs):
        whole_ref[pl.ds(pl.multiple_of((place.depth ^ t) * rows, 16), rows), :] = ref[...]


def join_halves(counts_ref, half_refs, first_ref, second_ref):
    place = Place(counts_ref)
    for t, ref in enumerate(half_refs):
        piece = ref.shape[0] // len(SLOTS)
        row = 0
        for target in (first_ref, second_ref):
            rows = target.shape[0] // 2 // len(SLOTS)
            for z in range(len(SLOTS)):
                at = ((place.parity ^ t) * len(SLOTS) + z) * rows
                source = ref[z * piece + row : z * piece + row + rows, :]
                target[pl.ds(pl.multiple_of(at, 16), rows), :] = source.astype(F32)
            row += rows


def unpack(
    joined,
    counts_ref,
    term_refs,
    in_ref,
    gain_in_ref,
    shift_in_ref,
    mid_ref,
    gain_mid_ref,
    shift_mid_ref,
    squeeze_ref,
    gain_gate_ref,
    shift_gate_ref,
    excite_ref,
    bias_ref,
    out_ref,
    gain_out_ref,
    shift_out_ref,
    first_ref,
    second_ref,
):
    if joined:
        first_ref[...] = term_refs[0][...].astype(F32)
        second_ref[...] = term_refs[1][...].astype(F32)
    else:
        join_halves(counts_ref, term_refs, first_ref, second_ref)
    own, lanes = squeeze_ref.shape
    width = out_ref.shape[0]

    def halves(target, row):
        target[0:1, :] = second_ref[row : row + 1, :own]
        target[1:2, :] = second_ref[row : row + 1, own:]

    mid_ref[...] = first_ref[...]
    out_ref[:, :lanes] = second_ref[0:width, :]
    out_ref[:, lanes:] = second_ref[width : 2 * width, :]
    row = 2 * width
    excite_ref[...] = second_ref[row : row + 2 * own, :]
    row += 2 * own
    halves(bias_ref, row)
    row += 16
    for block in range(in_ref.shape[1] // lanes):
        in_ref[:, block * lanes : (block + 1) * lanes] = second_ref[row : row + own, :]
        row += own
    squeeze_ref[...] = second_ref[row : row + own, :]
    row += own
    gain_in_ref[...] = second_ref[row : row + 1, :own]
    shift_in_ref[...] = second_ref[row : row + 1, own:]
    halves(gain_mid_ref, row + 1)
    halves(shift_mid_ref, row + 2)
    gain_gate_ref[...] = second_ref[row + 3 : row + 4, :]
    shift_gate_ref[...] = second_ref[row + 4 : row + 5, :]
    for t, target in enumerate((gain_out_ref, shift_out_ref)):
        target[:, :lanes] = second_ref[row + 5 + 2 * t : row + 6 + 2 * t, :]
        target[:, lanes:] = second_ref[row + 6 + 2 * t : row + 7 + 2 * t, :]


def per_device(
    activations,
    counts,
    weight_in,
    gain_in,
    shift_in,
    weight_mid,
    gain_mid,
    shift_mid,
    weight_squeeze,
    gain_gate,
    shift_gate,
    weight_excite,
    shift_excite,
    weight_out,
    gain_out,
    shift_out,
    cotangent,
    *,
    groups,
    parts,
):
    batches, rows, lanes = activations.shape
    images = rows // PIXELS
    own = weight_in.shape[1]
    width = own * parts
    inter = gain_gate.shape[0]
    wide_rows = images * PADDED
    gap_rows = WIDE + images * STRIDE
    chan, group = lax.axis_index("chan"), lax.axis_index("dp")
    depth = groups // 2

    def permute(tensor, to):
        pairs = []
        for index in range(groups * parts):
            z, x, y, c = index // parts // 2, index // parts % 2, index % parts // 2, index % 2
            z, x, y, c = to(z, x, y, c)
            pairs.append((index, (2 * z + x) * parts + 2 * y + c))
        return lax.ppermute(tensor, ("dp", "chan"), pairs)

    def home(tensor, s):
        return permute(tensor, lambda z, x, y, c: (z, c ^ (s & 1), y ^ (s >> 1), x))

    def away_plane(tensor, odd=0):
        return permute(tensor, lambda z, x, y, c: (z, c, y, x ^ odd))

    def cross(even, odd):
        return even, odd, across(jnp.stack([even[1], odd[1]]))

    def core(tensor):
        return permute(tensor, lambda z, x, y, c: (z, x, y, c ^ 1))

    def across(tensor):
        return permute(tensor, lambda z, x, y, c: (z, x, y ^ 1, c))

    def parity(tensor):
        return permute(tensor, lambda z, x, y, c: (z, x ^ 1, y, c))

    def along(tensor, t):
        return permute(tensor, lambda z, x, y, c: (z ^ t, x, y, c))

    def after(tensor, *others):
        return lax.optimization_barrier((tensor,) + others)[0]

    def after_all(tensors, *others):
        return lax.optimization_barrier(tuple(tensors) + others)[: len(tensors)]

    def exchange(total, gather):
        def merge(mine, other):
            cut = 0 if total is None else total
            joined = [mine[:cut] + other[:cut]] if cut else []
            if gather:
                joined += [mine[cut : cut + gather], other[cut : cut + gather]]
            return jnp.concatenate(joined) if len(joined) > 1 else joined[0]

        def run(mine):
            nonlocal gather
            mine = merge(mine, core(mine))
            gather = 2 * gather
            if depth <= 4:
                return (mine,) + tuple(along(mine, t) for t in range(1, depth))
            step = 1
            while step < depth:
                mine = merge(mine, along(mine, step))
                gather, step = 2 * gather, 2 * step
            return (mine,)

        return run

    def padded(rows):
        return -(-rows // (16 * groups)) * 16 * groups

    def kernel(body, outs, *args, smem=1):
        return call(body, outs, [], 0, *args, smem=smem)

    def add_over_all(first, second, low, result):
        first_rows, second_rows = first[0].shape[1], sum(k.shape[1] for k in second[0])
        if groups != 8:
            rows = padded(first_rows + second_rows)
            keep, send = kernel(
                add_core,
                [shape((rows, 2 * own), BF16)] * 2,
                (first[0],) + second[0],
                (first[1],) + second[1],
                smem=0,
            )
            terms = (keep.astype(F32) + across(send).astype(F32)).astype(BF16)
            terms = lax.all_to_all(terms.reshape(groups, rows // groups, -1), "dp", 0, 0)
            (terms,) = kernel(add_groups, [shape(terms.shape, BF16)], terms, smem=0)
            terms = lax.all_to_all(terms, "dp", 0, 0).reshape(rows, -1)
            terms = terms[:first_rows], terms[first_rows : first_rows + second_rows]
            low = away_plane(low)
            return terms, low, across(low)
        second_rows = padded(second_rows)
        halves = (first_rows // 2, second_rows // 2)
        pieces = (first_rows // groups, second_rows // groups)

        def rows(number, kind=F32):
            return shape((number, 2 * own), kind)

        keep, send = kernel(add_core, [rows(second_rows, BF16)] * 2, *second, smem=0)
        arrived = after(across(send), result)
        pair = (2, halves[0], 2 * own)
        first_keep, send = call(
            add_core_first,
            [shape(pair), shape(pair, BF16)],
            [pltpu.VMEM((2, first_rows, 2 * own), F32)],
            0,
            counts,
            *first,
        )
        first_arrived = parity(send)
        keep, send = call(
            add_chip,
            [rows(halves[1]), rows(halves[1], BF16)],
            [pltpu.VMEM((second_rows, 2 * own), F32)],
            0,
            counts,
            keep,
            arrived,
        )
        arrived = parity(send)
        first_keep, send = kernel(
            add_parity_first,
            [rows(halves[0]), rows(halves[0], BF16)],
            first_keep,
            first_arrived,
            smem=0,
        )
        first_arrived = across(send)
        arrived = after(arrived, first_arrived)
        low = away_plane(after(low, arrived))
        keep, *send = call(
            add_last,
            [rows(sum(pieces))] + [rows(sum(pieces), BF16)] * (depth - 1),
            [tuple(pltpu.VMEM((half, 2 * own), F32) for half in halves)],
            0,
            counts,
            (first_keep, keep),
            (first_arrived, arrived),
        )
        arrived = tuple(along(send[t - 1], t) for t in range(1, depth))
        (mine,) = kernel(add_depth, [rows(sum(pieces), BF16)], keep, arrived, smem=0)
        mine = (mine,) + tuple(along(mine, t) for t in range(1, depth))
        low, low_other = after_all((low, across(low)), *mine)
        (mine,) = kernel(join_depth, [rows(sum(halves), BF16)], counts, mine)
        return (mine, parity(mine)), low, low_other

    def slots_of(tensor, *which):
        return [lax.dynamic_index_in_dim(tensor, chan ^ s, 0, keepdims=False) for s in which]

    first = weight_in.T
    other, near = across(first), core(first)
    far = slots_of(activations, 2, 3)
    x = slots_of(after(activations, near, far[0]), 0, 1) + far
    x = tuple(home(piece, s) for s, piece in enumerate(x))

    small = jnp.concatenate(
        [
            jnp.concatenate([gain_in, shift_in])[None],
            gain_mid.reshape(1, 2 * own),
            shift_mid.reshape(1, 2 * own),
            shift_excite.reshape(1, 2 * own),
            gain_out.reshape(-1, 2 * own),
            shift_out.reshape(-1, 2 * own),
            jnp.zeros((8, 2 * own), BF16),
        ]
    )

    def lane_blocks(tensor):
        return [tensor[:, at : at + 2 * own] for at in range(0, tensor.shape[1], 2 * own)]

    weights = jnp.concatenate(
        [weight_mid.transpose(0, 1, 3, 4, 2).reshape(-1, 2 * own), weight_squeeze, small]
        + [weight_excite.transpose(1, 2, 0).reshape(-1, inter)]
        + lane_blocks(weight_out)
    )
    other = after(other, weights)
    first = (first, near, other, core(other))
    near = core(weights)
    cot = slots_of(after(cotangent, x[0], x[1]), *SLOTS)
    even, odd = jnp.stack([cot[0], cot[2]]), jnp.stack([cot[1], cot[3]])
    other = across(after(weights, x[2], x[3], first[3]))
    even = home(after(even, x[2], x[3]), 0)
    gate_affine = jnp.stack([gain_gate, shift_gate]).astype(F32)

    product = 2 * rows * lanes * parts * width
    pre_in, msg, w_in, wall = call(
        reduce_in,
        [
            shape((wide_rows, width)),
            shape((2, width)),
            shape((parts, width, lanes), BF16),
            shape((groups * images, inter)),
        ],
        [pltpu.VMEM((rows, width), F32)],
        product,
        counts,
        *x,
        *first,
    )
    in_sums = exchange(2, 0)(after(msg, near, odd))
    other = after(other, *in_sums)
    odd = home(after(odd, *in_sums), 1)
    weights = (weights, near, other, core(other))
    w_mid, w_mid_back, squeeze, in_affine, mid_affine, bias, out_affine = call(
        place_mid,
        [
            shape((2, width, 9 * inter), BF16),
            shape((2, 9 * width, inter), BF16),
            shape((width, inter), BF16),
            shape((2, width)),
            shape((2, 2 * width)),
            shape((1, 2 * width)),
            shape((2, parts, 1, lanes)),
        ],
        [pltpu.VMEM((parts, 16, 2 * own), F32)],
        0,
        counts,
        *weights,
    )
    conv = 2 * wide_rows * 9 * width * width
    taps, mid, msg = call(
        conv_mid,
        [
            shape((3, gap_rows, width), BF16),
            shape((wide_rows, 2 * width)),
            shape((2, 2 * width)),
        ],
        [],
        conv,
        counts,
        pre_in,
        in_sums,
        in_affine,
        w_mid,
    )
    mid_sums = exchange(2, 0)(msg)
    even, odd = after_all((even, odd), *mid_sums)
    cot = cross(even, odd)
    excite, w_out = call(
        place_rest,
        [
            shape((2 * width, inter), BF16),
            shape((parts, width, lanes), BF16),
        ],
        [],
        0,
        counts,
        *weights,
    )
    pooled, msg = call(
        pool,
        [shape((images, width)), shape((GATHERED, inter))],
        [],
        0,
        counts,
        mid,
        mid_sums,
        mid_affine,
        squeeze,
    )
    gathered = exchange(None, GATHERED)(msg)
    gate, attention, weighted, out, msg = call(
        attend,
        [
            shape((2, images, inter)),
            shape((images, 2 * width)),
            shape((rows, width), BF16),
            shape((parts, rows, lanes)),
            shape((2 * parts, lanes)),
        ],
        [pltpu.VMEM((wide_rows, width), F32), pltpu.VMEM((rows, width), F32)],
        product,
        counts,
        gathered,
        wall,
        gate_affine,
        excite,
        bias,
        mid,
        mid_sums,
        mid_affine,
        w_out,
    )
    out_sums = exchange(2 * parts, 0)(msg)
    *summed, grad, msg = call(
        finish,
        [shape((2, rows, lanes), BF16)] * 2
        + [shape((parts, rows, lanes)), shape((2 * parts, lanes))],
        [],
        0,
        counts,
        out,
        out_sums,
        out_affine,
        x,
        *cot,
    )
    out_back = exchange(2 * parts, 0)(msg)

    summed = [away_plane(pair, odd) for odd, pair in enumerate(summed)]

    sums_rows = 2 * 2 * width // inter
    low_out, grad_weighted, grad_logits, msg = call(
        back_out,
        [
            shape((parts, rows, lanes), BF16),
            shape((wide_rows, width)),
            shape((images, 2 * width)),
            shape((sums_rows + images, inter)),
        ],
        [pltpu.VMEM((rows, width), F32)],
        product,
        counts,
        grad,
        out,
        out_sums,
        out_back,
        out_affine,
        w_out,
        mid,
        mid_sums,
        mid_affine,
        attention,
        gate,
        excite,
    )
    mid_back = exchange(sums_rows, images)(msg)
    term_rows = 2 * width + 2 * own + 16
    keep, send = call(
        weight_out_term,
        [shape((2, term_rows, 2 * own), BF16)] * 2,
        [pltpu.VMEM((2 * width, inter), F32), pltpu.VMEM((parts, 16, 2 * own), F32)],
        product,
        counts,
        after(weighted, mid_back[0]),
        low_out,
        gate,
        grad_logits,
    )
    out_keep, out_arrived = keep, core(send)
    mid_back = after_all(mid_back, keep, *summed)
    summed = cross(*after_all(summed, mid_back[0]))
    low_mid, grad_hidden, grad_squeeze, vectors, msg = call(
        back_mid,
        [
            shape((gap_rows, 2 * width), BF16),
            shape((wide_rows, width)),
            shape((images, inter)),
            shape((8, 2 * width)),
            shape((2, width)),
        ],
        [pltpu.VMEM((3, gap_rows, 2 * width), BF16)],
        conv,
        counts,
        mid_back,
        gathered,
        wall,
        gate_affine,
        squeeze,
        attention,
        grad_weighted,
        mid,
        mid_sums,
        mid_affine,
        pre_in,
        in_sums,
        in_affine,
        w_mid_back,
    )
    in_back = exchange(2, 0)(msg)
    in_rows = parts * lanes // (2 * own) * own
    low_in, in_keep, in_send = call(
        functools.partial(back_in, 1.0 / groups),
        [shape((rows, width), BF16)] + [shape((2, in_rows + own + 16, 2 * own), BF16)] * 2,
        [
            pltpu.VMEM((rows, width), F32),
            pltpu.VMEM((width, lanes), F32),
            pltpu.VMEM((width, inter), F32),
            pltpu.VMEM((parts, 16, 2 * own), F32),
        ],
        product,
        counts,
        grad_hidden,
        pre_in,
        in_sums,
        in_back,
        in_affine,
        *x,
        vectors,
        out_back,
        pooled,
        gathered,
        grad_squeeze,
    )
    keep, send = call(
        weight_mid_term,
        [shape((2, 18 * own, 2 * own), BF16)] * 2,
        [pltpu.VMEM((width, 9 * inter), F32)],
        conv,
        counts,
        after(taps, low_in),
        low_mid,
    )
    owned = shape((batches, rows, lanes), BF16)
    result, grad_summed = call(finish_owned, [owned, owned], [], 0, counts, *summed, cotangent)
    send = after(send, summed[2])
    terms, low_in, low_other = add_over_all(
        (keep, core(send)),
        ((out_keep, in_keep), (out_arrived, core(in_send))),
        low_in,
        result,
    )
    lows = (low_in, core(low_in), low_other, core(low_other))
    (grad_x,) = call(grad_owned, [owned], [], product, lows, w_in, grad_summed, smem=0)
    terms = after_all(terms, grad_x)
    (
        g_in,
        g_gain_in,
        g_shift_in,
        g_mid,
        g_gain_mid,
        g_shift_mid,
        g_squeeze,
        g_gain_gate,
        g_shift_gate,
        g_excite,
        g_bias,
        g_out,
        g_gain_out,
        g_shift_out,
    ) = call(
        functools.partial(unpack, groups != 8),
        [
            shape((own, parts * lanes)),
            shape((1, own)),
            shape((1, own)),
            shape((18 * own, inter)),
            shape((2, own)),
            shape((2, own)),
            shape((own, inter)),
            shape((1, inter)),
            shape((1, inter)),
            shape((2 * own, inter)),
            shape((2, own)),
            shape((width, lanes)),
            shape((1, lanes)),
            shape((1, lanes)),
        ],
        [
            pltpu.VMEM((18 * own, 2 * own), F32),
            pltpu.VMEM((terms[0].shape[0] * 2 - 18 * own, 2 * own), F32)
            if groups == 8
            else pltpu.VMEM(terms[1].shape, F32),
        ],
        0,
        counts,
        terms,
    )
    return (
        result,
        grad_x,
        g_in.T,
        g_gain_in.reshape(-1),
        g_shift_in.reshape(-1),
        g_mid.reshape(3, 3, 2, own, inter).transpose(0, 1, 4, 2, 3),
        g_gain_mid,
        g_shift_mid,
        g_squeeze,
        g_gain_gate.reshape(-1),
        g_shift_gate.reshape(-1),
        g_excite.reshape(2, own, inter).transpose(2, 0, 1),
        g_bias,
        g_out,
        g_gain_out.reshape(-1),
        g_shift_out.reshape(-1),
    )


def solution(mesh):
    placed = (
        P(None, "dp", "chan"),
        P(),
        P(None, "chan"),
        P("chan"),
        P("chan"),
        P(None, None, None, None, "chan"),
        P(None, "chan"),
        P(None, "chan"),
        P("chan", None),
        P(),
        P(),
        P(None, None, "chan"),
        P(None, "chan"),
        P(None, "chan"),
        P("chan"),
        P("chan"),
        P(None, "dp", "chan"),
    )
    return jax.shard_map(
        functools.partial(per_device, groups=mesh.shape["dp"], parts=mesh.shape["chan"]),
        mesh=mesh,
        in_specs=placed,
        out_specs=placed[:1] + placed[:1] + placed[2:16],
        check_vma=False,
    )
```

```python
import functools

import jax
import jax.numpy as jnp
from jax import lax
from jax.experimental import pallas as pl
from jax.experimental.pallas import tpu as pltpu
from jax.sharding import PartitionSpec as P

SIDE = 14
PIXELS = SIDE * SIDE
WIDE = 16
PADDED = SIDE * WIDE
STRIDE = PADDED + WIDE
CHUNK = 16
UNROLL = 7
VMEM_LIMIT = 24 * 2**20
SLOTS = (0, 1, 2, 3)
GATHERED = 40
ORDER = (0, 2, 1, 3)
EPSILON = 1e-05
HIGHEST = lax.Precision.HIGHEST
F32 = jnp.float32
BF16 = jnp.bfloat16


def dot_nn(left, right, precision=None):
    return lax.dot_general(
        left, right, (((1,), (0,)), ((), ())), preferred_element_type=F32, precision=precision
    )


def parts_of(value):
    high = value.astype(BF16)
    rest = value - high.astype(F32)
    middle = rest.astype(BF16)
    return jnp.concatenate([high, middle, (rest - middle.astype(F32)).astype(BF16)], axis=0)


def exact_dot(dot, left, right):
    rows = -(-left.shape[0] // 16) * 16
    if rows > left.shape[0]:
        left = jnp.concatenate([left, jnp.zeros((rows - left.shape[0], left.shape[1]), F32)], axis=0)
    value = dot(parts_of(left), right)
    return value[:rows] + value[rows : 2 * rows] + value[2 * rows :]


def dot_nt(left, right, precision=None):
    return lax.dot_general(
        left, right, (((1,), (1,)), ((), ())), preferred_element_type=F32, precision=precision
    )


def dot_tn(left, right, precision=None):
    return lax.dot_general(
        left, right, (((0,), (0,)), ((), ())), preferred_element_type=F32, precision=precision
    )


def logistic(value):
    return 0.5 + 0.5 * jnp.tanh(0.5 * value)


def silu(value):
    return value * logistic(value)


def slope(value):
    share = logistic(value)
    return share + value * (share * (1.0 - share))


def moments(first, second, total):
    center = first / total
    return center, lax.rsqrt(second / total - center * center + EPSILON)


def fold(value):
    return jnp.sum(value.reshape(-1, 8, value.shape[-1]), axis=0)


def total_of(value):
    return jnp.sum(value, axis=0, keepdims=True)


def columns_real(rows):
    spot = lax.broadcasted_iota(jnp.int32, (rows, 1), 0)
    return (lax.rem(spot, WIDE) < SIDE).astype(F32)


def summed_over(refs):
    values = [ref[...] for ref in refs]
    while len(values) > 1:
        values = [left + right for left, right in zip(values[::2], values[1::2])]
    return values[0]


def slot_rows(refs, size, first, count, skip=0):
    return jnp.concatenate(
        [
            ref[at + first : at + first + count, :]
            for ref in refs
            for at in range(skip, ref.shape[0], size)
        ],
        axis=0,
    )


class Place:
    def __init__(self, counts_ref):
        group = lax.axis_index("dp")
        self.chan = lax.axis_index("chan")
        self.parity, self.depth, self.core = group & 1, group >> 1, self.chan & 1
        self.batch = (self.chan & 2) | self.parity
        self.counts = counts_ref
        self.groups = counts_ref.shape[1]

    def images(self, depth, core):
        return self.counts[self.batch, 2 * depth + core]

    def real(self, image):
        return jnp.where(self.images(self.depth, self.core) > image, 1.0, 0.0).astype(F32)

    def total(self):
        every = [self.counts[self.batch, g] for g in range(self.groups)]
        return functools.reduce(jnp.add, every).astype(F32)


def spread_map_rows(flat_ref, wide_ref):
    for line in range(flat_ref.shape[0] // SIDE):
        wide_ref[line * WIDE : line * WIDE + SIDE, :] = flat_ref[line * SIDE : (line + 1) * SIDE, :]
        wide_ref[line * WIDE + SIDE : (line + 1) * WIDE, :] = jnp.zeros(
            (WIDE - SIDE, wide_ref.shape[1]), wide_ref.dtype
        )


def pack_map_rows(wide_ref, flat_ref):
    for line in range(flat_ref.shape[0] // SIDE):
        flat_ref[line * SIDE : (line + 1) * SIDE, :] = wide_ref[line * WIDE : line * WIDE + SIDE, :]


def clear_gaps(taps_ref, images):
    for gap in range(images + 1):
        taps_ref[:, gap * STRIDE : gap * STRIDE + WIDE, :] = jnp.zeros(
            (3, WIDE, taps_ref.shape[2]), taps_ref.dtype
        )


def store_taps(taps_ref, at, value):
    here = pl.ds(pl.multiple_of(at, WIDE), WIDE)
    taps_ref[0, here, :] = pltpu.roll(value, 1, 0).astype(taps_ref.dtype)
    taps_ref[1, here, :] = value.astype(taps_ref.dtype)
    taps_ref[2, here, :] = pltpu.roll(value, WIDE - 1, 0).astype(taps_ref.dtype)


def call(body, outs, scratch, flops, *args, smem=1):
    specs = tuple(
        pl.BlockSpec(memory_space=pltpu.SMEM)
        if place < smem
        else jax.tree.map(lambda _: pl.BlockSpec(memory_space=pltpu.VMEM), arg)
        for place, arg in enumerate(args)
    )
    moved = sum(a.size * a.dtype.itemsize for a in jax.tree.leaves((args, outs)))
    return pl.pallas_call(
        body,
        out_shape=outs,
        in_specs=specs,
        out_specs=[pl.BlockSpec(memory_space=pltpu.VMEM)] * len(outs),
        scratch_shapes=scratch,
        compiler_params=pltpu.CompilerParams(vmem_limit_bytes=VMEM_LIMIT),
        cost_estimate=pl.CostEstimate(flops=flops, bytes_accessed=moved, transcendentals=0),
        name=getattr(body, "func", body).__name__,
    )(*args)


def shape(dims, kind=F32):
    return jax.ShapeDtypeStruct(dims, kind)


def slot_refs(even_ref, odd_ref, across_ref):
    return even_ref.at[0], odd_ref.at[0], across_ref.at[0], across_ref.at[1]


def pack(
    mid_ref,
    squeeze_ref,
    gain_in_ref,
    shift_in_ref,
    gain_mid_ref,
    shift_mid_ref,
    bias_ref,
    gain_out_ref,
    shift_out_ref,
    excite_ref,
    out_ref,
    target_ref,
    small_ref,
):
    lanes = target_ref.shape[1]
    own = lanes // 2
    small_ref[...] = jnp.zeros_like(small_ref)
    small_ref[0:1, :own] = gain_in_ref[...].astype(F32)
    small_ref[0:1, own:] = shift_in_ref[...].astype(F32)
    for row, ref in enumerate((gain_mid_ref, shift_mid_ref, bias_ref)):
        value = ref[...].astype(F32)
        small_ref[row + 1 : row + 2, :own] = value[0:1]
        small_ref[row + 1 : row + 2, own:] = value[1:2]
    for t, ref in enumerate((gain_out_ref, shift_out_ref)):
        value = ref[...].astype(F32)
        small_ref[4 + 2 * t : 5 + 2 * t, :] = value[:, :lanes]
        small_ref[5 + 2 * t : 6 + 2 * t, :] = value[:, lanes:]
    row = 0
    for ref in (mid_ref, squeeze_ref, small_ref, excite_ref):
        target_ref[row : row + ref.shape[0], :] = ref[...].astype(BF16)
        row += ref.shape[0]
    for block in range(out_ref.shape[1] // lanes):
        rows = out_ref.shape[0]
        target_ref[row : row + rows, :] = out_ref[:, block * lanes : (block + 1) * lanes]
        row += rows


def reduce_in(
    counts_ref, x0, x1, x2, x3, a0, a1, a2, a3, pre_ref, msg_ref, w_ref, wall_ref, flat_ref
):
    place = Place(counts_ref)
    images = wall_ref.shape[0] // place.groups
    spot = lax.broadcasted_iota(jnp.int32, wall_ref.shape, 0)
    real = jnp.zeros(wall_ref.shape, jnp.int32)
    for slot in range(place.groups):
        number = place.images(place.depth ^ (slot >> 1), place.core ^ (slot & 1))
        here = (spot >= slot * images) & (spot < slot * images + number)
        real = jnp.where(here, 1, real)
    wall_ref[...] = real.astype(F32)
    own = w_ref.shape[1] // len(SLOTS)
    lanes = w_ref.shape[2]
    for s, piece in enumerate((a0, a1, a2, a3)):
        here = pl.ds(pl.multiple_of((place.chan ^ s) * own, own), own)
        for block in range(w_ref.shape[0]):
            w_ref[block, here, :] = piece[:, block * lanes : (block + 1) * lanes]
    parts = [dot_nt(x[...], w_ref[place.batch ^ s]) for s, x in enumerate((x0, x1, x2, x3))]
    flat_ref[...] = functools.reduce(jnp.add, parts)
    spread_map_rows(flat_ref, pre_ref)
    first = jnp.zeros((1, pre_ref.shape[1]), F32)
    second = jnp.zeros((1, pre_ref.shape[1]), F32)
    for image in range(pre_ref.shape[0] // PADDED):
        real = place.real(image)
        value = pre_ref[image * PADDED : (image + 1) * PADDED, :]
        first = first + real * total_of(value)
        second = second + real * total_of(value * value)
    msg_ref[...] = jnp.concatenate([first, second], axis=0)


def place_mid(
    counts_ref,
    b0,
    b1,
    b2,
    b3,
    w_ref,
    w_back_ref,
    squeeze_ref,
    in_affine_ref,
    mid_affine_ref,
    bias_ref,
    out_affine_ref,
    small_ref,
):
    place = Place(counts_ref)
    width, lanes = w_ref.shape[1], b0.shape[1]
    own = width // len(SLOTS)
    for s, piece in enumerate((b0, b1, b2, b3)):
        at = pl.multiple_of((place.chan ^ s) * own, own)
        for tap in range(9):
            for r in range(2):
                block = piece[(2 * tap + r) * own : (2 * tap + r + 1) * own, :]
                w_ref[r, pl.ds(at, own), tap * lanes : (tap + 1) * lanes] = block
                w_back_ref[r, pl.ds(tap * width + at, own), :] = block
        squeeze_ref[pl.ds(at, own), :] = piece[18 * own : 19 * own, :]
        small = piece[19 * own : 19 * own + 16, :].astype(F32)
        small_ref[place.chan ^ s] = small
        for t in range(2):
            out_affine_ref[t, place.chan ^ s, :, :lanes] = small[4 + 2 * t : 5 + 2 * t, :]
            out_affine_ref[t, place.chan ^ s, :, lanes:] = small[5 + 2 * t : 6 + 2 * t, :]
    for k in range(len(SLOTS)):
        here = slice(k * own, (k + 1) * own)
        there = slice(width + k * own, width + (k + 1) * own)
        in_affine_ref[0:1, here] = small_ref[k, 0:1, :own]
        in_affine_ref[1:2, here] = small_ref[k, 0:1, own:]
        for t in range(2):
            mid_affine_ref[t : t + 1, here] = small_ref[k, 1 + t : 2 + t, :own]
            mid_affine_ref[t : t + 1, there] = small_ref[k, 1 + t : 2 + t, own:]
        bias_ref[0:1, here] = small_ref[k, 3:4, :own]
        bias_ref[0:1, there] = small_ref[k, 3:4, own:]


def place_rest(counts_ref, b0, b1, b2, b3, excite_ref, w_out_ref):
    place = Place(counts_ref)
    width, lanes = w_out_ref.shape[1], b0.shape[1]
    own = width // len(SLOTS)
    for s, piece in enumerate((b0, b1, b2, b3)):
        row = 19 * own + 16
        for r in range(2):
            at = pl.multiple_of(r * width + (place.chan ^ s) * own, own)
            excite_ref[pl.ds(at, own), :] = piece[row : row + own, :]
            row += own
        w_out_ref[place.chan ^ s, :, :lanes] = piece[row : row + width, :]
        w_out_ref[place.chan ^ s, :, lanes:] = piece[row + width : row + 2 * width, :]


def conv_mid(
    counts_ref,
    pre_ref,
    sums_refs,
    affine_ref,
    w_ref,
    taps_ref,
    mid_ref,
    msg_ref,
):
    place = Place(counts_ref)
    images = pre_ref.shape[0] // PADDED
    total = place.total() * PIXELS
    sums = summed_over(sums_refs)
    center, scale = moments(sums[0:1], sums[1:2], total)
    gain = affine_ref[0:1, :] * scale
    shift = affine_ref[1:2, :] - center * gain
    clear_gaps(taps_ref, images)
    keep = columns_real(WIDE)
    for image in range(images):

        def normalize(step, carry, image=image):
            rows = pl.multiple_of(step * WIDE, WIDE)
            value = pre_ref[pl.ds(image * PADDED + rows, WIDE), :]
            value = silu(value * gain + shift) * keep
            store_taps(taps_ref, image * STRIDE + WIDE + rows, value)
            return carry

        lax.fori_loop(0, SIDE, normalize, 0, unroll=UNROLL)
    half = pre_ref.shape[1] // 2
    width = pre_ref.shape[1]
    keep = columns_real(PADDED)
    firsts = [jnp.zeros((1, width), F32) for _ in range(2)]
    seconds = [jnp.zeros((1, width), F32) for _ in range(2)]
    for image in range(images):
        real = place.real(image)
        for r in range(2):
            left = jnp.concatenate(
                [
                    taps_ref[
                        b,
                        image * STRIDE + a * WIDE : image * STRIDE + a * WIDE + PADDED,
                        r * half : (r + 1) * half,
                    ]
                    for a in range(3)
                    for b in range(3)
                ],
                axis=1,
            )
            value = dot_nt(left, w_ref[r])
            mid_ref[image * PADDED : (image + 1) * PADDED, r * width : (r + 1) * width] = value
            held = value * keep
            firsts[r] = firsts[r] + real * total_of(held)
            seconds[r] = seconds[r] + real * total_of(held * held)
    sums = jnp.concatenate(
        [jnp.concatenate(firsts, axis=1), jnp.concatenate(seconds, axis=1)], axis=0
    )
    msg_ref[...] = sums


def mid_norm(
    place,
    sums_refs,
    affine_ref,
):
    sums = summed_over(sums_refs)
    center, scale = moments(sums[0:1], sums[1:2], place.total() * PIXELS)
    gain = affine_ref[0:1, :] * scale
    return center, scale, gain, affine_ref[1:2, :] - center * gain


def pool(
    counts_ref,
    mid_ref,
    sums_refs,
    affine_ref,
    squeeze_ref,
    pooled_ref,
    msg_ref,
):
    place = Place(counts_ref)
    images = mid_ref.shape[0] // PADDED
    width = mid_ref.shape[1] // 2
    lanes = msg_ref.shape[1]
    center, scale, gain, shift = mid_norm(place, sums_refs, affine_ref)
    keep = columns_real(CHUNK)
    inclines = [[], []]
    for image in range(images):

        def gather(step, carry, image=image):
            active, rise, lean = carry
            at = pl.multiple_of(image * PADDED + step * CHUNK, CHUNK)
            before = mid_ref[pl.ds(at, CHUNK), :]
            value = before * gain + shift
            share = logistic(value) * keep
            active = active + fold(value * share)
            inclined = share + value * (share * (1.0 - share))
            return active, rise + fold(inclined), lean + fold(inclined * before)

        nothing = jnp.zeros((8, 2 * width), F32)
        active, rise, lean = lax.fori_loop(
            0, PADDED // CHUNK, gather, (nothing, nothing, nothing), unroll=UNROLL
        )
        active = total_of(active)
        pooled_ref[image : image + 1, :] = (active[:, :width] + active[:, width:]) / PIXELS
        rise = total_of(rise)
        inclines[0].append(rise)
        inclines[1].append(scale * (total_of(lean) - center * rise))
    inclined = jnp.concatenate(inclines[0] + inclines[1], axis=0)
    msg_ref[...] = jnp.zeros_like(msg_ref)
    for q in range(2 * width // lanes):
        row = 8 + q * 2 * images
        msg_ref[row : row + 2 * images, :] = inclined[:, q * lanes : (q + 1) * lanes]
    msg_ref[0:images, :] = exact_dot(dot_nn, pooled_ref[...], squeeze_ref[...])[:images]
    real = [place.real(image) * pooled_ref[image : image + 1, :] for image in range(images)]
    real = functools.reduce(jnp.add, real)
    for q in range(width // lanes):
        msg_ref[images + q : images + q + 1, :] = real[:, q * lanes : (q + 1) * lanes]


def gate_norm(
    place,
    rows,
    wall,
):
    return moments(total_of(wall * rows), total_of(wall * rows * rows), place.total())


def attend(
    counts_ref,
    gathered_refs,
    wall_ref,
    gate_affine_ref,
    excite_ref,
    bias_ref,
    mid_ref,
    mid_sums_refs,
    mid_affine_ref,
    w_out_ref,
    gate_ref,
    attention_ref,
    weighted_ref,
    out_ref,
    msg_ref,
    wide_ref,
    flat_ref,
):
    place = Place(counts_ref)
    images = mid_ref.shape[0] // PADDED
    width = mid_ref.shape[1] // 2
    rows = slot_rows(gathered_refs, GATHERED, 0, images)
    center, scale = gate_norm(place, rows, wall_ref[...])
    normed = (rows[0:images] - center) * scale
    gate_pre = normed * gate_affine_ref[0:1, :] + gate_affine_ref[1:2, :]
    gate = silu(gate_pre)
    gate_ref[0] = gate
    gate_ref[1] = slope(gate_pre)
    logits = (
        exact_dot(dot_nt, gate, excite_ref[...])[:images] + bias_ref[...]
    )
    lean = 0.5 * jnp.tanh(0.5 * (logits[:, :width] - logits[:, width:]))
    attention_ref[:, :width] = 0.5 + lean
    attention_ref[:, width:] = 0.5 - lean
    center, scale, gain, shift = mid_norm(place, mid_sums_refs, mid_affine_ref)
    for image in range(images):
        share = attention_ref[image : image + 1, :]

        def weigh(step, carry, image=image, share=share):
            at = pl.multiple_of(image * PADDED + step * CHUNK, CHUNK)
            value = share * silu(mid_ref[pl.ds(at, CHUNK), :] * gain + shift)
            wide_ref[pl.ds(at, CHUNK), :] = value[:, :width] + value[:, width:]
            return carry

        lax.fori_loop(0, PADDED // CHUNK, weigh, 0, unroll=UNROLL)
    pack_map_rows(wide_ref, flat_ref)
    weighted_ref[...] = flat_ref[...].astype(BF16)
    spot = lax.broadcasted_iota(jnp.int32, (flat_ref.shape[0], 1), 0)
    real = (spot < place.images(place.depth, place.core) * PIXELS).astype(F32)
    blocks = w_out_ref.shape[0]
    for k in range(blocks):
        value = dot_nn(weighted_ref[...], w_out_ref[place.batch ^ k])
        out_ref[k] = value
        held = value * real
        for t, row in enumerate((total_of(held), total_of(held * value))):
            msg_ref[t * blocks + k : t * blocks + k + 1, :] = row


def finish(
    counts_ref,
    out_ref,
    sums_refs,
    affine_ref,
    x_refs,
    cot_even_ref,
    cot_odd_ref,
    cot_across_ref,
    even_ref,
    odd_ref,
    grad_ref,
    msg_ref,
):
    place = Place(counts_ref)
    cot_refs = slot_refs(cot_even_ref, cot_odd_ref, cot_across_ref)
    blocks, rows, lanes = out_ref.shape
    sums = summed_over(sums_refs)
    center, scale = moments(sums[:blocks], sums[blocks:], place.total() * PIXELS)
    limit = place.images(place.depth, place.core) * PIXELS
    for k in range(blocks):
        mu, r = center[k : k + 1], scale[k : k + 1]
        block = place.batch ^ k
        gain = affine_ref[0, block] * r
        shift = affine_ref[1, block] - mu * gain
        x_ref, upstream_ref = x_refs[k], cot_refs[k]
        summed_ref = (even_ref, odd_ref)[k & 1].at[k >> 1]

        def chunk(
            step, carry, k=k, gain=gain, shift=shift,
            x_ref=x_ref, upstream_ref=upstream_ref, summed_ref=summed_ref,
        ):
            first, second = carry
            at = pl.multiple_of(step * CHUNK, CHUNK)
            here = pl.ds(at, CHUNK)
            spot = lax.broadcasted_iota(jnp.int32, (CHUNK, 1), 0) + at
            real = (spot < limit).astype(F32)
            before = out_ref[k, here, :]
            summed = x_ref[here, :].astype(F32) + (before * gain + shift)
            summed_ref[here, :] = summed.astype(BF16)
            share = logistic(summed)
            grad = upstream_ref[here, :].astype(F32) * real * (share * (1.0 + summed * (1.0 - share)))
            grad_ref[k, here, :] = grad
            return first + fold(grad), second + fold(grad * before)

        nothing = jnp.zeros((8, lanes), F32)
        first, second = lax.fori_loop(
            0, rows // CHUNK, chunk, (nothing, nothing), unroll=UNROLL
        )
        first = total_of(first)
        for t, row in enumerate((first, r * (total_of(second) - mu * first))):
            msg_ref[t * blocks + k : t * blocks + k + 1, :] = row


def finish_owned(counts_ref, even_ref, odd_ref, across_ref, cot_ref, result_ref, grad_ref):
    chan, group = lax.axis_index("chan"), lax.axis_index("dp")
    pieces = slot_refs(even_ref, odd_ref, across_ref)
    rows = cot_ref.shape[1]
    for s, piece in enumerate(pieces):
        batch = chan ^ s
        limit = counts_ref[batch, group] * PIXELS

        def chunk(step, carry, piece=piece, batch=batch, limit=limit):
            at = pl.multiple_of(step * CHUNK, CHUNK)
            here = pl.ds(at, CHUNK)
            spot = lax.broadcasted_iota(jnp.int32, (CHUNK, 1), 0) + at
            real = (spot < limit).astype(F32)
            summed = piece[here, :].astype(F32)
            share = logistic(summed)
            held = share * real
            result_ref[batch, here, :] = (summed * held).astype(BF16)
            grad = cot_ref[batch, here, :].astype(F32) * (held * (1.0 + summed * (1.0 - share)))
            grad_ref[batch, here, :] = grad.astype(BF16)
            return carry

        lax.fori_loop(0, rows // CHUNK, chunk, 0, unroll=UNROLL)


def back_out(
    counts_ref,
    grad_ref,
    out_ref,
    sums_refs,
    back_refs,
    affine_ref,
    w_out_ref,
    mid_ref,
    mid_sums_refs,
    mid_affine_ref,
    attention_ref,
    gate_ref,
    excite_ref,
    low_ref,
    gw_ref,
    logits_ref,
    msg_ref,
    flat_ref,
):
    place = Place(counts_ref)
    blocks, rows, lanes = out_ref.shape
    images = attention_ref.shape[0]
    width = attention_ref.shape[1] // 2
    total = place.total() * PIXELS
    sums = summed_over(sums_refs)
    center, scale = moments(sums[:blocks], sums[blocks:], total)
    back = summed_over(back_refs) / total
    limit = place.images(place.depth, place.core) * PIXELS
    for k in range(blocks):
        mu, r = center[k : k + 1], scale[k : k + 1]
        gain = affine_ref[0, place.batch ^ k] * r
        second = gain * r * back[blocks + k : blocks + k + 1]
        first = gain * back[k : k + 1] - mu * second

        def chunk(step, carry, k=k, gain=gain, first=first, second=second):
            at = pl.multiple_of(step * CHUNK, CHUNK)
            here = pl.ds(at, CHUNK)
            spot = lax.broadcasted_iota(jnp.int32, (CHUNK, 1), 0) + at
            real = (spot < limit).astype(F32)
            value = gain * grad_ref[k, here, :] - real * (first + out_ref[k, here, :] * second)
            low_ref[k, here, :] = value.astype(BF16)
            return carry

        lax.fori_loop(0, rows // CHUNK, chunk, 0, unroll=UNROLL)
    parts = [dot_nt(low_ref[k], w_out_ref[place.batch ^ k]) for k in range(blocks)]
    flat_ref[...] = functools.reduce(jnp.add, parts)
    spread_map_rows(flat_ref, gw_ref)
    center, scale, gain, shift = mid_norm(place, mid_sums_refs, mid_affine_ref)
    rises, leans, attended = [], [], []
    for image in range(images):

        def gather(step, carry, image=image):
            attended, rise, lean = carry
            at = pl.multiple_of(image * PADDED + step * CHUNK, CHUNK)
            before = mid_ref[pl.ds(at, CHUNK), :]
            value = before * gain + shift
            share = logistic(value)
            grad = gw_ref[pl.ds(at, CHUNK), :]
            grad = jnp.concatenate([grad, grad], axis=1)
            active = grad * share
            attended = attended + fold(active * value)
            inclined = active * (1.0 + value * (1.0 - share))
            return attended, rise + fold(inclined), lean + fold(inclined * before)

        nothing = jnp.zeros((8, 2 * width), F32)
        parts = lax.fori_loop(
            0, PADDED // CHUNK, gather, (nothing, nothing, nothing), unroll=UNROLL
        )
        share = attention_ref[image : image + 1, :]
        attended.append(total_of(parts[0]))
        rise = total_of(parts[1])
        rises.append(share * rise)
        leans.append(share * (scale * (total_of(parts[2]) - center * rise)))
    grad = jnp.concatenate(attended, axis=0)
    attention = attention_ref[...]
    inner = attention * grad
    inner = inner[:, :width] + inner[:, width:]
    logits = attention * (grad - jnp.concatenate([inner, inner], axis=1))
    logits_ref[...] = logits
    gate = exact_dot(dot_nn, logits, excite_ref[...])[:images] * gate_ref[1]
    pack = msg_ref.shape[1]
    pieces = 2 * width // pack
    for t, row in enumerate((functools.reduce(jnp.add, rises), functools.reduce(jnp.add, leans))):
        for q in range(pieces):
            msg_ref[t * pieces + q : t * pieces + q + 1, :] = row[:, q * pack : (q + 1) * pack]
    msg_ref[2 * pieces : 2 * pieces + images, :] = gate


def back_mid(
    counts_ref,
    back_refs,
    gathered_refs,
    wall_ref,
    gate_affine_ref,
    squeeze_ref,
    attention_ref,
    gw_ref,
    mid_ref,
    mid_sums_refs,
    mid_affine_ref,
    pre_ref,
    sums_refs,
    affine_ref,
    w_ref,
    low_ref,
    grad_ref,
    gate_ref,
    vector_ref,
    msg_ref,
    taps_ref,
):
    place = Place(counts_ref)
    images = attention_ref.shape[0]
    width = attention_ref.shape[1] // 2
    lanes = wall_ref.shape[1]
    pieces = 2 * width // lanes
    total = place.total() * PIXELS
    wall = wall_ref[...]
    rows = slot_rows(gathered_refs, GATHERED, 0, images)
    center, scale = gate_norm(place, rows, wall)
    gain = gate_affine_ref[0:1, :] * scale
    normed = (rows - center) * scale
    grads = slot_rows(back_refs, images, 0, images, 2 * pieces)
    first, second = total_of(wall * grads), total_of(wall * grads * normed)
    vector_ref[0:1, 0:lanes] = second
    vector_ref[0:1, lanes : 2 * lanes] = first
    squeezed = gain * (grads - wall * (first + normed * second) / place.total())
    gate_ref[...] = squeezed[0:images]
    pooled_grad = exact_dot(dot_nt, squeezed, squeeze_ref[...]) / PIXELS
    pooled_grad = jnp.concatenate([pooled_grad, pooled_grad], axis=1)
    slot = 0
    terms = jnp.zeros((2 * images, 2 * width), F32)
    for ref in gathered_refs:
        for at in range(8, ref.shape[0], GATHERED):
            inclines = [
                ref[at + q * 2 * images : at + (q + 1) * 2 * images, :] for q in range(pieces)
            ]
            grad = pooled_grad[slot * images : (slot + 1) * images, :]
            grad = jnp.concatenate([grad, grad], axis=0)
            terms = terms + jnp.concatenate(inclines, axis=1) * grad
            slot += 1
    sums = functools.reduce(jnp.add, [ref[0 : 2 * pieces, :] for ref in back_refs])
    back = []
    for t in range(2):
        row = [sums[t * pieces + q : t * pieces + q + 1, :] for q in range(pieces)]
        back.append(
            jnp.concatenate(row, axis=1) + total_of(terms[t * images : (t + 1) * images])
        )
    vector_ref[1:2, :] = back[1]
    vector_ref[2:3, :] = back[0]
    own = pooled_grad[0:images]
    center, scale, gain, shift = mid_norm(place, mid_sums_refs, mid_affine_ref)
    second = gain * scale * back[1] / total
    first = gain * back[0] / total - center * second
    clear_gaps(taps_ref, images)
    keep = columns_real(WIDE)
    for image in range(images):
        share = gain * attention_ref[image : image + 1, :]
        offset = gain * own[image : image + 1, :]
        real = place.real(image)
        lead, lag = real * first, real * second

        def chunk(step, carry, image=image, share=share, offset=offset, lead=lead, lag=lag):
            rows = pl.multiple_of(step * WIDE, WIDE)
            here = pl.ds(image * PADDED + rows, WIDE)
            before = mid_ref[here, :]
            grad = gw_ref[here, :]
            grad = jnp.concatenate([grad, grad], axis=1)
            grad = (share * grad + offset) * slope(before * gain + shift)
            value = (grad - (lead + before * lag)) * keep
            store_taps(taps_ref, image * STRIDE + WIDE + rows, value)
            return carry

        lax.fori_loop(0, SIDE, chunk, 0, unroll=UNROLL)
    low_ref[...] = taps_ref[1]
    sums = summed_over(sums_refs)
    center, scale = moments(sums[0:1], sums[1:2], total)
    gain = affine_ref[0:1, :] * scale
    shift = affine_ref[1:2, :] - center * gain
    half = width // 2
    keep = columns_real(PADDED)
    firsts = [jnp.zeros((1, half), F32) for _ in range(2)]
    seconds = [jnp.zeros((1, half), F32) for _ in range(2)]
    for image in range(images):
        real = place.real(image)
        here = slice(image * PADDED, (image + 1) * PADDED)
        for r in range(2):
            left = jnp.concatenate(
                [
                    taps_ref[
                        2 - b,
                        image * STRIDE + (2 - a) * WIDE : image * STRIDE + (2 - a) * WIDE + PADDED,
                        r * width : (r + 1) * width,
                    ]
                    for a in range(3)
                    for b in range(3)
                ],
                axis=1,
            )
            lane = slice(r * half, (r + 1) * half)
            before = pre_ref[here, lane]
            value = dot_nn(left, w_ref[r]) * slope(before * gain[:, lane] + shift[:, lane])
            value = value * (keep * real)
            grad_ref[here, lane] = value
            firsts[r] = firsts[r] + total_of(value)
            seconds[r] = seconds[r] + total_of(value * before)
    first = jnp.concatenate(firsts, axis=1)
    second = scale * (jnp.concatenate(seconds, axis=1) - center * first)
    sums = jnp.concatenate([first, second], axis=0)
    msg_ref[...] = sums


def sort_pieces(
    place,
    source_ref,
    keep_ref,
    send_ref,
    row,
):
    for turn, s in enumerate(ORDER):
        target = keep_ref if turn < 2 else send_ref
        rows = source_ref.shape[1]
        target[turn % 2, row : row + rows, :] = source_ref[place.chan ^ s].astype(BF16)


def weight_out_term(
    counts_ref,
    weighted_ref,
    low_ref,
    gate_ref,
    logits_ref,
    keep_ref,
    send_ref,
    wide_ref,
    small_ref,
):
    place = Place(counts_ref)
    width = weighted_ref.shape[1]
    lanes = keep_ref.shape[2]
    own = width // len(SLOTS)
    for turn, s in enumerate(ORDER):
        target = keep_ref if turn < 2 else send_ref
        held = place.batch ^ place.chan ^ s
        term = dot_tn(weighted_ref[...], low_ref[held]).astype(BF16)
        target[turn % 2, 0:width, :] = term[:, :lanes]
        target[turn % 2, width : 2 * width, :] = term[:, lanes:]
    wide_ref[...] = dot_tn(logits_ref[...], gate_ref[0], HIGHEST)
    for turn, s in enumerate(ORDER):
        target = keep_ref if turn < 2 else send_ref
        for r in range(2):
            at = pl.multiple_of(r * width + (place.chan ^ s) * own, own)
            row = 2 * width + r * own
            target[turn % 2, row : row + own, :] = wide_ref[pl.ds(at, own), :].astype(BF16)
    small_ref[...] = jnp.zeros_like(small_ref)
    bias = total_of(logits_ref[...])
    for k in range(len(SLOTS)):
        small_ref[k, 0:1, :own] = bias[:, k * own : (k + 1) * own]
        small_ref[k, 0:1, own:] = bias[:, width + k * own : width + (k + 1) * own]
    sort_pieces(place, small_ref, keep_ref, send_ref, 2 * width + 2 * own)


def weight_mid_term(
    counts_ref,
    taps_ref,
    low_ref,
    keep_ref,
    send_ref,
    wide_ref,
):
    place = Place(counts_ref)
    half = taps_ref.shape[2] // 2
    width = low_ref.shape[1] // 2
    own = width // len(SLOTS)
    rows = low_ref.shape[0] - 2 * WIDE
    for r in range(2):
        right = jnp.concatenate(
            [
                taps_ref[b, a * WIDE : a * WIDE + rows, r * half : (r + 1) * half]
                for a in range(3)
                for b in range(3)
            ],
            axis=1,
        )
        wide_ref[...] = dot_tn(low_ref[WIDE : WIDE + rows, r * width : (r + 1) * width], right)
        for turn, s in enumerate(ORDER):
            target = keep_ref if turn < 2 else send_ref
            here = pl.ds(pl.multiple_of((place.chan ^ s) * own, own), own)
            for tap in range(9):
                row = (2 * tap + r) * own
                target[turn % 2, row : row + own, :] = wide_ref[
                    here, tap * half : (tap + 1) * half
                ].astype(BF16)


def back_in(
    share,
    counts_ref,
    grad_ref,
    pre_ref,
    sums_refs,
    back_refs,
    affine_ref,
    x0,
    x1,
    x2,
    x3,
    vector_ref,
    out_back_refs,
    pooled_ref,
    gathered_refs,
    squeezed_ref,
    low_ref,
    keep_ref,
    send_ref,
    flat_ref,
    wide_ref,
    narrow_ref,
    small_ref,
):
    place = Place(counts_ref)
    images = pre_ref.shape[0] // PADDED
    width = pre_ref.shape[1]
    own = width // len(SLOTS)
    chan, batch = place.chan, place.batch
    total = place.total() * PIXELS
    sums = summed_over(sums_refs)
    center, scale = moments(sums[0:1], sums[1:2], total)
    back = summed_over(back_refs)
    gain = affine_ref[0:1, :] * scale
    second = gain * scale * back[1:2] / total
    first = gain * back[0:1] / total - center * second
    for image in range(images):
        real = place.real(image)
        lead, lag = real * first, real * second
        for line in range(SIDE):
            at = image * PADDED + line * WIDE
            before = pre_ref[at : at + WIDE, :]
            value = gain * grad_ref[at : at + WIDE, :] - (lead + before * lag)
            at = image * PIXELS + line * SIDE
            flat_ref[at : at + SIDE, :] = value[:SIDE]
    low_ref[...] = flat_ref[...].astype(BF16)
    lanes = keep_ref.shape[2]
    for k, x in enumerate((x0, x1, x2, x3)):
        wide_ref[...] = dot_tn(low_ref[...], x[...])
        for turn, s in enumerate(ORDER):
            target = keep_ref if turn < 2 else send_ref
            here = pl.ds(pl.multiple_of((chan ^ s) * own, own), own)
            for part in range(wide_ref.shape[1] // lanes):
                at = pl.multiple_of(((batch ^ k) * (wide_ref.shape[1] // lanes) + part) * own, own)
                target[turn % 2, pl.ds(at, own), :] = wide_ref[
                    here, part * lanes : (part + 1) * lanes
                ].astype(BF16)
    mean = [
        total_of(slot_rows(gathered_refs, GATHERED, images + q, 1)) for q in range(width // lanes)
    ]
    mean = jnp.concatenate(mean, axis=1) / place.total()
    narrow_ref[...] = dot_tn(pooled_ref[...] - mean, squeezed_ref[...], HIGHEST)
    row = keep_ref.shape[1] - small_ref.shape[1] - own
    for turn, s in enumerate(ORDER):
        target = keep_ref if turn < 2 else send_ref
        here = pl.ds(pl.multiple_of((chan ^ s) * own, own), own)
        target[turn % 2, row : row + own, :] = narrow_ref[here, :].astype(BF16)
    small_ref[...] = jnp.zeros_like(small_ref)
    outs = summed_over(out_back_refs)
    for k in range(len(SLOTS)):
        here = slice(k * own, (k + 1) * own)
        there = slice(width + k * own, width + (k + 1) * own)
        small_ref[k, 0:1, :own] = back[1:2, here]
        small_ref[k, 0:1, own:] = back[0:1, here]
        for t in range(2):
            small_ref[k, 1 + t : 2 + t, :own] = vector_ref[1 + t : 2 + t, here]
            small_ref[k, 1 + t : 2 + t, own:] = vector_ref[1 + t : 2 + t, there]
        small_ref[k, 3:4, :] = vector_ref[0:1, 0:lanes]
        small_ref[k, 4:5, :] = vector_ref[0:1, lanes : 2 * lanes]
    for s in SLOTS:
        for t in range(2):
            row = outs[(1 - t) * len(SLOTS) + s : (1 - t) * len(SLOTS) + s + 1, :]
            small_ref[batch ^ s, 5 + 2 * t : 6 + 2 * t, :] = row[:, :lanes]
            small_ref[batch ^ s, 6 + 2 * t : 7 + 2 * t, :] = row[:, lanes:]
    small_ref[...] = small_ref[...] * share
    sort_pieces(place, small_ref, keep_ref, send_ref, keep_ref.shape[1] - small_ref.shape[1])


def grad_owned(low_refs, w_ref, summed_ref, result_ref):
    chan = lax.axis_index("chan")
    for s, low_ref in enumerate(low_refs):
        value = dot_nn(low_ref[...], w_ref[chan]) + summed_ref[chan ^ s].astype(F32)
        result_ref[chan ^ s] = value.astype(BF16)


def add_groups(terms_ref, sum_ref):
    value = jnp.sum(terms_ref[...].astype(F32), axis=0).astype(BF16)
    sum_ref[...] = jnp.broadcast_to(value[None], sum_ref.shape)


def added(left_ref, right_ref):
    return left_ref[...].astype(F32) + right_ref[...].astype(F32)


def add_core(keep_refs, arrived_refs, kept_ref, send_ref):
    at = 0
    for keep_ref, arrived_ref in zip(keep_refs, arrived_refs):
        value = added(keep_ref, arrived_ref).astype(BF16)
        rows = keep_ref.shape[1]
        kept_ref[at : at + rows, :] = value[0]
        send_ref[at : at + rows, :] = value[1]
        at += rows
    if at < kept_ref.shape[0]:
        for ref in (kept_ref, send_ref):
            ref[at:, :] = jnp.zeros((kept_ref.shape[0] - at, ref.shape[1]), BF16)


def split_rows(parity, whole_ref, kept_ref, send_ref):
    rows = kept_ref.shape[-2]
    mine = pl.ds(pl.multiple_of(parity * rows, 16), rows)
    other = pl.ds(pl.multiple_of((1 - parity) * rows, 16), rows)
    if whole_ref.ndim == 2:
        kept_ref[...] = whole_ref[mine, :]
        send_ref[...] = whole_ref[other, :].astype(BF16)
    else:
        kept_ref[...] = whole_ref[:, mine, :]
        send_ref[...] = whole_ref[:, other, :].astype(BF16)


def add_core_first(counts_ref, keep_ref, arrived_ref, kept_ref, send_ref, whole_ref):
    whole_ref[...] = added(keep_ref, arrived_ref)
    split_rows(Place(counts_ref).parity, whole_ref, kept_ref, send_ref)


def add_parity_first(keep_ref, arrived_ref, kept_ref, send_ref):
    value = added(keep_ref, arrived_ref)
    kept_ref[...] = value[0]
    send_ref[...] = value[1].astype(BF16)


def add_chip(counts_ref, keep_ref, arrived_ref, kept_ref, send_ref, whole_ref):
    whole_ref[...] = added(keep_ref, arrived_ref)
    split_rows(Place(counts_ref).parity, whole_ref, kept_ref, send_ref)


def add_last(counts_ref, keep_refs, arrived_refs, kept_ref, s1, s2, s3, whole_refs):
    place = Place(counts_ref)
    at = 0
    for keep_ref, arrived_ref, whole_ref in zip(keep_refs, arrived_refs, whole_refs):
        whole_ref[...] = added(keep_ref, arrived_ref)
        rows = keep_ref.shape[0] // len(SLOTS)
        for t, target in enumerate((kept_ref, s1, s2, s3)):
            here = pl.ds(pl.multiple_of((place.depth ^ t) * rows, 16), rows)
            target[at : at + rows, :] = whole_ref[here, :].astype(target.dtype)
        at += rows


def add_depth(keep_ref, arrived_refs, sum_ref):
    value = keep_ref[...]
    for ref in arrived_refs:
        value = value + ref[...].astype(F32)
    sum_ref[...] = value.astype(BF16)


def join_depth(
    counts_ref,
    piece_refs,
    whole_ref,
):
    place = Place(counts_ref)
    rows = piece_refs[0].shape[0]
    for t, ref in enumerate(piece_refs):
        whole_ref[pl.ds(pl.multiple_of((place.depth ^ t) * rows, 16), rows), :] = ref[...]


def join_halves(counts_ref, half_refs, first_ref, second_ref):
    place = Place(counts_ref)
    for t, ref in enumerate(half_refs):
        piece = ref.shape[0] // len(SLOTS)
        row = 0
        for target in (first_ref, second_ref):
            rows = target.shape[0] // 2 // len(SLOTS)
            for z in range(len(SLOTS)):
                at = ((place.parity ^ t) * len(SLOTS) + z) * rows
                source = ref[z * piece + row : z * piece + row + rows, :]
                target[pl.ds(pl.multiple_of(at, 16), rows), :] = source.astype(F32)
            row += rows


def unpack(
    joined,
    counts_ref,
    term_refs,
    in_ref,
    gain_in_ref,
    shift_in_ref,
    mid_ref,
    gain_mid_ref,
    shift_mid_ref,
    squeeze_ref,
    gain_gate_ref,
    shift_gate_ref,
    excite_ref,
    bias_ref,
    out_ref,
    gain_out_ref,
    shift_out_ref,
    first_ref,
    second_ref,
):
    if joined:
        first_ref[...] = term_refs[0][...].astype(F32)
        second_ref[...] = term_refs[1][...].astype(F32)
    else:
        join_halves(counts_ref, term_refs, first_ref, second_ref)
    own, lanes = squeeze_ref.shape
    width = out_ref.shape[0]

    def halves(target, row):
        target[0:1, :] = second_ref[row : row + 1, :own]
        target[1:2, :] = second_ref[row : row + 1, own:]

    mid_ref[...] = first_ref[...]
    out_ref[:, :lanes] = second_ref[0:width, :]
    out_ref[:, lanes:] = second_ref[width : 2 * width, :]
    row = 2 * width
    excite_ref[...] = second_ref[row : row + 2 * own, :]
    row += 2 * own
    halves(bias_ref, row)
    row += 16
    for block in range(in_ref.shape[1] // lanes):
        in_ref[:, block * lanes : (block + 1) * lanes] = second_ref[row : row + own, :]
        row += own
    squeeze_ref[...] = second_ref[row : row + own, :]
    row += own
    gain_in_ref[...] = second_ref[row : row + 1, :own]
    shift_in_ref[...] = second_ref[row : row + 1, own:]
    halves(gain_mid_ref, row + 1)
    halves(shift_mid_ref, row + 2)
    gain_gate_ref[...] = second_ref[row + 3 : row + 4, :]
    shift_gate_ref[...] = second_ref[row + 4 : row + 5, :]
    for t, target in enumerate((gain_out_ref, shift_out_ref)):
        target[:, :lanes] = second_ref[row + 5 + 2 * t : row + 6 + 2 * t, :]
        target[:, lanes:] = second_ref[row + 6 + 2 * t : row + 7 + 2 * t, :]


def per_device(
    activations,
    counts,
    weight_in,
    gain_in,
    shift_in,
    weight_mid,
    gain_mid,
    shift_mid,
    weight_squeeze,
    gain_gate,
    shift_gate,
    weight_excite,
    shift_excite,
    weight_out,
    gain_out,
    shift_out,
    cotangent,
    *,
    groups,
    parts,
):
    batches, rows, lanes = activations.shape
    images = rows // PIXELS
    own = weight_in.shape[1]
    width = own * parts
    inter = gain_gate.shape[0]
    wide_rows = images * PADDED
    gap_rows = WIDE + images * STRIDE
    chan, group = lax.axis_index("chan"), lax.axis_index("dp")
    depth = groups // 2

    def permute(tensor, to):
        pairs = []
        for index in range(groups * parts):
            z, x, y, c = index // parts // 2, index // parts % 2, index % parts // 2, index % 2
            z, x, y, c = to(z, x, y, c)
            pairs.append((index, (2 * z + x) * parts + 2 * y + c))
        return lax.ppermute(tensor, ("dp", "chan"), pairs)

    def home(tensor, s):
        return permute(tensor, lambda z, x, y, c: (z, c ^ (s & 1), y ^ (s >> 1), x))

    def away_plane(tensor, odd=0):
        return permute(tensor, lambda z, x, y, c: (z, c, y, x ^ odd))

    def cross(even, odd):
        return even, odd, across(jnp.stack([even[1], odd[1]]))

    def core(tensor):
        return permute(tensor, lambda z, x, y, c: (z, x, y, c ^ 1))

    def across(tensor):
        return permute(tensor, lambda z, x, y, c: (z, x, y ^ 1, c))

    def parity(tensor):
        return permute(tensor, lambda z, x, y, c: (z, x ^ 1, y, c))

    def along(tensor, t):
        return permute(tensor, lambda z, x, y, c: (z ^ t, x, y, c))

    def after(tensor, *others):
        return lax.optimization_barrier((tensor,) + others)[0]

    def after_all(tensors, *others):
        return lax.optimization_barrier(tuple(tensors) + others)[: len(tensors)]

    def exchange(total, gather):
        def merge(mine, other):
            cut = 0 if total is None else total
            joined = [mine[:cut] + other[:cut]] if cut else []
            if gather:
                joined += [mine[cut : cut + gather], other[cut : cut + gather]]
            return jnp.concatenate(joined) if len(joined) > 1 else joined[0]

        def run(mine):
            nonlocal gather
            mine = merge(mine, core(mine))
            gather = 2 * gather
            if depth <= 4:
                return (mine,) + tuple(along(mine, t) for t in range(1, depth))
            step = 1
            while step < depth:
                mine = merge(mine, along(mine, step))
                gather, step = 2 * gather, 2 * step
            return (mine,)

        return run

    def padded(rows):
        return -(-rows // (16 * groups)) * 16 * groups

    def kernel(body, outs, *args, smem=1):
        return call(body, outs, [], 0, *args, smem=smem)

    def add_over_all(first, second, low, result):
        first_rows, second_rows = first[0].shape[1], sum(k.shape[1] for k in second[0])
        if groups != 8:
            rows = padded(first_rows + second_rows)
            keep, send = kernel(
                add_core,
                [shape((rows, 2 * own), BF16)] * 2,
                (first[0],) + second[0],
                (first[1],) + second[1],
                smem=0,
            )
            terms = (keep.astype(F32) + across(send).astype(F32)).astype(BF16)
            terms = lax.all_to_all(terms.reshape(groups, rows // groups, -1), "dp", 0, 0)
            (terms,) = kernel(add_groups, [shape(terms.shape, BF16)], terms, smem=0)
            terms = lax.all_to_all(terms, "dp", 0, 0).reshape(rows, -1)
            terms = terms[:first_rows], terms[first_rows : first_rows + second_rows]
            return terms, low, across(low)
        second_rows = padded(second_rows)
        halves = (first_rows // 2, second_rows // 2)
        pieces = (first_rows // groups, second_rows // groups)

        def rows(number, kind=F32):
            return shape((number, 2 * own), kind)

        keep, send = kernel(add_core, [rows(second_rows, BF16)] * 2, *second, smem=0)
        arrived = after(across(send), result)
        pair = (2, halves[0], 2 * own)
        first_keep, send = call(
            add_core_first,
            [shape(pair), shape(pair, BF16)],
            [pltpu.VMEM((2, first_rows, 2 * own), F32)],
            0,
            counts,
            *first,
        )
        first_arrived = parity(send)
        keep, send = call(
            add_chip,
            [rows(halves[1]), rows(halves[1], BF16)],
            [pltpu.VMEM((second_rows, 2 * own), F32)],
            0,
            counts,
            keep,
            arrived,
        )
        arrived = parity(send)
        first_keep, send = kernel(
            add_parity_first,
            [rows(halves[0]), rows(halves[0], BF16)],
            first_keep,
            first_arrived,
            smem=0,
        )
        first_arrived = across(send)
        arrived = after(arrived, first_arrived)
        keep, *send = call(
            add_last,
            [rows(sum(pieces))] + [rows(sum(pieces), BF16)] * (depth - 1),
            [tuple(pltpu.VMEM((half, 2 * own), F32) for half in halves)],
            0,
            counts,
            (first_keep, keep),
            (first_arrived, arrived),
        )
        low_other = across(after(low, keep))
        arrived = tuple(along(send[t - 1], t) for t in range(1, depth))
        (mine,) = kernel(add_depth, [rows(sum(pieces), BF16)], keep, arrived, smem=0)
        mine = (mine,) + tuple(along(mine, t) for t in range(1, depth))
        low, low_other = after_all((low, low_other), *mine)
        (mine,) = kernel(join_depth, [rows(sum(halves), BF16)], counts, mine)
        return (mine, parity(mine)), low, low_other

    def slots_of(tensor, *which):
        return [lax.dynamic_index_in_dim(tensor, chan ^ s, 0, keepdims=False) for s in which]

    far = slots_of(activations, 2, 3)
    first = after(weight_in.T, *far)
    other, near = across(first), core(first)
    x = slots_of(after(activations, near), 0, 1) + far
    x = tuple(home(piece, s) for s, piece in enumerate(x))

    (weights,) = call(
        pack,
        [shape((19 * own + 16 + inter + 2 * width, 2 * own), BF16)],
        [pltpu.VMEM((16, 2 * own), F32)],
        0,
        weight_mid.transpose(0, 1, 3, 4, 2).reshape(-1, 2 * own),
        weight_squeeze,
        gain_in.reshape(1, -1),
        shift_in.reshape(1, -1),
        gain_mid,
        shift_mid,
        shift_excite,
        gain_out.reshape(1, -1),
        shift_out.reshape(1, -1),
        weight_excite.transpose(1, 2, 0).reshape(-1, inter),
        weight_out,
        smem=0,
    )
    other = after(other, weights)
    first = (first, near, other, core(other))
    near = core(weights)
    cot = slots_of(after(cotangent, x[0], x[1]), *SLOTS)
    even, odd = jnp.stack([cot[0], cot[2]]), jnp.stack([cot[1], cot[3]])
    other = across(after(weights, x[2], x[3], first[3]))
    even = home(after(even, x[2], x[3]), 0)
    gate_affine = jnp.stack([gain_gate, shift_gate]).astype(F32)

    product = 2 * rows * lanes * parts * width
    pre_in, msg, w_in, wall = call(
        reduce_in,
        [
            shape((wide_rows, width)),
            shape((2, width)),
            shape((parts, width, lanes), BF16),
            shape((groups * images, inter)),
        ],
        [pltpu.VMEM((rows, width), F32)],
        product,
        counts,
        *x,
        *first,
    )
    in_sums = exchange(2, 0)(after(msg, near, odd))
    other = after(other, *in_sums)
    odd = home(after(odd, *in_sums), 1)
    weights = (weights, near, other, core(other))
    w_mid, w_mid_back, squeeze, in_affine, mid_affine, bias, out_affine = call(
        place_mid,
        [
            shape((2, width, 9 * inter), BF16),
            shape((2, 9 * width, inter), BF16),
            shape((width, inter), BF16),
            shape((2, width)),
            shape((2, 2 * width)),
            shape((1, 2 * width)),
            shape((2, parts, 1, lanes)),
        ],
        [pltpu.VMEM((parts, 16, 2 * own), F32)],
        0,
        counts,
        *weights,
    )
    conv = 2 * wide_rows * 9 * width * width
    taps, mid, msg = call(
        conv_mid,
        [
            shape((3, gap_rows, width), BF16),
            shape((wide_rows, 2 * width)),
            shape((2, 2 * width)),
        ],
        [],
        conv,
        counts,
        pre_in,
        in_sums,
        in_affine,
        w_mid,
    )
    mid_sums = exchange(2, 0)(msg)
    excite, w_out = call(
        place_rest,
        [
            shape((2 * width, inter), BF16),
            shape((parts, width, lanes), BF16),
        ],
        [],
        0,
        counts,
        *weights,
    )
    pooled, msg = call(
        pool,
        [shape((images, width)), shape((GATHERED, inter))],
        [],
        0,
        counts,
        mid,
        mid_sums,
        mid_affine,
        squeeze,
    )
    cot = cross(*after_all((even, odd), msg))
    gathered = exchange(None, GATHERED)(msg)
    gate, attention, weighted, out, msg = call(
        attend,
        [
            shape((2, images, inter)),
            shape((images, 2 * width)),
            shape((rows, width), BF16),
            shape((parts, rows, lanes)),
            shape((2 * parts, lanes)),
        ],
        [pltpu.VMEM((wide_rows, width), F32), pltpu.VMEM((rows, width), F32)],
        product,
        counts,
        gathered,
        wall,
        gate_affine,
        excite,
        bias,
        mid,
        mid_sums,
        mid_affine,
        w_out,
    )
    out_sums = exchange(2 * parts, 0)(msg)
    *summed, grad, msg = call(
        finish,
        [shape((2, rows, lanes), BF16)] * 2
        + [shape((parts, rows, lanes)), shape((2 * parts, lanes))],
        [],
        0,
        counts,
        out,
        out_sums,
        out_affine,
        x,
        *cot,
    )
    out_back = exchange(2 * parts, 0)(msg)

    summed = [away_plane(pair, odd) for odd, pair in enumerate(summed)]

    sums_rows = 2 * 2 * width // inter
    low_out, grad_weighted, grad_logits, msg = call(
        back_out,
        [
            shape((parts, rows, lanes), BF16),
            shape((wide_rows, width)),
            shape((images, 2 * width)),
            shape((sums_rows + images, inter)),
        ],
        [pltpu.VMEM((rows, width), F32)],
        product,
        counts,
        grad,
        out,
        out_sums,
        out_back,
        out_affine,
        w_out,
        mid,
        mid_sums,
        mid_affine,
        attention,
        gate,
        excite,
    )
    mid_back = exchange(sums_rows, images)(msg)
    term_rows = 2 * width + 2 * own + 16
    keep, send = call(
        weight_out_term,
        [shape((2, term_rows, 2 * own), BF16)] * 2,
        [pltpu.VMEM((2 * width, inter), F32), pltpu.VMEM((parts, 16, 2 * own), F32)],
        product,
        counts,
        after(weighted, mid_back[0]),
        low_out,
        gate,
        grad_logits,
    )
    out_keep, out_arrived = keep, core(send)
    mid_back = after_all(mid_back, keep, *summed)
    summed = cross(*after_all(summed, mid_back[0]))
    low_mid, grad_hidden, grad_squeeze, vectors, msg = call(
        back_mid,
        [
            shape((gap_rows, 2 * width), BF16),
            shape((wide_rows, width)),
            shape((images, inter)),
            shape((8, 2 * width)),
            shape((2, width)),
        ],
        [pltpu.VMEM((3, gap_rows, 2 * width), BF16)],
        conv,
        counts,
        mid_back,
        gathered,
        wall,
        gate_affine,
        squeeze,
        attention,
        grad_weighted,
        mid,
        mid_sums,
        mid_affine,
        pre_in,
        in_sums,
        in_affine,
        w_mid_back,
    )
    in_back = exchange(2, 0)(after(msg, out_arrived))
    in_rows = parts * lanes // (2 * own) * own
    low_in, in_keep, in_send = call(
        functools.partial(back_in, 1.0 / groups),
        [shape((rows, width), BF16)] + [shape((2, in_rows + own + 16, 2 * own), BF16)] * 2,
        [
            pltpu.VMEM((rows, width), F32),
            pltpu.VMEM((width, lanes), F32),
            pltpu.VMEM((width, inter), F32),
            pltpu.VMEM((parts, 16, 2 * own), F32),
        ],
        product,
        counts,
        grad_hidden,
        pre_in,
        in_sums,
        in_back,
        in_affine,
        *x,
        vectors,
        out_back,
        pooled,
        gathered,
        grad_squeeze,
    )
    keep, send = call(
        weight_mid_term,
        [shape((2, 18 * own, 2 * own), BF16)] * 2,
        [pltpu.VMEM((width, 9 * inter), F32)],
        conv,
        counts,
        after(taps, low_in),
        low_mid,
    )
    owned = shape((batches, rows, lanes), BF16)
    result, grad_summed = call(finish_owned, [owned, owned], [], 0, counts, *summed, cotangent)
    send = after(send, summed[2])
    low_in = away_plane(low_in)
    terms, low_in, low_other = add_over_all(
        (keep, core(send)),
        ((out_keep, in_keep), (out_arrived, core(in_send))),
        low_in,
        result,
    )
    lows = (low_in, core(low_in), low_other, core(low_other))
    (grad_x,) = call(grad_owned, [owned], [], product, lows, w_in, grad_summed, smem=0)
    terms = after_all(terms, grad_x)
    (
        g_in,
        g_gain_in,
        g_shift_in,
        g_mid,
        g_gain_mid,
        g_shift_mid,
        g_squeeze,
        g_gain_gate,
        g_shift_gate,
        g_excite,
        g_bias,
        g_out,
        g_gain_out,
        g_shift_out,
    ) = call(
        functools.partial(unpack, groups != 8),
        [
            shape((own, parts * lanes)),
            shape((1, own)),
            shape((1, own)),
            shape((18 * own, inter)),
            shape((2, own)),
            shape((2, own)),
            shape((own, inter)),
            shape((1, inter)),
            shape((1, inter)),
            shape((2 * own, inter)),
            shape((2, own)),
            shape((width, lanes)),
            shape((1, lanes)),
            shape((1, lanes)),
        ],
        [
            pltpu.VMEM((18 * own, 2 * own), F32),
            pltpu.VMEM((terms[0].shape[0] * 2 - 18 * own, 2 * own), F32)
            if groups == 8
            else pltpu.VMEM(terms[1].shape, F32),
        ],
        0,
        counts,
        terms,
    )
    return (
        result,
        grad_x,
        g_in.T,
        g_gain_in.reshape(-1),
        g_shift_in.reshape(-1),
        g_mid.reshape(3, 3, 2, own, inter).transpose(0, 1, 4, 2, 3),
        g_gain_mid,
        g_shift_mid,
        g_squeeze,
        g_gain_gate.reshape(-1),
        g_shift_gate.reshape(-1),
        g_excite.reshape(2, own, inter).transpose(2, 0, 1),
        g_bias,
        g_out,
        g_gain_out.reshape(-1),
        g_shift_out.reshape(-1),
    )


def solution(mesh):
    placed = (
        P(None, "dp", "chan"),
        P(),
        P(None, "chan"),
        P("chan"),
        P("chan"),
        P(None, None, None, None, "chan"),
        P(None, "chan"),
        P(None, "chan"),
        P("chan", None),
        P(),
        P(),
        P(None, None, "chan"),
        P(None, "chan"),
        P(None, "chan"),
        P("chan"),
        P("chan"),
        P(None, "dp", "chan"),
    )
    return jax.shard_map(
        functools.partial(per_device, groups=mesh.shape["dp"], parts=mesh.shape["chan"]),
        mesh=mesh,
        in_specs=placed,
        out_specs=placed[:1] + placed[:1] + placed[2:16],
        check_vma=False,
    )
```

```python
import functools

import jax
import jax.numpy as jnp
from jax import lax
from jax.experimental import pallas as pl
from jax.experimental.pallas import tpu as pltpu
from jax.sharding import PartitionSpec as P

SIDE = 14
PIXELS = SIDE * SIDE
WIDE = 16
PADDED = SIDE * WIDE
STRIDE = PADDED + WIDE
CHUNK = 16
UNROLL = 49
VMEM_LIMIT = 24 * 2**20
SLOTS = (0, 1, 2, 3)
GATHERED = 40
ORDER = (0, 2, 1, 3)
EPSILON = 1e-05
HIGHEST = lax.Precision.HIGHEST
F32 = jnp.float32
BF16 = jnp.bfloat16


def dot_nn(left, right, precision=None):
    return lax.dot_general(
        left, right, (((1,), (0,)), ((), ())), preferred_element_type=F32, precision=precision
    )


def parts_of(value):
    high = value.astype(BF16)
    rest = value - high.astype(F32)
    middle = rest.astype(BF16)
    return jnp.concatenate([high, middle, (rest - middle.astype(F32)).astype(BF16)], axis=0)


def exact_dot(dot, left, right):
    rows = -(-left.shape[0] // 16) * 16
    if rows > left.shape[0]:
        left = jnp.concatenate([left, jnp.zeros((rows - left.shape[0], left.shape[1]), F32)], axis=0)
    value = dot(parts_of(left), right)
    return value[:rows] + value[rows : 2 * rows] + value[2 * rows :]


def dot_nt(left, right, precision=None):
    return lax.dot_general(
        left, right, (((1,), (1,)), ((), ())), preferred_element_type=F32, precision=precision
    )


def dot_tn(left, right, precision=None):
    return lax.dot_general(
        left, right, (((0,), (0,)), ((), ())), preferred_element_type=F32, precision=precision
    )


def row_sums(matrix):
    return dot_nn(jnp.ones((16, matrix.shape[0]), BF16), matrix)[0:1]


def outer(column, row, row_exact=False):
    exact, rounded = (row, column) if row_exact else (column, row)
    high = exact.astype(BF16).astype(F32)
    middle = (exact - high).astype(BF16).astype(F32)
    empty = jnp.zeros((13, exact.shape[1]), F32)
    exact = jnp.concatenate([high, middle, exact - high - middle, empty], axis=0).astype(BF16)
    rounded = jnp.broadcast_to(rounded, (16, rounded.shape[1])).astype(BF16)
    return dot_tn(rounded, exact) if row_exact else dot_tn(exact, rounded)


def expected(gain, shift):
    reach = 3.0**0.5 * gain
    return (4.0 * silu(shift) + silu(shift + reach) + silu(shift - reach)) / 6.0


def logistic(value):
    return 0.5 + 0.5 * jnp.tanh(0.5 * value)


def silu(value):
    return value * logistic(value)


def slope(value):
    share = logistic(value)
    return share + value * (share * (1.0 - share))


def moments(first, second, total):
    center = first / total
    return center, lax.rsqrt(second / total - center * center + EPSILON)


def fold(value):
    return jnp.sum(value.reshape(-1, 8, value.shape[-1]), axis=0)


def total_of(value):
    return jnp.sum(value, axis=0, keepdims=True)


def columns_real(rows):
    spot = lax.broadcasted_iota(jnp.int32, (rows, 1), 0)
    return (lax.rem(spot, WIDE) < SIDE).astype(F32)


def summed_over(refs):
    values = [ref[...] for ref in refs]
    while len(values) > 1:
        values = [left + right for left, right in zip(values[::2], values[1::2])]
    return values[0]


def slot_rows(refs, size, first, count, skip=0):
    return jnp.concatenate(
        [
            ref[at + first : at + first + count, :]
            for ref in refs
            for at in range(skip, ref.shape[0], size)
        ],
        axis=0,
    )


class Place:
    def __init__(self, counts_ref):
        group = lax.axis_index("dp")
        self.chan = lax.axis_index("chan")
        self.parity, self.depth, self.core = group & 1, group >> 1, self.chan & 1
        self.batch = (self.chan & 2) | self.parity
        self.counts = counts_ref
        self.groups = counts_ref.shape[1]

    def images(self, depth, core):
        return self.counts[self.batch, 2 * depth + core]

    def real(self, image):
        return jnp.where(self.images(self.depth, self.core) > image, 1.0, 0.0).astype(F32)

    def total(self):
        every = [self.counts[self.batch, g] for g in range(self.groups)]
        return functools.reduce(jnp.add, every).astype(F32)


def spread_map_rows(flat_ref, wide_ref):
    for line in range(flat_ref.shape[0] // SIDE):
        wide_ref[line * WIDE : line * WIDE + SIDE, :] = flat_ref[line * SIDE : (line + 1) * SIDE, :]
        wide_ref[line * WIDE + SIDE : (line + 1) * WIDE, :] = jnp.zeros(
            (WIDE - SIDE, wide_ref.shape[1]), wide_ref.dtype
        )


def pack_map_rows(wide_ref, flat_ref):
    for line in range(flat_ref.shape[0] // SIDE):
        flat_ref[line * SIDE : (line + 1) * SIDE, :] = wide_ref[line * WIDE : line * WIDE + SIDE, :]


def clear_gaps(taps_ref, images):
    for gap in range(images + 1):
        taps_ref[:, gap * STRIDE : gap * STRIDE + WIDE, :] = jnp.zeros(
            (3, WIDE, taps_ref.shape[2]), taps_ref.dtype
        )


def store_taps(taps_ref, at, value):
    here = pl.ds(pl.multiple_of(at, WIDE), WIDE)
    taps_ref[0, here, :] = pltpu.roll(value, 1, 0).astype(taps_ref.dtype)
    taps_ref[1, here, :] = value.astype(taps_ref.dtype)
    taps_ref[2, here, :] = pltpu.roll(value, WIDE - 1, 0).astype(taps_ref.dtype)


def call(body, outs, scratch, flops, *args, smem=1):
    specs = tuple(
        pl.BlockSpec(memory_space=pltpu.SMEM)
        if place < smem
        else jax.tree.map(lambda _: pl.BlockSpec(memory_space=pltpu.VMEM), arg)
        for place, arg in enumerate(args)
    )
    moved = sum(a.size * a.dtype.itemsize for a in jax.tree.leaves((args, outs)))
    return pl.pallas_call(
        body,
        out_shape=outs,
        in_specs=specs,
        out_specs=[pl.BlockSpec(memory_space=pltpu.VMEM)] * len(outs),
        scratch_shapes=scratch,
        compiler_params=pltpu.CompilerParams(vmem_limit_bytes=VMEM_LIMIT),
        cost_estimate=pl.CostEstimate(flops=flops, bytes_accessed=moved, transcendentals=0),
        name=getattr(body, "func", body).__name__,
    )(*args)


def shape(dims, kind=F32):
    return jax.ShapeDtypeStruct(dims, kind)


def slot_refs(even_ref, odd_ref, across_ref):
    return even_ref.at[0], odd_ref.at[0], across_ref.at[0], across_ref.at[1]


def pack(
    mid_ref,
    squeeze_ref,
    gain_in_ref,
    shift_in_ref,
    gain_mid_ref,
    shift_mid_ref,
    bias_ref,
    gain_out_ref,
    shift_out_ref,
    excite_ref,
    out_ref,
    target_ref,
    small_ref,
):
    lanes = target_ref.shape[1]
    own = lanes // 2
    small_ref[...] = jnp.zeros_like(small_ref)
    small_ref[0:1, :own] = gain_in_ref[...].astype(F32)
    small_ref[0:1, own:] = shift_in_ref[...].astype(F32)
    for row, ref in enumerate((gain_mid_ref, shift_mid_ref, bias_ref)):
        value = ref[...].astype(F32)
        small_ref[row + 1 : row + 2, :own] = value[0:1]
        small_ref[row + 1 : row + 2, own:] = value[1:2]
    for t, ref in enumerate((gain_out_ref, shift_out_ref)):
        value = ref[...].astype(F32)
        small_ref[4 + 2 * t : 5 + 2 * t, :] = value[:, :lanes]
        small_ref[5 + 2 * t : 6 + 2 * t, :] = value[:, lanes:]
    row = 0
    for ref in (mid_ref, squeeze_ref, small_ref, excite_ref):
        target_ref[row : row + ref.shape[0], :] = ref[...].astype(BF16)
        row += ref.shape[0]
    for block in range(out_ref.shape[1] // lanes):
        rows = out_ref.shape[0]
        target_ref[row : row + rows, :] = out_ref[:, block * lanes : (block + 1) * lanes]
        row += rows


def reduce_in(
    counts_ref, x0, x1, x2, x3, a0, a1, a2, a3, pre_ref, msg_ref, w_ref, wall_ref, flat_ref
):
    place = Place(counts_ref)
    images = wall_ref.shape[0] // place.groups
    spot = lax.broadcasted_iota(jnp.int32, wall_ref.shape, 0)
    real = jnp.zeros(wall_ref.shape, jnp.int32)
    for slot in range(place.groups):
        number = place.images(place.depth ^ (slot >> 1), place.core ^ (slot & 1))
        here = (spot >= slot * images) & (spot < slot * images + number)
        real = jnp.where(here, 1, real)
    wall_ref[...] = real.astype(F32)
    own = w_ref.shape[1] // len(SLOTS)
    lanes = w_ref.shape[2]
    for s, piece in enumerate((a0, a1, a2, a3)):
        here = pl.ds(pl.multiple_of((place.chan ^ s) * own, own), own)
        for block in range(w_ref.shape[0]):
            w_ref[block, here, :] = piece[:, block * lanes : (block + 1) * lanes]
    parts = [dot_nt(x[...], w_ref[place.batch ^ s]) for s, x in enumerate((x0, x1, x2, x3))]
    flat_ref[...] = functools.reduce(jnp.add, parts)
    spread_map_rows(flat_ref, pre_ref)
    first = jnp.zeros((1, pre_ref.shape[1]), F32)
    second = jnp.zeros((1, pre_ref.shape[1]), F32)
    for image in range(pre_ref.shape[0] // PADDED):
        real = place.real(image)
        value = pre_ref[image * PADDED : (image + 1) * PADDED, :]
        first = first + real * total_of(value)
        second = second + real * total_of(value * value)
    rows = x0.shape[0]
    spot = lax.broadcasted_iota(jnp.int32, (16, rows), 1)
    real = (spot < place.images(place.depth, place.core) * PIXELS).astype(BF16)
    columns = [dot_nn(real, x[...])[0:1] for x in (x0, x1, x2, x3)]
    msg_ref[...] = jnp.concatenate([first, second] + columns, axis=0)


def place_mid(
    counts_ref,
    b0,
    b1,
    b2,
    b3,
    w_ref,
    w_back_ref,
    squeeze_ref,
    in_affine_ref,
    mid_affine_ref,
    bias_ref,
    out_affine_ref,
    small_ref,
):
    place = Place(counts_ref)
    width, lanes = w_ref.shape[1], b0.shape[1]
    own = width // len(SLOTS)
    for s, piece in enumerate((b0, b1, b2, b3)):
        at = pl.multiple_of((place.chan ^ s) * own, own)
        for tap in range(9):
            for r in range(2):
                block = piece[(2 * tap + r) * own : (2 * tap + r + 1) * own, :]
                w_ref[r, pl.ds(at, own), tap * lanes : (tap + 1) * lanes] = block
                w_back_ref[r, pl.ds(tap * width + at, own), :] = block
        squeeze_ref[pl.ds(at, own), :] = piece[18 * own : 19 * own, :]
        small = piece[19 * own : 19 * own + 16, :].astype(F32)
        small_ref[place.chan ^ s] = small
        for t in range(2):
            out_affine_ref[t, place.chan ^ s, :, :lanes] = small[4 + 2 * t : 5 + 2 * t, :]
            out_affine_ref[t, place.chan ^ s, :, lanes:] = small[5 + 2 * t : 6 + 2 * t, :]
    for k in range(len(SLOTS)):
        here = slice(k * own, (k + 1) * own)
        there = slice(width + k * own, width + (k + 1) * own)
        in_affine_ref[0:1, here] = small_ref[k, 0:1, :own]
        in_affine_ref[1:2, here] = small_ref[k, 0:1, own:]
        for t in range(2):
            mid_affine_ref[t : t + 1, here] = small_ref[k, 1 + t : 2 + t, :own]
            mid_affine_ref[t : t + 1, there] = small_ref[k, 1 + t : 2 + t, own:]
        bias_ref[0:1, here] = small_ref[k, 3:4, :own]
        bias_ref[0:1, there] = small_ref[k, 3:4, own:]


def place_rest(counts_ref, b0, b1, b2, b3, excite_ref, w_out_ref):
    place = Place(counts_ref)
    width, lanes = w_out_ref.shape[1], b0.shape[1]
    own = width // len(SLOTS)
    for s, piece in enumerate((b0, b1, b2, b3)):
        row = 19 * own + 16
        for r in range(2):
            at = pl.multiple_of(r * width + (place.chan ^ s) * own, own)
            excite_ref[pl.ds(at, own), :] = piece[row : row + own, :]
            row += own
        w_out_ref[place.chan ^ s, :, :lanes] = piece[row : row + width, :]
        w_out_ref[place.chan ^ s, :, lanes:] = piece[row + width : row + 2 * width, :]


def conv_mid(
    counts_ref,
    pre_ref,
    sums_refs,
    affine_ref,
    w_ref,
    taps_ref,
    mid_ref,
    msg_ref,
):
    place = Place(counts_ref)
    images = pre_ref.shape[0] // PADDED
    total = place.total() * PIXELS
    sums = summed_over(sums_refs)
    center, scale = moments(sums[0:1], sums[1:2], total)
    gain = affine_ref[0:1, :] * scale
    shift = affine_ref[1:2, :] - center * gain
    clear_gaps(taps_ref, images)
    keep = columns_real(WIDE)
    for image in range(images):

        def normalize(step, carry, image=image):
            rows = pl.multiple_of(step * WIDE, WIDE)
            value = pre_ref[pl.ds(image * PADDED + rows, WIDE), :]
            value = silu(value * gain + shift) * keep
            store_taps(taps_ref, image * STRIDE + WIDE + rows, value)
            return carry

        lax.fori_loop(0, SIDE, normalize, 0, unroll=SIDE)
    half = pre_ref.shape[1] // 2
    width = pre_ref.shape[1]
    keep = columns_real(PADDED)
    firsts = [jnp.zeros((1, width), F32) for _ in range(2)]
    seconds = [jnp.zeros((1, width), F32) for _ in range(2)]
    for image in range(images):
        real = place.real(image)
        for r in range(2):
            left = jnp.concatenate(
                [
                    taps_ref[
                        b,
                        image * STRIDE + a * WIDE : image * STRIDE + a * WIDE + PADDED,
                        r * half : (r + 1) * half,
                    ]
                    for a in range(3)
                    for b in range(3)
                ],
                axis=1,
            )
            value = dot_nt(left, w_ref[r])
            mid_ref[image * PADDED : (image + 1) * PADDED, r * width : (r + 1) * width] = value
            held = value * keep
            firsts[r] = firsts[r] + real * total_of(held)
            seconds[r] = seconds[r] + real * total_of(held * held)
    sums = jnp.concatenate(
        [jnp.concatenate(firsts, axis=1), jnp.concatenate(seconds, axis=1)], axis=0
    )
    msg_ref[...] = sums


def mid_norm(
    place,
    sums_refs,
    affine_ref,
):
    sums = summed_over(sums_refs)
    center, scale = moments(sums[0:1], sums[1:2], place.total() * PIXELS)
    gain = affine_ref[0:1, :] * scale
    return center, scale, gain, affine_ref[1:2, :] - center * gain


def pool(
    counts_ref,
    mid_ref,
    sums_refs,
    affine_ref,
    squeeze_ref,
    pooled_ref,
    msg_ref,
):
    place = Place(counts_ref)
    images = mid_ref.shape[0] // PADDED
    width = mid_ref.shape[1] // 2
    lanes = msg_ref.shape[1]
    center, scale, gain, shift = mid_norm(place, sums_refs, affine_ref)
    keep = columns_real(CHUNK)
    inclines = [[], []]
    for image in range(images):

        def gather(step, carry, image=image):
            active, rise, lean = carry
            at = pl.multiple_of(image * PADDED + step * CHUNK, CHUNK)
            before = mid_ref[pl.ds(at, CHUNK), :]
            value = before * gain + shift
            share = logistic(value) * keep
            active = active + fold(value * share)
            inclined = share + value * (share * (1.0 - share))
            return active, rise + fold(inclined), lean + fold(inclined * before)

        nothing = jnp.zeros((8, 2 * width), F32)
        active, rise, lean = lax.fori_loop(
            0, SIDE, gather, (nothing, nothing, nothing), unroll=SIDE
        )
        active = total_of(active)
        pooled_ref[image : image + 1, :] = (active[:, :width] + active[:, width:]) / PIXELS
        rise = total_of(rise)
        inclines[0].append(rise)
        inclines[1].append(scale * (total_of(lean) - center * rise))
    inclined = jnp.concatenate(inclines[0] + inclines[1], axis=0)
    msg_ref[...] = jnp.zeros_like(msg_ref)
    for q in range(2 * width // lanes):
        row = 8 + q * 2 * images
        msg_ref[row : row + 2 * images, :] = inclined[:, q * lanes : (q + 1) * lanes]
    msg_ref[0:images, :] = exact_dot(dot_nn, pooled_ref[...], squeeze_ref[...])[:images]
    real = [place.real(image) * pooled_ref[image : image + 1, :] for image in range(images)]
    real = functools.reduce(jnp.add, real)
    for q in range(width // lanes):
        msg_ref[images + q : images + q + 1, :] = real[:, q * lanes : (q + 1) * lanes]


def gate_norm(
    place,
    rows,
    wall,
):
    return moments(total_of(wall * rows), total_of(wall * rows * rows), place.total())


def attend(
    counts_ref,
    gathered_refs,
    wall_ref,
    gate_affine_ref,
    excite_ref,
    bias_ref,
    mid_ref,
    mid_sums_refs,
    mid_affine_ref,
    w_out_ref,
    gate_ref,
    attention_ref,
    weighted_ref,
    out_ref,
    msg_ref,
    wide_ref,
    flat_ref,
):
    place = Place(counts_ref)
    images = mid_ref.shape[0] // PADDED
    width = mid_ref.shape[1] // 2
    rows = slot_rows(gathered_refs, GATHERED, 0, images)
    center, scale = gate_norm(place, rows, wall_ref[...])
    normed = (rows[0:images] - center) * scale
    gate_pre = normed * gate_affine_ref[0:1, :] + gate_affine_ref[1:2, :]
    gate = silu(gate_pre)
    gate_ref[0] = gate
    gate_ref[1] = slope(gate_pre)
    logits = (
        exact_dot(dot_nt, gate, excite_ref[...])[:images] + bias_ref[...]
    )
    lean = 0.5 * jnp.tanh(0.5 * (logits[:, :width] - logits[:, width:]))
    attention_ref[:, :width] = 0.5 + lean
    attention_ref[:, width:] = 0.5 - lean
    center, scale, gain, shift = mid_norm(place, mid_sums_refs, mid_affine_ref)
    for image in range(images):
        share = attention_ref[image : image + 1, :]

        def weigh(step, carry, image=image, share=share):
            at = pl.multiple_of(image * PADDED + step * CHUNK, CHUNK)
            value = share * silu(mid_ref[pl.ds(at, CHUNK), :] * gain + shift)
            wide_ref[pl.ds(at, CHUNK), :] = value[:, :width] + value[:, width:]
            return carry

        lax.fori_loop(0, SIDE, weigh, 0, unroll=SIDE)
    pack_map_rows(wide_ref, flat_ref)
    weighted_ref[...] = flat_ref[...].astype(BF16)
    spot = lax.broadcasted_iota(jnp.int32, (flat_ref.shape[0], 1), 0)
    real = (spot < place.images(place.depth, place.core) * PIXELS).astype(F32)
    blocks = w_out_ref.shape[0]
    for k in range(blocks):
        value = dot_nn(weighted_ref[...], w_out_ref[place.batch ^ k])
        out_ref[k] = value
        held = value * real
        for t, row in enumerate((total_of(held), total_of(held * value))):
            msg_ref[t * blocks + k : t * blocks + k + 1, :] = row


def finish(
    counts_ref,
    out_ref,
    sums_refs,
    affine_ref,
    x_refs,
    cot_even_ref,
    cot_odd_ref,
    cot_across_ref,
    near_ref,
    far_ref,
    grad_ref,
    msg_ref,
):
    place = Place(counts_ref)
    cot_refs = slot_refs(cot_even_ref, cot_odd_ref, cot_across_ref)
    blocks, rows, lanes = out_ref.shape
    sums = summed_over(sums_refs)
    center, scale = moments(sums[:blocks], sums[blocks:], place.total() * PIXELS)
    limit = place.images(place.depth, place.core) * PIXELS
    for k in range(blocks):
        mu, r = center[k : k + 1], scale[k : k + 1]
        block = place.batch ^ k
        gain = affine_ref[0, block] * r
        shift = affine_ref[1, block] - mu * gain
        x_ref, upstream_ref = x_refs[k], cot_refs[k]
        summed_ref = (near_ref, far_ref)[k >> 1].at[k & 1]

        def chunk(
            step, carry, k=k, gain=gain, shift=shift,
            x_ref=x_ref, upstream_ref=upstream_ref, summed_ref=summed_ref,
        ):
            first, second = carry
            at = pl.multiple_of(step * CHUNK, CHUNK)
            here = pl.ds(at, CHUNK)
            spot = lax.broadcasted_iota(jnp.int32, (CHUNK, 1), 0) + at
            real = (spot < limit).astype(F32)
            before = out_ref[k, here, :]
            summed = x_ref[here, :].astype(F32) + (before * gain + shift)
            summed_ref[here, :] = summed.astype(BF16)
            share = logistic(summed)
            grad = upstream_ref[here, :].astype(F32) * real * (share * (1.0 + summed * (1.0 - share)))
            grad_ref[k, here, :] = grad
            return first + fold(grad), second + fold(grad * before)

        nothing = jnp.zeros((8, lanes), F32)
        first, second = lax.fori_loop(
            0, rows // CHUNK, chunk, (nothing, nothing), unroll=UNROLL
        )
        first = total_of(first)
        for t, row in enumerate((first, r * (total_of(second) - mu * first))):
            msg_ref[t * blocks + k : t * blocks + k + 1, :] = row


def finish_owned(counts_ref, summed_ref, swapped_ref, cot_ref, result_ref, grad_ref):
    chan, group = lax.axis_index("chan"), lax.axis_index("dp")
    pieces = summed_ref.at[0], swapped_ref.at[0], summed_ref.at[2], swapped_ref.at[1]
    rows = cot_ref.shape[1]
    for s, piece in enumerate(pieces):
        batch = chan ^ s
        limit = counts_ref[batch, group] * PIXELS

        def chunk(step, carry, piece=piece, batch=batch, limit=limit):
            at = pl.multiple_of(step * CHUNK, CHUNK)
            here = pl.ds(at, CHUNK)
            spot = lax.broadcasted_iota(jnp.int32, (CHUNK, 1), 0) + at
            real = (spot < limit).astype(F32)
            summed = piece[here, :].astype(F32)
            share = logistic(summed)
            held = share * real
            result_ref[batch, here, :] = (summed * held).astype(BF16)
            grad = cot_ref[batch, here, :].astype(F32) * (held * (1.0 + summed * (1.0 - share)))
            grad_ref[batch, here, :] = grad.astype(BF16)
            return carry

        lax.fori_loop(0, rows // CHUNK, chunk, 0, unroll=UNROLL)


def back_out(
    counts_ref,
    grad_ref,
    out_ref,
    sums_refs,
    back_refs,
    affine_ref,
    w_out_ref,
    mid_ref,
    mid_sums_refs,
    mid_affine_ref,
    attention_ref,
    gate_ref,
    excite_ref,
    low_ref,
    gw_ref,
    logits_ref,
    msg_ref,
    flat_ref,
):
    place = Place(counts_ref)
    blocks, rows, lanes = out_ref.shape
    images = attention_ref.shape[0]
    width = attention_ref.shape[1] // 2
    total = place.total() * PIXELS
    sums = summed_over(sums_refs)
    center, scale = moments(sums[:blocks], sums[blocks:], total)
    back = summed_over(back_refs) / total
    limit = place.images(place.depth, place.core) * PIXELS
    for k in range(blocks):
        mu, r = center[k : k + 1], scale[k : k + 1]
        gain = affine_ref[0, place.batch ^ k] * r
        second = gain * r * back[blocks + k : blocks + k + 1]
        first = gain * back[k : k + 1] - mu * second

        def chunk(step, carry, k=k, gain=gain, first=first, second=second):
            at = pl.multiple_of(step * CHUNK, CHUNK)
            here = pl.ds(at, CHUNK)
            spot = lax.broadcasted_iota(jnp.int32, (CHUNK, 1), 0) + at
            real = (spot < limit).astype(F32)
            value = gain * grad_ref[k, here, :] - real * (first + out_ref[k, here, :] * second)
            low_ref[k, here, :] = value.astype(BF16)
            return carry

        lax.fori_loop(0, rows // CHUNK, chunk, 0, unroll=UNROLL)
    parts = [dot_nt(low_ref[k], w_out_ref[place.batch ^ k]) for k in range(blocks)]
    flat_ref[...] = functools.reduce(jnp.add, parts)
    spread_map_rows(flat_ref, gw_ref)
    center, scale, gain, shift = mid_norm(place, mid_sums_refs, mid_affine_ref)
    rises, leans, attended = [], [], []
    for image in range(images):

        def gather(step, carry, image=image):
            attended, rise, lean = carry
            at = pl.multiple_of(image * PADDED + step * CHUNK, CHUNK)
            before = mid_ref[pl.ds(at, CHUNK), :]
            value = before * gain + shift
            share = logistic(value)
            grad = gw_ref[pl.ds(at, CHUNK), :]
            grad = jnp.concatenate([grad, grad], axis=1)
            active = grad * share
            attended = attended + fold(active * value)
            inclined = active * (1.0 + value * (1.0 - share))
            return attended, rise + fold(inclined), lean + fold(inclined * before)

        nothing = jnp.zeros((8, 2 * width), F32)
        parts = lax.fori_loop(
            0, SIDE, gather, (nothing, nothing, nothing), unroll=SIDE
        )
        share = attention_ref[image : image + 1, :]
        attended.append(total_of(parts[0]))
        rise = total_of(parts[1])
        rises.append(share * rise)
        leans.append(share * (scale * (total_of(parts[2]) - center * rise)))
    grad = jnp.concatenate(attended, axis=0)
    attention = attention_ref[...]
    inner = attention * grad
    inner = inner[:, :width] + inner[:, width:]
    logits = attention * (grad - jnp.concatenate([inner, inner], axis=1))
    logits_ref[...] = logits
    gate = exact_dot(dot_nn, logits, excite_ref[...])[:images] * gate_ref[1]
    pack = msg_ref.shape[1]
    pieces = 2 * width // pack
    for t, row in enumerate((functools.reduce(jnp.add, rises), functools.reduce(jnp.add, leans))):
        for q in range(pieces):
            msg_ref[t * pieces + q : t * pieces + q + 1, :] = row[:, q * pack : (q + 1) * pack]
    msg_ref[2 * pieces : 2 * pieces + images, :] = gate


def back_mid(
    counts_ref,
    back_refs,
    gathered_refs,
    wall_ref,
    gate_affine_ref,
    squeeze_ref,
    attention_ref,
    gw_ref,
    mid_ref,
    mid_sums_refs,
    mid_affine_ref,
    pre_ref,
    sums_refs,
    affine_ref,
    w_ref,
    low_ref,
    grad_ref,
    gate_ref,
    vector_ref,
    msg_ref,
    taps_ref,
):
    place = Place(counts_ref)
    images = attention_ref.shape[0]
    width = attention_ref.shape[1] // 2
    lanes = wall_ref.shape[1]
    pieces = 2 * width // lanes
    total = place.total() * PIXELS
    wall = wall_ref[...]
    rows = slot_rows(gathered_refs, GATHERED, 0, images)
    center, scale = gate_norm(place, rows, wall)
    gain = gate_affine_ref[0:1, :] * scale
    normed = (rows - center) * scale
    grads = slot_rows(back_refs, images, 0, images, 2 * pieces)
    first, second = total_of(wall * grads), total_of(wall * grads * normed)
    vector_ref[0:1, 0:lanes] = second
    vector_ref[0:1, lanes : 2 * lanes] = first
    squeezed = gain * (grads - wall * (first + normed * second) / place.total())
    gate_ref[...] = squeezed[0:images]
    pooled_grad = exact_dot(dot_nt, squeezed, squeeze_ref[...]) / PIXELS
    pooled_grad = jnp.concatenate([pooled_grad, pooled_grad], axis=1)
    slot = 0
    terms = jnp.zeros((2 * images, 2 * width), F32)
    for ref in gathered_refs:
        for at in range(8, ref.shape[0], GATHERED):
            inclines = [
                ref[at + q * 2 * images : at + (q + 1) * 2 * images, :] for q in range(pieces)
            ]
            grad = pooled_grad[slot * images : (slot + 1) * images, :]
            grad = jnp.concatenate([grad, grad], axis=0)
            terms = terms + jnp.concatenate(inclines, axis=1) * grad
            slot += 1
    sums = functools.reduce(jnp.add, [ref[0 : 2 * pieces, :] for ref in back_refs])
    back = []
    for t in range(2):
        row = [sums[t * pieces + q : t * pieces + q + 1, :] for q in range(pieces)]
        back.append(
            jnp.concatenate(row, axis=1) + total_of(terms[t * images : (t + 1) * images])
        )
    vector_ref[1:2, :] = back[1]
    vector_ref[2:3, :] = back[0]
    own = pooled_grad[0:images]
    center, scale, gain, shift = mid_norm(place, mid_sums_refs, mid_affine_ref)
    second = gain * scale * back[1] / total
    first = gain * back[0] / total - center * second
    clear_gaps(taps_ref, images)
    keep = columns_real(WIDE)
    for image in range(images):
        share = gain * attention_ref[image : image + 1, :]
        offset = gain * own[image : image + 1, :]
        real = place.real(image)
        lead, lag = real * first, real * second

        def chunk(step, carry, image=image, share=share, offset=offset, lead=lead, lag=lag):
            rows = pl.multiple_of(step * WIDE, WIDE)
            here = pl.ds(image * PADDED + rows, WIDE)
            before = mid_ref[here, :]
            grad = gw_ref[here, :]
            grad = jnp.concatenate([grad, grad], axis=1)
            grad = (share * grad + offset) * slope(before * gain + shift)
            value = (grad - (lead + before * lag)) * keep
            store_taps(taps_ref, image * STRIDE + WIDE + rows, value)
            return carry

        lax.fori_loop(0, SIDE, chunk, 0, unroll=SIDE)
    low_ref[...] = taps_ref[1]
    sums = summed_over(sums_refs)
    center, scale = moments(sums[0:1], sums[1:2], total)
    gain = affine_ref[0:1, :] * scale
    shift = affine_ref[1:2, :] - center * gain
    half = width // 2
    keep = columns_real(PADDED)
    firsts = [jnp.zeros((1, half), F32) for _ in range(2)]
    seconds = [jnp.zeros((1, half), F32) for _ in range(2)]
    for image in range(images):
        real = place.real(image)
        here = slice(image * PADDED, (image + 1) * PADDED)
        for r in range(2):
            left = jnp.concatenate(
                [
                    taps_ref[
                        2 - b,
                        image * STRIDE + (2 - a) * WIDE : image * STRIDE + (2 - a) * WIDE + PADDED,
                        r * width : (r + 1) * width,
                    ]
                    for a in range(3)
                    for b in range(3)
                ],
                axis=1,
            )
            lane = slice(r * half, (r + 1) * half)
            before = pre_ref[here, lane]
            value = dot_nn(left, w_ref[r]) * slope(before * gain[:, lane] + shift[:, lane])
            value = value * (keep * real)
            grad_ref[here, lane] = value
            firsts[r] = firsts[r] + total_of(value)
            seconds[r] = seconds[r] + total_of(value * before)
    first = jnp.concatenate(firsts, axis=1)
    second = scale * (jnp.concatenate(seconds, axis=1) - center * first)
    sums = jnp.concatenate([first, second], axis=0)
    msg_ref[...] = sums


def sort_pieces(
    place,
    source_ref,
    keep_ref,
    send_ref,
    row,
):
    for turn, s in enumerate(ORDER):
        target = keep_ref if turn < 2 else send_ref
        rows = source_ref.shape[1]
        target[turn % 2, row : row + rows, :] = source_ref[place.chan ^ s].astype(BF16)


def weight_out_term(
    counts_ref,
    weighted_ref,
    low_ref,
    gate_ref,
    logits_ref,
    affine_ref,
    keep_ref,
    send_ref,
    wide_ref,
    small_ref,
):
    place = Place(counts_ref)
    width = weighted_ref.shape[1]
    lanes = keep_ref.shape[2]
    own = width // len(SLOTS)
    center = expected(affine_ref[0:1, :], affine_ref[1:2, :])
    center = 0.5 * (center[:, :width] + center[:, width:])
    for turn, s in enumerate(ORDER):
        target = keep_ref if turn < 2 else send_ref
        held = place.batch ^ place.chan ^ s
        term = dot_tn(weighted_ref[...], low_ref[held])
        term = (term - outer(center, row_sums(low_ref[held]), True)).astype(BF16)
        target[turn % 2, 0:width, :] = term[:, :lanes]
        target[turn % 2, width : 2 * width, :] = term[:, lanes:]
    wide_ref[...] = dot_tn(logits_ref[...], gate_ref[0], HIGHEST)
    for turn, s in enumerate(ORDER):
        target = keep_ref if turn < 2 else send_ref
        for r in range(2):
            at = pl.multiple_of(r * width + (place.chan ^ s) * own, own)
            row = 2 * width + r * own
            target[turn % 2, row : row + own, :] = wide_ref[pl.ds(at, own), :].astype(BF16)
    small_ref[...] = jnp.zeros_like(small_ref)
    bias = total_of(logits_ref[...])
    for k in range(len(SLOTS)):
        small_ref[k, 0:1, :own] = bias[:, k * own : (k + 1) * own]
        small_ref[k, 0:1, own:] = bias[:, width + k * own : width + (k + 1) * own]
    sort_pieces(place, small_ref, keep_ref, send_ref, 2 * width + 2 * own)


def weight_mid_term(
    counts_ref,
    taps_ref,
    low_ref,
    affine_ref,
    keep_ref,
    send_ref,
    wide_ref,
):
    place = Place(counts_ref)
    center = expected(affine_ref[0:1, :], affine_ref[1:2, :])
    half = taps_ref.shape[2] // 2
    width = low_ref.shape[1] // 2
    own = width // len(SLOTS)
    rows = low_ref.shape[0] - 2 * WIDE
    for r in range(2):
        right = jnp.concatenate(
            [
                taps_ref[b, a * WIDE : a * WIDE + rows, r * half : (r + 1) * half]
                for a in range(3)
                for b in range(3)
            ],
            axis=1,
        )
        low = low_ref[WIDE : WIDE + rows, r * width : (r + 1) * width]
        offset = jnp.concatenate([center[:, r * half : (r + 1) * half]] * 9, axis=1)
        wide_ref[...] = dot_tn(low, right) - outer(row_sums(low), offset)
        for turn, s in enumerate(ORDER):
            target = keep_ref if turn < 2 else send_ref
            here = pl.ds(pl.multiple_of((place.chan ^ s) * own, own), own)
            for tap in range(9):
                row = (2 * tap + r) * own
                target[turn % 2, row : row + own, :] = wide_ref[
                    here, tap * half : (tap + 1) * half
                ].astype(BF16)


def back_in(
    share,
    counts_ref,
    grad_ref,
    pre_ref,
    sums_refs,
    back_refs,
    affine_ref,
    x0,
    x1,
    x2,
    x3,
    vector_ref,
    out_back_refs,
    pooled_ref,
    gathered_refs,
    squeezed_ref,
    low_ref,
    keep_ref,
    send_ref,
    flat_ref,
    wide_ref,
    narrow_ref,
    small_ref,
):
    place = Place(counts_ref)
    images = pre_ref.shape[0] // PADDED
    width = pre_ref.shape[1]
    own = width // len(SLOTS)
    chan, batch = place.chan, place.batch
    total = place.total() * PIXELS
    sums = summed_over(sums_refs)
    center, scale = moments(sums[0:1], sums[1:2], total)
    back = summed_over(back_refs)
    gain = affine_ref[0:1, :] * scale
    second = gain * scale * back[1:2] / total
    first = gain * back[0:1] / total - center * second
    for image in range(images):
        real = place.real(image)
        lead, lag = real * first, real * second
        for line in range(SIDE):
            at = image * PADDED + line * WIDE
            before = pre_ref[at : at + WIDE, :]
            value = gain * grad_ref[at : at + WIDE, :] - (lead + before * lag)
            at = image * PIXELS + line * SIDE
            flat_ref[at : at + SIDE, :] = value[:SIDE]
    low_ref[...] = flat_ref[...].astype(BF16)
    lanes = keep_ref.shape[2]
    low_sums = row_sums(low_ref[...])
    for k, x in enumerate((x0, x1, x2, x3)):
        wide_ref[...] = dot_tn(low_ref[...], x[...]) - outer(low_sums, sums[2 + k : 3 + k] / total)
        for turn, s in enumerate(ORDER):
            target = keep_ref if turn < 2 else send_ref
            here = pl.ds(pl.multiple_of((chan ^ s) * own, own), own)
            for part in range(wide_ref.shape[1] // lanes):
                at = pl.multiple_of(((batch ^ k) * (wide_ref.shape[1] // lanes) + part) * own, own)
                target[turn % 2, pl.ds(at, own), :] = wide_ref[
                    here, part * lanes : (part + 1) * lanes
                ].astype(BF16)
    mean = [
        total_of(slot_rows(gathered_refs, GATHERED, images + q, 1)) for q in range(width // lanes)
    ]
    mean = jnp.concatenate(mean, axis=1) / place.total()
    narrow_ref[...] = dot_tn(pooled_ref[...] - mean, squeezed_ref[...], HIGHEST)
    row = keep_ref.shape[1] - small_ref.shape[1] - own
    for turn, s in enumerate(ORDER):
        target = keep_ref if turn < 2 else send_ref
        here = pl.ds(pl.multiple_of((chan ^ s) * own, own), own)
        target[turn % 2, row : row + own, :] = narrow_ref[here, :].astype(BF16)
    small_ref[...] = jnp.zeros_like(small_ref)
    outs = summed_over(out_back_refs)
    for k in range(len(SLOTS)):
        here = slice(k * own, (k + 1) * own)
        there = slice(width + k * own, width + (k + 1) * own)
        small_ref[k, 0:1, :own] = back[1:2, here]
        small_ref[k, 0:1, own:] = back[0:1, here]
        for t in range(2):
            small_ref[k, 1 + t : 2 + t, :own] = vector_ref[1 + t : 2 + t, here]
            small_ref[k, 1 + t : 2 + t, own:] = vector_ref[1 + t : 2 + t, there]
        small_ref[k, 3:4, :] = vector_ref[0:1, 0:lanes]
        small_ref[k, 4:5, :] = vector_ref[0:1, lanes : 2 * lanes]
    for s in SLOTS:
        for t in range(2):
            row = outs[(1 - t) * len(SLOTS) + s : (1 - t) * len(SLOTS) + s + 1, :]
            small_ref[batch ^ s, 5 + 2 * t : 6 + 2 * t, :] = row[:, :lanes]
            small_ref[batch ^ s, 6 + 2 * t : 7 + 2 * t, :] = row[:, lanes:]
    small_ref[...] = small_ref[...] * share
    sort_pieces(place, small_ref, keep_ref, send_ref, keep_ref.shape[1] - small_ref.shape[1])


def grad_owned(low_refs, w_ref, summed_ref, result_ref):
    chan = lax.axis_index("chan")
    for s, low_ref in enumerate(low_refs):
        value = dot_nn(low_ref[...], w_ref[chan]) + summed_ref[chan ^ s].astype(F32)
        result_ref[chan ^ s] = value.astype(BF16)


def add_groups(terms_ref, sum_ref):
    value = jnp.sum(terms_ref[...].astype(F32), axis=0).astype(BF16)
    sum_ref[...] = jnp.broadcast_to(value[None], sum_ref.shape)


def added(left_ref, right_ref):
    return left_ref[...].astype(F32) + right_ref[...].astype(F32)


def add_core(keep_refs, arrived_refs, kept_ref, send_ref):
    at = 0
    for keep_ref, arrived_ref in zip(keep_refs, arrived_refs):
        value = added(keep_ref, arrived_ref).astype(BF16)
        rows = keep_ref.shape[1]
        kept_ref[at : at + rows, :] = value[0]
        send_ref[at : at + rows, :] = value[1]
        at += rows
    if at < kept_ref.shape[0]:
        for ref in (kept_ref, send_ref):
            ref[at:, :] = jnp.zeros((kept_ref.shape[0] - at, ref.shape[1]), BF16)


def split_rows(parity, keep_ref, arrived_ref, kept_ref, send_ref):
    rows = kept_ref.shape[-2]
    for own, target in ((parity, kept_ref), (1 - parity, send_ref)):
        here = pl.ds(pl.multiple_of(own * rows, 16), rows)
        if target.ndim == 2:
            value = added(keep_ref.at[here, :], arrived_ref.at[here, :])
        else:
            value = added(keep_ref.at[:, here, :], arrived_ref.at[:, here, :])
        target[...] = value.astype(target.dtype)


def add_core_first(counts_ref, keep_ref, arrived_ref, kept_ref, send_ref):
    split_rows(Place(counts_ref).parity, keep_ref, arrived_ref, kept_ref, send_ref)


def add_parity_first(keep_ref, arrived_ref, kept_ref, send_ref):
    kept_ref[...] = added(keep_ref.at[0], arrived_ref.at[0])
    send_ref[...] = added(keep_ref.at[1], arrived_ref.at[1]).astype(BF16)


def add_chip(counts_ref, keep_ref, arrived_ref, kept_ref, send_ref):
    split_rows(Place(counts_ref).parity, keep_ref, arrived_ref, kept_ref, send_ref)


def add_last(counts_ref, keep_refs, arrived_refs, kept_ref, s1, s2, s3):
    place = Place(counts_ref)
    at = 0
    for keep_ref, arrived_ref in zip(keep_refs, arrived_refs):
        rows = keep_ref.shape[0] // len(SLOTS)
        for t, target in enumerate((kept_ref, s1, s2, s3)):
            here = pl.ds(pl.multiple_of((place.depth ^ t) * rows, 16), rows)
            value = added(keep_ref.at[here, :], arrived_ref.at[here, :])
            target[at : at + rows, :] = value.astype(target.dtype)
        at += rows


def add_depth(keep_ref, arrived_refs, sum_ref):
    value = keep_ref[...]
    for ref in arrived_refs:
        value = value + ref[...].astype(F32)
    sum_ref[...] = value.astype(BF16)


def join_depth(
    counts_ref,
    piece_refs,
    whole_ref,
):
    place = Place(counts_ref)
    rows = piece_refs[0].shape[0]
    for t, ref in enumerate(piece_refs):
        whole_ref[pl.ds(pl.multiple_of((place.depth ^ t) * rows, 16), rows), :] = ref[...]


def unpack(
    joined,
    counts_ref,
    term_refs,
    in_ref,
    gain_in_ref,
    shift_in_ref,
    mid_ref,
    gain_mid_ref,
    shift_mid_ref,
    squeeze_ref,
    gain_gate_ref,
    shift_gate_ref,
    excite_ref,
    bias_ref,
    out_ref,
    gain_out_ref,
    shift_out_ref,
    second_ref,
):
    own, lanes = squeeze_ref.shape
    width = out_ref.shape[0]
    places = [(out_ref, 0, 0, width), (out_ref, 0, 1, width), (excite_ref, 0, 0, 2 * own)]
    places += [(second_ref, 0, 0, 16)]
    places += [(in_ref, 0, block, own) for block in range(in_ref.shape[1] // lanes)]
    places += [(squeeze_ref, 0, 0, own), (second_ref, 16, 0, 16)]

    def write(value, row):
        start = 0
        for target, at, block, rows in places:
            first, last = max(row, start), min(row + value.shape[0], start + rows)
            if first < last:
                there = slice(at + first - start, at + last - start)
                target[there, block * lanes : (block + 1) * lanes] = value[first - row : last - row]
            start += rows

    if joined:
        mid_ref[...] = term_refs[0][...].astype(F32)
        write(term_refs[1][...].astype(F32), 0)
    else:
        even = Place(counts_ref).parity == 0
        piece = term_refs[0].shape[0] // len(SLOTS)
        rows = mid_ref.shape[0] // 2 // len(SLOTS)
        for half in range(2):
            mine, other = term_refs[half], term_refs[1 - half]
            for z in range(len(SLOTS)):
                here = slice(z * piece, (z + 1) * piece)
                value = jnp.where(even, mine[here, :].astype(F32), other[here, :].astype(F32))
                at = (half * len(SLOTS) + z) * rows
                mid_ref[at : at + rows, :] = value[:rows]
                write(value[rows:], (half * len(SLOTS) + z) * (piece - rows))

    def halves(target, row):
        target[0:1, :] = second_ref[row : row + 1, :own]
        target[1:2, :] = second_ref[row : row + 1, own:]

    halves(bias_ref, 0)
    row = 16
    gain_in_ref[...] = second_ref[row : row + 1, :own]
    shift_in_ref[...] = second_ref[row : row + 1, own:]
    halves(gain_mid_ref, row + 1)
    halves(shift_mid_ref, row + 2)
    gain_gate_ref[...] = second_ref[row + 3 : row + 4, :]
    shift_gate_ref[...] = second_ref[row + 4 : row + 5, :]
    for t, target in enumerate((gain_out_ref, shift_out_ref)):
        target[:, :lanes] = second_ref[row + 5 + 2 * t : row + 6 + 2 * t, :]
        target[:, lanes:] = second_ref[row + 6 + 2 * t : row + 7 + 2 * t, :]


def per_device(
    activations,
    counts,
    weight_in,
    gain_in,
    shift_in,
    weight_mid,
    gain_mid,
    shift_mid,
    weight_squeeze,
    gain_gate,
    shift_gate,
    weight_excite,
    shift_excite,
    weight_out,
    gain_out,
    shift_out,
    cotangent,
    *,
    groups,
    parts,
):
    batches, rows, lanes = activations.shape
    images = rows // PIXELS
    own = weight_in.shape[1]
    width = own * parts
    inter = gain_gate.shape[0]
    wide_rows = images * PADDED
    gap_rows = WIDE + images * STRIDE
    chan, group = lax.axis_index("chan"), lax.axis_index("dp")
    depth = groups // 2

    def permute(tensor, to):
        pairs = []
        for index in range(groups * parts):
            z, x, y, c = index // parts // 2, index // parts % 2, index % parts // 2, index % 2
            z, x, y, c = to(z, x, y, c)
            pairs.append((index, (2 * z + x) * parts + 2 * y + c))
        return lax.ppermute(tensor, ("dp", "chan"), pairs)

    def home(tensor, s):
        return permute(tensor, lambda z, x, y, c: (z, c ^ (s & 1), y ^ (s >> 1), x))

    def away_plane(tensor):
        return permute(tensor, lambda z, x, y, c: (z, c, y, x))

    def cross(even, odd):
        return even, odd, across(jnp.stack([even[1], odd[1]]))

    def core(tensor):
        return permute(tensor, lambda z, x, y, c: (z, x, y, c ^ 1))

    def across(tensor):
        return permute(tensor, lambda z, x, y, c: (z, x, y ^ 1, c))

    def parity(tensor):
        return permute(tensor, lambda z, x, y, c: (z, x ^ 1, y, c))

    def along(tensor, t):
        return permute(tensor, lambda z, x, y, c: (z ^ t, x, y, c))

    def after(tensor, *others):
        return lax.optimization_barrier((tensor,) + others)[0]

    def after_all(tensors, *others):
        return lax.optimization_barrier(tuple(tensors) + others)[: len(tensors)]

    def exchange(total, gather):
        def merge(mine, other):
            cut = 0 if total is None else total
            joined = [mine[:cut] + other[:cut]] if cut else []
            if gather:
                joined += [mine[cut : cut + gather], other[cut : cut + gather]]
            return jnp.concatenate(joined) if len(joined) > 1 else joined[0]

        def run(mine):
            nonlocal gather
            mine = merge(mine, core(mine))
            gather = 2 * gather
            if depth <= 4:
                return (mine,) + tuple(along(mine, t) for t in range(1, depth))
            step = 1
            while step < depth:
                mine = merge(mine, along(mine, step))
                gather, step = 2 * gather, 2 * step
            return (mine,)

        return run

    def padded(rows):
        return -(-rows // (16 * groups)) * 16 * groups

    def kernel(body, outs, *args, smem=1):
        return call(body, outs, [], 0, *args, smem=smem)

    def add_over_all(first, second, low, summed, finish_own):
        first_rows, second_rows = first[0].shape[1], sum(k.shape[1] for k in second[0])
        if groups != 8:
            rows = padded(first_rows + second_rows)
            keep, send = kernel(
                add_core,
                [shape((rows, 2 * own), BF16)] * 2,
                (first[0],) + second[0],
                (first[1],) + second[1],
                smem=0,
            )
            terms = (keep.astype(F32) + across(send).astype(F32)).astype(BF16)
            terms = lax.all_to_all(terms.reshape(groups, rows // groups, -1), "dp", 0, 0)
            (terms,) = kernel(add_groups, [shape(terms.shape, BF16)], terms, smem=0)
            terms = lax.all_to_all(terms, "dp", 0, 0).reshape(rows, -1)
            terms = terms[:first_rows], terms[first_rows : first_rows + second_rows]
            return (terms, low, across(low)) + tuple(finish_own(summed))
        second_rows = padded(second_rows)
        halves = (first_rows // 2, second_rows // 2)
        pieces = (first_rows // groups, second_rows // groups)

        def rows(number, kind=F32):
            return shape((number, 2 * own), kind)

        keep, second_send = kernel(add_core, [rows(second_rows, BF16)] * 2, *second, smem=0)
        arrived = across(second_send)
        pair = (2, halves[0], 2 * own)
        first_keep, send = call(
            add_core_first,
            [shape(pair), shape(pair, BF16)],
            [],
            0,
            counts,
            *first,
        )
        first_arrived = parity(send)
        arrived = after(arrived, summed, low)
        keep, send = call(
            add_chip,
            [rows(halves[1]), rows(halves[1], BF16)],
            [],
            0,
            counts,
            keep,
            arrived,
        )
        arrived = parity(send)
        first_keep, send = kernel(
            add_parity_first,
            [rows(halves[0]), rows(halves[0], BF16)],
            first_keep,
            first_arrived,
            smem=0,
        )
        first_arrived = across(send)
        arrived = after(arrived, first_arrived)
        keep, *send = call(
            add_last,
            [rows(sum(pieces))] + [rows(sum(pieces), BF16)] * (depth - 1),
            [],
            0,
            counts,
            (first_keep, keep),
            (first_arrived, arrived),
        )
        low_other = across(after(low, keep))
        result, grad_summed = finish_own(after(summed, keep))
        arrived = tuple(along(send[t - 1], t) for t in range(1, depth))
        arrived = after_all(arrived, result)
        (mine,) = kernel(add_depth, [rows(sum(pieces), BF16)], keep, arrived, smem=0)
        mine = (mine,) + tuple(along(mine, t) for t in range(1, depth))
        low, low_other = after_all((low, low_other), *mine)
        (mine,) = kernel(join_depth, [rows(sum(halves), BF16)], counts, mine)
        return (mine, parity(mine)), low, low_other, result, grad_summed

    def slots_of(tensor, *which):
        return [lax.dynamic_index_in_dim(tensor, chan ^ s, 0, keepdims=False) for s in which]

    far = slots_of(activations, 2, 3)
    first = after(weight_in.T, *far)
    other, near = across(first), core(first)
    x = slots_of(after(activations, near), 0, 1) + far
    x = tuple(home(piece, s) for s, piece in enumerate(x))

    (weights,) = call(
        pack,
        [shape((19 * own + 16 + inter + 2 * width, 2 * own), BF16)],
        [pltpu.VMEM((16, 2 * own), F32)],
        0,
        weight_mid.transpose(0, 1, 3, 4, 2).reshape(-1, 2 * own),
        weight_squeeze,
        gain_in.reshape(1, -1),
        shift_in.reshape(1, -1),
        gain_mid,
        shift_mid,
        shift_excite,
        gain_out.reshape(1, -1),
        shift_out.reshape(1, -1),
        weight_excite.transpose(1, 2, 0).reshape(-1, inter),
        weight_out,
        smem=0,
    )
    other = after(other, weights)
    first = (first, near, other, core(other))
    near = core(weights)
    cot = slots_of(after(cotangent, x[0], x[1]), *SLOTS)
    even, odd = jnp.stack([cot[0], cot[2]]), jnp.stack([cot[1], cot[3]])
    other = across(after(weights, x[2], x[3], first[3]))
    even = home(after(even, x[2], x[3]), 0)
    gate_affine = jnp.stack([gain_gate, shift_gate]).astype(F32)

    product = 2 * rows * lanes * parts * width
    pre_in, msg, w_in, wall = call(
        reduce_in,
        [
            shape((wide_rows, width)),
            shape((2 + parts, lanes)),
            shape((parts, width, lanes), BF16),
            shape((groups * images, inter)),
        ],
        [pltpu.VMEM((rows, width), F32)],
        product,
        counts,
        *x,
        *first,
    )
    in_sums = exchange(2 + parts, 0)(after(msg, near, odd))
    other = after(other, *in_sums)
    odd = home(after(odd, *in_sums), 1)
    weights = (weights, near, other, core(other))
    w_mid, w_mid_back, squeeze, in_affine, mid_affine, bias, out_affine = call(
        place_mid,
        [
            shape((2, width, 9 * inter), BF16),
            shape((2, 9 * width, inter), BF16),
            shape((width, inter), BF16),
            shape((2, width)),
            shape((2, 2 * width)),
            shape((1, 2 * width)),
            shape((2, parts, 1, lanes)),
        ],
        [pltpu.VMEM((parts, 16, 2 * own), F32)],
        0,
        counts,
        *weights,
    )
    conv = 2 * wide_rows * 9 * width * width
    taps, mid, msg = call(
        conv_mid,
        [
            shape((3, gap_rows, width), BF16),
            shape((wide_rows, 2 * width)),
            shape((2, 2 * width)),
        ],
        [],
        conv,
        counts,
        pre_in,
        in_sums,
        in_affine,
        w_mid,
    )
    mid_sums = exchange(2, 0)(msg)
    excite, w_out = call(
        place_rest,
        [
            shape((2 * width, inter), BF16),
            shape((parts, width, lanes), BF16),
        ],
        [],
        0,
        counts,
        *weights,
    )
    pooled, msg = call(
        pool,
        [shape((images, width)), shape((GATHERED, inter))],
        [],
        0,
        counts,
        mid,
        mid_sums,
        mid_affine,
        squeeze,
    )
    cot = cross(*after_all((even, odd), msg))
    gathered = exchange(None, GATHERED)(msg)
    gate, attention, weighted, out, msg = call(
        attend,
        [
            shape((2, images, inter)),
            shape((images, 2 * width)),
            shape((rows, width), BF16),
            shape((parts, rows, lanes)),
            shape((2 * parts, lanes)),
        ],
        [pltpu.VMEM((wide_rows, width), F32), pltpu.VMEM((rows, width), F32)],
        product,
        counts,
        gathered,
        wall,
        gate_affine,
        excite,
        bias,
        mid,
        mid_sums,
        mid_affine,
        w_out,
    )
    out_sums = exchange(2 * parts, 0)(msg)
    *summed, grad, msg = call(
        finish,
        [shape((2, rows, lanes), BF16)] * 2
        + [shape((parts, rows, lanes)), shape((2 * parts, lanes))],
        [],
        0,
        counts,
        out,
        out_sums,
        out_affine,
        x,
        *cot,
    )
    out_back = exchange(2 * parts, 0)(msg)

    near, far = summed
    far = across(far)

    sums_rows = 2 * 2 * width // inter
    low_out, grad_weighted, grad_logits, msg = call(
        back_out,
        [
            shape((parts, rows, lanes), BF16),
            shape((wide_rows, width)),
            shape((images, 2 * width)),
            shape((sums_rows + images, inter)),
        ],
        [pltpu.VMEM((rows, width), F32)],
        product,
        counts,
        grad,
        out,
        out_sums,
        out_back,
        out_affine,
        w_out,
        mid,
        mid_sums,
        mid_affine,
        attention,
        gate,
        excite,
    )
    mid_back = exchange(sums_rows, images)(msg)
    term_rows = 2 * width + 2 * own + 16
    keep, send = call(
        weight_out_term,
        [shape((2, term_rows, 2 * own), BF16)] * 2,
        [pltpu.VMEM((2 * width, inter), F32), pltpu.VMEM((parts, 16, 2 * own), F32)],
        product,
        counts,
        after(weighted, mid_back[0]),
        low_out,
        gate,
        grad_logits,
        mid_affine,
    )
    mid_back = after_all(mid_back, keep, far)
    summed = away_plane(after(jnp.concatenate([near, far]), mid_back[0]))
    out_keep, out_arrived = keep, core(after(send, mid_back[0]))
    low_mid, grad_hidden, grad_squeeze, vectors, msg = call(
        back_mid,
        [
            shape((gap_rows, 2 * width), BF16),
            shape((wide_rows, width)),
            shape((images, inter)),
            shape((8, 2 * width)),
            shape((2, width)),
        ],
        [pltpu.VMEM((3, gap_rows, 2 * width), BF16)],
        conv,
        counts,
        mid_back,
        gathered,
        wall,
        gate_affine,
        squeeze,
        attention,
        grad_weighted,
        mid,
        mid_sums,
        mid_affine,
        pre_in,
        in_sums,
        in_affine,
        w_mid_back,
    )
    in_back = exchange(2, 0)(after(msg, out_arrived))
    keep, send = call(
        weight_mid_term,
        [shape((2, 18 * own, 2 * own), BF16)] * 2,
        [pltpu.VMEM((width, 9 * inter), F32)],
        conv,
        counts,
        after(taps, in_back[0]),
        low_mid,
        in_affine,
    )
    in_back = after_all(in_back, keep)
    in_rows = parts * lanes // (2 * own) * own
    low_in, in_keep, in_send = call(
        functools.partial(back_in, 1.0 / groups),
        [shape((rows, width), BF16)] + [shape((2, in_rows + own + 16, 2 * own), BF16)] * 2,
        [
            pltpu.VMEM((rows, width), F32),
            pltpu.VMEM((width, lanes), F32),
            pltpu.VMEM((width, inter), F32),
            pltpu.VMEM((parts, 16, 2 * own), F32),
        ],
        product,
        counts,
        grad_hidden,
        pre_in,
        in_sums,
        in_back,
        in_affine,
        *x,
        vectors,
        out_back,
        pooled,
        gathered,
        grad_squeeze,
    )
    owned = shape((batches, rows, lanes), BF16)

    def finish_own(summed):
        swapped = core(jnp.stack([summed[1], summed[3]]))
        return call(finish_owned, [owned, owned], [], 0, counts, summed, swapped, cotangent)

    send = after(send, low_in)
    low_in = away_plane(low_in)
    terms, low_in, low_other, result, grad_summed = add_over_all(
        (keep, core(send)),
        ((out_keep, in_keep), (out_arrived, core(in_send))),
        low_in,
        summed,
        finish_own,
    )
    lows = (low_in, core(low_in), low_other, core(low_other))
    (grad_x,) = call(grad_owned, [owned], [], product, lows, w_in, grad_summed, smem=0)
    terms = after_all(terms, grad_x)
    (
        g_in,
        g_gain_in,
        g_shift_in,
        g_mid,
        g_gain_mid,
        g_shift_mid,
        g_squeeze,
        g_gain_gate,
        g_shift_gate,
        g_excite,
        g_bias,
        g_out,
        g_gain_out,
        g_shift_out,
    ) = call(
        functools.partial(unpack, groups != 8),
        [
            shape((own, parts * lanes)),
            shape((1, own)),
            shape((1, own)),
            shape((18 * own, inter)),
            shape((2, own)),
            shape((2, own)),
            shape((own, inter)),
            shape((1, inter)),
            shape((1, inter)),
            shape((2 * own, inter)),
            shape((2, own)),
            shape((width, lanes)),
            shape((1, lanes)),
            shape((1, lanes)),
        ],
        [pltpu.VMEM((32, 2 * own), F32)],
        0,
        counts,
        terms,
    )
    return (
        result,
        grad_x,
        g_in.T,
        g_gain_in.reshape(-1),
        g_shift_in.reshape(-1),
        g_mid.reshape(3, 3, 2, own, inter).transpose(0, 1, 4, 2, 3),
        g_gain_mid,
        g_shift_mid,
        g_squeeze,
        g_gain_gate.reshape(-1),
        g_shift_gate.reshape(-1),
        g_excite.reshape(2, own, inter).transpose(2, 0, 1),
        g_bias,
        g_out,
        g_gain_out.reshape(-1),
        g_shift_out.reshape(-1),
    )


def solution(mesh):
    placed = (
        P(None, "dp", "chan"),
        P(),
        P(None, "chan"),
        P("chan"),
        P("chan"),
        P(None, None, None, None, "chan"),
        P(None, "chan"),
        P(None, "chan"),
        P("chan", None),
        P(),
        P(),
        P(None, None, "chan"),
        P(None, "chan"),
        P(None, "chan"),
        P("chan"),
        P("chan"),
        P(None, "dp", "chan"),
    )
    return jax.shard_map(
        functools.partial(per_device, groups=mesh.shape["dp"], parts=mesh.shape["chan"]),
        mesh=mesh,
        in_specs=placed,
        out_specs=placed[:1] + placed[:1] + placed[2:16],
        check_vma=False,
    )
```

```python
import functools

import jax
import jax.numpy as jnp
from jax import lax
from jax.experimental import pallas as pl
from jax.experimental.pallas import tpu as pltpu
from jax.sharding import PartitionSpec as P

SIDE = 14
PIXELS = SIDE * SIDE
WIDE = 16
PADDED = SIDE * WIDE
STRIDE = PADDED + WIDE
CHUNK = 16
UNROLL = 49
VMEM_LIMIT = 24 * 2**20
SLOTS = (0, 1, 2, 3)
GATHERED = 40
ORDER = (0, 2, 1, 3)
EPSILON = 1e-05
HIGHEST = lax.Precision.HIGHEST
F32 = jnp.float32
BF16 = jnp.bfloat16


def dot_nn(left, right, precision=None):
    return lax.dot_general(
        left, right, (((1,), (0,)), ((), ())), preferred_element_type=F32, precision=precision
    )


def parts_of(value):
    high = value.astype(BF16)
    rest = value - high.astype(F32)
    middle = rest.astype(BF16)
    return jnp.concatenate([high, middle, (rest - middle.astype(F32)).astype(BF16)], axis=0)


def exact_dot(dot, left, right):
    rows = -(-left.shape[0] // 16) * 16
    if rows > left.shape[0]:
        left = jnp.concatenate([left, jnp.zeros((rows - left.shape[0], left.shape[1]), F32)], axis=0)
    value = dot(parts_of(left), right)
    return value[:rows] + value[rows : 2 * rows] + value[2 * rows :]


def dot_nt(left, right, precision=None):
    return lax.dot_general(
        left, right, (((1,), (1,)), ((), ())), preferred_element_type=F32, precision=precision
    )


def dot_tn(left, right, precision=None):
    return lax.dot_general(
        left, right, (((0,), (0,)), ((), ())), preferred_element_type=F32, precision=precision
    )


def sum_rows(matrix):
    value = dot_nn(jnp.ones((16, matrix.shape[0]), BF16), matrix)[0:1]
    high = value.astype(BF16).astype(F32)
    middle = (value - high).astype(BF16).astype(F32)
    empty = jnp.zeros((13, value.shape[1]), F32)
    rows = jnp.concatenate([high, middle, value - high - middle, empty], axis=0)
    return rows.astype(BF16)


def same_rows(row):
    return jnp.broadcast_to(row, (16, row.shape[1])).astype(BF16)


def centred_dot(centred, center, other):
    left = jnp.concatenate([centred, same_rows(-center)], axis=0)
    return dot_tn(left, jnp.concatenate([other, sum_rows(other)], axis=0))


def dot_centred(other, centred, center):
    right = jnp.concatenate([centred, same_rows(-center)], axis=0)
    return dot_tn(jnp.concatenate([other, sum_rows(other)], axis=0), right)


def expected(gain, shift):
    reach = 3.0**0.5 * gain
    return (4.0 * silu(shift) + silu(shift + reach) + silu(shift - reach)) / 6.0


def logistic(value):
    return 0.5 + 0.5 * jnp.tanh(0.5 * value)


def silu(value):
    return value * logistic(value)


def slope(value):
    share = logistic(value)
    return share + value * (share * (1.0 - share))


def moments(first, second, total):
    center = first / total
    return center, lax.rsqrt(second / total - center * center + EPSILON)


def fold(value):
    return jnp.sum(value.reshape(-1, 8, value.shape[-1]), axis=0)


def total_of(value):
    return jnp.sum(value, axis=0, keepdims=True)


def columns_real(rows):
    spot = lax.broadcasted_iota(jnp.int32, (rows, 1), 0)
    return (lax.rem(spot, WIDE) < SIDE).astype(F32)


def summed_over(refs):
    values = [ref[...] for ref in refs]
    while len(values) > 1:
        values = [left + right for left, right in zip(values[::2], values[1::2])]
    return values[0]


def slot_rows(refs, size, first, count, skip=0):
    return jnp.concatenate(
        [
            ref[at + first : at + first + count, :]
            for ref in refs
            for at in range(skip, ref.shape[0], size)
        ],
        axis=0,
    )


class Place:
    def __init__(self, counts_ref):
        group = lax.axis_index("dp")
        self.chan = lax.axis_index("chan")
        self.parity, self.depth, self.core = group & 1, group >> 1, self.chan & 1
        self.batch = (self.chan & 2) | self.parity
        self.counts = counts_ref
        self.groups = counts_ref.shape[1]

    def images(self, depth, core):
        return self.counts[self.batch, 2 * depth + core]

    def real(self, image):
        return jnp.where(self.images(self.depth, self.core) > image, 1.0, 0.0).astype(F32)

    def total(self):
        every = [self.counts[self.batch, g] for g in range(self.groups)]
        return functools.reduce(jnp.add, every).astype(F32)


def spread_map_rows(flat_ref, wide_ref):
    for line in range(flat_ref.shape[0] // SIDE):
        wide_ref[line * WIDE : line * WIDE + SIDE, :] = flat_ref[line * SIDE : (line + 1) * SIDE, :]
        wide_ref[line * WIDE + SIDE : (line + 1) * WIDE, :] = jnp.zeros(
            (WIDE - SIDE, wide_ref.shape[1]), wide_ref.dtype
        )


def pack_map_rows(wide_ref, flat_ref):
    for line in range(flat_ref.shape[0] // SIDE):
        flat_ref[line * SIDE : (line + 1) * SIDE, :] = wide_ref[line * WIDE : line * WIDE + SIDE, :]


def clear_gaps(taps_ref, images):
    for gap in range(images + 1):
        taps_ref[:, gap * STRIDE : gap * STRIDE + WIDE, :] = jnp.zeros(
            (3, WIDE, taps_ref.shape[2]), taps_ref.dtype
        )


def store_taps(taps_ref, at, value):
    here = pl.ds(pl.multiple_of(at, WIDE), WIDE)
    taps_ref[0, here, :] = pltpu.roll(value, 1, 0).astype(taps_ref.dtype)
    taps_ref[1, here, :] = value.astype(taps_ref.dtype)
    taps_ref[2, here, :] = pltpu.roll(value, WIDE - 1, 0).astype(taps_ref.dtype)


def call(body, outs, scratch, flops, *args, smem=1):
    specs = tuple(
        pl.BlockSpec(memory_space=pltpu.SMEM)
        if place < smem
        else jax.tree.map(lambda _: pl.BlockSpec(memory_space=pltpu.VMEM), arg)
        for place, arg in enumerate(args)
    )
    moved = sum(a.size * a.dtype.itemsize for a in jax.tree.leaves((args, outs)))
    return pl.pallas_call(
        body,
        out_shape=outs,
        in_specs=specs,
        out_specs=[pl.BlockSpec(memory_space=pltpu.VMEM)] * len(outs),
        scratch_shapes=scratch,
        compiler_params=pltpu.CompilerParams(vmem_limit_bytes=VMEM_LIMIT),
        cost_estimate=pl.CostEstimate(flops=flops, bytes_accessed=moved, transcendentals=0),
        name=getattr(body, "func", body).__name__,
    )(*args)


def shape(dims, kind=F32):
    return jax.ShapeDtypeStruct(dims, kind)


def slot_refs(even_ref, odd_ref, across_ref):
    return even_ref.at[0], odd_ref.at[0], across_ref.at[0], across_ref.at[1]


def pack(
    mid_ref,
    squeeze_ref,
    gain_in_ref,
    shift_in_ref,
    gain_mid_ref,
    shift_mid_ref,
    bias_ref,
    gain_out_ref,
    shift_out_ref,
    excite_ref,
    out_ref,
    target_ref,
    small_ref,
):
    lanes = target_ref.shape[1]
    own = lanes // 2
    small_ref[...] = jnp.zeros_like(small_ref)
    small_ref[0:1, :own] = gain_in_ref[...].astype(F32)
    small_ref[0:1, own:] = shift_in_ref[...].astype(F32)
    for row, ref in enumerate((gain_mid_ref, shift_mid_ref, bias_ref)):
        value = ref[...].astype(F32)
        small_ref[row + 1 : row + 2, :own] = value[0:1]
        small_ref[row + 1 : row + 2, own:] = value[1:2]
    for t, ref in enumerate((gain_out_ref, shift_out_ref)):
        value = ref[...].astype(F32)
        small_ref[4 + 2 * t : 5 + 2 * t, :] = value[:, :lanes]
        small_ref[5 + 2 * t : 6 + 2 * t, :] = value[:, lanes:]
    row = 0
    for ref in (mid_ref, squeeze_ref, small_ref, excite_ref):
        target_ref[row : row + ref.shape[0], :] = ref[...].astype(BF16)
        row += ref.shape[0]
    for block in range(out_ref.shape[1] // lanes):
        rows = out_ref.shape[0]
        target_ref[row : row + rows, :] = out_ref[:, block * lanes : (block + 1) * lanes]
        row += rows


def reduce_in(
    counts_ref, x0, x1, x2, x3, a0, a1, a2, a3, pre_ref, msg_ref, w_ref, wall_ref, flat_ref
):
    place = Place(counts_ref)
    images = wall_ref.shape[0] // place.groups
    spot = lax.broadcasted_iota(jnp.int32, wall_ref.shape, 0)
    real = jnp.zeros(wall_ref.shape, jnp.int32)
    for slot in range(place.groups):
        number = place.images(place.depth ^ (slot >> 1), place.core ^ (slot & 1))
        here = (spot >= slot * images) & (spot < slot * images + number)
        real = jnp.where(here, 1, real)
    wall_ref[...] = real.astype(F32)
    own = w_ref.shape[1] // len(SLOTS)
    lanes = w_ref.shape[2]
    for s, piece in enumerate((a0, a1, a2, a3)):
        here = pl.ds(pl.multiple_of((place.chan ^ s) * own, own), own)
        for block in range(w_ref.shape[0]):
            w_ref[block, here, :] = piece[:, block * lanes : (block + 1) * lanes]
    parts = [dot_nt(x[...], w_ref[place.batch ^ s]) for s, x in enumerate((x0, x1, x2, x3))]
    flat_ref[...] = functools.reduce(jnp.add, parts)
    spread_map_rows(flat_ref, pre_ref)
    first = jnp.zeros((1, pre_ref.shape[1]), F32)
    second = jnp.zeros((1, pre_ref.shape[1]), F32)
    for image in range(pre_ref.shape[0] // PADDED):
        real = place.real(image)
        value = pre_ref[image * PADDED : (image + 1) * PADDED, :]
        first = first + real * total_of(value)
        second = second + real * total_of(value * value)
    rows = x0.shape[0]
    spot = lax.broadcasted_iota(jnp.int32, (16, rows), 1)
    real = (spot < place.images(place.depth, place.core) * PIXELS).astype(BF16)
    columns = [dot_nn(real, x[...])[0:1] for x in (x0, x1, x2, x3)]
    msg_ref[...] = jnp.concatenate([first, second] + columns, axis=0)


def place_mid(
    counts_ref,
    b0,
    b1,
    b2,
    b3,
    w_ref,
    w_back_ref,
    squeeze_ref,
    in_affine_ref,
    mid_affine_ref,
    bias_ref,
    out_affine_ref,
    small_ref,
):
    place = Place(counts_ref)
    width, lanes = w_ref.shape[1], b0.shape[1]
    own = width // len(SLOTS)
    for s, piece in enumerate((b0, b1, b2, b3)):
        at = pl.multiple_of((place.chan ^ s) * own, own)
        for tap in range(9):
            for r in range(2):
                block = piece[(2 * tap + r) * own : (2 * tap + r + 1) * own, :]
                w_ref[r, pl.ds(at, own), tap * lanes : (tap + 1) * lanes] = block
                w_back_ref[r, pl.ds(tap * width + at, own), :] = block
        squeeze_ref[pl.ds(at, own), :] = piece[18 * own : 19 * own, :]
        small = piece[19 * own : 19 * own + 16, :].astype(F32)
        small_ref[place.chan ^ s] = small
        for t in range(2):
            out_affine_ref[t, place.chan ^ s, :, :lanes] = small[4 + 2 * t : 5 + 2 * t, :]
            out_affine_ref[t, place.chan ^ s, :, lanes:] = small[5 + 2 * t : 6 + 2 * t, :]
    for k in range(len(SLOTS)):
        here = slice(k * own, (k + 1) * own)
        there = slice(width + k * own, width + (k + 1) * own)
        in_affine_ref[0:1, here] = small_ref[k, 0:1, :own]
        in_affine_ref[1:2, here] = small_ref[k, 0:1, own:]
        for t in range(2):
            mid_affine_ref[t : t + 1, here] = small_ref[k, 1 + t : 2 + t, :own]
            mid_affine_ref[t : t + 1, there] = small_ref[k, 1 + t : 2 + t, own:]
        bias_ref[0:1, here] = small_ref[k, 3:4, :own]
        bias_ref[0:1, there] = small_ref[k, 3:4, own:]


def place_rest(counts_ref, b0, b1, b2, b3, excite_ref, w_out_ref):
    place = Place(counts_ref)
    width, lanes = w_out_ref.shape[1], b0.shape[1]
    own = width // len(SLOTS)
    for s, piece in enumerate((b0, b1, b2, b3)):
        row = 19 * own + 16
        for r in range(2):
            at = pl.multiple_of(r * width + (place.chan ^ s) * own, own)
            excite_ref[pl.ds(at, own), :] = piece[row : row + own, :]
            row += own
        w_out_ref[place.chan ^ s, :, :lanes] = piece[row : row + width, :]
        w_out_ref[place.chan ^ s, :, lanes:] = piece[row + width : row + 2 * width, :]


def conv_mid(
    counts_ref,
    pre_ref,
    sums_refs,
    affine_ref,
    w_ref,
    taps_ref,
    mid_ref,
    msg_ref,
):
    place = Place(counts_ref)
    images = pre_ref.shape[0] // PADDED
    total = place.total() * PIXELS
    sums = summed_over(sums_refs)
    center, scale = moments(sums[0:1], sums[1:2], total)
    gain = affine_ref[0:1, :] * scale
    shift = affine_ref[1:2, :] - center * gain
    clear_gaps(taps_ref, images)
    keep = columns_real(WIDE)
    for image in range(images):

        def normalize(step, carry, image=image):
            rows = pl.multiple_of(step * WIDE, WIDE)
            value = pre_ref[pl.ds(image * PADDED + rows, WIDE), :]
            value = silu(value * gain + shift) * keep
            store_taps(taps_ref, image * STRIDE + WIDE + rows, value)
            return carry

        lax.fori_loop(0, SIDE, normalize, 0, unroll=SIDE)
    half = pre_ref.shape[1] // 2
    width = pre_ref.shape[1]
    keep = columns_real(PADDED)
    firsts = [jnp.zeros((1, width), F32) for _ in range(2)]
    seconds = [jnp.zeros((1, width), F32) for _ in range(2)]
    for image in range(images):
        real = place.real(image)
        for r in range(2):
            left = jnp.concatenate(
                [
                    taps_ref[
                        b,
                        image * STRIDE + a * WIDE : image * STRIDE + a * WIDE + PADDED,
                        r * half : (r + 1) * half,
                    ]
                    for a in range(3)
                    for b in range(3)
                ],
                axis=1,
            )
            value = dot_nt(left, w_ref[r])
            mid_ref[image * PADDED : (image + 1) * PADDED, r * width : (r + 1) * width] = value
            held = value * keep
            firsts[r] = firsts[r] + real * total_of(held)
            seconds[r] = seconds[r] + real * total_of(held * held)
    sums = jnp.concatenate(
        [jnp.concatenate(firsts, axis=1), jnp.concatenate(seconds, axis=1)], axis=0
    )
    msg_ref[...] = sums


def mid_norm(
    place,
    sums_refs,
    affine_ref,
):
    sums = summed_over(sums_refs)
    center, scale = moments(sums[0:1], sums[1:2], place.total() * PIXELS)
    gain = affine_ref[0:1, :] * scale
    return center, scale, gain, affine_ref[1:2, :] - center * gain


def pool(
    counts_ref,
    mid_ref,
    sums_refs,
    affine_ref,
    squeeze_ref,
    pooled_ref,
    msg_ref,
):
    place = Place(counts_ref)
    images = mid_ref.shape[0] // PADDED
    width = mid_ref.shape[1] // 2
    lanes = msg_ref.shape[1]
    center, scale, gain, shift = mid_norm(place, sums_refs, affine_ref)
    keep = columns_real(CHUNK)
    inclines = [[], []]
    for image in range(images):

        def gather(step, carry, image=image):
            active, rise, lean = carry
            at = pl.multiple_of(image * PADDED + step * CHUNK, CHUNK)
            before = mid_ref[pl.ds(at, CHUNK), :]
            value = before * gain + shift
            share = logistic(value) * keep
            active = active + fold(value * share)
            inclined = share + value * (share * (1.0 - share))
            return active, rise + fold(inclined), lean + fold(inclined * before)

        nothing = jnp.zeros((8, 2 * width), F32)
        active, rise, lean = lax.fori_loop(
            0, SIDE, gather, (nothing, nothing, nothing), unroll=SIDE
        )
        active = total_of(active)
        pooled_ref[image : image + 1, :] = (active[:, :width] + active[:, width:]) / PIXELS
        rise = total_of(rise)
        inclines[0].append(rise)
        inclines[1].append(scale * (total_of(lean) - center * rise))
    inclined = jnp.concatenate(inclines[0] + inclines[1], axis=0)
    msg_ref[...] = jnp.zeros_like(msg_ref)
    for q in range(2 * width // lanes):
        row = 8 + q * 2 * images
        msg_ref[row : row + 2 * images, :] = inclined[:, q * lanes : (q + 1) * lanes]
    msg_ref[0:images, :] = exact_dot(dot_nn, pooled_ref[...], squeeze_ref[...])[:images]
    real = [place.real(image) * pooled_ref[image : image + 1, :] for image in range(images)]
    real = functools.reduce(jnp.add, real)
    for q in range(width // lanes):
        msg_ref[images + q : images + q + 1, :] = real[:, q * lanes : (q + 1) * lanes]


def gate_norm(
    place,
    rows,
    wall,
):
    return moments(total_of(wall * rows), total_of(wall * rows * rows), place.total())


def attend(
    counts_ref,
    gathered_refs,
    wall_ref,
    gate_affine_ref,
    excite_ref,
    bias_ref,
    mid_ref,
    mid_sums_refs,
    mid_affine_ref,
    w_out_ref,
    gate_ref,
    attention_ref,
    weighted_ref,
    out_ref,
    msg_ref,
    wide_ref,
    flat_ref,
):
    place = Place(counts_ref)
    images = mid_ref.shape[0] // PADDED
    width = mid_ref.shape[1] // 2
    rows = slot_rows(gathered_refs, GATHERED, 0, images)
    center, scale = gate_norm(place, rows, wall_ref[...])
    normed = (rows[0:images] - center) * scale
    gate_pre = normed * gate_affine_ref[0:1, :] + gate_affine_ref[1:2, :]
    gate = silu(gate_pre)
    gate_ref[0] = gate
    gate_ref[1] = slope(gate_pre)
    logits = (
        exact_dot(dot_nt, gate, excite_ref[...])[:images] + bias_ref[...]
    )
    lean = 0.5 * jnp.tanh(0.5 * (logits[:, :width] - logits[:, width:]))
    attention_ref[:, :width] = 0.5 + lean
    attention_ref[:, width:] = 0.5 - lean
    center, scale, gain, shift = mid_norm(place, mid_sums_refs, mid_affine_ref)
    for image in range(images):
        share = attention_ref[image : image + 1, :]

        def weigh(step, carry, image=image, share=share):
            at = pl.multiple_of(image * PADDED + step * CHUNK, CHUNK)
            value = share * silu(mid_ref[pl.ds(at, CHUNK), :] * gain + shift)
            wide_ref[pl.ds(at, CHUNK), :] = value[:, :width] + value[:, width:]
            return carry

        lax.fori_loop(0, SIDE, weigh, 0, unroll=SIDE)
    pack_map_rows(wide_ref, flat_ref)
    weighted_ref[...] = flat_ref[...].astype(BF16)
    spot = lax.broadcasted_iota(jnp.int32, (flat_ref.shape[0], 1), 0)
    real = (spot < place.images(place.depth, place.core) * PIXELS).astype(F32)
    blocks = w_out_ref.shape[0]
    for k in range(blocks):
        value = dot_nn(weighted_ref[...], w_out_ref[place.batch ^ k])
        out_ref[k] = value
        held = value * real
        for t, row in enumerate((total_of(held), total_of(held * value))):
            msg_ref[t * blocks + k : t * blocks + k + 1, :] = row


def finish(
    counts_ref,
    out_ref,
    sums_refs,
    affine_ref,
    weighted_ref,
    x_refs,
    cot_near_ref,
    cot_odd_ref,
    cot_across_ref,
    shared_ref,
    grad_ref,
    msg_ref,
    map_ref,
):
    place = Place(counts_ref)
    cot_refs = slot_refs(cot_near_ref, cot_odd_ref, cot_across_ref)
    blocks, rows, lanes = out_ref.shape
    sums = summed_over(sums_refs)
    center, scale = moments(sums[:blocks], sums[blocks:], place.total() * PIXELS)
    limit = place.images(place.depth, place.core) * PIXELS
    for k in range(blocks):
        mu, r = center[k : k + 1], scale[k : k + 1]
        block = place.batch ^ k
        gain = affine_ref[0, block] * r
        shift = affine_ref[1, block] - mu * gain
        map_ref[block] = gain
        map_ref[blocks + block] = shift
        x_ref, upstream_ref = x_refs[k], cot_refs[k]

        def chunk(
            step, carry, k=k, gain=gain, shift=shift, x_ref=x_ref, upstream_ref=upstream_ref
        ):
            first, second = carry
            at = pl.multiple_of(step * CHUNK, CHUNK)
            here = pl.ds(at, CHUNK)
            spot = lax.broadcasted_iota(jnp.int32, (CHUNK, 1), 0) + at
            real = (spot < limit).astype(F32)
            before = out_ref[k, here, :]
            summed = x_ref[here, :].astype(F32) + (before * gain + shift)
            share = logistic(summed)
            grad = upstream_ref[here, :].astype(F32) * real
            grad = grad * (share * (1.0 + summed * (1.0 - share)))
            grad_ref[k, here, :] = grad
            return first + fold(grad), second + fold(grad * before)

        nothing = jnp.zeros((8, lanes), F32)
        first, second = lax.fori_loop(
            0, rows // CHUNK, chunk, (nothing, nothing), unroll=UNROLL
        )
        first = total_of(first)
        for t, row in enumerate((first, r * (total_of(second) - mu * first))):
            msg_ref[t * blocks + k : t * blocks + k + 1, :] = row
    shared_ref[0:rows, :] = weighted_ref[...]
    exact = jnp.concatenate([map_ref[n] for n in range(2 * blocks)], axis=0)
    high = exact.astype(BF16).astype(F32)
    middle = (exact - high).astype(BF16).astype(F32)
    shared_ref[rows : rows + 16, :] = jnp.concatenate([high, middle], axis=0).astype(BF16)
    rest = jnp.concatenate([exact - high - middle, jnp.zeros_like(exact)], axis=0)
    shared_ref[rows + 16 : rows + 32, :] = rest.astype(BF16)


def finish_owned(
    counts_ref, near_ref, swapped_ref, far_ref, w_ref, x_ref, cot_ref, result_ref, grad_ref, out_ref
):
    chan, group = lax.axis_index("chan"), lax.axis_index("dp")
    rows = cot_ref.shape[1]
    blocks = len(SLOTS)
    for s, piece in enumerate((near_ref, swapped_ref.at[0], far_ref, swapped_ref.at[1])):
        batch = chan ^ s
        limit = counts_ref[batch, group] * PIXELS
        out_ref[...] = dot_nn(piece[0:rows, :], w_ref[chan])
        exact = piece[rows : rows + 32, :].astype(F32)
        exact = exact[0:8] + exact[8:16] + exact[16:24]
        gain, shift = exact[0:1], exact[blocks : blocks + 1]
        for k in range(1, blocks):
            gain = jnp.where(chan == k, exact[k : k + 1], gain)
            shift = jnp.where(chan == k, exact[blocks + k : blocks + k + 1], shift)

        def chunk(step, carry, batch=batch, limit=limit, gain=gain, shift=shift):
            at = pl.multiple_of(step * CHUNK, CHUNK)
            here = pl.ds(at, CHUNK)
            spot = lax.broadcasted_iota(jnp.int32, (CHUNK, 1), 0) + at
            real = (spot < limit).astype(F32)
            summed = x_ref[batch, here, :].astype(F32) + (out_ref[here, :] * gain + shift)
            share = logistic(summed)
            held = share * real
            result_ref[batch, here, :] = (summed * held).astype(BF16)
            grad = cot_ref[batch, here, :].astype(F32) * (held * (1.0 + summed * (1.0 - share)))
            grad_ref[batch, here, :] = grad.astype(BF16)
            return carry

        lax.fori_loop(0, rows // CHUNK, chunk, 0, unroll=UNROLL)


def back_out(
    counts_ref,
    grad_ref,
    out_ref,
    sums_refs,
    back_refs,
    affine_ref,
    w_out_ref,
    mid_ref,
    mid_sums_refs,
    mid_affine_ref,
    attention_ref,
    gate_ref,
    excite_ref,
    low_ref,
    gw_ref,
    logits_ref,
    msg_ref,
    flat_ref,
):
    place = Place(counts_ref)
    blocks, rows, lanes = out_ref.shape
    images = attention_ref.shape[0]
    width = attention_ref.shape[1] // 2
    total = place.total() * PIXELS
    sums = summed_over(sums_refs)
    center, scale = moments(sums[:blocks], sums[blocks:], total)
    back = summed_over(back_refs) / total
    limit = place.images(place.depth, place.core) * PIXELS
    for k in range(blocks):
        mu, r = center[k : k + 1], scale[k : k + 1]
        gain = affine_ref[0, place.batch ^ k] * r
        second = gain * r * back[blocks + k : blocks + k + 1]
        first = gain * back[k : k + 1] - mu * second

        def chunk(step, carry, k=k, gain=gain, first=first, second=second):
            at = pl.multiple_of(step * CHUNK, CHUNK)
            here = pl.ds(at, CHUNK)
            spot = lax.broadcasted_iota(jnp.int32, (CHUNK, 1), 0) + at
            real = (spot < limit).astype(F32)
            value = gain * grad_ref[k, here, :] - real * (first + out_ref[k, here, :] * second)
            low_ref[k, here, :] = value.astype(BF16)
            return carry

        lax.fori_loop(0, rows // CHUNK, chunk, 0, unroll=UNROLL)
    parts = [dot_nt(low_ref[k], w_out_ref[place.batch ^ k]) for k in range(blocks)]
    flat_ref[...] = functools.reduce(jnp.add, parts)
    spread_map_rows(flat_ref, gw_ref)
    center, scale, gain, shift = mid_norm(place, mid_sums_refs, mid_affine_ref)
    rises, leans, attended = [], [], []
    for image in range(images):

        def gather(step, carry, image=image):
            attended, rise, lean = carry
            at = pl.multiple_of(image * PADDED + step * CHUNK, CHUNK)
            before = mid_ref[pl.ds(at, CHUNK), :]
            value = before * gain + shift
            share = logistic(value)
            grad = gw_ref[pl.ds(at, CHUNK), :]
            grad = jnp.concatenate([grad, grad], axis=1)
            active = grad * share
            attended = attended + fold(active * value)
            inclined = active * (1.0 + value * (1.0 - share))
            return attended, rise + fold(inclined), lean + fold(inclined * before)

        nothing = jnp.zeros((8, 2 * width), F32)
        parts = lax.fori_loop(
            0, SIDE, gather, (nothing, nothing, nothing), unroll=SIDE
        )
        share = attention_ref[image : image + 1, :]
        attended.append(total_of(parts[0]))
        rise = total_of(parts[1])
        rises.append(share * rise)
        leans.append(share * (scale * (total_of(parts[2]) - center * rise)))
    grad = jnp.concatenate(attended, axis=0)
    attention = attention_ref[...]
    inner = attention * grad
    inner = inner[:, :width] + inner[:, width:]
    logits = attention * (grad - jnp.concatenate([inner, inner], axis=1))
    logits_ref[...] = logits
    gate = exact_dot(dot_nn, logits, excite_ref[...])[:images] * gate_ref[1]
    pack = msg_ref.shape[1]
    pieces = 2 * width // pack
    for t, row in enumerate((functools.reduce(jnp.add, rises), functools.reduce(jnp.add, leans))):
        for q in range(pieces):
            msg_ref[t * pieces + q : t * pieces + q + 1, :] = row[:, q * pack : (q + 1) * pack]
    msg_ref[2 * pieces : 2 * pieces + images, :] = gate


def back_mid(
    counts_ref,
    back_refs,
    gathered_refs,
    wall_ref,
    gate_affine_ref,
    squeeze_ref,
    attention_ref,
    gw_ref,
    mid_ref,
    mid_sums_refs,
    mid_affine_ref,
    pre_ref,
    sums_refs,
    affine_ref,
    w_ref,
    low_ref,
    grad_ref,
    gate_ref,
    vector_ref,
    msg_ref,
    taps_ref,
):
    place = Place(counts_ref)
    images = attention_ref.shape[0]
    width = attention_ref.shape[1] // 2
    lanes = wall_ref.shape[1]
    pieces = 2 * width // lanes
    total = place.total() * PIXELS
    wall = wall_ref[...]
    rows = slot_rows(gathered_refs, GATHERED, 0, images)
    center, scale = gate_norm(place, rows, wall)
    gain = gate_affine_ref[0:1, :] * scale
    normed = (rows - center) * scale
    grads = slot_rows(back_refs, images, 0, images, 2 * pieces)
    first, second = total_of(wall * grads), total_of(wall * grads * normed)
    vector_ref[0:1, 0:lanes] = second
    vector_ref[0:1, lanes : 2 * lanes] = first
    squeezed = gain * (grads - wall * (first + normed * second) / place.total())
    gate_ref[...] = squeezed[0:images]
    pooled_grad = exact_dot(dot_nt, squeezed, squeeze_ref[...]) / PIXELS
    pooled_grad = jnp.concatenate([pooled_grad, pooled_grad], axis=1)
    slot = 0
    terms = jnp.zeros((2 * images, 2 * width), F32)
    for ref in gathered_refs:
        for at in range(8, ref.shape[0], GATHERED):
            inclines = [
                ref[at + q * 2 * images : at + (q + 1) * 2 * images, :] for q in range(pieces)
            ]
            grad = pooled_grad[slot * images : (slot + 1) * images, :]
            grad = jnp.concatenate([grad, grad], axis=0)
            terms = terms + jnp.concatenate(inclines, axis=1) * grad
            slot += 1
    sums = functools.reduce(jnp.add, [ref[0 : 2 * pieces, :] for ref in back_refs])
    back = []
    for t in range(2):
        row = [sums[t * pieces + q : t * pieces + q + 1, :] for q in range(pieces)]
        back.append(
            jnp.concatenate(row, axis=1) + total_of(terms[t * images : (t + 1) * images])
        )
    vector_ref[1:2, :] = back[1]
    vector_ref[2:3, :] = back[0]
    own = pooled_grad[0:images]
    center, scale, gain, shift = mid_norm(place, mid_sums_refs, mid_affine_ref)
    second = gain * scale * back[1] / total
    first = gain * back[0] / total - center * second
    clear_gaps(taps_ref, images)
    keep = columns_real(WIDE)
    for image in range(images):
        share = gain * attention_ref[image : image + 1, :]
        offset = gain * own[image : image + 1, :]
        real = place.real(image)
        lead, lag = real * first, real * second

        def chunk(step, carry, image=image, share=share, offset=offset, lead=lead, lag=lag):
            rows = pl.multiple_of(step * WIDE, WIDE)
            here = pl.ds(image * PADDED + rows, WIDE)
            before = mid_ref[here, :]
            grad = gw_ref[here, :]
            grad = jnp.concatenate([grad, grad], axis=1)
            grad = (share * grad + offset) * slope(before * gain + shift)
            value = (grad - (lead + before * lag)) * keep
            store_taps(taps_ref, image * STRIDE + WIDE + rows, value)
            return carry

        lax.fori_loop(0, SIDE, chunk, 0, unroll=SIDE)
    low_ref[...] = taps_ref[1]
    sums = summed_over(sums_refs)
    center, scale = moments(sums[0:1], sums[1:2], total)
    gain = affine_ref[0:1, :] * scale
    shift = affine_ref[1:2, :] - center * gain
    half = width // 2
    keep = columns_real(PADDED)
    firsts = [jnp.zeros((1, half), F32) for _ in range(2)]
    seconds = [jnp.zeros((1, half), F32) for _ in range(2)]
    for image in range(images):
        real = place.real(image)
        here = slice(image * PADDED, (image + 1) * PADDED)
        for r in range(2):
            left = jnp.concatenate(
                [
                    taps_ref[
                        2 - b,
                        image * STRIDE + (2 - a) * WIDE : image * STRIDE + (2 - a) * WIDE + PADDED,
                        r * width : (r + 1) * width,
                    ]
                    for a in range(3)
                    for b in range(3)
                ],
                axis=1,
            )
            lane = slice(r * half, (r + 1) * half)
            before = pre_ref[here, lane]
            value = dot_nn(left, w_ref[r]) * slope(before * gain[:, lane] + shift[:, lane])
            value = value * (keep * real)
            grad_ref[here, lane] = value
            firsts[r] = firsts[r] + total_of(value)
            seconds[r] = seconds[r] + total_of(value * before)
    first = jnp.concatenate(firsts, axis=1)
    second = scale * (jnp.concatenate(seconds, axis=1) - center * first)
    sums = jnp.concatenate([first, second], axis=0)
    msg_ref[...] = sums


def sort_pieces(
    place,
    source_ref,
    keep_ref,
    send_ref,
    row,
):
    for turn, s in enumerate(ORDER):
        target = keep_ref if turn < 2 else send_ref
        rows = source_ref.shape[1]
        target[turn % 2, row : row + rows, :] = source_ref[place.chan ^ s].astype(BF16)


def weight_out_term(
    counts_ref,
    weighted_ref,
    low_ref,
    gate_ref,
    logits_ref,
    affine_ref,
    keep_ref,
    send_ref,
    wide_ref,
    small_ref,
):
    place = Place(counts_ref)
    width = weighted_ref.shape[1]
    lanes = keep_ref.shape[2]
    own = width // len(SLOTS)
    center = expected(affine_ref[0:1, :], affine_ref[1:2, :])
    center = 0.5 * (center[:, :width] + center[:, width:])
    for turn, s in enumerate(ORDER):
        target = keep_ref if turn < 2 else send_ref
        held = place.batch ^ place.chan ^ s
        term = centred_dot(weighted_ref[...], center, low_ref[held]).astype(BF16)
        target[turn % 2, 0:width, :] = term[:, :lanes]
        target[turn % 2, width : 2 * width, :] = term[:, lanes:]
    wide_ref[...] = dot_tn(logits_ref[...], gate_ref[0], HIGHEST)
    for turn, s in enumerate(ORDER):
        target = keep_ref if turn < 2 else send_ref
        for r in range(2):
            at = pl.multiple_of(r * width + (place.chan ^ s) * own, own)
            row = 2 * width + r * own
            target[turn % 2, row : row + own, :] = wide_ref[pl.ds(at, own), :].astype(BF16)
    small_ref[...] = jnp.zeros_like(small_ref)
    bias = total_of(logits_ref[...])
    for k in range(len(SLOTS)):
        small_ref[k, 0:1, :own] = bias[:, k * own : (k + 1) * own]
        small_ref[k, 0:1, own:] = bias[:, width + k * own : width + (k + 1) * own]
    sort_pieces(place, small_ref, keep_ref, send_ref, 2 * width + 2 * own)


def weight_mid_term(
    counts_ref,
    taps_ref,
    low_ref,
    affine_ref,
    keep_ref,
    send_ref,
    wide_ref,
):
    place = Place(counts_ref)
    center = expected(affine_ref[0:1, :], affine_ref[1:2, :])
    half = taps_ref.shape[2] // 2
    width = low_ref.shape[1] // 2
    own = width // len(SLOTS)
    rows = low_ref.shape[0] - 2 * WIDE
    for r in range(2):
        right = jnp.concatenate(
            [
                taps_ref[b, a * WIDE : a * WIDE + rows, r * half : (r + 1) * half]
                for a in range(3)
                for b in range(3)
            ],
            axis=1,
        )
        low = low_ref[WIDE : WIDE + rows, r * width : (r + 1) * width]
        offset = jnp.concatenate([center[:, r * half : (r + 1) * half]] * 9, axis=1)
        wide_ref[...] = dot_centred(low, right, offset)
        for turn, s in enumerate(ORDER):
            target = keep_ref if turn < 2 else send_ref
            here = pl.ds(pl.multiple_of((place.chan ^ s) * own, own), own)
            for tap in range(9):
                row = (2 * tap + r) * own
                target[turn % 2, row : row + own, :] = wide_ref[
                    here, tap * half : (tap + 1) * half
                ].astype(BF16)


def back_in(
    share,
    counts_ref,
    grad_ref,
    pre_ref,
    sums_refs,
    back_refs,
    affine_ref,
    x0,
    x1,
    x2,
    x3,
    vector_ref,
    out_back_refs,
    pooled_ref,
    gathered_refs,
    squeezed_ref,
    low_ref,
    keep_ref,
    send_ref,
    flat_ref,
    wide_ref,
    narrow_ref,
    small_ref,
):
    place = Place(counts_ref)
    images = pre_ref.shape[0] // PADDED
    width = pre_ref.shape[1]
    own = width // len(SLOTS)
    chan, batch = place.chan, place.batch
    total = place.total() * PIXELS
    sums = summed_over(sums_refs)
    center, scale = moments(sums[0:1], sums[1:2], total)
    back = summed_over(back_refs)
    gain = affine_ref[0:1, :] * scale
    second = gain * scale * back[1:2] / total
    first = gain * back[0:1] / total - center * second
    for image in range(images):
        real = place.real(image)
        lead, lag = real * first, real * second
        for line in range(SIDE):
            at = image * PADDED + line * WIDE
            before = pre_ref[at : at + WIDE, :]
            value = gain * grad_ref[at : at + WIDE, :] - (lead + before * lag)
            at = image * PIXELS + line * SIDE
            flat_ref[at : at + SIDE, :] = value[:SIDE]
    low_ref[...] = flat_ref[...].astype(BF16)
    lanes = keep_ref.shape[2]
    low = jnp.concatenate([low_ref[...], sum_rows(low_ref[...])], axis=0)
    for k, x in enumerate((x0, x1, x2, x3)):
        center = same_rows(-sums[2 + k : 3 + k] / total)
        wide_ref[...] = dot_tn(low, jnp.concatenate([x[...], center], axis=0))
        for turn, s in enumerate(ORDER):
            target = keep_ref if turn < 2 else send_ref
            here = pl.ds(pl.multiple_of((chan ^ s) * own, own), own)
            for part in range(wide_ref.shape[1] // lanes):
                at = pl.multiple_of(((batch ^ k) * (wide_ref.shape[1] // lanes) + part) * own, own)
                target[turn % 2, pl.ds(at, own), :] = wide_ref[
                    here, part * lanes : (part + 1) * lanes
                ].astype(BF16)
    mean = [
        total_of(slot_rows(gathered_refs, GATHERED, images + q, 1)) for q in range(width // lanes)
    ]
    mean = jnp.concatenate(mean, axis=1) / place.total()
    narrow_ref[...] = dot_tn(pooled_ref[...] - mean, squeezed_ref[...], HIGHEST)
    row = keep_ref.shape[1] - small_ref.shape[1] - own
    for turn, s in enumerate(ORDER):
        target = keep_ref if turn < 2 else send_ref
        here = pl.ds(pl.multiple_of((chan ^ s) * own, own), own)
        target[turn % 2, row : row + own, :] = narrow_ref[here, :].astype(BF16)
    small_ref[...] = jnp.zeros_like(small_ref)
    outs = summed_over(out_back_refs)
    for k in range(len(SLOTS)):
        here = slice(k * own, (k + 1) * own)
        there = slice(width + k * own, width + (k + 1) * own)
        small_ref[k, 0:1, :own] = back[1:2, here]
        small_ref[k, 0:1, own:] = back[0:1, here]
        for t in range(2):
            small_ref[k, 1 + t : 2 + t, :own] = vector_ref[1 + t : 2 + t, here]
            small_ref[k, 1 + t : 2 + t, own:] = vector_ref[1 + t : 2 + t, there]
        small_ref[k, 3:4, :] = vector_ref[0:1, 0:lanes]
        small_ref[k, 4:5, :] = vector_ref[0:1, lanes : 2 * lanes]
    for s in SLOTS:
        for t in range(2):
            row = outs[(1 - t) * len(SLOTS) + s : (1 - t) * len(SLOTS) + s + 1, :]
            small_ref[batch ^ s, 5 + 2 * t : 6 + 2 * t, :] = row[:, :lanes]
            small_ref[batch ^ s, 6 + 2 * t : 7 + 2 * t, :] = row[:, lanes:]
    small_ref[...] = small_ref[...] * share
    sort_pieces(place, small_ref, keep_ref, send_ref, keep_ref.shape[1] - small_ref.shape[1])


def grad_owned(low_refs, w_ref, summed_ref, result_ref):
    chan = lax.axis_index("chan")
    for s, low_ref in enumerate(low_refs):
        value = dot_nn(low_ref[...], w_ref[chan]) + summed_ref[chan ^ s].astype(F32)
        result_ref[chan ^ s] = value.astype(BF16)


def add_groups(terms_ref, sum_ref):
    value = jnp.sum(terms_ref[...].astype(F32), axis=0).astype(BF16)
    sum_ref[...] = jnp.broadcast_to(value[None], sum_ref.shape)


def added(left_ref, right_ref):
    return left_ref[...].astype(F32) + right_ref[...].astype(F32)


def add_core(keep_refs, arrived_refs, kept_ref, send_ref):
    at = 0
    for keep_ref, arrived_ref in zip(keep_refs, arrived_refs):
        value = added(keep_ref, arrived_ref).astype(BF16)
        rows = keep_ref.shape[1]
        kept_ref[at : at + rows, :] = value[0]
        send_ref[at : at + rows, :] = value[1]
        at += rows
    if at < kept_ref.shape[0]:
        for ref in (kept_ref, send_ref):
            ref[at:, :] = jnp.zeros((kept_ref.shape[0] - at, ref.shape[1]), BF16)


def split_rows(parity, keep_ref, arrived_ref, kept_ref, send_ref):
    rows = kept_ref.shape[-2]
    for own, target in ((parity, kept_ref), (1 - parity, send_ref)):
        here = pl.ds(pl.multiple_of(own * rows, 16), rows)
        if target.ndim == 2:
            value = added(keep_ref.at[here, :], arrived_ref.at[here, :])
        else:
            value = added(keep_ref.at[:, here, :], arrived_ref.at[:, here, :])
        target[...] = value.astype(target.dtype)


def add_core_first(counts_ref, keep_ref, arrived_ref, kept_ref, send_ref):
    split_rows(Place(counts_ref).parity, keep_ref, arrived_ref, kept_ref, send_ref)


def add_parity_first(keep_ref, arrived_ref, kept_ref, send_ref):
    kept_ref[...] = added(keep_ref.at[0], arrived_ref.at[0])
    send_ref[...] = added(keep_ref.at[1], arrived_ref.at[1]).astype(BF16)


def add_chip(counts_ref, keep_ref, arrived_ref, kept_ref, send_ref):
    split_rows(Place(counts_ref).parity, keep_ref, arrived_ref, kept_ref, send_ref)


def add_last(counts_ref, keep_refs, arrived_refs, kept_ref, s1, s2, s3):
    place = Place(counts_ref)
    at = 0
    for keep_ref, arrived_ref in zip(keep_refs, arrived_refs):
        rows = keep_ref.shape[0] // len(SLOTS)
        for t, target in enumerate((kept_ref, s1, s2, s3)):
            here = pl.ds(pl.multiple_of((place.depth ^ t) * rows, 16), rows)
            value = added(keep_ref.at[here, :], arrived_ref.at[here, :])
            target[at : at + rows, :] = value.astype(target.dtype)
        at += rows


def add_depth(keep_ref, arrived_refs, sum_ref):
    value = keep_ref[...]
    for ref in arrived_refs:
        value = value + ref[...].astype(F32)
    sum_ref[...] = value.astype(BF16)


def unpack(
    joined,
    counts_ref,
    term_refs,
    in_ref,
    gain_in_ref,
    shift_in_ref,
    mid_ref,
    gain_mid_ref,
    shift_mid_ref,
    squeeze_ref,
    gain_gate_ref,
    shift_gate_ref,
    excite_ref,
    bias_ref,
    out_ref,
    gain_out_ref,
    shift_out_ref,
    second_ref,
):
    own, lanes = squeeze_ref.shape
    width = out_ref.shape[0]
    places = [(out_ref, 0, 0, width), (out_ref, 0, 1, width), (excite_ref, 0, 0, 2 * own)]
    places += [(second_ref, 0, 0, 16)]
    places += [(in_ref, 0, block, own) for block in range(in_ref.shape[1] // lanes)]
    places += [(squeeze_ref, 0, 0, own), (second_ref, 16, 0, 16)]

    def write(value, row):
        start = 0
        for target, at, block, rows in places:
            first, last = max(row, start), min(row + value.shape[0], start + rows)
            if first < last:
                there = slice(at + first - start, at + last - start)
                target[there, block * lanes : (block + 1) * lanes] = value[first - row : last - row]
            start += rows

    if joined:
        mid_ref[...] = term_refs[0][...].astype(F32)
        write(term_refs[1][...].astype(F32), 0)
    else:
        place = Place(counts_ref)
        even = place.parity == 0
        piece = term_refs[0].shape[0] // len(SLOTS)
        rows = mid_ref.shape[0] // 2 // len(SLOTS)
        for half in range(2):
            mine, other = term_refs[half], term_refs[1 - half]
            for z in range(len(SLOTS)):
                here = pl.ds(pl.multiple_of((place.depth ^ z) * piece, 16), piece)
                value = jnp.where(even, mine[here, :].astype(F32), other[here, :].astype(F32))
                at = (half * len(SLOTS) + z) * rows
                mid_ref[at : at + rows, :] = value[:rows]
                write(value[rows:], (half * len(SLOTS) + z) * (piece - rows))

    def halves(target, row):
        target[0:1, :] = second_ref[row : row + 1, :own]
        target[1:2, :] = second_ref[row : row + 1, own:]

    halves(bias_ref, 0)
    row = 16
    gain_in_ref[...] = second_ref[row : row + 1, :own]
    shift_in_ref[...] = second_ref[row : row + 1, own:]
    halves(gain_mid_ref, row + 1)
    halves(shift_mid_ref, row + 2)
    gain_gate_ref[...] = second_ref[row + 3 : row + 4, :]
    shift_gate_ref[...] = second_ref[row + 4 : row + 5, :]
    for t, target in enumerate((gain_out_ref, shift_out_ref)):
        target[:, :lanes] = second_ref[row + 5 + 2 * t : row + 6 + 2 * t, :]
        target[:, lanes:] = second_ref[row + 6 + 2 * t : row + 7 + 2 * t, :]


def per_device(
    activations,
    counts,
    weight_in,
    gain_in,
    shift_in,
    weight_mid,
    gain_mid,
    shift_mid,
    weight_squeeze,
    gain_gate,
    shift_gate,
    weight_excite,
    shift_excite,
    weight_out,
    gain_out,
    shift_out,
    cotangent,
    *,
    groups,
    parts,
):
    batches, rows, lanes = activations.shape
    images = rows // PIXELS
    own = weight_in.shape[1]
    width = own * parts
    inter = gain_gate.shape[0]
    wide_rows = images * PADDED
    gap_rows = WIDE + images * STRIDE
    chan, group = lax.axis_index("chan"), lax.axis_index("dp")
    depth = groups // 2

    def permute(tensor, to):
        pairs = []
        for index in range(groups * parts):
            z, x, y, c = index // parts // 2, index // parts % 2, index % parts // 2, index % 2
            z, x, y, c = to(z, x, y, c)
            pairs.append((index, (2 * z + x) * parts + 2 * y + c))
        return lax.ppermute(tensor, ("dp", "chan"), pairs)

    def home(tensor, s):
        return permute(tensor, lambda z, x, y, c: (z, c ^ (s & 1), y ^ (s >> 1), x))

    def away_plane(tensor):
        return permute(tensor, lambda z, x, y, c: (z, c, y, x))

    def cross(even, odd):
        return even, odd, across(jnp.stack([even[1], odd[1]]))

    def core(tensor):
        return permute(tensor, lambda z, x, y, c: (z, x, y, c ^ 1))

    def across(tensor):
        return permute(tensor, lambda z, x, y, c: (z, x, y ^ 1, c))

    def parity(tensor):
        return permute(tensor, lambda z, x, y, c: (z, x ^ 1, y, c))

    def along(tensor, t):
        return permute(tensor, lambda z, x, y, c: (z ^ t, x, y, c))

    def after(tensor, *others):
        return lax.optimization_barrier((tensor,) + others)[0]

    def after_all(tensors, *others):
        return lax.optimization_barrier(tuple(tensors) + others)[: len(tensors)]

    def exchange(total, gather):
        def merge(mine, other):
            cut = 0 if total is None else total
            joined = [mine[:cut] + other[:cut]] if cut else []
            if gather:
                joined += [mine[cut : cut + gather], other[cut : cut + gather]]
            return jnp.concatenate(joined) if len(joined) > 1 else joined[0]

        def run(mine):
            nonlocal gather
            mine = merge(mine, core(mine))
            gather = 2 * gather
            if depth <= 4:
                return (mine,) + tuple(along(mine, t) for t in range(1, depth))
            step = 1
            while step < depth:
                mine = merge(mine, along(mine, step))
                gather, step = 2 * gather, 2 * step
            return (mine,)

        return run

    def padded(rows):
        return -(-rows // (16 * groups)) * 16 * groups

    def kernel(body, outs, *args, smem=1):
        return call(body, outs, [], 0, *args, smem=smem)

    def add_over_all(first, second, low, shared, finish_own):
        first_rows, second_rows = first[0].shape[1], sum(k.shape[1] for k in second[0])
        if groups != 8:
            rows = padded(first_rows + second_rows)
            keep, send = kernel(
                add_core,
                [shape((rows, 2 * own), BF16)] * 2,
                (first[0],) + second[0],
                (first[1],) + second[1],
                smem=0,
            )
            terms = (keep.astype(F32) + across(send).astype(F32)).astype(BF16)
            terms = lax.all_to_all(terms.reshape(groups, rows // groups, -1), "dp", 0, 0)
            (terms,) = kernel(add_groups, [shape(terms.shape, BF16)], terms, smem=0)
            terms = lax.all_to_all(terms, "dp", 0, 0).reshape(rows, -1)
            terms = terms[:first_rows], terms[first_rows : first_rows + second_rows]
            return (terms, low, across(low)) + tuple(finish_own(*shared))
        second_rows = padded(second_rows)
        halves = (first_rows // 2, second_rows // 2)
        pieces = (first_rows // groups, second_rows // groups)

        def rows(number, kind=F32):
            return shape((number, 2 * own), kind)

        keep, second_send = kernel(add_core, [rows(second_rows, BF16)] * 2, *second, smem=0)
        arrived = across(second_send)
        pair = (2, halves[0], 2 * own)
        first_keep, send = call(
            add_core_first,
            [shape(pair), shape(pair, BF16)],
            [],
            0,
            counts,
            *first,
        )
        first_arrived = parity(send)
        arrived = after(arrived, shared[1])
        keep, send = call(
            add_chip,
            [rows(halves[1]), rows(halves[1], BF16)],
            [],
            0,
            counts,
            keep,
            arrived,
        )
        arrived = parity(send)
        first_keep, send = kernel(
            add_parity_first,
            [rows(halves[0]), rows(halves[0], BF16)],
            first_keep,
            first_arrived,
            smem=0,
        )
        first_arrived = across(send)
        arrived = after(arrived, first_arrived)
        keep, *send = call(
            add_last,
            [rows(sum(pieces))] + [rows(sum(pieces), BF16)] * (depth - 1),
            [],
            0,
            counts,
            (first_keep, keep),
            (first_arrived, arrived),
        )
        low = away_plane(after(low, keep))
        result, grad_summed = finish_own(*after_all(shared, keep))
        arrived = tuple(along(send[t - 1], t) for t in range(1, depth))
        arrived = after_all(arrived, result)
        low_other = across(after(low, *arrived))
        (mine,) = kernel(add_depth, [rows(sum(pieces), BF16)], keep, arrived, smem=0)
        mine = (mine,) + tuple(along(mine, t) for t in range(1, depth))
        low, low_other = after_all((low, low_other), *mine)
        mine = jnp.concatenate(mine)
        return (mine, parity(mine)), low, low_other, result, grad_summed

    def slots_of(tensor, *which):
        return [lax.dynamic_index_in_dim(tensor, chan ^ s, 0, keepdims=False) for s in which]

    first = weight_in.T
    other, near = across(first), core(first)
    far = slots_of(activations, 2, 3)
    x = slots_of(after(activations, near), 0, 1) + far
    x = tuple(home(piece, s) for s, piece in enumerate(x))

    (weights,) = call(
        pack,
        [shape((19 * own + 16 + inter + 2 * width, 2 * own), BF16)],
        [pltpu.VMEM((16, 2 * own), F32)],
        0,
        weight_mid.transpose(0, 1, 3, 4, 2).reshape(-1, 2 * own),
        weight_squeeze,
        gain_in.reshape(1, -1),
        shift_in.reshape(1, -1),
        gain_mid,
        shift_mid,
        shift_excite,
        gain_out.reshape(1, -1),
        shift_out.reshape(1, -1),
        weight_excite.transpose(1, 2, 0).reshape(-1, inter),
        weight_out,
        smem=0,
    )
    other = after(other, weights)
    first = (first, near, other, core(other))
    near = core(weights)
    cot = slots_of(after(cotangent, x[0], x[1]), *SLOTS)
    even, odd = jnp.stack([cot[0], cot[2]]), jnp.stack([cot[1], cot[3]])
    other = across(after(weights, x[2], x[3], first[3]))
    even = home(after(even, x[2], x[3]), 0)
    gate_affine = jnp.stack([gain_gate, shift_gate]).astype(F32)

    product = 2 * rows * lanes * parts * width
    pre_in, msg, w_in, wall = call(
        reduce_in,
        [
            shape((wide_rows, width)),
            shape((2 + parts, lanes)),
            shape((parts, width, lanes), BF16),
            shape((groups * images, inter)),
        ],
        [pltpu.VMEM((rows, width), F32)],
        product,
        counts,
        *x,
        *first,
    )
    in_sums = exchange(2 + parts, 0)(after(msg, near, odd))
    other = after(other, *in_sums)
    odd = home(after(odd, *in_sums), 1)
    weights = (weights, near, other, core(other))
    w_mid, w_mid_back, squeeze, in_affine, mid_affine, bias, out_affine = call(
        place_mid,
        [
            shape((2, width, 9 * inter), BF16),
            shape((2, 9 * width, inter), BF16),
            shape((width, inter), BF16),
            shape((2, width)),
            shape((2, 2 * width)),
            shape((1, 2 * width)),
            shape((2, parts, 1, lanes)),
        ],
        [pltpu.VMEM((parts, 16, 2 * own), F32)],
        0,
        counts,
        *weights,
    )
    conv = 2 * wide_rows * 9 * width * width
    taps, mid, msg = call(
        conv_mid,
        [
            shape((3, gap_rows, width), BF16),
            shape((wide_rows, 2 * width)),
            shape((2, 2 * width)),
        ],
        [],
        conv,
        counts,
        pre_in,
        in_sums,
        in_affine,
        w_mid,
    )
    mid_sums = exchange(2, 0)(msg)
    excite, w_out = call(
        place_rest,
        [
            shape((2 * width, inter), BF16),
            shape((parts, width, lanes), BF16),
        ],
        [],
        0,
        counts,
        *weights,
    )
    pooled, msg = call(
        pool,
        [shape((images, width)), shape((GATHERED, inter))],
        [],
        0,
        counts,
        mid,
        mid_sums,
        mid_affine,
        squeeze,
    )
    cot = cross(*after_all((even, odd), msg))
    gathered = exchange(None, GATHERED)(msg)
    gate, attention, weighted, out, msg = call(
        attend,
        [
            shape((2, images, inter)),
            shape((images, 2 * width)),
            shape((rows, width), BF16),
            shape((parts, rows, lanes)),
            shape((2 * parts, lanes)),
        ],
        [pltpu.VMEM((wide_rows, width), F32), pltpu.VMEM((rows, width), F32)],
        product,
        counts,
        gathered,
        wall,
        gate_affine,
        excite,
        bias,
        mid,
        mid_sums,
        mid_affine,
        w_out,
    )
    out_sums = exchange(2 * parts, 0)(msg)
    shared, grad, msg = call(
        finish,
        [
            shape((rows + 32, width), BF16),
            shape((parts, rows, lanes)),
            shape((2 * parts, lanes)),
        ],
        [pltpu.VMEM((2 * parts, 1, lanes), F32)],
        0,
        counts,
        out,
        out_sums,
        out_affine,
        weighted,
        x,
        *cot,
    )
    out_back = exchange(2 * parts, 0)(msg)

    shared = away_plane(shared)

    sums_rows = 2 * 2 * width // inter
    low_out, grad_weighted, grad_logits, msg = call(
        back_out,
        [
            shape((parts, rows, lanes), BF16),
            shape((wide_rows, width)),
            shape((images, 2 * width)),
            shape((sums_rows + images, inter)),
        ],
        [pltpu.VMEM((rows, width), F32)],
        product,
        counts,
        grad,
        out,
        out_sums,
        out_back,
        out_affine,
        w_out,
        mid,
        mid_sums,
        mid_affine,
        attention,
        gate,
        excite,
    )
    mid_back = exchange(sums_rows, images)(msg)
    term_rows = 2 * width + 2 * own + 16
    keep, send = call(
        weight_out_term,
        [shape((2, term_rows, 2 * own), BF16)] * 2,
        [pltpu.VMEM((2 * width, inter), F32), pltpu.VMEM((parts, 16, 2 * own), F32)],
        product,
        counts,
        after(weighted, mid_back[0]),
        low_out,
        gate,
        grad_logits,
        mid_affine,
    )
    mid_back = after_all(mid_back, keep, shared)
    shared = after(shared, mid_back[0])
    shared = (shared, across(shared))
    out_keep, out_arrived = keep, core(after(send, mid_back[0]))
    low_mid, grad_hidden, grad_squeeze, vectors, msg = call(
        back_mid,
        [
            shape((gap_rows, 2 * width), BF16),
            shape((wide_rows, width)),
            shape((images, inter)),
            shape((8, 2 * width)),
            shape((2, width)),
        ],
        [pltpu.VMEM((3, gap_rows, 2 * width), BF16)],
        conv,
        counts,
        mid_back,
        gathered,
        wall,
        gate_affine,
        squeeze,
        attention,
        grad_weighted,
        mid,
        mid_sums,
        mid_affine,
        pre_in,
        in_sums,
        in_affine,
        w_mid_back,
    )
    in_back = exchange(2, 0)(after(msg, out_arrived))
    keep, send = call(
        weight_mid_term,
        [shape((2, 18 * own, 2 * own), BF16)] * 2,
        [pltpu.VMEM((width, 9 * inter), F32)],
        conv,
        counts,
        after(taps, in_back[0]),
        low_mid,
        in_affine,
    )
    in_back = after_all(in_back, keep, shared[1])
    in_rows = parts * lanes // (2 * own) * own
    low_in, in_keep, in_send = call(
        functools.partial(back_in, 1.0 / groups),
        [shape((rows, width), BF16)] + [shape((2, in_rows + own + 16, 2 * own), BF16)] * 2,
        [
            pltpu.VMEM((rows, width), F32),
            pltpu.VMEM((width, lanes), F32),
            pltpu.VMEM((width, inter), F32),
            pltpu.VMEM((parts, 16, 2 * own), F32),
        ],
        product,
        counts,
        grad_hidden,
        pre_in,
        in_sums,
        in_back,
        in_affine,
        *x,
        vectors,
        out_back,
        pooled,
        gathered,
        grad_squeeze,
    )
    owned = shape((batches, rows, lanes), BF16)

    def finish_own(near, far):
        swapped = core(jnp.stack([near, far]))
        return call(
            finish_owned,
            [owned, owned],
            [pltpu.VMEM((rows, lanes), F32)],
            product,
            counts,
            near,
            swapped,
            far,
            w_out,
            activations,
            cotangent,
        )

    send = after(send, low_in)
    terms, low_in, low_other, result, grad_summed = add_over_all(
        (keep, core(send)),
        ((out_keep, in_keep), (out_arrived, core(in_send))),
        low_in,
        shared,
        finish_own,
    )
    lows = (low_in, core(low_in), low_other, core(low_other))
    (grad_x,) = call(grad_owned, [owned], [], product, lows, w_in, grad_summed, smem=0)
    terms = after_all(terms, grad_x)
    (
        g_in,
        g_gain_in,
        g_shift_in,
        g_mid,
        g_gain_mid,
        g_shift_mid,
        g_squeeze,
        g_gain_gate,
        g_shift_gate,
        g_excite,
        g_bias,
        g_out,
        g_gain_out,
        g_shift_out,
    ) = call(
        functools.partial(unpack, groups != 8),
        [
            shape((own, parts * lanes)),
            shape((1, own)),
            shape((1, own)),
            shape((18 * own, inter)),
            shape((2, own)),
            shape((2, own)),
            shape((own, inter)),
            shape((1, inter)),
            shape((1, inter)),
            shape((2 * own, inter)),
            shape((2, own)),
            shape((width, lanes)),
            shape((1, lanes)),
            shape((1, lanes)),
        ],
        [pltpu.VMEM((32, 2 * own), F32)],
        0,
        counts,
        terms,
    )
    return (
        result,
        grad_x,
        g_in.T,
        g_gain_in.reshape(-1),
        g_shift_in.reshape(-1),
        g_mid.reshape(3, 3, 2, own, inter).transpose(0, 1, 4, 2, 3),
        g_gain_mid,
        g_shift_mid,
        g_squeeze,
        g_gain_gate.reshape(-1),
        g_shift_gate.reshape(-1),
        g_excite.reshape(2, own, inter).transpose(2, 0, 1),
        g_bias,
        g_out,
        g_gain_out.reshape(-1),
        g_shift_out.reshape(-1),
    )


def solution(mesh):
    placed = (
        P(None, "dp", "chan"),
        P(),
        P(None, "chan"),
        P("chan"),
        P("chan"),
        P(None, None, None, None, "chan"),
        P(None, "chan"),
        P(None, "chan"),
        P("chan", None),
        P(),
        P(),
        P(None, None, "chan"),
        P(None, "chan"),
        P(None, "chan"),
        P("chan"),
        P("chan"),
        P(None, "dp", "chan"),
    )
    return jax.shard_map(
        functools.partial(per_device, groups=mesh.shape["dp"], parts=mesh.shape["chan"]),
        mesh=mesh,
        in_specs=placed,
        out_specs=placed[:1] + placed[:1] + placed[2:16],
        check_vma=False,
    )
```

```python
import functools

import jax
import jax.numpy as jnp
from jax import lax
from jax.experimental import pallas as pl
from jax.experimental.pallas import tpu as pltpu
from jax.sharding import PartitionSpec as P

SIDE = 14
PIXELS = SIDE * SIDE
WIDE = 16
PADDED = SIDE * WIDE
STRIDE = PADDED + WIDE
CHUNK = 16
UNROLL = 49
VMEM_LIMIT = 24 * 2**20
SLOTS = (0, 1, 2, 3)
GATHERED = 40
ORDER = (0, 2, 1, 3)
EPSILON = 1e-05
HIGHEST = lax.Precision.HIGHEST
F32 = jnp.float32
BF16 = jnp.bfloat16


def dot_nn(left, right, precision=None):
    return lax.dot_general(
        left, right, (((1,), (0,)), ((), ())), preferred_element_type=F32, precision=precision
    )


def parts_of(value):
    high = value.astype(BF16)
    rest = value - high.astype(F32)
    middle = rest.astype(BF16)
    return jnp.concatenate([high, middle, (rest - middle.astype(F32)).astype(BF16)], axis=0)


def exact_dot(dot, left, right):
    rows = -(-left.shape[0] // 16) * 16
    if rows > left.shape[0]:
        left = jnp.concatenate([left, jnp.zeros((rows - left.shape[0], left.shape[1]), F32)], axis=0)
    value = dot(parts_of(left), right)
    return value[:rows] + value[rows : 2 * rows] + value[2 * rows :]


def dot_nt(left, right, precision=None):
    return lax.dot_general(
        left, right, (((1,), (1,)), ((), ())), preferred_element_type=F32, precision=precision
    )


def dot_tn(left, right, precision=None):
    return lax.dot_general(
        left, right, (((0,), (0,)), ((), ())), preferred_element_type=F32, precision=precision
    )


def sum_rows(matrix):
    value = dot_nn(jnp.ones((16, matrix.shape[0]), BF16), matrix)[0:1]
    high = value.astype(BF16).astype(F32)
    middle = (value - high).astype(BF16).astype(F32)
    empty = jnp.zeros((13, value.shape[1]), F32)
    rows = jnp.concatenate([high, middle, value - high - middle, empty], axis=0)
    return rows.astype(BF16)


def same_rows(row):
    return jnp.broadcast_to(row, (16, row.shape[1])).astype(BF16)


def centred_dot(centred, center, other):
    left = jnp.concatenate([centred, same_rows(-center)], axis=0)
    return dot_tn(left, jnp.concatenate([other, sum_rows(other)], axis=0))


def dot_centred(other, centred, center):
    right = jnp.concatenate([centred, same_rows(-center)], axis=0)
    return dot_tn(jnp.concatenate([other, sum_rows(other)], axis=0), right)


def expected(gain, shift):
    reach = 3.0**0.5 * gain
    return (4.0 * silu(shift) + silu(shift + reach) + silu(shift - reach)) / 6.0


def logistic(value):
    return 0.5 + 0.5 * jnp.tanh(0.5 * value)


def silu(value):
    return value * logistic(value)


def slope(value):
    share = logistic(value)
    return share + value * (share * (1.0 - share))


def moments(first, second, total):
    center = first / total
    return center, lax.rsqrt(second / total - center * center + EPSILON)


def fold(value):
    return jnp.sum(value.reshape(-1, 8, value.shape[-1]), axis=0)


def total_of(value):
    return jnp.sum(value, axis=0, keepdims=True)


def columns_real(rows):
    spot = lax.broadcasted_iota(jnp.int32, (rows, 1), 0)
    return (lax.rem(spot, WIDE) < SIDE).astype(F32)


def summed_over(refs):
    values = [ref[...] for ref in refs]
    while len(values) > 1:
        values = [left + right for left, right in zip(values[::2], values[1::2])]
    return values[0]


def slot_rows(refs, size, first, count, skip=0):
    return jnp.concatenate(
        [
            ref[at + first : at + first + count, :]
            for ref in refs
            for at in range(skip, ref.shape[0], size)
        ],
        axis=0,
    )


class Place:
    def __init__(self, counts_ref):
        group = lax.axis_index("dp")
        self.chan = lax.axis_index("chan")
        self.parity, self.depth, self.core = group & 1, group >> 1, self.chan & 1
        self.batch = (self.chan & 2) | self.parity
        self.counts = counts_ref
        self.groups = counts_ref.shape[1]

    def images(self, depth, core):
        return self.counts[self.batch, 2 * depth + core]

    def real(self, image):
        return jnp.where(self.images(self.depth, self.core) > image, 1.0, 0.0).astype(F32)

    def total(self):
        every = [self.counts[self.batch, g] for g in range(self.groups)]
        return functools.reduce(jnp.add, every).astype(F32)


def spread_map_rows(flat_ref, wide_ref):
    for line in range(flat_ref.shape[0] // SIDE):
        wide_ref[line * WIDE : line * WIDE + SIDE, :] = flat_ref[line * SIDE : (line + 1) * SIDE, :]
        wide_ref[line * WIDE + SIDE : (line + 1) * WIDE, :] = jnp.zeros(
            (WIDE - SIDE, wide_ref.shape[1]), wide_ref.dtype
        )


def pack_map_rows(wide_ref, flat_ref):
    for line in range(flat_ref.shape[0] // SIDE):
        flat_ref[line * SIDE : (line + 1) * SIDE, :] = wide_ref[line * WIDE : line * WIDE + SIDE, :]


def clear_gaps(taps_ref, images):
    for gap in range(images + 1):
        taps_ref[:, gap * STRIDE : gap * STRIDE + WIDE, :] = jnp.zeros(
            (3, WIDE, taps_ref.shape[2]), taps_ref.dtype
        )


def store_taps(taps_ref, at, value):
    here = pl.ds(pl.multiple_of(at, WIDE), WIDE)
    taps_ref[0, here, :] = pltpu.roll(value, 1, 0).astype(taps_ref.dtype)
    taps_ref[1, here, :] = value.astype(taps_ref.dtype)
    taps_ref[2, here, :] = pltpu.roll(value, WIDE - 1, 0).astype(taps_ref.dtype)


def call(body, outs, scratch, flops, *args, smem=1):
    specs = tuple(
        pl.BlockSpec(memory_space=pltpu.SMEM)
        if place < smem
        else jax.tree.map(lambda _: pl.BlockSpec(memory_space=pltpu.VMEM), arg)
        for place, arg in enumerate(args)
    )
    moved = sum(a.size * a.dtype.itemsize for a in jax.tree.leaves((args, outs)))
    return pl.pallas_call(
        body,
        out_shape=outs,
        in_specs=specs,
        out_specs=[pl.BlockSpec(memory_space=pltpu.VMEM)] * len(outs),
        scratch_shapes=scratch,
        compiler_params=pltpu.CompilerParams(vmem_limit_bytes=VMEM_LIMIT),
        cost_estimate=pl.CostEstimate(flops=flops, bytes_accessed=moved, transcendentals=0),
        name=getattr(body, "func", body).__name__,
    )(*args)


def shape(dims, kind=F32):
    return jax.ShapeDtypeStruct(dims, kind)


def slot_refs(even_ref, odd_ref, across_ref):
    return even_ref.at[0], odd_ref.at[0], across_ref.at[0], across_ref.at[1]


def pack(
    mid_ref,
    squeeze_ref,
    gain_in_ref,
    shift_in_ref,
    gain_mid_ref,
    shift_mid_ref,
    bias_ref,
    gain_out_ref,
    shift_out_ref,
    excite_ref,
    out_ref,
    target_ref,
    small_ref,
):
    lanes = target_ref.shape[1]
    own = lanes // 2
    small_ref[...] = jnp.zeros_like(small_ref)
    small_ref[0:1, :own] = gain_in_ref[...].astype(F32)
    small_ref[0:1, own:] = shift_in_ref[...].astype(F32)
    for row, ref in enumerate((gain_mid_ref, shift_mid_ref, bias_ref)):
        value = ref[...].astype(F32)
        small_ref[row + 1 : row + 2, :own] = value[0:1]
        small_ref[row + 1 : row + 2, own:] = value[1:2]
    for t, ref in enumerate((gain_out_ref, shift_out_ref)):
        value = ref[...].astype(F32)
        small_ref[4 + 2 * t : 5 + 2 * t, :] = value[:, :lanes]
        small_ref[5 + 2 * t : 6 + 2 * t, :] = value[:, lanes:]
    row = 0
    for ref in (mid_ref, squeeze_ref, small_ref, excite_ref):
        target_ref[row : row + ref.shape[0], :] = ref[...].astype(BF16)
        row += ref.shape[0]
    for block in range(out_ref.shape[1] // lanes):
        rows = out_ref.shape[0]
        target_ref[row : row + rows, :] = out_ref[:, block * lanes : (block + 1) * lanes]
        row += rows


def reduce_in(
    counts_ref, x0, x1, x2, x3, a0, a1, a2, a3, pre_ref, msg_ref, w_ref, wall_ref, flat_ref
):
    place = Place(counts_ref)
    images = wall_ref.shape[0] // place.groups
    spot = lax.broadcasted_iota(jnp.int32, wall_ref.shape, 0)
    real = jnp.zeros(wall_ref.shape, jnp.int32)
    for slot in range(place.groups):
        number = place.images(place.depth ^ (slot >> 1), place.core ^ (slot & 1))
        here = (spot >= slot * images) & (spot < slot * images + number)
        real = jnp.where(here, 1, real)
    wall_ref[...] = real.astype(F32)
    own = w_ref.shape[1] // len(SLOTS)
    lanes = w_ref.shape[2]
    for s, piece in enumerate((a0, a1, a2, a3)):
        here = pl.ds(pl.multiple_of((place.chan ^ s) * own, own), own)
        for block in range(w_ref.shape[0]):
            w_ref[block, here, :] = piece[:, block * lanes : (block + 1) * lanes]
    parts = [dot_nt(x[...], w_ref[place.batch ^ s]) for s, x in enumerate((x0, x1, x2, x3))]
    flat_ref[...] = functools.reduce(jnp.add, parts)
    spread_map_rows(flat_ref, pre_ref)
    first = jnp.zeros((1, pre_ref.shape[1]), F32)
    second = jnp.zeros((1, pre_ref.shape[1]), F32)
    for image in range(pre_ref.shape[0] // PADDED):
        real = place.real(image)
        value = pre_ref[image * PADDED : (image + 1) * PADDED, :]
        first = first + real * total_of(value)
        second = second + real * total_of(value * value)
    rows = x0.shape[0]
    spot = lax.broadcasted_iota(jnp.int32, (16, rows), 1)
    real = (spot < place.images(place.depth, place.core) * PIXELS).astype(BF16)
    columns = [dot_nn(real, x[...])[0:1] for x in (x0, x1, x2, x3)]
    msg_ref[...] = jnp.concatenate([first, second] + columns, axis=0)


def place_mid(
    counts_ref,
    b0,
    b1,
    b2,
    b3,
    w_ref,
    w_back_ref,
    squeeze_ref,
    in_affine_ref,
    mid_affine_ref,
    bias_ref,
    out_affine_ref,
    small_ref,
):
    place = Place(counts_ref)
    width, lanes = w_ref.shape[1], b0.shape[1]
    own = width // len(SLOTS)
    for s, piece in enumerate((b0, b1, b2, b3)):
        at = pl.multiple_of((place.chan ^ s) * own, own)
        for tap in range(9):
            for r in range(2):
                block = piece[(2 * tap + r) * own : (2 * tap + r + 1) * own, :]
                w_ref[r, pl.ds(at, own), tap * lanes : (tap + 1) * lanes] = block
                w_back_ref[r, pl.ds(tap * width + at, own), :] = block
        squeeze_ref[pl.ds(at, own), :] = piece[18 * own : 19 * own, :]
        small = piece[19 * own : 19 * own + 16, :].astype(F32)
        small_ref[place.chan ^ s] = small
        for t in range(2):
            out_affine_ref[t, place.chan ^ s, :, :lanes] = small[4 + 2 * t : 5 + 2 * t, :]
            out_affine_ref[t, place.chan ^ s, :, lanes:] = small[5 + 2 * t : 6 + 2 * t, :]
    for k in range(len(SLOTS)):
        here = slice(k * own, (k + 1) * own)
        there = slice(width + k * own, width + (k + 1) * own)
        in_affine_ref[0:1, here] = small_ref[k, 0:1, :own]
        in_affine_ref[1:2, here] = small_ref[k, 0:1, own:]
        for t in range(2):
            mid_affine_ref[t : t + 1, here] = small_ref[k, 1 + t : 2 + t, :own]
            mid_affine_ref[t : t + 1, there] = small_ref[k, 1 + t : 2 + t, own:]
        bias_ref[0:1, here] = small_ref[k, 3:4, :own]
        bias_ref[0:1, there] = small_ref[k, 3:4, own:]


def place_rest(counts_ref, b0, b1, b2, b3, excite_ref, w_out_ref):
    place = Place(counts_ref)
    width, lanes = w_out_ref.shape[1], b0.shape[1]
    own = width // len(SLOTS)
    for s, piece in enumerate((b0, b1, b2, b3)):
        row = 19 * own + 16
        for r in range(2):
            at = pl.multiple_of(r * width + (place.chan ^ s) * own, own)
            excite_ref[pl.ds(at, own), :] = piece[row : row + own, :]
            row += own
        w_out_ref[place.chan ^ s, :, :lanes] = piece[row : row + width, :]
        w_out_ref[place.chan ^ s, :, lanes:] = piece[row + width : row + 2 * width, :]


def conv_mid(
    counts_ref,
    pre_ref,
    sums_refs,
    affine_ref,
    w_ref,
    taps_ref,
    mid_ref,
    msg_ref,
):
    place = Place(counts_ref)
    images = pre_ref.shape[0] // PADDED
    total = place.total() * PIXELS
    sums = summed_over(sums_refs)
    center, scale = moments(sums[0:1], sums[1:2], total)
    gain = affine_ref[0:1, :] * scale
    shift = affine_ref[1:2, :] - center * gain
    clear_gaps(taps_ref, images)
    keep = columns_real(WIDE)
    for image in range(images):

        def normalize(step, carry, image=image):
            rows = pl.multiple_of(step * WIDE, WIDE)
            value = pre_ref[pl.ds(image * PADDED + rows, WIDE), :]
            value = silu(value * gain + shift) * keep
            store_taps(taps_ref, image * STRIDE + WIDE + rows, value)
            return carry

        lax.fori_loop(0, SIDE, normalize, 0, unroll=SIDE)
    half = pre_ref.shape[1] // 2
    width = pre_ref.shape[1]
    keep = columns_real(PADDED)
    firsts = [jnp.zeros((1, width), F32) for _ in range(2)]
    seconds = [jnp.zeros((1, width), F32) for _ in range(2)]
    for image in range(images):
        real = place.real(image)
        for r in range(2):
            left = jnp.concatenate(
                [
                    taps_ref[
                        b,
                        image * STRIDE + a * WIDE : image * STRIDE + a * WIDE + PADDED,
                        r * half : (r + 1) * half,
                    ]
                    for a in range(3)
                    for b in range(3)
                ],
                axis=1,
            )
            value = dot_nt(left, w_ref[r])
            mid_ref[image * PADDED : (image + 1) * PADDED, r * width : (r + 1) * width] = value
            held = value * keep
            firsts[r] = firsts[r] + real * total_of(held)
            seconds[r] = seconds[r] + real * total_of(held * held)
    sums = jnp.concatenate(
        [jnp.concatenate(firsts, axis=1), jnp.concatenate(seconds, axis=1)], axis=0
    )
    msg_ref[...] = sums


def mid_norm(
    place,
    sums_refs,
    affine_ref,
):
    sums = summed_over(sums_refs)
    center, scale = moments(sums[0:1], sums[1:2], place.total() * PIXELS)
    gain = affine_ref[0:1, :] * scale
    return center, scale, gain, affine_ref[1:2, :] - center * gain


def pool(
    counts_ref,
    mid_ref,
    sums_refs,
    affine_ref,
    squeeze_ref,
    pooled_ref,
    msg_ref,
):
    place = Place(counts_ref)
    images = mid_ref.shape[0] // PADDED
    width = mid_ref.shape[1] // 2
    lanes = msg_ref.shape[1]
    center, scale, gain, shift = mid_norm(place, sums_refs, affine_ref)
    keep = columns_real(CHUNK)
    inclines = [[], []]
    for image in range(images):

        def gather(step, carry, image=image):
            active, rise, lean = carry
            at = pl.multiple_of(image * PADDED + step * CHUNK, CHUNK)
            before = mid_ref[pl.ds(at, CHUNK), :]
            value = before * gain + shift
            share = logistic(value) * keep
            active = active + fold(value * share)
            inclined = share + value * (share * (1.0 - share))
            return active, rise + fold(inclined), lean + fold(inclined * before)

        nothing = jnp.zeros((8, 2 * width), F32)
        active, rise, lean = lax.fori_loop(
            0, SIDE, gather, (nothing, nothing, nothing), unroll=SIDE
        )
        active = total_of(active)
        pooled_ref[image : image + 1, :] = (active[:, :width] + active[:, width:]) / PIXELS
        rise = total_of(rise)
        inclines[0].append(rise)
        inclines[1].append(scale * (total_of(lean) - center * rise))
    inclined = jnp.concatenate(inclines[0] + inclines[1], axis=0)
    msg_ref[...] = jnp.zeros_like(msg_ref)
    for q in range(2 * width // lanes):
        row = 8 + q * 2 * images
        msg_ref[row : row + 2 * images, :] = inclined[:, q * lanes : (q + 1) * lanes]
    msg_ref[0:images, :] = exact_dot(dot_nn, pooled_ref[...], squeeze_ref[...])[:images]
    real = [place.real(image) * pooled_ref[image : image + 1, :] for image in range(images)]
    real = functools.reduce(jnp.add, real)
    for q in range(width // lanes):
        msg_ref[images + q : images + q + 1, :] = real[:, q * lanes : (q + 1) * lanes]


def gate_norm(
    place,
    rows,
    wall,
):
    return moments(total_of(wall * rows), total_of(wall * rows * rows), place.total())


def attend(
    counts_ref,
    gathered_refs,
    wall_ref,
    gate_affine_ref,
    excite_ref,
    bias_ref,
    mid_ref,
    mid_sums_refs,
    mid_affine_ref,
    w_out_ref,
    gate_ref,
    attention_ref,
    weighted_ref,
    out_ref,
    msg_ref,
    wide_ref,
    flat_ref,
):
    place = Place(counts_ref)
    images = mid_ref.shape[0] // PADDED
    width = mid_ref.shape[1] // 2
    rows = slot_rows(gathered_refs, GATHERED, 0, images)
    center, scale = gate_norm(place, rows, wall_ref[...])
    normed = (rows[0:images] - center) * scale
    gate_pre = normed * gate_affine_ref[0:1, :] + gate_affine_ref[1:2, :]
    gate = silu(gate_pre)
    gate_ref[0] = gate
    gate_ref[1] = slope(gate_pre)
    logits = (
        exact_dot(dot_nt, gate, excite_ref[...])[:images] + bias_ref[...]
    )
    lean = 0.5 * jnp.tanh(0.5 * (logits[:, :width] - logits[:, width:]))
    attention_ref[:, :width] = 0.5 + lean
    attention_ref[:, width:] = 0.5 - lean
    center, scale, gain, shift = mid_norm(place, mid_sums_refs, mid_affine_ref)
    for image in range(images):
        share = attention_ref[image : image + 1, :]

        def weigh(step, carry, image=image, share=share):
            at = pl.multiple_of(image * PADDED + step * CHUNK, CHUNK)
            value = share * silu(mid_ref[pl.ds(at, CHUNK), :] * gain + shift)
            wide_ref[pl.ds(at, CHUNK), :] = value[:, :width] + value[:, width:]
            return carry

        lax.fori_loop(0, SIDE, weigh, 0, unroll=SIDE)
    pack_map_rows(wide_ref, flat_ref)
    weighted_ref[...] = flat_ref[...].astype(BF16)
    spot = lax.broadcasted_iota(jnp.int32, (flat_ref.shape[0], 1), 0)
    real = (spot < place.images(place.depth, place.core) * PIXELS).astype(F32)
    blocks = w_out_ref.shape[0]
    for k in range(blocks):
        value = dot_nn(weighted_ref[...], w_out_ref[place.batch ^ k])
        out_ref[k] = value
        held = value * real
        for t, row in enumerate((total_of(held), total_of(held * value))):
            msg_ref[t * blocks + k : t * blocks + k + 1, :] = row


def finish(
    counts_ref,
    out_ref,
    sums_refs,
    affine_ref,
    weighted_ref,
    x_refs,
    cot_near_ref,
    cot_odd_ref,
    cot_across_ref,
    shared_ref,
    grad_ref,
    msg_ref,
    map_ref,
):
    place = Place(counts_ref)
    cot_refs = slot_refs(cot_near_ref, cot_odd_ref, cot_across_ref)
    blocks, rows, lanes = out_ref.shape
    sums = summed_over(sums_refs)
    center, scale = moments(sums[:blocks], sums[blocks:], place.total() * PIXELS)
    limit = place.images(place.depth, place.core) * PIXELS
    for k in range(blocks):
        mu, r = center[k : k + 1], scale[k : k + 1]
        block = place.batch ^ k
        gain = affine_ref[0, block] * r
        shift = affine_ref[1, block] - mu * gain
        map_ref[block] = gain
        map_ref[blocks + block] = shift
        x_ref, upstream_ref = x_refs[k], cot_refs[k]

        def chunk(
            step, carry, k=k, gain=gain, shift=shift, x_ref=x_ref, upstream_ref=upstream_ref
        ):
            first, second = carry
            at = pl.multiple_of(step * CHUNK, CHUNK)
            here = pl.ds(at, CHUNK)
            spot = lax.broadcasted_iota(jnp.int32, (CHUNK, 1), 0) + at
            real = (spot < limit).astype(F32)
            before = out_ref[k, here, :]
            summed = x_ref[here, :].astype(F32) + (before * gain + shift)
            share = logistic(summed)
            grad = upstream_ref[here, :].astype(F32) * real
            grad = grad * (share * (1.0 + summed * (1.0 - share)))
            grad_ref[k, here, :] = grad
            return first + fold(grad), second + fold(grad * before)

        nothing = jnp.zeros((8, lanes), F32)
        first, second = lax.fori_loop(
            0, rows // CHUNK, chunk, (nothing, nothing), unroll=UNROLL
        )
        first = total_of(first)
        for t, row in enumerate((first, r * (total_of(second) - mu * first))):
            msg_ref[t * blocks + k : t * blocks + k + 1, :] = row
    shared_ref[0:rows, :] = weighted_ref[...]
    exact = jnp.concatenate([map_ref[n] for n in range(2 * blocks)], axis=0)
    high = exact.astype(BF16).astype(F32)
    middle = (exact - high).astype(BF16).astype(F32)
    shared_ref[rows : rows + 16, :] = jnp.concatenate([high, middle], axis=0).astype(BF16)
    rest = jnp.concatenate([exact - high - middle, jnp.zeros_like(exact)], axis=0)
    shared_ref[rows + 16 : rows + 32, :] = rest.astype(BF16)


def finish_owned(
    counts_ref, near_ref, swapped_ref, far_ref, w_ref, x_ref, cot_ref, result_ref, grad_ref, out_ref
):
    chan, group = lax.axis_index("chan"), lax.axis_index("dp")
    rows = cot_ref.shape[1]
    blocks = len(SLOTS)
    for s, piece in enumerate((near_ref, swapped_ref.at[0], far_ref, swapped_ref.at[1])):
        batch = chan ^ s
        limit = counts_ref[batch, group] * PIXELS
        out_ref[...] = dot_nn(piece[0:rows, :], w_ref[chan])
        exact = piece[rows : rows + 32, :].astype(F32)
        exact = exact[0:8] + exact[8:16] + exact[16:24]
        gain, shift = exact[0:1], exact[blocks : blocks + 1]
        for k in range(1, blocks):
            gain = jnp.where(chan == k, exact[k : k + 1], gain)
            shift = jnp.where(chan == k, exact[blocks + k : blocks + k + 1], shift)

        def chunk(step, carry, batch=batch, limit=limit, gain=gain, shift=shift):
            at = pl.multiple_of(step * CHUNK, CHUNK)
            here = pl.ds(at, CHUNK)
            spot = lax.broadcasted_iota(jnp.int32, (CHUNK, 1), 0) + at
            real = (spot < limit).astype(F32)
            summed = x_ref[batch, here, :].astype(F32) + (out_ref[here, :] * gain + shift)
            share = logistic(summed)
            held = share * real
            result_ref[batch, here, :] = (summed * held).astype(BF16)
            grad = cot_ref[batch, here, :].astype(F32) * (held * (1.0 + summed * (1.0 - share)))
            grad_ref[batch, here, :] = grad.astype(BF16)
            return carry

        lax.fori_loop(0, rows // CHUNK, chunk, 0, unroll=UNROLL)


def back_out(
    counts_ref,
    grad_ref,
    out_ref,
    sums_refs,
    back_refs,
    affine_ref,
    w_out_ref,
    mid_ref,
    mid_sums_refs,
    mid_affine_ref,
    attention_ref,
    gate_ref,
    excite_ref,
    low_ref,
    gw_ref,
    logits_ref,
    msg_ref,
    flat_ref,
):
    place = Place(counts_ref)
    blocks, rows, lanes = out_ref.shape
    images = attention_ref.shape[0]
    width = attention_ref.shape[1] // 2
    total = place.total() * PIXELS
    sums = summed_over(sums_refs)
    center, scale = moments(sums[:blocks], sums[blocks:], total)
    back = summed_over(back_refs) / total
    limit = place.images(place.depth, place.core) * PIXELS
    for k in range(blocks):
        mu, r = center[k : k + 1], scale[k : k + 1]
        gain = affine_ref[0, place.batch ^ k] * r
        second = gain * r * back[blocks + k : blocks + k + 1]
        first = gain * back[k : k + 1] - mu * second

        def chunk(step, carry, k=k, gain=gain, first=first, second=second):
            at = pl.multiple_of(step * CHUNK, CHUNK)
            here = pl.ds(at, CHUNK)
            spot = lax.broadcasted_iota(jnp.int32, (CHUNK, 1), 0) + at
            real = (spot < limit).astype(F32)
            value = gain * grad_ref[k, here, :] - real * (first + out_ref[k, here, :] * second)
            low_ref[k, here, :] = value.astype(BF16)
            return carry

        lax.fori_loop(0, rows // CHUNK, chunk, 0, unroll=UNROLL)
    parts = [dot_nt(low_ref[k], w_out_ref[place.batch ^ k]) for k in range(blocks)]
    flat_ref[...] = functools.reduce(jnp.add, parts)
    spread_map_rows(flat_ref, gw_ref)
    center, scale, gain, shift = mid_norm(place, mid_sums_refs, mid_affine_ref)
    rises, leans, attended = [], [], []
    for image in range(images):

        def gather(step, carry, image=image):
            attended, rise, lean = carry
            at = pl.multiple_of(image * PADDED + step * CHUNK, CHUNK)
            before = mid_ref[pl.ds(at, CHUNK), :]
            value = before * gain + shift
            share = logistic(value)
            grad = gw_ref[pl.ds(at, CHUNK), :]
            grad = jnp.concatenate([grad, grad], axis=1)
            active = grad * share
            attended = attended + fold(active * value)
            inclined = active * (1.0 + value * (1.0 - share))
            return attended, rise + fold(inclined), lean + fold(inclined * before)

        nothing = jnp.zeros((8, 2 * width), F32)
        parts = lax.fori_loop(
            0, SIDE, gather, (nothing, nothing, nothing), unroll=SIDE
        )
        share = attention_ref[image : image + 1, :]
        attended.append(total_of(parts[0]))
        rise = total_of(parts[1])
        rises.append(share * rise)
        leans.append(share * (scale * (total_of(parts[2]) - center * rise)))
    grad = jnp.concatenate(attended, axis=0)
    attention = attention_ref[...]
    inner = attention * grad
    inner = inner[:, :width] + inner[:, width:]
    logits = attention * (grad - jnp.concatenate([inner, inner], axis=1))
    logits_ref[...] = logits
    gate = exact_dot(dot_nn, logits, excite_ref[...])[:images] * gate_ref[1]
    pack = msg_ref.shape[1]
    pieces = 2 * width // pack
    for t, row in enumerate((functools.reduce(jnp.add, rises), functools.reduce(jnp.add, leans))):
        for q in range(pieces):
            msg_ref[t * pieces + q : t * pieces + q + 1, :] = row[:, q * pack : (q + 1) * pack]
    msg_ref[2 * pieces : 2 * pieces + images, :] = gate


def back_mid(
    counts_ref,
    back_refs,
    gathered_refs,
    wall_ref,
    gate_affine_ref,
    squeeze_ref,
    attention_ref,
    gw_ref,
    mid_ref,
    mid_sums_refs,
    mid_affine_ref,
    pre_ref,
    sums_refs,
    affine_ref,
    w_ref,
    low_ref,
    grad_ref,
    gate_ref,
    vector_ref,
    msg_ref,
    taps_ref,
):
    place = Place(counts_ref)
    images = attention_ref.shape[0]
    width = attention_ref.shape[1] // 2
    lanes = wall_ref.shape[1]
    pieces = 2 * width // lanes
    total = place.total() * PIXELS
    wall = wall_ref[...]
    rows = slot_rows(gathered_refs, GATHERED, 0, images)
    center, scale = gate_norm(place, rows, wall)
    gain = gate_affine_ref[0:1, :] * scale
    normed = (rows - center) * scale
    grads = slot_rows(back_refs, images, 0, images, 2 * pieces)
    first, second = total_of(wall * grads), total_of(wall * grads * normed)
    vector_ref[0:1, 0:lanes] = second
    vector_ref[0:1, lanes : 2 * lanes] = first
    squeezed = gain * (grads - wall * (first + normed * second) / place.total())
    gate_ref[...] = squeezed[0:images]
    pooled_grad = exact_dot(dot_nt, squeezed, squeeze_ref[...]) / PIXELS
    pooled_grad = jnp.concatenate([pooled_grad, pooled_grad], axis=1)
    slot = 0
    terms = jnp.zeros((2 * images, 2 * width), F32)
    for ref in gathered_refs:
        for at in range(8, ref.shape[0], GATHERED):
            inclines = [
                ref[at + q * 2 * images : at + (q + 1) * 2 * images, :] for q in range(pieces)
            ]
            grad = pooled_grad[slot * images : (slot + 1) * images, :]
            grad = jnp.concatenate([grad, grad], axis=0)
            terms = terms + jnp.concatenate(inclines, axis=1) * grad
            slot += 1
    sums = functools.reduce(jnp.add, [ref[0 : 2 * pieces, :] for ref in back_refs])
    back = []
    for t in range(2):
        row = [sums[t * pieces + q : t * pieces + q + 1, :] for q in range(pieces)]
        back.append(
            jnp.concatenate(row, axis=1) + total_of(terms[t * images : (t + 1) * images])
        )
    vector_ref[1:2, :] = back[1]
    vector_ref[2:3, :] = back[0]
    own = pooled_grad[0:images]
    center, scale, gain, shift = mid_norm(place, mid_sums_refs, mid_affine_ref)
    second = gain * scale * back[1] / total
    first = gain * back[0] / total - center * second
    clear_gaps(taps_ref, images)
    keep = columns_real(WIDE)
    for image in range(images):
        share = gain * attention_ref[image : image + 1, :]
        offset = gain * own[image : image + 1, :]
        real = place.real(image)
        lead, lag = real * first, real * second

        def chunk(step, carry, image=image, share=share, offset=offset, lead=lead, lag=lag):
            rows = pl.multiple_of(step * WIDE, WIDE)
            here = pl.ds(image * PADDED + rows, WIDE)
            before = mid_ref[here, :]
            grad = gw_ref[here, :]
            grad = jnp.concatenate([grad, grad], axis=1)
            grad = (share * grad + offset) * slope(before * gain + shift)
            value = (grad - (lead + before * lag)) * keep
            store_taps(taps_ref, image * STRIDE + WIDE + rows, value)
            return carry

        lax.fori_loop(0, SIDE, chunk, 0, unroll=SIDE)
    low_ref[...] = taps_ref[1]
    sums = summed_over(sums_refs)
    center, scale = moments(sums[0:1], sums[1:2], total)
    gain = affine_ref[0:1, :] * scale
    shift = affine_ref[1:2, :] - center * gain
    half = width // 2
    keep = columns_real(PADDED)
    firsts = [jnp.zeros((1, half), F32) for _ in range(2)]
    seconds = [jnp.zeros((1, half), F32) for _ in range(2)]
    for image in range(images):
        real = place.real(image)
        here = slice(image * PADDED, (image + 1) * PADDED)
        for r in range(2):
            left = jnp.concatenate(
                [
                    taps_ref[
                        2 - b,
                        image * STRIDE + (2 - a) * WIDE : image * STRIDE + (2 - a) * WIDE + PADDED,
                        r * width : (r + 1) * width,
                    ]
                    for a in range(3)
                    for b in range(3)
                ],
                axis=1,
            )
            lane = slice(r * half, (r + 1) * half)
            before = pre_ref[here, lane]
            value = dot_nn(left, w_ref[r]) * slope(before * gain[:, lane] + shift[:, lane])
            value = value * (keep * real)
            grad_ref[here, lane] = value
            firsts[r] = firsts[r] + total_of(value)
            seconds[r] = seconds[r] + total_of(value * before)
    first = jnp.concatenate(firsts, axis=1)
    second = scale * (jnp.concatenate(seconds, axis=1) - center * first)
    sums = jnp.concatenate([first, second], axis=0)
    msg_ref[...] = sums


def sort_pieces(
    place,
    source_ref,
    keep_ref,
    send_ref,
    row,
):
    for turn, s in enumerate(ORDER):
        target = keep_ref if turn < 2 else send_ref
        rows = source_ref.shape[1]
        target[turn % 2, row : row + rows, :] = source_ref[place.chan ^ s].astype(BF16)


def weight_out_term(
    counts_ref,
    weighted_ref,
    low_ref,
    gate_ref,
    logits_ref,
    affine_ref,
    keep_ref,
    send_ref,
    wide_ref,
    small_ref,
):
    place = Place(counts_ref)
    width = weighted_ref.shape[1]
    lanes = keep_ref.shape[2]
    own = width // len(SLOTS)
    center = expected(affine_ref[0:1, :], affine_ref[1:2, :])
    center = 0.5 * (center[:, :width] + center[:, width:])
    for turn, s in enumerate(ORDER):
        target = keep_ref if turn < 2 else send_ref
        held = place.batch ^ place.chan ^ s
        term = centred_dot(weighted_ref[...], center, low_ref[held]).astype(BF16)
        target[turn % 2, 0:width, :] = term[:, :lanes]
        target[turn % 2, width : 2 * width, :] = term[:, lanes:]
    wide_ref[...] = dot_tn(logits_ref[...], gate_ref[0], HIGHEST)
    for turn, s in enumerate(ORDER):
        target = keep_ref if turn < 2 else send_ref
        for r in range(2):
            at = pl.multiple_of(r * width + (place.chan ^ s) * own, own)
            row = 2 * width + r * own
            target[turn % 2, row : row + own, :] = wide_ref[pl.ds(at, own), :].astype(BF16)
    small_ref[...] = jnp.zeros_like(small_ref)
    bias = total_of(logits_ref[...])
    for k in range(len(SLOTS)):
        small_ref[k, 0:1, :own] = bias[:, k * own : (k + 1) * own]
        small_ref[k, 0:1, own:] = bias[:, width + k * own : width + (k + 1) * own]
    sort_pieces(place, small_ref, keep_ref, send_ref, 2 * width + 2 * own)


def weight_mid_term(
    counts_ref,
    taps_ref,
    low_ref,
    affine_ref,
    keep_ref,
    send_ref,
    wide_ref,
):
    place = Place(counts_ref)
    center = expected(affine_ref[0:1, :], affine_ref[1:2, :])
    half = taps_ref.shape[2] // 2
    width = low_ref.shape[1] // 2
    own = width // len(SLOTS)
    rows = low_ref.shape[0] - 2 * WIDE
    for r in range(2):
        right = jnp.concatenate(
            [
                taps_ref[b, a * WIDE : a * WIDE + rows, r * half : (r + 1) * half]
                for a in range(3)
                for b in range(3)
            ],
            axis=1,
        )
        low = low_ref[WIDE : WIDE + rows, r * width : (r + 1) * width]
        offset = jnp.concatenate([center[:, r * half : (r + 1) * half]] * 9, axis=1)
        wide_ref[...] = dot_centred(low, right, offset)
        for turn, s in enumerate(ORDER):
            target = keep_ref if turn < 2 else send_ref
            here = pl.ds(pl.multiple_of((place.chan ^ s) * own, own), own)
            for tap in range(9):
                row = (2 * tap + r) * own
                target[turn % 2, row : row + own, :] = wide_ref[
                    here, tap * half : (tap + 1) * half
                ].astype(BF16)


def back_in(
    share,
    counts_ref,
    grad_ref,
    pre_ref,
    sums_refs,
    back_refs,
    affine_ref,
    x0,
    x1,
    x2,
    x3,
    vector_ref,
    out_back_refs,
    pooled_ref,
    gathered_refs,
    squeezed_ref,
    low_ref,
    keep_ref,
    send_ref,
    flat_ref,
    wide_ref,
    narrow_ref,
    small_ref,
):
    place = Place(counts_ref)
    images = pre_ref.shape[0] // PADDED
    width = pre_ref.shape[1]
    own = width // len(SLOTS)
    chan, batch = place.chan, place.batch
    total = place.total() * PIXELS
    sums = summed_over(sums_refs)
    center, scale = moments(sums[0:1], sums[1:2], total)
    back = summed_over(back_refs)
    gain = affine_ref[0:1, :] * scale
    second = gain * scale * back[1:2] / total
    first = gain * back[0:1] / total - center * second
    for image in range(images):
        real = place.real(image)
        lead, lag = real * first, real * second
        for line in range(SIDE):
            at = image * PADDED + line * WIDE
            before = pre_ref[at : at + WIDE, :]
            value = gain * grad_ref[at : at + WIDE, :] - (lead + before * lag)
            at = image * PIXELS + line * SIDE
            flat_ref[at : at + SIDE, :] = value[:SIDE]
    low_ref[...] = flat_ref[...].astype(BF16)
    lanes = keep_ref.shape[2]
    low = jnp.concatenate([low_ref[...], sum_rows(low_ref[...])], axis=0)
    for k, x in enumerate((x0, x1, x2, x3)):
        center = same_rows(-sums[2 + k : 3 + k] / total)
        wide_ref[...] = dot_tn(low, jnp.concatenate([x[...], center], axis=0))
        for turn, s in enumerate(ORDER):
            target = keep_ref if turn < 2 else send_ref
            here = pl.ds(pl.multiple_of((chan ^ s) * own, own), own)
            for part in range(wide_ref.shape[1] // lanes):
                at = pl.multiple_of(((batch ^ k) * (wide_ref.shape[1] // lanes) + part) * own, own)
                target[turn % 2, pl.ds(at, own), :] = wide_ref[
                    here, part * lanes : (part + 1) * lanes
                ].astype(BF16)
    mean = [
        total_of(slot_rows(gathered_refs, GATHERED, images + q, 1)) for q in range(width // lanes)
    ]
    mean = jnp.concatenate(mean, axis=1) / place.total()
    narrow_ref[...] = dot_tn(pooled_ref[...] - mean, squeezed_ref[...], HIGHEST)
    row = keep_ref.shape[1] - small_ref.shape[1] - own
    for turn, s in enumerate(ORDER):
        target = keep_ref if turn < 2 else send_ref
        here = pl.ds(pl.multiple_of((chan ^ s) * own, own), own)
        target[turn % 2, row : row + own, :] = narrow_ref[here, :].astype(BF16)
    small_ref[...] = jnp.zeros_like(small_ref)
    outs = summed_over(out_back_refs)
    for k in range(len(SLOTS)):
        here = slice(k * own, (k + 1) * own)
        there = slice(width + k * own, width + (k + 1) * own)
        small_ref[k, 0:1, :own] = back[1:2, here]
        small_ref[k, 0:1, own:] = back[0:1, here]
        for t in range(2):
            small_ref[k, 1 + t : 2 + t, :own] = vector_ref[1 + t : 2 + t, here]
            small_ref[k, 1 + t : 2 + t, own:] = vector_ref[1 + t : 2 + t, there]
        small_ref[k, 3:4, :] = vector_ref[0:1, 0:lanes]
        small_ref[k, 4:5, :] = vector_ref[0:1, lanes : 2 * lanes]
    for s in SLOTS:
        for t in range(2):
            row = outs[(1 - t) * len(SLOTS) + s : (1 - t) * len(SLOTS) + s + 1, :]
            small_ref[batch ^ s, 5 + 2 * t : 6 + 2 * t, :] = row[:, :lanes]
            small_ref[batch ^ s, 6 + 2 * t : 7 + 2 * t, :] = row[:, lanes:]
    small_ref[...] = small_ref[...] * share
    sort_pieces(place, small_ref, keep_ref, send_ref, keep_ref.shape[1] - small_ref.shape[1])


def grad_owned(low_refs, w_ref, summed_ref, result_ref):
    chan = lax.axis_index("chan")
    for s, low_ref in enumerate(low_refs):
        value = dot_nn(low_ref[...], w_ref[chan]) + summed_ref[chan ^ s].astype(F32)
        result_ref[chan ^ s] = value.astype(BF16)


def add_groups(terms_ref, sum_ref):
    value = jnp.sum(terms_ref[...].astype(F32), axis=0).astype(BF16)
    sum_ref[...] = jnp.broadcast_to(value[None], sum_ref.shape)


def added(left_ref, right_ref):
    return left_ref[...].astype(F32) + right_ref[...].astype(F32)


def add_core(keep_refs, arrived_refs, kept_ref, send_ref):
    at = 0
    for keep_ref, arrived_ref in zip(keep_refs, arrived_refs):
        value = added(keep_ref, arrived_ref).astype(BF16)
        rows = keep_ref.shape[1]
        kept_ref[at : at + rows, :] = value[0]
        send_ref[at : at + rows, :] = value[1]
        at += rows
    if at < kept_ref.shape[0]:
        for ref in (kept_ref, send_ref):
            ref[at:, :] = jnp.zeros((kept_ref.shape[0] - at, ref.shape[1]), BF16)


def split_rows(parity, keep_ref, arrived_ref, kept_ref, send_ref):
    rows = kept_ref.shape[-2]
    for own, target in ((parity, kept_ref), (1 - parity, send_ref)):
        here = pl.ds(pl.multiple_of(own * rows, 16), rows)
        if target.ndim == 2:
            value = added(keep_ref.at[here, :], arrived_ref.at[here, :])
        else:
            value = added(keep_ref.at[:, here, :], arrived_ref.at[:, here, :])
        target[...] = value.astype(target.dtype)


def add_core_first(counts_ref, keep_ref, arrived_ref, kept_ref, send_ref):
    split_rows(Place(counts_ref).parity, keep_ref, arrived_ref, kept_ref, send_ref)


def add_parity_first(keep_ref, arrived_ref, kept_ref, send_ref):
    kept_ref[...] = added(keep_ref.at[0], arrived_ref.at[0])
    send_ref[...] = added(keep_ref.at[1], arrived_ref.at[1]).astype(BF16)


def add_chip(counts_ref, keep_ref, arrived_ref, kept_ref, send_ref):
    split_rows(Place(counts_ref).parity, keep_ref, arrived_ref, kept_ref, send_ref)


def add_last(counts_ref, keep_refs, arrived_refs, kept_ref, s1, s2, s3):
    place = Place(counts_ref)
    at = 0
    for keep_ref, arrived_ref in zip(keep_refs, arrived_refs):
        rows = keep_ref.shape[0] // len(SLOTS)
        for t, target in enumerate((kept_ref, s1, s2, s3)):
            here = pl.ds(pl.multiple_of((place.depth ^ t) * rows, 16), rows)
            value = added(keep_ref.at[here, :], arrived_ref.at[here, :])
            target[at : at + rows, :] = value.astype(target.dtype)
        at += rows


def add_depth(keep_ref, arrived_refs, sum_ref):
    value = keep_ref[...]
    for ref in arrived_refs:
        value = value + ref[...].astype(F32)
    sum_ref[...] = value.astype(BF16)


def unpack(
    joined,
    counts_ref,
    term_refs,
    in_ref,
    gain_in_ref,
    shift_in_ref,
    mid_ref,
    gain_mid_ref,
    shift_mid_ref,
    squeeze_ref,
    gain_gate_ref,
    shift_gate_ref,
    excite_ref,
    bias_ref,
    out_ref,
    gain_out_ref,
    shift_out_ref,
    second_ref,
):
    own, lanes = squeeze_ref.shape
    width = out_ref.shape[0]
    places = [(out_ref, 0, 0, width), (out_ref, 0, 1, width), (excite_ref, 0, 0, 2 * own)]
    places += [(second_ref, 0, 0, 16)]
    places += [(in_ref, 0, block, own) for block in range(in_ref.shape[1] // lanes)]
    places += [(squeeze_ref, 0, 0, own), (second_ref, 16, 0, 16)]

    def write(value, row):
        start = 0
        for target, at, block, rows in places:
            first, last = max(row, start), min(row + value.shape[0], start + rows)
            if first < last:
                there = slice(at + first - start, at + last - start)
                target[there, block * lanes : (block + 1) * lanes] = value[first - row : last - row]
            start += rows

    if joined:
        mid_ref[...] = term_refs[0][...].astype(F32)
        write(term_refs[1][...].astype(F32), 0)
    else:
        place = Place(counts_ref)
        even = place.parity == 0
        piece = term_refs[0].shape[0] // len(SLOTS)
        rows = mid_ref.shape[0] // 2 // len(SLOTS)
        for half in range(2):
            mine, other = term_refs[half], term_refs[1 - half]
            for z in range(len(SLOTS)):
                here = pl.ds(pl.multiple_of((place.depth ^ z) * piece, 16), piece)
                value = jnp.where(even, mine[here, :].astype(F32), other[here, :].astype(F32))
                at = (half * len(SLOTS) + z) * rows
                mid_ref[at : at + rows, :] = value[:rows]
                write(value[rows:], (half * len(SLOTS) + z) * (piece - rows))

    def halves(target, row):
        target[0:1, :] = second_ref[row : row + 1, :own]
        target[1:2, :] = second_ref[row : row + 1, own:]

    halves(bias_ref, 0)
    row = 16
    gain_in_ref[...] = second_ref[row : row + 1, :own]
    shift_in_ref[...] = second_ref[row : row + 1, own:]
    halves(gain_mid_ref, row + 1)
    halves(shift_mid_ref, row + 2)
    gain_gate_ref[...] = second_ref[row + 3 : row + 4, :]
    shift_gate_ref[...] = second_ref[row + 4 : row + 5, :]
    for t, target in enumerate((gain_out_ref, shift_out_ref)):
        target[:, :lanes] = second_ref[row + 5 + 2 * t : row + 6 + 2 * t, :]
        target[:, lanes:] = second_ref[row + 6 + 2 * t : row + 7 + 2 * t, :]


def per_device(
    activations,
    counts,
    weight_in,
    gain_in,
    shift_in,
    weight_mid,
    gain_mid,
    shift_mid,
    weight_squeeze,
    gain_gate,
    shift_gate,
    weight_excite,
    shift_excite,
    weight_out,
    gain_out,
    shift_out,
    cotangent,
    *,
    groups,
    parts,
):
    batches, rows, lanes = activations.shape
    images = rows // PIXELS
    own = weight_in.shape[1]
    width = own * parts
    inter = gain_gate.shape[0]
    wide_rows = images * PADDED
    gap_rows = WIDE + images * STRIDE
    chan, group = lax.axis_index("chan"), lax.axis_index("dp")
    depth = groups // 2

    def permute(tensor, to):
        pairs = []
        for index in range(groups * parts):
            z, x, y, c = index // parts // 2, index // parts % 2, index % parts // 2, index % 2
            z, x, y, c = to(z, x, y, c)
            pairs.append((index, (2 * z + x) * parts + 2 * y + c))
        return lax.ppermute(tensor, ("dp", "chan"), pairs)

    def home(tensor, s):
        return permute(tensor, lambda z, x, y, c: (z, c ^ (s & 1), y ^ (s >> 1), x))

    def away_plane(tensor):
        return permute(tensor, lambda z, x, y, c: (z, c, y, x))

    def cross(even, odd):
        return even, odd, across(jnp.stack([even[1], odd[1]]))

    def core(tensor):
        return permute(tensor, lambda z, x, y, c: (z, x, y, c ^ 1))

    def across(tensor):
        return permute(tensor, lambda z, x, y, c: (z, x, y ^ 1, c))

    def parity(tensor):
        return permute(tensor, lambda z, x, y, c: (z, x ^ 1, y, c))

    def along(tensor, t):
        return permute(tensor, lambda z, x, y, c: (z ^ t, x, y, c))

    def after(tensor, *others):
        return lax.optimization_barrier((tensor,) + others)[0]

    def after_all(tensors, *others):
        return lax.optimization_barrier(tuple(tensors) + others)[: len(tensors)]

    def exchange(total, gather):
        def merge(mine, other):
            cut = 0 if total is None else total
            joined = [mine[:cut] + other[:cut]] if cut else []
            if gather:
                joined += [mine[cut : cut + gather], other[cut : cut + gather]]
            return jnp.concatenate(joined) if len(joined) > 1 else joined[0]

        def run(mine):
            nonlocal gather
            mine = merge(mine, core(mine))
            gather = 2 * gather
            if depth <= 4:
                return (mine,) + tuple(along(mine, t) for t in range(1, depth))
            step = 1
            while step < depth:
                mine = merge(mine, along(mine, step))
                gather, step = 2 * gather, 2 * step
            return (mine,)

        return run

    def padded(rows):
        return -(-rows // (16 * groups)) * 16 * groups

    def kernel(body, outs, *args, smem=1):
        return call(body, outs, [], 0, *args, smem=smem)

    def add_over_all(first, second, low, shared, finish_own):
        first_rows, second_rows = first[0].shape[1], sum(k.shape[1] for k in second[0])
        if groups != 8:
            rows = padded(first_rows + second_rows)
            keep, send = kernel(
                add_core,
                [shape((rows, 2 * own), BF16)] * 2,
                (first[0],) + second[0],
                (first[1],) + second[1],
                smem=0,
            )
            terms = (keep.astype(F32) + across(send).astype(F32)).astype(BF16)
            terms = lax.all_to_all(terms.reshape(groups, rows // groups, -1), "dp", 0, 0)
            (terms,) = kernel(add_groups, [shape(terms.shape, BF16)], terms, smem=0)
            terms = lax.all_to_all(terms, "dp", 0, 0).reshape(rows, -1)
            terms = terms[:first_rows], terms[first_rows : first_rows + second_rows]
            low = away_plane(low)
            return (terms, low, across(low)) + tuple(finish_own(*shared))
        second_rows = padded(second_rows)
        halves = (first_rows // 2, second_rows // 2)
        pieces = (first_rows // groups, second_rows // groups)

        def rows(number, kind=F32):
            return shape((number, 2 * own), kind)

        keep, second_send = kernel(add_core, [rows(second_rows, BF16)] * 2, *second, smem=0)
        arrived = across(second_send)
        pair = (2, halves[0], 2 * own)
        first_keep, send = call(
            add_core_first,
            [shape(pair), shape(pair, BF16)],
            [],
            0,
            counts,
            *first,
        )
        first_arrived = parity(send)
        arrived = after(arrived, shared[1])
        keep, send = call(
            add_chip,
            [rows(halves[1]), rows(halves[1], BF16)],
            [],
            0,
            counts,
            keep,
            arrived,
        )
        arrived = parity(send)
        first_keep, send = kernel(
            add_parity_first,
            [rows(halves[0]), rows(halves[0], BF16)],
            first_keep,
            first_arrived,
            smem=0,
        )
        first_arrived = across(send)
        arrived = after(arrived, first_arrived)
        keep, *send = call(
            add_last,
            [rows(sum(pieces))] + [rows(sum(pieces), BF16)] * (depth - 1),
            [],
            0,
            counts,
            (first_keep, keep),
            (first_arrived, arrived),
        )
        low = away_plane(after(low, keep))
        result, grad_summed = finish_own(*after_all(shared, keep))
        arrived = tuple(along(send[t - 1], t) for t in range(1, depth))
        arrived = after_all(arrived, result)
        low_other = across(after(low, *arrived))
        (mine,) = kernel(add_depth, [rows(sum(pieces), BF16)], keep, arrived, smem=0)
        mine = (mine,) + tuple(along(mine, t) for t in range(1, depth))
        low, low_other = after_all((low, low_other), *mine)
        mine = jnp.concatenate(mine)
        return (mine, parity(mine)), low, low_other, result, grad_summed

    def slots_of(tensor, *which):
        return [lax.dynamic_index_in_dim(tensor, chan ^ s, 0, keepdims=False) for s in which]

    first = weight_in.T
    other, near = across(first), core(first)
    far = slots_of(activations, 2, 3)
    x = slots_of(after(activations, near), 0, 1) + far
    x = tuple(home(piece, s) for s, piece in enumerate(x))

    (weights,) = call(
        pack,
        [shape((19 * own + 16 + inter + 2 * width, 2 * own), BF16)],
        [pltpu.VMEM((16, 2 * own), F32)],
        0,
        weight_mid.transpose(0, 1, 3, 4, 2).reshape(-1, 2 * own),
        weight_squeeze,
        gain_in.reshape(1, -1),
        shift_in.reshape(1, -1),
        gain_mid,
        shift_mid,
        shift_excite,
        gain_out.reshape(1, -1),
        shift_out.reshape(1, -1),
        weight_excite.transpose(1, 2, 0).reshape(-1, inter),
        weight_out,
        smem=0,
    )
    other = after(other, weights)
    first = (first, near, other, core(other))
    near = core(weights)
    cot = slots_of(after(cotangent, x[0], x[1]), *SLOTS)
    even, odd = jnp.stack([cot[0], cot[2]]), jnp.stack([cot[1], cot[3]])
    other = across(after(weights, x[2], x[3], first[3]))
    even = home(after(even, x[2], x[3]), 0)
    gate_affine = jnp.stack([gain_gate, shift_gate]).astype(F32)

    product = 2 * rows * lanes * parts * width
    pre_in, msg, w_in, wall = call(
        reduce_in,
        [
            shape((wide_rows, width)),
            shape((2 + parts, lanes)),
            shape((parts, width, lanes), BF16),
            shape((groups * images, inter)),
        ],
        [pltpu.VMEM((rows, width), F32)],
        product,
        counts,
        *x,
        *first,
    )
    in_sums = exchange(2 + parts, 0)(after(msg, near, odd))
    other = after(other, *in_sums)
    odd = home(after(odd, *in_sums), 1)
    weights = (weights, near, other, core(other))
    w_mid, w_mid_back, squeeze, in_affine, mid_affine, bias, out_affine = call(
        place_mid,
        [
            shape((2, width, 9 * inter), BF16),
            shape((2, 9 * width, inter), BF16),
            shape((width, inter), BF16),
            shape((2, width)),
            shape((2, 2 * width)),
            shape((1, 2 * width)),
            shape((2, parts, 1, lanes)),
        ],
        [pltpu.VMEM((parts, 16, 2 * own), F32)],
        0,
        counts,
        *weights,
    )
    conv = 2 * wide_rows * 9 * width * width
    taps, mid, msg = call(
        conv_mid,
        [
            shape((3, gap_rows, width), BF16),
            shape((wide_rows, 2 * width)),
            shape((2, 2 * width)),
        ],
        [],
        conv,
        counts,
        pre_in,
        in_sums,
        in_affine,
        w_mid,
    )
    mid_sums = exchange(2, 0)(msg)
    excite, w_out = call(
        place_rest,
        [
            shape((2 * width, inter), BF16),
            shape((parts, width, lanes), BF16),
        ],
        [],
        0,
        counts,
        *weights,
    )
    pooled, msg = call(
        pool,
        [shape((images, width)), shape((GATHERED, inter))],
        [],
        0,
        counts,
        mid,
        mid_sums,
        mid_affine,
        squeeze,
    )
    cot = cross(*after_all((even, odd), msg))
    gathered = exchange(None, GATHERED)(msg)
    gate, attention, weighted, out, msg = call(
        attend,
        [
            shape((2, images, inter)),
            shape((images, 2 * width)),
            shape((rows, width), BF16),
            shape((parts, rows, lanes)),
            shape((2 * parts, lanes)),
        ],
        [pltpu.VMEM((wide_rows, width), F32), pltpu.VMEM((rows, width), F32)],
        product,
        counts,
        gathered,
        wall,
        gate_affine,
        excite,
        bias,
        mid,
        mid_sums,
        mid_affine,
        w_out,
    )
    out_sums = exchange(2 * parts, 0)(msg)
    shared, grad, msg = call(
        finish,
        [
            shape((rows + 32, width), BF16),
            shape((parts, rows, lanes)),
            shape((2 * parts, lanes)),
        ],
        [pltpu.VMEM((2 * parts, 1, lanes), F32)],
        0,
        counts,
        out,
        out_sums,
        out_affine,
        weighted,
        x,
        *cot,
    )
    out_back = exchange(2 * parts, 0)(msg)

    shared = away_plane(shared)

    sums_rows = 2 * 2 * width // inter
    low_out, grad_weighted, grad_logits, msg = call(
        back_out,
        [
            shape((parts, rows, lanes), BF16),
            shape((wide_rows, width)),
            shape((images, 2 * width)),
            shape((sums_rows + images, inter)),
        ],
        [pltpu.VMEM((rows, width), F32)],
        product,
        counts,
        grad,
        out,
        out_sums,
        out_back,
        out_affine,
        w_out,
        mid,
        mid_sums,
        mid_affine,
        attention,
        gate,
        excite,
    )
    mid_back = exchange(sums_rows, images)(msg)
    term_rows = 2 * width + 2 * own + 16
    keep, send = call(
        weight_out_term,
        [shape((2, term_rows, 2 * own), BF16)] * 2,
        [pltpu.VMEM((2 * width, inter), F32), pltpu.VMEM((parts, 16, 2 * own), F32)],
        product,
        counts,
        after(weighted, mid_back[0]),
        low_out,
        gate,
        grad_logits,
        mid_affine,
    )
    mid_back = after_all(mid_back, keep, shared)
    shared = after(shared, mid_back[0])
    shared = (shared, across(shared))
    out_keep, out_arrived = keep, core(after(send, mid_back[0]))
    low_mid, grad_hidden, grad_squeeze, vectors, msg = call(
        back_mid,
        [
            shape((gap_rows, 2 * width), BF16),
            shape((wide_rows, width)),
            shape((images, inter)),
            shape((8, 2 * width)),
            shape((2, width)),
        ],
        [pltpu.VMEM((3, gap_rows, 2 * width), BF16)],
        conv,
        counts,
        mid_back,
        gathered,
        wall,
        gate_affine,
        squeeze,
        attention,
        grad_weighted,
        mid,
        mid_sums,
        mid_affine,
        pre_in,
        in_sums,
        in_affine,
        w_mid_back,
    )
    in_back = exchange(2, 0)(after(msg, out_arrived))
    keep, send = call(
        weight_mid_term,
        [shape((2, 18 * own, 2 * own), BF16)] * 2,
        [pltpu.VMEM((width, 9 * inter), F32)],
        conv,
        counts,
        after(taps, in_back[0]),
        low_mid,
        in_affine,
    )
    in_back = after_all(in_back, keep, shared[1])
    in_rows = parts * lanes // (2 * own) * own
    low_in, in_keep, in_send = call(
        functools.partial(back_in, 1.0 / groups),
        [shape((rows, width), BF16)] + [shape((2, in_rows + own + 16, 2 * own), BF16)] * 2,
        [
            pltpu.VMEM((rows, width), F32),
            pltpu.VMEM((width, lanes), F32),
            pltpu.VMEM((width, inter), F32),
            pltpu.VMEM((parts, 16, 2 * own), F32),
        ],
        product,
        counts,
        grad_hidden,
        pre_in,
        in_sums,
        in_back,
        in_affine,
        *x,
        vectors,
        out_back,
        pooled,
        gathered,
        grad_squeeze,
    )
    owned = shape((batches, rows, lanes), BF16)

    def finish_own(near, far):
        swapped = core(jnp.stack([near, far]))
        return call(
            finish_owned,
            [owned, owned],
            [pltpu.VMEM((rows, lanes), F32)],
            product,
            counts,
            near,
            swapped,
            far,
            w_out,
            activations,
            cotangent,
        )

    send = after(send, low_in)
    terms, low_in, low_other, result, grad_summed = add_over_all(
        (keep, core(send)),
        ((out_keep, in_keep), (out_arrived, core(in_send))),
        low_in,
        shared,
        finish_own,
    )
    lows = (low_in, core(low_in), low_other, core(low_other))
    (grad_x,) = call(grad_owned, [owned], [], product, lows, w_in, grad_summed, smem=0)
    terms = after_all(terms, grad_x)
    (
        g_in,
        g_gain_in,
        g_shift_in,
        g_mid,
        g_gain_mid,
        g_shift_mid,
        g_squeeze,
        g_gain_gate,
        g_shift_gate,
        g_excite,
        g_bias,
        g_out,
        g_gain_out,
        g_shift_out,
    ) = call(
        functools.partial(unpack, groups != 8),
        [
            shape((own, parts * lanes)),
            shape((1, own)),
            shape((1, own)),
            shape((18 * own, inter)),
            shape((2, own)),
            shape((2, own)),
            shape((own, inter)),
            shape((1, inter)),
            shape((1, inter)),
            shape((2 * own, inter)),
            shape((2, own)),
            shape((width, lanes)),
            shape((1, lanes)),
            shape((1, lanes)),
        ],
        [pltpu.VMEM((32, 2 * own), F32)],
        0,
        counts,
        terms,
    )
    return (
        result,
        grad_x,
        g_in.T,
        g_gain_in.reshape(-1),
        g_shift_in.reshape(-1),
        g_mid.reshape(3, 3, 2, own, inter).transpose(0, 1, 4, 2, 3),
        g_gain_mid,
        g_shift_mid,
        g_squeeze,
        g_gain_gate.reshape(-1),
        g_shift_gate.reshape(-1),
        g_excite.reshape(2, own, inter).transpose(2, 0, 1),
        g_bias,
        g_out,
        g_gain_out.reshape(-1),
        g_shift_out.reshape(-1),
    )


def solution(mesh):
    placed = (
        P(None, "dp", "chan"),
        P(),
        P(None, "chan"),
        P("chan"),
        P("chan"),
        P(None, None, None, None, "chan"),
        P(None, "chan"),
        P(None, "chan"),
        P("chan", None),
        P(),
        P(),
        P(None, None, "chan"),
        P(None, "chan"),
        P(None, "chan"),
        P("chan"),
        P("chan"),
        P(None, "dp", "chan"),
    )
    return jax.shard_map(
        functools.partial(per_device, groups=mesh.shape["dp"], parts=mesh.shape["chan"]),
        mesh=mesh,
        in_specs=placed,
        out_specs=placed[:1] + placed[:1] + placed[2:16],
        check_vma=False,
    )
```

```python
import functools

import jax
import jax.numpy as jnp
from jax import lax
from jax.experimental import pallas as pl
from jax.experimental.pallas import tpu as pltpu
from jax.sharding import PartitionSpec as P

SIDE = 14
PIXELS = SIDE * SIDE
WIDE = 16
PADDED = SIDE * WIDE
STRIDE = PADDED + WIDE
CHUNK = 16
UNROLL = 49
VMEM_LIMIT = 24 * 2**20
SLOTS = (0, 1, 2, 3)
GATHERED = 40
ORDER = (0, 2, 1, 3)
EPSILON = 1e-05
HIGHEST = lax.Precision.HIGHEST
F32 = jnp.float32
BF16 = jnp.bfloat16


def dot_nn(left, right, precision=None):
    return lax.dot_general(
        left, right, (((1,), (0,)), ((), ())), preferred_element_type=F32, precision=precision
    )


def parts_of(value):
    high = value.astype(BF16)
    rest = value - high.astype(F32)
    middle = rest.astype(BF16)
    return jnp.concatenate([high, middle, (rest - middle.astype(F32)).astype(BF16)], axis=0)


def exact_dot(dot, left, right):
    rows = -(-left.shape[0] // 16) * 16
    if rows > left.shape[0]:
        left = jnp.concatenate([left, jnp.zeros((rows - left.shape[0], left.shape[1]), F32)], axis=0)
    value = dot(parts_of(left), right)
    return value[:rows] + value[rows : 2 * rows] + value[2 * rows :]


def dot_nt(left, right, precision=None):
    return lax.dot_general(
        left, right, (((1,), (1,)), ((), ())), preferred_element_type=F32, precision=precision
    )


def dot_tn(left, right, precision=None):
    return lax.dot_general(
        left, right, (((0,), (0,)), ((), ())), preferred_element_type=F32, precision=precision
    )


def sum_rows(matrix):
    value = dot_nn(jnp.ones((16, matrix.shape[0]), BF16), matrix)[0:1]
    high = value.astype(BF16).astype(F32)
    middle = (value - high).astype(BF16).astype(F32)
    empty = jnp.zeros((13, value.shape[1]), F32)
    rows = jnp.concatenate([high, middle, value - high - middle, empty], axis=0)
    return rows.astype(BF16)


def same_rows(row):
    return jnp.broadcast_to(row, (16, row.shape[1])).astype(BF16)


def centred_dot(centred, center, other):
    left = jnp.concatenate([centred, same_rows(-center)], axis=0)
    return dot_tn(left, jnp.concatenate([other, sum_rows(other)], axis=0))


def dot_centred(other, centred, center):
    right = jnp.concatenate([centred, same_rows(-center)], axis=0)
    return dot_tn(jnp.concatenate([other, sum_rows(other)], axis=0), right)


def expected(gain, shift):
    reach = 3.0**0.5 * gain
    return (4.0 * silu(shift) + silu(shift + reach) + silu(shift - reach)) / 6.0


def logistic(value):
    return 0.5 + 0.5 * jnp.tanh(0.5 * value)


def silu(value):
    return value * logistic(value)


def slope(value):
    share = logistic(value)
    return share + value * (share * (1.0 - share))


def moments(first, second, total):
    center = first / total
    return center, lax.rsqrt(second / total - center * center + EPSILON)


def fold(value):
    return jnp.sum(value.reshape(-1, 8, value.shape[-1]), axis=0)


def total_of(value):
    return jnp.sum(value, axis=0, keepdims=True)


def columns_real(rows):
    spot = lax.broadcasted_iota(jnp.int32, (rows, 1), 0)
    return (lax.rem(spot, WIDE) < SIDE).astype(F32)


def summed_over(refs):
    values = [ref[...] for ref in refs]
    while len(values) > 1:
        values = [left + right for left, right in zip(values[::2], values[1::2])]
    return values[0]


def slot_rows(refs, size, first, count, skip=0):
    return jnp.concatenate(
        [
            ref[at + first : at + first + count, :]
            for ref in refs
            for at in range(skip, ref.shape[0], size)
        ],
        axis=0,
    )


class Place:
    def __init__(self, counts_ref):
        group = lax.axis_index("dp")
        self.chan = lax.axis_index("chan")
        self.parity, self.depth, self.core = group & 1, group >> 1, self.chan & 1
        self.batch = (self.chan & 2) | self.parity
        self.counts = counts_ref
        self.groups = counts_ref.shape[1]

    def images(self, depth, core):
        return self.counts[self.batch, 2 * depth + core]

    def real(self, image):
        return jnp.where(self.images(self.depth, self.core) > image, 1.0, 0.0).astype(F32)

    def total(self):
        every = [self.counts[self.batch, g] for g in range(self.groups)]
        return functools.reduce(jnp.add, every).astype(F32)


def spread_map_rows(flat_ref, wide_ref):
    for line in range(flat_ref.shape[0] // SIDE):
        wide_ref[line * WIDE : line * WIDE + SIDE, :] = flat_ref[line * SIDE : (line + 1) * SIDE, :]
        wide_ref[line * WIDE + SIDE : (line + 1) * WIDE, :] = jnp.zeros(
            (WIDE - SIDE, wide_ref.shape[1]), wide_ref.dtype
        )


def pack_map_rows(wide_ref, flat_ref):
    for line in range(flat_ref.shape[0] // SIDE):
        flat_ref[line * SIDE : (line + 1) * SIDE, :] = wide_ref[line * WIDE : line * WIDE + SIDE, :]


def clear_gaps(taps_ref, images):
    for gap in range(images + 1):
        taps_ref[:, gap * STRIDE : gap * STRIDE + WIDE, :] = jnp.zeros(
            (3, WIDE, taps_ref.shape[2]), taps_ref.dtype
        )


def store_taps(taps_ref, at, value):
    here = pl.ds(pl.multiple_of(at, WIDE), WIDE)
    taps_ref[0, here, :] = pltpu.roll(value, 1, 0).astype(taps_ref.dtype)
    taps_ref[1, here, :] = value.astype(taps_ref.dtype)
    taps_ref[2, here, :] = pltpu.roll(value, WIDE - 1, 0).astype(taps_ref.dtype)


def call(body, outs, scratch, flops, *args, smem=1):
    specs = tuple(
        pl.BlockSpec(memory_space=pltpu.SMEM)
        if place < smem
        else jax.tree.map(lambda _: pl.BlockSpec(memory_space=pltpu.VMEM), arg)
        for place, arg in enumerate(args)
    )
    moved = sum(a.size * a.dtype.itemsize for a in jax.tree.leaves((args, outs)))
    return pl.pallas_call(
        body,
        out_shape=outs,
        in_specs=specs,
        out_specs=[pl.BlockSpec(memory_space=pltpu.VMEM)] * len(outs),
        scratch_shapes=scratch,
        compiler_params=pltpu.CompilerParams(vmem_limit_bytes=VMEM_LIMIT),
        cost_estimate=pl.CostEstimate(flops=flops, bytes_accessed=moved, transcendentals=0),
        name=getattr(body, "func", body).__name__,
    )(*args)


def shape(dims, kind=F32):
    return jax.ShapeDtypeStruct(dims, kind)


def slot_refs(even_ref, odd_ref, across_ref):
    return even_ref.at[0], odd_ref.at[0], across_ref.at[0], across_ref.at[1]


def pack(
    mid_ref,
    squeeze_ref,
    gain_in_ref,
    shift_in_ref,
    gain_mid_ref,
    shift_mid_ref,
    bias_ref,
    gain_out_ref,
    shift_out_ref,
    excite_ref,
    out_ref,
    target_ref,
    small_ref,
):
    lanes = target_ref.shape[1]
    own = lanes // 2
    small_ref[...] = jnp.zeros_like(small_ref)
    small_ref[0:1, :own] = gain_in_ref[...].astype(F32)
    small_ref[0:1, own:] = shift_in_ref[...].astype(F32)
    for row, ref in enumerate((gain_mid_ref, shift_mid_ref, bias_ref)):
        value = ref[...].astype(F32)
        small_ref[row + 1 : row + 2, :own] = value[0:1]
        small_ref[row + 1 : row + 2, own:] = value[1:2]
    for t, ref in enumerate((gain_out_ref, shift_out_ref)):
        value = ref[...].astype(F32)
        small_ref[4 + 2 * t : 5 + 2 * t, :] = value[:, :lanes]
        small_ref[5 + 2 * t : 6 + 2 * t, :] = value[:, lanes:]
    row = 0
    for ref in (mid_ref, squeeze_ref, small_ref, excite_ref):
        target_ref[row : row + ref.shape[0], :] = ref[...].astype(BF16)
        row += ref.shape[0]
    for block in range(out_ref.shape[1] // lanes):
        rows = out_ref.shape[0]
        target_ref[row : row + rows, :] = out_ref[:, block * lanes : (block + 1) * lanes]
        row += rows


def reduce_in(
    counts_ref, x0, x1, x2, x3, a0, a1, a2, a3, pre_ref, msg_ref, w_ref, wall_ref, flat_ref
):
    place = Place(counts_ref)
    images = wall_ref.shape[0] // place.groups
    spot = lax.broadcasted_iota(jnp.int32, wall_ref.shape, 0)
    real = jnp.zeros(wall_ref.shape, jnp.int32)
    for slot in range(place.groups):
        number = place.images(place.depth ^ (slot >> 1), place.core ^ (slot & 1))
        here = (spot >= slot * images) & (spot < slot * images + number)
        real = jnp.where(here, 1, real)
    wall_ref[...] = real.astype(F32)
    own = w_ref.shape[1] // len(SLOTS)
    lanes = w_ref.shape[2]
    for s, piece in enumerate((a0, a1, a2, a3)):
        here = pl.ds(pl.multiple_of((place.chan ^ s) * own, own), own)
        for block in range(w_ref.shape[0]):
            w_ref[block, here, :] = piece[:, block * lanes : (block + 1) * lanes]
    parts = [dot_nt(x[...], w_ref[place.batch ^ s]) for s, x in enumerate((x0, x1, x2, x3))]
    flat_ref[...] = functools.reduce(jnp.add, parts)
    spread_map_rows(flat_ref, pre_ref)
    first = jnp.zeros((1, pre_ref.shape[1]), F32)
    second = jnp.zeros((1, pre_ref.shape[1]), F32)
    for image in range(pre_ref.shape[0] // PADDED):
        real = place.real(image)
        value = pre_ref[image * PADDED : (image + 1) * PADDED, :]
        first = first + real * total_of(value)
        second = second + real * total_of(value * value)
    rows = x0.shape[0]
    spot = lax.broadcasted_iota(jnp.int32, (16, rows), 1)
    real = (spot < place.images(place.depth, place.core) * PIXELS).astype(BF16)
    columns = [dot_nn(real, x[...])[0:1] for x in (x0, x1, x2, x3)]
    msg_ref[...] = jnp.concatenate([first, second] + columns, axis=0)


def place_mid(
    counts_ref,
    b0,
    b1,
    b2,
    b3,
    w_ref,
    w_back_ref,
    squeeze_ref,
    in_affine_ref,
    mid_affine_ref,
    bias_ref,
    out_affine_ref,
    small_ref,
):
    place = Place(counts_ref)
    width, lanes = w_ref.shape[1], b0.shape[1]
    own = width // len(SLOTS)
    for s, piece in enumerate((b0, b1, b2, b3)):
        at = pl.multiple_of((place.chan ^ s) * own, own)
        for tap in range(9):
            for r in range(2):
                block = piece[(2 * tap + r) * own : (2 * tap + r + 1) * own, :]
                w_ref[r, pl.ds(at, own), tap * lanes : (tap + 1) * lanes] = block
                w_back_ref[r, pl.ds(tap * width + at, own), :] = block
        squeeze_ref[pl.ds(at, own), :] = piece[18 * own : 19 * own, :]
        small = piece[19 * own : 19 * own + 16, :].astype(F32)
        small_ref[place.chan ^ s] = small
        for t in range(2):
            out_affine_ref[t, place.chan ^ s, :, :lanes] = small[4 + 2 * t : 5 + 2 * t, :]
            out_affine_ref[t, place.chan ^ s, :, lanes:] = small[5 + 2 * t : 6 + 2 * t, :]
    for k in range(len(SLOTS)):
        here = slice(k * own, (k + 1) * own)
        there = slice(width + k * own, width + (k + 1) * own)
        in_affine_ref[0:1, here] = small_ref[k, 0:1, :own]
        in_affine_ref[1:2, here] = small_ref[k, 0:1, own:]
        for t in range(2):
            mid_affine_ref[t : t + 1, here] = small_ref[k, 1 + t : 2 + t, :own]
            mid_affine_ref[t : t + 1, there] = small_ref[k, 1 + t : 2 + t, own:]
        bias_ref[0:1, here] = small_ref[k, 3:4, :own]
        bias_ref[0:1, there] = small_ref[k, 3:4, own:]


def place_rest(counts_ref, b0, b1, b2, b3, excite_ref, w_out_ref):
    place = Place(counts_ref)
    width, lanes = w_out_ref.shape[1], b0.shape[1]
    own = width // len(SLOTS)
    for s, piece in enumerate((b0, b1, b2, b3)):
        row = 19 * own + 16
        for r in range(2):
            at = pl.multiple_of(r * width + (place.chan ^ s) * own, own)
            excite_ref[pl.ds(at, own), :] = piece[row : row + own, :]
            row += own
        w_out_ref[place.chan ^ s, :, :lanes] = piece[row : row + width, :]
        w_out_ref[place.chan ^ s, :, lanes:] = piece[row + width : row + 2 * width, :]


def conv_mid(
    counts_ref,
    pre_ref,
    sums_refs,
    affine_ref,
    w_ref,
    taps_ref,
    mid_ref,
    msg_ref,
):
    place = Place(counts_ref)
    images = pre_ref.shape[0] // PADDED
    total = place.total() * PIXELS
    sums = summed_over(sums_refs)
    center, scale = moments(sums[0:1], sums[1:2], total)
    gain = affine_ref[0:1, :] * scale
    shift = affine_ref[1:2, :] - center * gain
    clear_gaps(taps_ref, images)
    keep = columns_real(WIDE)
    for image in range(images):

        def normalize(step, carry, image=image):
            rows = pl.multiple_of(step * WIDE, WIDE)
            value = pre_ref[pl.ds(image * PADDED + rows, WIDE), :]
            value = silu(value * gain + shift) * keep
            store_taps(taps_ref, image * STRIDE + WIDE + rows, value)
            return carry

        lax.fori_loop(0, SIDE, normalize, 0, unroll=SIDE)
    half = pre_ref.shape[1] // 2
    width = pre_ref.shape[1]
    keep = columns_real(PADDED)
    firsts = [jnp.zeros((1, width), F32) for _ in range(2)]
    seconds = [jnp.zeros((1, width), F32) for _ in range(2)]
    for image in range(images):
        real = place.real(image)
        for r in range(2):
            left = jnp.concatenate(
                [
                    taps_ref[
                        b,
                        image * STRIDE + a * WIDE : image * STRIDE + a * WIDE + PADDED,
                        r * half : (r + 1) * half,
                    ]
                    for a in range(3)
                    for b in range(3)
                ],
                axis=1,
            )
            value = dot_nt(left, w_ref[r])
            mid_ref[image * PADDED : (image + 1) * PADDED, r * width : (r + 1) * width] = value
            held = value * keep
            firsts[r] = firsts[r] + real * total_of(held)
            seconds[r] = seconds[r] + real * total_of(held * held)
    sums = jnp.concatenate(
        [jnp.concatenate(firsts, axis=1), jnp.concatenate(seconds, axis=1)], axis=0
    )
    msg_ref[...] = sums


def mid_norm(
    place,
    sums_refs,
    affine_ref,
):
    sums = summed_over(sums_refs)
    center, scale = moments(sums[0:1], sums[1:2], place.total() * PIXELS)
    gain = affine_ref[0:1, :] * scale
    return center, scale, gain, affine_ref[1:2, :] - center * gain


def pool(
    counts_ref,
    mid_ref,
    sums_refs,
    affine_ref,
    squeeze_ref,
    pooled_ref,
    msg_ref,
):
    place = Place(counts_ref)
    images = mid_ref.shape[0] // PADDED
    width = mid_ref.shape[1] // 2
    lanes = msg_ref.shape[1]
    center, scale, gain, shift = mid_norm(place, sums_refs, affine_ref)
    keep = columns_real(CHUNK)
    inclines = [[], []]
    for image in range(images):

        def gather(step, carry, image=image):
            active, rise, lean = carry
            at = pl.multiple_of(image * PADDED + step * CHUNK, CHUNK)
            before = mid_ref[pl.ds(at, CHUNK), :]
            value = before * gain + shift
            share = logistic(value) * keep
            active = active + fold(value * share)
            inclined = share + value * (share * (1.0 - share))
            return active, rise + fold(inclined), lean + fold(inclined * before)

        nothing = jnp.zeros((8, 2 * width), F32)
        active, rise, lean = lax.fori_loop(
            0, SIDE, gather, (nothing, nothing, nothing), unroll=SIDE
        )
        active = total_of(active)
        pooled_ref[image : image + 1, :] = (active[:, :width] + active[:, width:]) / PIXELS
        rise = total_of(rise)
        inclines[0].append(rise)
        inclines[1].append(scale * (total_of(lean) - center * rise))
    inclined = jnp.concatenate(inclines[0] + inclines[1], axis=0)
    msg_ref[...] = jnp.zeros_like(msg_ref)
    for q in range(2 * width // lanes):
        row = 8 + q * 2 * images
        msg_ref[row : row + 2 * images, :] = inclined[:, q * lanes : (q + 1) * lanes]
    msg_ref[0:images, :] = exact_dot(dot_nn, pooled_ref[...], squeeze_ref[...])[:images]
    real = [place.real(image) * pooled_ref[image : image + 1, :] for image in range(images)]
    real = functools.reduce(jnp.add, real)
    for q in range(width // lanes):
        msg_ref[images + q : images + q + 1, :] = real[:, q * lanes : (q + 1) * lanes]


def gate_norm(
    place,
    rows,
    wall,
):
    return moments(total_of(wall * rows), total_of(wall * rows * rows), place.total())


def attend(
    counts_ref,
    gathered_refs,
    wall_ref,
    gate_affine_ref,
    excite_ref,
    bias_ref,
    mid_ref,
    mid_sums_refs,
    mid_affine_ref,
    w_out_ref,
    gate_ref,
    attention_ref,
    weighted_ref,
    out_ref,
    msg_ref,
    wide_ref,
    flat_ref,
):
    place = Place(counts_ref)
    images = mid_ref.shape[0] // PADDED
    width = mid_ref.shape[1] // 2
    rows = slot_rows(gathered_refs, GATHERED, 0, images)
    center, scale = gate_norm(place, rows, wall_ref[...])
    normed = (rows[0:images] - center) * scale
    gate_pre = normed * gate_affine_ref[0:1, :] + gate_affine_ref[1:2, :]
    gate = silu(gate_pre)
    gate_ref[0] = gate
    gate_ref[1] = slope(gate_pre)
    logits = (
        exact_dot(dot_nt, gate, excite_ref[...])[:images] + bias_ref[...]
    )
    lean = 0.5 * jnp.tanh(0.5 * (logits[:, :width] - logits[:, width:]))
    attention_ref[:, :width] = 0.5 + lean
    attention_ref[:, width:] = 0.5 - lean
    center, scale, gain, shift = mid_norm(place, mid_sums_refs, mid_affine_ref)
    for image in range(images):
        share = attention_ref[image : image + 1, :]

        def weigh(step, carry, image=image, share=share):
            at = pl.multiple_of(image * PADDED + step * CHUNK, CHUNK)
            value = share * silu(mid_ref[pl.ds(at, CHUNK), :] * gain + shift)
            wide_ref[pl.ds(at, CHUNK), :] = value[:, :width] + value[:, width:]
            return carry

        lax.fori_loop(0, SIDE, weigh, 0, unroll=SIDE)
    pack_map_rows(wide_ref, flat_ref)
    weighted_ref[...] = flat_ref[...].astype(BF16)
    spot = lax.broadcasted_iota(jnp.int32, (flat_ref.shape[0], 1), 0)
    real = (spot < place.images(place.depth, place.core) * PIXELS).astype(F32)
    blocks = w_out_ref.shape[0]
    for k in range(blocks):
        value = dot_nn(weighted_ref[...], w_out_ref[place.batch ^ k])
        out_ref[k] = value
        held = value * real
        for t, row in enumerate((total_of(held), total_of(held * value))):
            msg_ref[t * blocks + k : t * blocks + k + 1, :] = row


def finish(
    counts_ref,
    out_ref,
    sums_refs,
    affine_ref,
    weighted_ref,
    x_refs,
    cot_near_ref,
    cot_odd_ref,
    cot_across_ref,
    shared_ref,
    grad_ref,
    msg_ref,
    map_ref,
):
    place = Place(counts_ref)
    cot_refs = slot_refs(cot_near_ref, cot_odd_ref, cot_across_ref)
    blocks, rows, lanes = out_ref.shape
    sums = summed_over(sums_refs)
    center, scale = moments(sums[:blocks], sums[blocks:], place.total() * PIXELS)
    limit = place.images(place.depth, place.core) * PIXELS
    for k in range(blocks):
        mu, r = center[k : k + 1], scale[k : k + 1]
        block = place.batch ^ k
        gain = affine_ref[0, block] * r
        shift = affine_ref[1, block] - mu * gain
        map_ref[block] = gain
        map_ref[blocks + block] = shift
        x_ref, upstream_ref = x_refs[k], cot_refs[k]

        def chunk(
            step, carry, k=k, gain=gain, shift=shift, x_ref=x_ref, upstream_ref=upstream_ref
        ):
            first, second = carry
            at = pl.multiple_of(step * CHUNK, CHUNK)
            here = pl.ds(at, CHUNK)
            spot = lax.broadcasted_iota(jnp.int32, (CHUNK, 1), 0) + at
            real = (spot < limit).astype(F32)
            before = out_ref[k, here, :]
            summed = x_ref[here, :].astype(F32) + (before * gain + shift)
            share = logistic(summed)
            grad = upstream_ref[here, :].astype(F32) * real
            grad = grad * (share * (1.0 + summed * (1.0 - share)))
            grad_ref[k, here, :] = grad
            return first + fold(grad), second + fold(grad * before)

        nothing = jnp.zeros((8, lanes), F32)
        first, second = lax.fori_loop(
            0, rows // CHUNK, chunk, (nothing, nothing), unroll=UNROLL
        )
        first = total_of(first)
        for t, row in enumerate((first, r * (total_of(second) - mu * first))):
            msg_ref[t * blocks + k : t * blocks + k + 1, :] = row
    shared_ref[0:rows, :] = weighted_ref[...]
    exact = jnp.concatenate([map_ref[n] for n in range(2 * blocks)], axis=0)
    high = exact.astype(BF16).astype(F32)
    middle = (exact - high).astype(BF16).astype(F32)
    shared_ref[rows : rows + 16, :] = jnp.concatenate([high, middle], axis=0).astype(BF16)
    rest = jnp.concatenate([exact - high - middle, jnp.zeros_like(exact)], axis=0)
    shared_ref[rows + 16 : rows + 32, :] = rest.astype(BF16)


def finish_owned(
    counts_ref, near_ref, swapped_ref, far_ref, w_ref, x_ref, cot_ref, result_ref, grad_ref, out_ref
):
    chan, group = lax.axis_index("chan"), lax.axis_index("dp")
    rows = cot_ref.shape[1]
    blocks = len(SLOTS)
    for s, piece in enumerate((near_ref, swapped_ref.at[0], far_ref, swapped_ref.at[1])):
        batch = chan ^ s
        limit = counts_ref[batch, group] * PIXELS
        out_ref[...] = dot_nn(piece[0:rows, :], w_ref[chan])
        exact = piece[rows : rows + 32, :].astype(F32)
        exact = exact[0:8] + exact[8:16] + exact[16:24]
        gain, shift = exact[0:1], exact[blocks : blocks + 1]
        for k in range(1, blocks):
            gain = jnp.where(chan == k, exact[k : k + 1], gain)
            shift = jnp.where(chan == k, exact[blocks + k : blocks + k + 1], shift)

        def chunk(step, carry, batch=batch, limit=limit, gain=gain, shift=shift):
            at = pl.multiple_of(step * CHUNK, CHUNK)
            here = pl.ds(at, CHUNK)
            spot = lax.broadcasted_iota(jnp.int32, (CHUNK, 1), 0) + at
            real = (spot < limit).astype(F32)
            summed = x_ref[batch, here, :].astype(F32) + (out_ref[here, :] * gain + shift)
            share = logistic(summed)
            held = share * real
            result_ref[batch, here, :] = (summed * held).astype(BF16)
            grad = cot_ref[batch, here, :].astype(F32) * (held * (1.0 + summed * (1.0 - share)))
            grad_ref[batch, here, :] = grad.astype(BF16)
            return carry

        lax.fori_loop(0, rows // CHUNK, chunk, 0, unroll=UNROLL)


def back_out(
    counts_ref,
    grad_ref,
    out_ref,
    sums_refs,
    back_refs,
    affine_ref,
    w_out_ref,
    mid_ref,
    mid_sums_refs,
    mid_affine_ref,
    attention_ref,
    gate_ref,
    excite_ref,
    low_ref,
    gw_ref,
    logits_ref,
    msg_ref,
    flat_ref,
):
    place = Place(counts_ref)
    blocks, rows, lanes = out_ref.shape
    images = attention_ref.shape[0]
    width = attention_ref.shape[1] // 2
    total = place.total() * PIXELS
    sums = summed_over(sums_refs)
    center, scale = moments(sums[:blocks], sums[blocks:], total)
    back = summed_over(back_refs) / total
    limit = place.images(place.depth, place.core) * PIXELS
    for k in range(blocks):
        mu, r = center[k : k + 1], scale[k : k + 1]
        gain = affine_ref[0, place.batch ^ k] * r
        second = gain * r * back[blocks + k : blocks + k + 1]
        first = gain * back[k : k + 1] - mu * second

        def chunk(step, carry, k=k, gain=gain, first=first, second=second):
            at = pl.multiple_of(step * CHUNK, CHUNK)
            here = pl.ds(at, CHUNK)
            spot = lax.broadcasted_iota(jnp.int32, (CHUNK, 1), 0) + at
            real = (spot < limit).astype(F32)
            value = gain * grad_ref[k, here, :] - real * (first + out_ref[k, here, :] * second)
            low_ref[k, here, :] = value.astype(BF16)
            return carry

        lax.fori_loop(0, rows // CHUNK, chunk, 0, unroll=UNROLL)
    parts = [dot_nt(low_ref[k], w_out_ref[place.batch ^ k]) for k in range(blocks)]
    flat_ref[...] = functools.reduce(jnp.add, parts)
    spread_map_rows(flat_ref, gw_ref)
    center, scale, gain, shift = mid_norm(place, mid_sums_refs, mid_affine_ref)
    rises, leans, attended = [], [], []
    for image in range(images):

        def gather(step, carry, image=image):
            attended, rise, lean = carry
            at = pl.multiple_of(image * PADDED + step * CHUNK, CHUNK)
            before = mid_ref[pl.ds(at, CHUNK), :]
            value = before * gain + shift
            share = logistic(value)
            grad = gw_ref[pl.ds(at, CHUNK), :]
            grad = jnp.concatenate([grad, grad], axis=1)
            active = grad * share
            attended = attended + fold(active * value)
            inclined = active * (1.0 + value * (1.0 - share))
            return attended, rise + fold(inclined), lean + fold(inclined * before)

        nothing = jnp.zeros((8, 2 * width), F32)
        parts = lax.fori_loop(
            0, SIDE, gather, (nothing, nothing, nothing), unroll=SIDE
        )
        share = attention_ref[image : image + 1, :]
        attended.append(total_of(parts[0]))
        rise = total_of(parts[1])
        rises.append(share * rise)
        leans.append(share * (scale * (total_of(parts[2]) - center * rise)))
    grad = jnp.concatenate(attended, axis=0)
    attention = attention_ref[...]
    inner = attention * grad
    inner = inner[:, :width] + inner[:, width:]
    logits = attention * (grad - jnp.concatenate([inner, inner], axis=1))
    logits_ref[...] = logits
    gate = exact_dot(dot_nn, logits, excite_ref[...])[:images] * gate_ref[1]
    pack = msg_ref.shape[1]
    pieces = 2 * width // pack
    for t, row in enumerate((functools.reduce(jnp.add, rises), functools.reduce(jnp.add, leans))):
        for q in range(pieces):
            msg_ref[t * pieces + q : t * pieces + q + 1, :] = row[:, q * pack : (q + 1) * pack]
    msg_ref[2 * pieces : 2 * pieces + images, :] = gate


def back_mid(
    counts_ref,
    back_refs,
    gathered_refs,
    wall_ref,
    gate_affine_ref,
    squeeze_ref,
    attention_ref,
    gw_ref,
    mid_ref,
    mid_sums_refs,
    mid_affine_ref,
    pre_ref,
    sums_refs,
    affine_ref,
    w_ref,
    low_ref,
    grad_ref,
    gate_ref,
    vector_ref,
    msg_ref,
    taps_ref,
):
    place = Place(counts_ref)
    images = attention_ref.shape[0]
    width = attention_ref.shape[1] // 2
    lanes = wall_ref.shape[1]
    pieces = 2 * width // lanes
    total = place.total() * PIXELS
    wall = wall_ref[...]
    rows = slot_rows(gathered_refs, GATHERED, 0, images)
    center, scale = gate_norm(place, rows, wall)
    gain = gate_affine_ref[0:1, :] * scale
    normed = (rows - center) * scale
    grads = slot_rows(back_refs, images, 0, images, 2 * pieces)
    first, second = total_of(wall * grads), total_of(wall * grads * normed)
    vector_ref[0:1, 0:lanes] = second
    vector_ref[0:1, lanes : 2 * lanes] = first
    squeezed = gain * (grads - wall * (first + normed * second) / place.total())
    gate_ref[...] = squeezed[0:images]
    pooled_grad = exact_dot(dot_nt, squeezed, squeeze_ref[...]) / PIXELS
    pooled_grad = jnp.concatenate([pooled_grad, pooled_grad], axis=1)
    slot = 0
    terms = jnp.zeros((2 * images, 2 * width), F32)
    for ref in gathered_refs:
        for at in range(8, ref.shape[0], GATHERED):
            inclines = [
                ref[at + q * 2 * images : at + (q + 1) * 2 * images, :] for q in range(pieces)
            ]
            grad = pooled_grad[slot * images : (slot + 1) * images, :]
            grad = jnp.concatenate([grad, grad], axis=0)
            terms = terms + jnp.concatenate(inclines, axis=1) * grad
            slot += 1
    sums = functools.reduce(jnp.add, [ref[0 : 2 * pieces, :] for ref in back_refs])
    back = []
    for t in range(2):
        row = [sums[t * pieces + q : t * pieces + q + 1, :] for q in range(pieces)]
        back.append(
            jnp.concatenate(row, axis=1) + total_of(terms[t * images : (t + 1) * images])
        )
    vector_ref[1:2, :] = back[1]
    vector_ref[2:3, :] = back[0]
    own = pooled_grad[0:images]
    center, scale, gain, shift = mid_norm(place, mid_sums_refs, mid_affine_ref)
    second = gain * scale * back[1] / total
    first = gain * back[0] / total - center * second
    clear_gaps(taps_ref, images)
    keep = columns_real(WIDE)
    for image in range(images):
        share = gain * attention_ref[image : image + 1, :]
        offset = gain * own[image : image + 1, :]
        real = place.real(image)
        lead, lag = real * first, real * second

        def chunk(step, carry, image=image, share=share, offset=offset, lead=lead, lag=lag):
            rows = pl.multiple_of(step * WIDE, WIDE)
            here = pl.ds(image * PADDED + rows, WIDE)
            before = mid_ref[here, :]
            grad = gw_ref[here, :]
            grad = jnp.concatenate([grad, grad], axis=1)
            grad = (share * grad + offset) * slope(before * gain + shift)
            value = (grad - (lead + before * lag)) * keep
            store_taps(taps_ref, image * STRIDE + WIDE + rows, value)
            return carry

        lax.fori_loop(0, SIDE, chunk, 0, unroll=SIDE)
    low_ref[...] = taps_ref[1]
    sums = summed_over(sums_refs)
    center, scale = moments(sums[0:1], sums[1:2], total)
    gain = affine_ref[0:1, :] * scale
    shift = affine_ref[1:2, :] - center * gain
    half = width // 2
    keep = columns_real(PADDED)
    firsts = [jnp.zeros((1, half), F32) for _ in range(2)]
    seconds = [jnp.zeros((1, half), F32) for _ in range(2)]
    for image in range(images):
        real = place.real(image)
        here = slice(image * PADDED, (image + 1) * PADDED)
        for r in range(2):
            left = jnp.concatenate(
                [
                    taps_ref[
                        2 - b,
                        image * STRIDE + (2 - a) * WIDE : image * STRIDE + (2 - a) * WIDE + PADDED,
                        r * width : (r + 1) * width,
                    ]
                    for a in range(3)
                    for b in range(3)
                ],
                axis=1,
            )
            lane = slice(r * half, (r + 1) * half)
            before = pre_ref[here, lane]
            value = dot_nn(left, w_ref[r]) * slope(before * gain[:, lane] + shift[:, lane])
            value = value * (keep * real)
            grad_ref[here, lane] = value
            firsts[r] = firsts[r] + total_of(value)
            seconds[r] = seconds[r] + total_of(value * before)
    first = jnp.concatenate(firsts, axis=1)
    second = scale * (jnp.concatenate(seconds, axis=1) - center * first)
    sums = jnp.concatenate([first, second], axis=0)
    msg_ref[...] = sums


def sort_pieces(
    place,
    source_ref,
    keep_ref,
    send_ref,
    row,
):
    for turn, s in enumerate(ORDER):
        target = keep_ref if turn < 2 else send_ref
        rows = source_ref.shape[1]
        target[turn % 2, row : row + rows, :] = source_ref[place.chan ^ s].astype(BF16)


def weight_out_term(
    counts_ref,
    weighted_ref,
    low_ref,
    gate_ref,
    logits_ref,
    affine_ref,
    keep_ref,
    send_ref,
    wide_ref,
    small_ref,
):
    place = Place(counts_ref)
    width = weighted_ref.shape[1]
    lanes = keep_ref.shape[2]
    own = width // len(SLOTS)
    center = expected(affine_ref[0:1, :], affine_ref[1:2, :])
    center = 0.5 * (center[:, :width] + center[:, width:])
    for turn, s in enumerate(ORDER):
        target = keep_ref if turn < 2 else send_ref
        held = place.batch ^ place.chan ^ s
        term = centred_dot(weighted_ref[...], center, low_ref[held]).astype(BF16)
        target[turn % 2, 0:width, :] = term[:, :lanes]
        target[turn % 2, width : 2 * width, :] = term[:, lanes:]
    wide_ref[...] = dot_tn(logits_ref[...], gate_ref[0], HIGHEST)
    for turn, s in enumerate(ORDER):
        target = keep_ref if turn < 2 else send_ref
        for r in range(2):
            at = pl.multiple_of(r * width + (place.chan ^ s) * own, own)
            row = 2 * width + r * own
            target[turn % 2, row : row + own, :] = wide_ref[pl.ds(at, own), :].astype(BF16)
    small_ref[...] = jnp.zeros_like(small_ref)
    bias = total_of(logits_ref[...])
    for k in range(len(SLOTS)):
        small_ref[k, 0:1, :own] = bias[:, k * own : (k + 1) * own]
        small_ref[k, 0:1, own:] = bias[:, width + k * own : width + (k + 1) * own]
    sort_pieces(place, small_ref, keep_ref, send_ref, 2 * width + 2 * own)


def weight_mid_term(
    counts_ref,
    taps_ref,
    low_ref,
    affine_ref,
    keep_ref,
    send_ref,
    wide_ref,
):
    place = Place(counts_ref)
    center = expected(affine_ref[0:1, :], affine_ref[1:2, :])
    half = taps_ref.shape[2] // 2
    width = low_ref.shape[1] // 2
    own = width // len(SLOTS)
    rows = low_ref.shape[0] - 2 * WIDE
    for r in range(2):
        right = jnp.concatenate(
            [
                taps_ref[b, a * WIDE : a * WIDE + rows, r * half : (r + 1) * half]
                for a in range(3)
                for b in range(3)
            ],
            axis=1,
        )
        low = low_ref[WIDE : WIDE + rows, r * width : (r + 1) * width]
        offset = jnp.concatenate([center[:, r * half : (r + 1) * half]] * 9, axis=1)
        wide_ref[...] = dot_centred(low, right, offset)
        for turn, s in enumerate(ORDER):
            target = keep_ref if turn < 2 else send_ref
            here = pl.ds(pl.multiple_of((place.chan ^ s) * own, own), own)
            for tap in range(9):
                row = (2 * tap + r) * own
                target[turn % 2, row : row + own, :] = wide_ref[
                    here, tap * half : (tap + 1) * half
                ].astype(BF16)


def back_in(
    share,
    counts_ref,
    grad_ref,
    pre_ref,
    sums_refs,
    back_refs,
    affine_ref,
    x0,
    x1,
    x2,
    x3,
    vector_ref,
    out_back_refs,
    pooled_ref,
    gathered_refs,
    squeezed_ref,
    low_ref,
    keep_ref,
    send_ref,
    flat_ref,
    wide_ref,
    narrow_ref,
    small_ref,
):
    place = Place(counts_ref)
    images = pre_ref.shape[0] // PADDED
    width = pre_ref.shape[1]
    own = width // len(SLOTS)
    chan, batch = place.chan, place.batch
    total = place.total() * PIXELS
    sums = summed_over(sums_refs)
    center, scale = moments(sums[0:1], sums[1:2], total)
    back = summed_over(back_refs)
    gain = affine_ref[0:1, :] * scale
    second = gain * scale * back[1:2] / total
    first = gain * back[0:1] / total - center * second
    for image in range(images):
        real = place.real(image)
        lead, lag = real * first, real * second
        for line in range(SIDE):
            at = image * PADDED + line * WIDE
            before = pre_ref[at : at + WIDE, :]
            value = gain * grad_ref[at : at + WIDE, :] - (lead + before * lag)
            at = image * PIXELS + line * SIDE
            flat_ref[at : at + SIDE, :] = value[:SIDE]
    low_ref[...] = flat_ref[...].astype(BF16)
    lanes = keep_ref.shape[2]
    low = jnp.concatenate([low_ref[...], sum_rows(low_ref[...])], axis=0)
    for k, x in enumerate((x0, x1, x2, x3)):
        center = same_rows(-sums[2 + k : 3 + k] / total)
        wide_ref[...] = dot_tn(low, jnp.concatenate([x[...], center], axis=0))
        for turn, s in enumerate(ORDER):
            target = keep_ref if turn < 2 else send_ref
            here = pl.ds(pl.multiple_of((chan ^ s) * own, own), own)
            for part in range(wide_ref.shape[1] // lanes):
                at = pl.multiple_of(((batch ^ k) * (wide_ref.shape[1] // lanes) + part) * own, own)
                target[turn % 2, pl.ds(at, own), :] = wide_ref[
                    here, part * lanes : (part + 1) * lanes
                ].astype(BF16)
    mean = [
        total_of(slot_rows(gathered_refs, GATHERED, images + q, 1)) for q in range(width // lanes)
    ]
    mean = jnp.concatenate(mean, axis=1) / place.total()
    narrow_ref[...] = dot_tn(pooled_ref[...] - mean, squeezed_ref[...], HIGHEST)
    row = keep_ref.shape[1] - small_ref.shape[1] - own
    for turn, s in enumerate(ORDER):
        target = keep_ref if turn < 2 else send_ref
        here = pl.ds(pl.multiple_of((chan ^ s) * own, own), own)
        target[turn % 2, row : row + own, :] = narrow_ref[here, :].astype(BF16)
    small_ref[...] = jnp.zeros_like(small_ref)
    outs = summed_over(out_back_refs)
    for k in range(len(SLOTS)):
        here = slice(k * own, (k + 1) * own)
        there = slice(width + k * own, width + (k + 1) * own)
        small_ref[k, 0:1, :own] = back[1:2, here]
        small_ref[k, 0:1, own:] = back[0:1, here]
        for t in range(2):
            small_ref[k, 1 + t : 2 + t, :own] = vector_ref[1 + t : 2 + t, here]
            small_ref[k, 1 + t : 2 + t, own:] = vector_ref[1 + t : 2 + t, there]
        small_ref[k, 3:4, :] = vector_ref[0:1, 0:lanes]
        small_ref[k, 4:5, :] = vector_ref[0:1, lanes : 2 * lanes]
    for s in SLOTS:
        for t in range(2):
            row = outs[(1 - t) * len(SLOTS) + s : (1 - t) * len(SLOTS) + s + 1, :]
            small_ref[batch ^ s, 5 + 2 * t : 6 + 2 * t, :] = row[:, :lanes]
            small_ref[batch ^ s, 6 + 2 * t : 7 + 2 * t, :] = row[:, lanes:]
    small_ref[...] = small_ref[...] * share
    sort_pieces(place, small_ref, keep_ref, send_ref, keep_ref.shape[1] - small_ref.shape[1])


def grad_owned(low_refs, w_ref, summed_ref, result_ref):
    chan = lax.axis_index("chan")
    for s, low_ref in enumerate(low_refs):
        value = dot_nn(low_ref[...], w_ref[chan]) + summed_ref[chan ^ s].astype(F32)
        result_ref[chan ^ s] = value.astype(BF16)


def add_groups(terms_ref, sum_ref):
    value = jnp.sum(terms_ref[...].astype(F32), axis=0).astype(BF16)
    sum_ref[...] = jnp.broadcast_to(value[None], sum_ref.shape)


def added(left_ref, right_ref):
    return left_ref[...].astype(F32) + right_ref[...].astype(F32)


def add_core(keep_refs, arrived_refs, kept_ref, send_ref):
    at = 0
    for keep_ref, arrived_ref in zip(keep_refs, arrived_refs):
        value = added(keep_ref, arrived_ref).astype(BF16)
        rows = keep_ref.shape[1]
        kept_ref[at : at + rows, :] = value[0]
        send_ref[at : at + rows, :] = value[1]
        at += rows
    if at < kept_ref.shape[0]:
        for ref in (kept_ref, send_ref):
            ref[at:, :] = jnp.zeros((kept_ref.shape[0] - at, ref.shape[1]), BF16)


def split_rows(parity, keep_ref, arrived_ref, kept_ref, send_ref):
    rows = kept_ref.shape[-2]
    for own, target in ((parity, kept_ref), (1 - parity, send_ref)):
        here = pl.ds(pl.multiple_of(own * rows, 16), rows)
        if target.ndim == 2:
            value = added(keep_ref.at[here, :], arrived_ref.at[here, :])
        else:
            value = added(keep_ref.at[:, here, :], arrived_ref.at[:, here, :])
        target[...] = value.astype(target.dtype)


def add_core_first(counts_ref, keep_ref, arrived_ref, kept_ref, send_ref):
    split_rows(Place(counts_ref).parity, keep_ref, arrived_ref, kept_ref, send_ref)


def add_parity_first(keep_ref, arrived_ref, kept_ref, send_ref):
    kept_ref[...] = added(keep_ref.at[0], arrived_ref.at[0])
    send_ref[...] = added(keep_ref.at[1], arrived_ref.at[1]).astype(BF16)


def add_chip(counts_ref, keep_ref, arrived_ref, kept_ref, send_ref):
    split_rows(Place(counts_ref).parity, keep_ref, arrived_ref, kept_ref, send_ref)


def add_last(counts_ref, keep_refs, arrived_refs, kept_ref, s1, s2, s3):
    place = Place(counts_ref)
    at = 0
    for keep_ref, arrived_ref in zip(keep_refs, arrived_refs):
        rows = keep_ref.shape[0] // len(SLOTS)
        for t, target in enumerate((kept_ref, s1, s2, s3)):
            here = pl.ds(pl.multiple_of((place.depth ^ t) * rows, 16), rows)
            value = added(keep_ref.at[here, :], arrived_ref.at[here, :])
            target[at : at + rows, :] = value.astype(target.dtype)
        at += rows


def add_depth(keep_ref, arrived_refs, sum_ref):
    value = keep_ref[...]
    for ref in arrived_refs:
        value = value + ref[...].astype(F32)
    sum_ref[...] = value.astype(BF16)


def unpack(
    joined,
    counts_ref,
    term_refs,
    in_ref,
    gain_in_ref,
    shift_in_ref,
    mid_ref,
    gain_mid_ref,
    shift_mid_ref,
    squeeze_ref,
    gain_gate_ref,
    shift_gate_ref,
    excite_ref,
    bias_ref,
    out_ref,
    gain_out_ref,
    shift_out_ref,
    second_ref,
):
    own, lanes = squeeze_ref.shape
    width = out_ref.shape[0]
    places = [(out_ref, 0, 0, width), (out_ref, 0, 1, width), (excite_ref, 0, 0, 2 * own)]
    places += [(second_ref, 0, 0, 16)]
    places += [(in_ref, 0, block, own) for block in range(in_ref.shape[1] // lanes)]
    places += [(squeeze_ref, 0, 0, own), (second_ref, 16, 0, 16)]

    def write(value, row):
        start = 0
        for target, at, block, rows in places:
            first, last = max(row, start), min(row + value.shape[0], start + rows)
            if first < last:
                there = slice(at + first - start, at + last - start)
                target[there, block * lanes : (block + 1) * lanes] = value[first - row : last - row]
            start += rows

    if joined:
        mid_ref[...] = term_refs[0][...].astype(F32)
        write(term_refs[1][...].astype(F32), 0)
    else:
        place = Place(counts_ref)
        even = place.parity == 0
        piece = term_refs[0].shape[0] // len(SLOTS)
        rows = mid_ref.shape[0] // 2 // len(SLOTS)
        for half in range(2):
            mine, other = term_refs[half], term_refs[1 - half]
            for z in range(len(SLOTS)):
                here = pl.ds(pl.multiple_of((place.depth ^ z) * piece, 16), piece)
                value = jnp.where(even, mine[here, :].astype(F32), other[here, :].astype(F32))
                at = (half * len(SLOTS) + z) * rows
                mid_ref[at : at + rows, :] = value[:rows]
                write(value[rows:], (half * len(SLOTS) + z) * (piece - rows))

    def halves(target, row):
        target[0:1, :] = second_ref[row : row + 1, :own]
        target[1:2, :] = second_ref[row : row + 1, own:]

    halves(bias_ref, 0)
    row = 16
    gain_in_ref[...] = second_ref[row : row + 1, :own]
    shift_in_ref[...] = second_ref[row : row + 1, own:]
    halves(gain_mid_ref, row + 1)
    halves(shift_mid_ref, row + 2)
    gain_gate_ref[...] = second_ref[row + 3 : row + 4, :]
    shift_gate_ref[...] = second_ref[row + 4 : row + 5, :]
    for t, target in enumerate((gain_out_ref, shift_out_ref)):
        target[:, :lanes] = second_ref[row + 5 + 2 * t : row + 6 + 2 * t, :]
        target[:, lanes:] = second_ref[row + 6 + 2 * t : row + 7 + 2 * t, :]


def per_device(
    activations,
    counts,
    weight_in,
    gain_in,
    shift_in,
    weight_mid,
    gain_mid,
    shift_mid,
    weight_squeeze,
    gain_gate,
    shift_gate,
    weight_excite,
    shift_excite,
    weight_out,
    gain_out,
    shift_out,
    cotangent,
    *,
    groups,
    parts,
):
    batches, rows, lanes = activations.shape
    images = rows // PIXELS
    own = weight_in.shape[1]
    width = own * parts
    inter = gain_gate.shape[0]
    wide_rows = images * PADDED
    gap_rows = WIDE + images * STRIDE
    chan, group = lax.axis_index("chan"), lax.axis_index("dp")
    depth = groups // 2

    def permute(tensor, to):
        pairs = []
        for index in range(groups * parts):
            z, x, y, c = index // parts // 2, index // parts % 2, index % parts // 2, index % 2
            z, x, y, c = to(z, x, y, c)
            pairs.append((index, (2 * z + x) * parts + 2 * y + c))
        return lax.ppermute(tensor, ("dp", "chan"), pairs)

    def home(tensor, s):
        return permute(tensor, lambda z, x, y, c: (z, c ^ (s & 1), y ^ (s >> 1), x))

    def away_plane(tensor):
        return permute(tensor, lambda z, x, y, c: (z, c, y, x))

    def cross(even, odd):
        return even, odd, across(jnp.stack([even[1], odd[1]]))

    def core(tensor):
        return permute(tensor, lambda z, x, y, c: (z, x, y, c ^ 1))

    def across(tensor):
        return permute(tensor, lambda z, x, y, c: (z, x, y ^ 1, c))

    def parity(tensor):
        return permute(tensor, lambda z, x, y, c: (z, x ^ 1, y, c))

    def along(tensor, t):
        return permute(tensor, lambda z, x, y, c: (z ^ t, x, y, c))

    def after(tensor, *others):
        return lax.optimization_barrier((tensor,) + others)[0]

    def after_all(tensors, *others):
        return lax.optimization_barrier(tuple(tensors) + others)[: len(tensors)]

    def exchange(total, gather):
        def merge(mine, other):
            cut = 0 if total is None else total
            joined = [mine[:cut] + other[:cut]] if cut else []
            if gather:
                joined += [mine[cut : cut + gather], other[cut : cut + gather]]
            return jnp.concatenate(joined) if len(joined) > 1 else joined[0]

        def run(mine):
            nonlocal gather
            mine = merge(mine, core(mine))
            gather = 2 * gather
            if depth <= 4:
                return (mine,) + tuple(along(mine, t) for t in range(1, depth))
            step = 1
            while step < depth:
                mine = merge(mine, along(mine, step))
                gather, step = 2 * gather, 2 * step
            return (mine,)

        return run

    def padded(rows):
        return -(-rows // (16 * groups)) * 16 * groups

    def kernel(body, outs, *args, smem=1):
        return call(body, outs, [], 0, *args, smem=smem)

    def add_over_all(first, second, low, shared, finish_own):
        first_rows, second_rows = first[0].shape[1], sum(k.shape[1] for k in second[0])
        if groups != 8:
            rows = padded(first_rows + second_rows)
            keep, send = kernel(
                add_core,
                [shape((rows, 2 * own), BF16)] * 2,
                (first[0],) + second[0],
                (first[1],) + second[1],
                smem=0,
            )
            terms = (keep.astype(F32) + across(send).astype(F32)).astype(BF16)
            terms = lax.all_to_all(terms.reshape(groups, rows // groups, -1), "dp", 0, 0)
            (terms,) = kernel(add_groups, [shape(terms.shape, BF16)], terms, smem=0)
            terms = lax.all_to_all(terms, "dp", 0, 0).reshape(rows, -1)
            terms = terms[:first_rows], terms[first_rows : first_rows + second_rows]
            low = away_plane(low)
            near, far = shared
            owned = finish_own(near, core(jnp.stack([near, far])), far)
            return (terms, low, across(low)) + tuple(owned)
        second_rows = padded(second_rows)
        halves = (first_rows // 2, second_rows // 2)
        pieces = (first_rows // groups, second_rows // groups)

        def rows(number, kind=F32):
            return shape((number, 2 * own), kind)

        keep, second_send = kernel(add_core, [rows(second_rows, BF16)] * 2, *second, smem=0)
        arrived = across(second_send)
        pair = (2, halves[0], 2 * own)
        first_keep, send = call(
            add_core_first,
            [shape(pair), shape(pair, BF16)],
            [],
            0,
            counts,
            *first,
        )
        first_arrived = parity(send)
        near, far = after_all(shared, send, second_send)
        swapped = core(jnp.stack([near, far]))
        arrived = after(arrived, swapped)
        low = away_plane(after(low, send))
        keep, send = call(
            add_chip,
            [rows(halves[1]), rows(halves[1], BF16)],
            [],
            0,
            counts,
            keep,
            arrived,
        )
        arrived = parity(send)
        first_keep, send = kernel(
            add_parity_first,
            [rows(halves[0]), rows(halves[0], BF16)],
            first_keep,
            first_arrived,
            smem=0,
        )
        first_arrived = across(send)
        arrived = after(arrived, first_arrived, low)
        keep, *send = call(
            add_last,
            [rows(sum(pieces))] + [rows(sum(pieces), BF16)] * (depth - 1),
            [],
            0,
            counts,
            (first_keep, keep),
            (first_arrived, arrived),
        )
        result, grad_summed = finish_own(*after_all((near, swapped, far), keep))
        arrived = tuple(along(send[t - 1], t) for t in range(1, depth))
        arrived = after_all(arrived, result)
        low_other = across(after(low, *arrived))
        (mine,) = kernel(add_depth, [rows(sum(pieces), BF16)], keep, arrived, smem=0)
        mine = (mine,) + tuple(along(mine, t) for t in range(1, depth))
        low, low_other = after_all((low, low_other), *mine)
        mine = jnp.concatenate(mine)
        return (mine, parity(mine)), low, low_other, result, grad_summed

    def slots_of(tensor, *which):
        return [lax.dynamic_index_in_dim(tensor, chan ^ s, 0, keepdims=False) for s in which]

    first = weight_in.T
    other, near = across(first), core(first)
    far = slots_of(activations, 2, 3)
    x = slots_of(after(activations, near), 0, 1) + far
    x = tuple(home(piece, s) for s, piece in enumerate(x))

    (weights,) = call(
        pack,
        [shape((19 * own + 16 + inter + 2 * width, 2 * own), BF16)],
        [pltpu.VMEM((16, 2 * own), F32)],
        0,
        weight_mid.transpose(0, 1, 3, 4, 2).reshape(-1, 2 * own),
        weight_squeeze,
        gain_in.reshape(1, -1),
        shift_in.reshape(1, -1),
        gain_mid,
        shift_mid,
        shift_excite,
        gain_out.reshape(1, -1),
        shift_out.reshape(1, -1),
        weight_excite.transpose(1, 2, 0).reshape(-1, inter),
        weight_out,
        smem=0,
    )
    other = after(other, weights)
    first = (first, near, other, core(other))
    near = core(weights)
    cot = slots_of(after(cotangent, x[0], x[1]), *SLOTS)
    even, odd = jnp.stack([cot[0], cot[2]]), jnp.stack([cot[1], cot[3]])
    other = across(after(weights, x[2], x[3], first[3]))
    even = home(after(even, x[2], x[3]), 0)
    gate_affine = jnp.stack([gain_gate, shift_gate]).astype(F32)

    product = 2 * rows * lanes * parts * width
    pre_in, msg, w_in, wall = call(
        reduce_in,
        [
            shape((wide_rows, width)),
            shape((2 + parts, lanes)),
            shape((parts, width, lanes), BF16),
            shape((groups * images, inter)),
        ],
        [pltpu.VMEM((rows, width), F32)],
        product,
        counts,
        *x,
        *first,
    )
    in_sums = exchange(2 + parts, 0)(after(msg, near, odd))
    other = after(other, *in_sums)
    odd = home(after(odd, *in_sums), 1)
    weights = (weights, near, other, core(other))
    w_mid, w_mid_back, squeeze, in_affine, mid_affine, bias, out_affine = call(
        place_mid,
        [
            shape((2, width, 9 * inter), BF16),
            shape((2, 9 * width, inter), BF16),
            shape((width, inter), BF16),
            shape((2, width)),
            shape((2, 2 * width)),
            shape((1, 2 * width)),
            shape((2, parts, 1, lanes)),
        ],
        [pltpu.VMEM((parts, 16, 2 * own), F32)],
        0,
        counts,
        *weights,
    )
    conv = 2 * wide_rows * 9 * width * width
    taps, mid, msg = call(
        conv_mid,
        [
            shape((3, gap_rows, width), BF16),
            shape((wide_rows, 2 * width)),
            shape((2, 2 * width)),
        ],
        [],
        conv,
        counts,
        pre_in,
        in_sums,
        in_affine,
        w_mid,
    )
    mid_sums = exchange(2, 0)(msg)
    excite, w_out = call(
        place_rest,
        [
            shape((2 * width, inter), BF16),
            shape((parts, width, lanes), BF16),
        ],
        [],
        0,
        counts,
        *weights,
    )
    pooled, msg = call(
        pool,
        [shape((images, width)), shape((GATHERED, inter))],
        [],
        0,
        counts,
        mid,
        mid_sums,
        mid_affine,
        squeeze,
    )
    cot = cross(*after_all((even, odd), msg))
    gathered = exchange(None, GATHERED)(msg)
    gate, attention, weighted, out, msg = call(
        attend,
        [
            shape((2, images, inter)),
            shape((images, 2 * width)),
            shape((rows, width), BF16),
            shape((parts, rows, lanes)),
            shape((2 * parts, lanes)),
        ],
        [pltpu.VMEM((wide_rows, width), F32), pltpu.VMEM((rows, width), F32)],
        product,
        counts,
        gathered,
        wall,
        gate_affine,
        excite,
        bias,
        mid,
        mid_sums,
        mid_affine,
        w_out,
    )
    out_sums = exchange(2 * parts, 0)(msg)
    shared, grad, msg = call(
        finish,
        [
            shape((rows + 32, width), BF16),
            shape((parts, rows, lanes)),
            shape((2 * parts, lanes)),
        ],
        [pltpu.VMEM((2 * parts, 1, lanes), F32)],
        0,
        counts,
        out,
        out_sums,
        out_affine,
        weighted,
        x,
        *cot,
    )
    out_back = exchange(2 * parts, 0)(msg)

    shared = away_plane(shared)

    sums_rows = 2 * 2 * width // inter
    low_out, grad_weighted, grad_logits, msg = call(
        back_out,
        [
            shape((parts, rows, lanes), BF16),
            shape((wide_rows, width)),
            shape((images, 2 * width)),
            shape((sums_rows + images, inter)),
        ],
        [pltpu.VMEM((rows, width), F32)],
        product,
        counts,
        grad,
        out,
        out_sums,
        out_back,
        out_affine,
        w_out,
        mid,
        mid_sums,
        mid_affine,
        attention,
        gate,
        excite,
    )
    mid_back = exchange(sums_rows, images)(msg)
    term_rows = 2 * width + 2 * own + 16
    keep, send = call(
        weight_out_term,
        [shape((2, term_rows, 2 * own), BF16)] * 2,
        [pltpu.VMEM((2 * width, inter), F32), pltpu.VMEM((parts, 16, 2 * own), F32)],
        product,
        counts,
        after(weighted, mid_back[0]),
        low_out,
        gate,
        grad_logits,
        mid_affine,
    )
    mid_back = after_all(mid_back, keep, shared)
    shared = after(shared, mid_back[0])
    shared = (shared, across(shared))
    out_keep, out_arrived = keep, core(after(send, mid_back[0]))
    low_mid, grad_hidden, grad_squeeze, vectors, msg = call(
        back_mid,
        [
            shape((gap_rows, 2 * width), BF16),
            shape((wide_rows, width)),
            shape((images, inter)),
            shape((8, 2 * width)),
            shape((2, width)),
        ],
        [pltpu.VMEM((3, gap_rows, 2 * width), BF16)],
        conv,
        counts,
        mid_back,
        gathered,
        wall,
        gate_affine,
        squeeze,
        attention,
        grad_weighted,
        mid,
        mid_sums,
        mid_affine,
        pre_in,
        in_sums,
        in_affine,
        w_mid_back,
    )
    in_back = exchange(2, 0)(after(msg, out_arrived))
    keep, send = call(
        weight_mid_term,
        [shape((2, 18 * own, 2 * own), BF16)] * 2,
        [pltpu.VMEM((width, 9 * inter), F32)],
        conv,
        counts,
        after(taps, in_back[0]),
        low_mid,
        in_affine,
    )
    in_back = after_all(in_back, keep, shared[1])
    in_rows = parts * lanes // (2 * own) * own
    low_in, in_keep, in_send = call(
        functools.partial(back_in, 1.0 / groups),
        [shape((rows, width), BF16)] + [shape((2, in_rows + own + 16, 2 * own), BF16)] * 2,
        [
            pltpu.VMEM((rows, width), F32),
            pltpu.VMEM((width, lanes), F32),
            pltpu.VMEM((width, inter), F32),
            pltpu.VMEM((parts, 16, 2 * own), F32),
        ],
        product,
        counts,
        grad_hidden,
        pre_in,
        in_sums,
        in_back,
        in_affine,
        *x,
        vectors,
        out_back,
        pooled,
        gathered,
        grad_squeeze,
    )
    owned = shape((batches, rows, lanes), BF16)

    def finish_own(near, swapped, far):
        return call(
            finish_owned,
            [owned, owned],
            [pltpu.VMEM((rows, lanes), F32)],
            product,
            counts,
            near,
            swapped,
            far,
            w_out,
            activations,
            cotangent,
        )

    send = after(send, low_in)
    terms, low_in, low_other, result, grad_summed = add_over_all(
        (keep, core(send)),
        ((out_keep, in_keep), (out_arrived, core(in_send))),
        low_in,
        shared,
        finish_own,
    )
    lows = (low_in, core(low_in), low_other, core(low_other))
    (grad_x,) = call(grad_owned, [owned], [], product, lows, w_in, grad_summed, smem=0)
    terms = after_all(terms, grad_x)
    (
        g_in,
        g_gain_in,
        g_shift_in,
        g_mid,
        g_gain_mid,
        g_shift_mid,
        g_squeeze,
        g_gain_gate,
        g_shift_gate,
        g_excite,
        g_bias,
        g_out,
        g_gain_out,
        g_shift_out,
    ) = call(
        functools.partial(unpack, groups != 8),
        [
            shape((own, parts * lanes)),
            shape((1, own)),
            shape((1, own)),
            shape((18 * own, inter)),
            shape((2, own)),
            shape((2, own)),
            shape((own, inter)),
            shape((1, inter)),
            shape((1, inter)),
            shape((2 * own, inter)),
            shape((2, own)),
            shape((width, lanes)),
            shape((1, lanes)),
            shape((1, lanes)),
        ],
        [pltpu.VMEM((32, 2 * own), F32)],
        0,
        counts,
        terms,
    )
    return (
        result,
        grad_x,
        g_in.T,
        g_gain_in.reshape(-1),
        g_shift_in.reshape(-1),
        g_mid.reshape(3, 3, 2, own, inter).transpose(0, 1, 4, 2, 3),
        g_gain_mid,
        g_shift_mid,
        g_squeeze,
        g_gain_gate.reshape(-1),
        g_shift_gate.reshape(-1),
        g_excite.reshape(2, own, inter).transpose(2, 0, 1),
        g_bias,
        g_out,
        g_gain_out.reshape(-1),
        g_shift_out.reshape(-1),
    )


def solution(mesh):
    placed = (
        P(None, "dp", "chan"),
        P(),
        P(None, "chan"),
        P("chan"),
        P("chan"),
        P(None, None, None, None, "chan"),
        P(None, "chan"),
        P(None, "chan"),
        P("chan", None),
        P(),
        P(),
        P(None, None, "chan"),
        P(None, "chan"),
        P(None, "chan"),
        P("chan"),
        P("chan"),
        P(None, "dp", "chan"),
    )
    return jax.shard_map(
        functools.partial(per_device, groups=mesh.shape["dp"], parts=mesh.shape["chan"]),
        mesh=mesh,
        in_specs=placed,
        out_specs=placed[:1] + placed[:1] + placed[2:16],
        check_vma=False,
    )
```

```python
import functools

import jax
import jax.numpy as jnp
from jax import lax
from jax.experimental import pallas as pl
from jax.experimental.pallas import tpu as pltpu
from jax.sharding import PartitionSpec as P

SIDE = 14
PIXELS = SIDE * SIDE
WIDE = 16
PADDED = SIDE * WIDE
STRIDE = PADDED + WIDE
CHUNK = 16
UNROLL = 49
VMEM_LIMIT = 24 * 2**20
SLOTS = (0, 1, 2, 3)
GATHERED = 40
ORDER = (0, 2, 1, 3)
EPSILON = 1e-05
HIGHEST = lax.Precision.HIGHEST
F32 = jnp.float32
BF16 = jnp.bfloat16


def dot_nn(left, right, precision=None):
    return lax.dot_general(
        left, right, (((1,), (0,)), ((), ())), preferred_element_type=F32, precision=precision
    )


def parts_of(value):
    high = value.astype(BF16)
    rest = value - high.astype(F32)
    middle = rest.astype(BF16)
    return jnp.concatenate([high, middle, (rest - middle.astype(F32)).astype(BF16)], axis=0)


def exact_dot(dot, left, right):
    rows = -(-left.shape[0] // 16) * 16
    if rows > left.shape[0]:
        left = jnp.concatenate([left, jnp.zeros((rows - left.shape[0], left.shape[1]), F32)], axis=0)
    value = dot(parts_of(left), right)
    return value[:rows] + value[rows : 2 * rows] + value[2 * rows :]


def dot_nt(left, right, precision=None):
    return lax.dot_general(
        left, right, (((1,), (1,)), ((), ())), preferred_element_type=F32, precision=precision
    )


def dot_tn(left, right, precision=None):
    return lax.dot_general(
        left, right, (((0,), (0,)), ((), ())), preferred_element_type=F32, precision=precision
    )


def sum_rows(matrix):
    value = dot_nn(jnp.ones((16, matrix.shape[0]), BF16), matrix)[0:1]
    high = value.astype(BF16).astype(F32)
    middle = (value - high).astype(BF16).astype(F32)
    empty = jnp.zeros((13, value.shape[1]), F32)
    rows = jnp.concatenate([high, middle, value - high - middle, empty], axis=0)
    return rows.astype(BF16)


def same_rows(row):
    return jnp.broadcast_to(row, (16, row.shape[1])).astype(BF16)


def centred_dot(centred, center, other):
    left = jnp.concatenate([centred, same_rows(-center)], axis=0)
    return dot_tn(left, jnp.concatenate([other, sum_rows(other)], axis=0))


def dot_centred(other, centred, center):
    right = jnp.concatenate([centred, same_rows(-center)], axis=0)
    return dot_tn(jnp.concatenate([other, sum_rows(other)], axis=0), right)


def expected(gain, shift):
    reach = 3.0**0.5 * gain
    return (4.0 * silu(shift) + silu(shift + reach) + silu(shift - reach)) / 6.0


def logistic(value):
    return 0.5 + 0.5 * jnp.tanh(0.5 * value)


def silu(value):
    return value * logistic(value)


def slope(value):
    share = logistic(value)
    return share + value * (share * (1.0 - share))


def moments(first, second, total):
    center = first / total
    return center, lax.rsqrt(second / total - center * center + EPSILON)


def fold(value):
    return jnp.sum(value.reshape(-1, 8, value.shape[-1]), axis=0)


def total_of(value):
    return jnp.sum(value, axis=0, keepdims=True)


def columns_real(rows):
    spot = lax.broadcasted_iota(jnp.int32, (rows, 1), 0)
    return (lax.rem(spot, WIDE) < SIDE).astype(F32)


def summed_over(refs):
    values = [ref[...] for ref in refs]
    while len(values) > 1:
        values = [left + right for left, right in zip(values[::2], values[1::2])]
    return values[0]


def slot_rows(refs, size, first, count, skip=0):
    return jnp.concatenate(
        [
            ref[at + first : at + first + count, :]
            for ref in refs
            for at in range(skip, ref.shape[0], size)
        ],
        axis=0,
    )


class Place:
    def __init__(self, counts_ref):
        group = lax.axis_index("dp")
        self.chan = lax.axis_index("chan")
        self.parity, self.depth, self.core = group & 1, group >> 1, self.chan & 1
        self.batch = (self.chan & 2) | self.parity
        self.counts = counts_ref
        self.groups = counts_ref.shape[1]

    def images(self, depth, core):
        return self.counts[self.batch, 2 * depth + core]

    def real(self, image):
        return jnp.where(self.images(self.depth, self.core) > image, 1.0, 0.0).astype(F32)

    def total(self):
        every = [self.counts[self.batch, g] for g in range(self.groups)]
        return functools.reduce(jnp.add, every).astype(F32)


def spread_map_rows(flat_ref, wide_ref):
    for line in range(flat_ref.shape[0] // SIDE):
        wide_ref[line * WIDE : line * WIDE + SIDE, :] = flat_ref[line * SIDE : (line + 1) * SIDE, :]
        wide_ref[line * WIDE + SIDE : (line + 1) * WIDE, :] = jnp.zeros(
            (WIDE - SIDE, wide_ref.shape[1]), wide_ref.dtype
        )


def pack_map_rows(wide_ref, flat_ref):
    for line in range(flat_ref.shape[0] // SIDE):
        flat_ref[line * SIDE : (line + 1) * SIDE, :] = wide_ref[line * WIDE : line * WIDE + SIDE, :]


def clear_gaps(taps_ref, images):
    for gap in range(images + 1):
        taps_ref[:, gap * STRIDE : gap * STRIDE + WIDE, :] = jnp.zeros(
            (3, WIDE, taps_ref.shape[2]), taps_ref.dtype
        )


def store_taps(taps_ref, at, value):
    here = pl.ds(pl.multiple_of(at, WIDE), WIDE)
    taps_ref[0, here, :] = pltpu.roll(value, 1, 0).astype(taps_ref.dtype)
    taps_ref[1, here, :] = value.astype(taps_ref.dtype)
    taps_ref[2, here, :] = pltpu.roll(value, WIDE - 1, 0).astype(taps_ref.dtype)


def call(body, outs, scratch, flops, *args, smem=1):
    specs = tuple(
        pl.BlockSpec(memory_space=pltpu.SMEM)
        if place < smem
        else jax.tree.map(lambda _: pl.BlockSpec(memory_space=pltpu.VMEM), arg)
        for place, arg in enumerate(args)
    )
    moved = sum(a.size * a.dtype.itemsize for a in jax.tree.leaves((args, outs)))
    return pl.pallas_call(
        body,
        out_shape=outs,
        in_specs=specs,
        out_specs=[pl.BlockSpec(memory_space=pltpu.VMEM)] * len(outs),
        scratch_shapes=scratch,
        compiler_params=pltpu.CompilerParams(vmem_limit_bytes=VMEM_LIMIT),
        cost_estimate=pl.CostEstimate(flops=flops, bytes_accessed=moved, transcendentals=0),
        name=getattr(body, "func", body).__name__,
    )(*args)


def shape(dims, kind=F32):
    return jax.ShapeDtypeStruct(dims, kind)


def slot_refs(even_ref, odd_ref, across_ref):
    return even_ref.at[0], odd_ref.at[0], across_ref.at[0], across_ref.at[1]


def pack(
    mid_ref,
    squeeze_ref,
    gain_in_ref,
    shift_in_ref,
    gain_mid_ref,
    shift_mid_ref,
    bias_ref,
    gain_out_ref,
    shift_out_ref,
    excite_ref,
    out_ref,
    target_ref,
    small_ref,
):
    lanes = target_ref.shape[1]
    own = lanes // 2
    small_ref[...] = jnp.zeros_like(small_ref)
    small_ref[0:1, :own] = gain_in_ref[...].astype(F32)
    small_ref[0:1, own:] = shift_in_ref[...].astype(F32)
    for row, ref in enumerate((gain_mid_ref, shift_mid_ref, bias_ref)):
        value = ref[...].astype(F32)
        small_ref[row + 1 : row + 2, :own] = value[0:1]
        small_ref[row + 1 : row + 2, own:] = value[1:2]
    for t, ref in enumerate((gain_out_ref, shift_out_ref)):
        value = ref[...].astype(F32)
        small_ref[4 + 2 * t : 5 + 2 * t, :] = value[:, :lanes]
        small_ref[5 + 2 * t : 6 + 2 * t, :] = value[:, lanes:]
    row = 0
    for ref in (mid_ref, squeeze_ref, small_ref, excite_ref):
        target_ref[row : row + ref.shape[0], :] = ref[...].astype(BF16)
        row += ref.shape[0]
    for block in range(out_ref.shape[1] // lanes):
        rows = out_ref.shape[0]
        target_ref[row : row + rows, :] = out_ref[:, block * lanes : (block + 1) * lanes]
        row += rows


def reduce_in(
    counts_ref, x0, x1, x2, x3, a0, a1, a2, a3, pre_ref, msg_ref, w_ref, wall_ref, flat_ref
):
    place = Place(counts_ref)
    images = wall_ref.shape[0] // place.groups
    spot = lax.broadcasted_iota(jnp.int32, wall_ref.shape, 0)
    real = jnp.zeros(wall_ref.shape, jnp.int32)
    for slot in range(place.groups):
        number = place.images(place.depth ^ (slot >> 1), place.core ^ (slot & 1))
        here = (spot >= slot * images) & (spot < slot * images + number)
        real = jnp.where(here, 1, real)
    wall_ref[...] = real.astype(F32)
    own = w_ref.shape[1] // len(SLOTS)
    lanes = w_ref.shape[2]
    for s, piece in enumerate((a0, a1, a2, a3)):
        here = pl.ds(pl.multiple_of((place.chan ^ s) * own, own), own)
        for block in range(w_ref.shape[0]):
            w_ref[block, here, :] = piece[:, block * lanes : (block + 1) * lanes]
    parts = [dot_nt(x[...], w_ref[place.batch ^ s]) for s, x in enumerate((x0, x1, x2, x3))]
    flat_ref[...] = functools.reduce(jnp.add, parts)
    spread_map_rows(flat_ref, pre_ref)
    first = jnp.zeros((1, pre_ref.shape[1]), F32)
    second = jnp.zeros((1, pre_ref.shape[1]), F32)
    for image in range(pre_ref.shape[0] // PADDED):
        real = place.real(image)
        value = pre_ref[image * PADDED : (image + 1) * PADDED, :]
        first = first + real * total_of(value)
        second = second + real * total_of(value * value)
    rows = x0.shape[0]
    spot = lax.broadcasted_iota(jnp.int32, (16, rows), 1)
    real = (spot < place.images(place.depth, place.core) * PIXELS).astype(BF16)
    columns = [dot_nn(real, x[...])[0:1] for x in (x0, x1, x2, x3)]
    msg_ref[...] = jnp.concatenate([first, second] + columns, axis=0)


def place_mid(
    counts_ref,
    b0,
    b1,
    b2,
    b3,
    w_ref,
    w_back_ref,
    squeeze_ref,
    in_affine_ref,
    mid_affine_ref,
    bias_ref,
    out_affine_ref,
    small_ref,
):
    place = Place(counts_ref)
    width, lanes = w_ref.shape[1], b0.shape[1]
    own = width // len(SLOTS)
    for s, piece in enumerate((b0, b1, b2, b3)):
        at = pl.multiple_of((place.chan ^ s) * own, own)
        for tap in range(9):
            for r in range(2):
                block = piece[(2 * tap + r) * own : (2 * tap + r + 1) * own, :]
                w_ref[r, pl.ds(at, own), tap * lanes : (tap + 1) * lanes] = block
                w_back_ref[r, pl.ds(tap * width + at, own), :] = block
        squeeze_ref[pl.ds(at, own), :] = piece[18 * own : 19 * own, :]
        small = piece[19 * own : 19 * own + 16, :].astype(F32)
        small_ref[place.chan ^ s] = small
        for t in range(2):
            out_affine_ref[t, place.chan ^ s, :, :lanes] = small[4 + 2 * t : 5 + 2 * t, :]
            out_affine_ref[t, place.chan ^ s, :, lanes:] = small[5 + 2 * t : 6 + 2 * t, :]
    for k in range(len(SLOTS)):
        here = slice(k * own, (k + 1) * own)
        there = slice(width + k * own, width + (k + 1) * own)
        in_affine_ref[0:1, here] = small_ref[k, 0:1, :own]
        in_affine_ref[1:2, here] = small_ref[k, 0:1, own:]
        for t in range(2):
            mid_affine_ref[t : t + 1, here] = small_ref[k, 1 + t : 2 + t, :own]
            mid_affine_ref[t : t + 1, there] = small_ref[k, 1 + t : 2 + t, own:]
        bias_ref[0:1, here] = small_ref[k, 3:4, :own]
        bias_ref[0:1, there] = small_ref[k, 3:4, own:]


def place_rest(counts_ref, b0, b1, b2, b3, excite_ref, w_out_ref):
    place = Place(counts_ref)
    width, lanes = w_out_ref.shape[1], b0.shape[1]
    own = width // len(SLOTS)
    for s, piece in enumerate((b0, b1, b2, b3)):
        row = 19 * own + 16
        for r in range(2):
            at = pl.multiple_of(r * width + (place.chan ^ s) * own, own)
            excite_ref[pl.ds(at, own), :] = piece[row : row + own, :]
            row += own
        w_out_ref[place.chan ^ s, :, :lanes] = piece[row : row + width, :]
        w_out_ref[place.chan ^ s, :, lanes:] = piece[row + width : row + 2 * width, :]


def conv_mid(
    counts_ref,
    pre_ref,
    sums_refs,
    affine_ref,
    w_ref,
    taps_ref,
    mid_ref,
    msg_ref,
):
    place = Place(counts_ref)
    images = pre_ref.shape[0] // PADDED
    total = place.total() * PIXELS
    sums = summed_over(sums_refs)
    center, scale = moments(sums[0:1], sums[1:2], total)
    gain = affine_ref[0:1, :] * scale
    shift = affine_ref[1:2, :] - center * gain
    clear_gaps(taps_ref, images)
    keep = columns_real(WIDE)
    for image in range(images):

        def normalize(step, carry, image=image):
            rows = pl.multiple_of(step * WIDE, WIDE)
            value = pre_ref[pl.ds(image * PADDED + rows, WIDE), :]
            value = silu(value * gain + shift) * keep
            store_taps(taps_ref, image * STRIDE + WIDE + rows, value)
            return carry

        lax.fori_loop(0, SIDE, normalize, 0, unroll=SIDE)
    half = pre_ref.shape[1] // 2
    width = pre_ref.shape[1]
    keep = columns_real(PADDED)
    firsts = [jnp.zeros((1, width), F32) for _ in range(2)]
    seconds = [jnp.zeros((1, width), F32) for _ in range(2)]
    for image in range(images):
        real = place.real(image)
        for r in range(2):
            left = jnp.concatenate(
                [
                    taps_ref[
                        b,
                        image * STRIDE + a * WIDE : image * STRIDE + a * WIDE + PADDED,
                        r * half : (r + 1) * half,
                    ]
                    for a in range(3)
                    for b in range(3)
                ],
                axis=1,
            )
            value = dot_nt(left, w_ref[r])
            mid_ref[image * PADDED : (image + 1) * PADDED, r * width : (r + 1) * width] = value
            held = value * keep
            firsts[r] = firsts[r] + real * total_of(held)
            seconds[r] = seconds[r] + real * total_of(held * held)
    sums = jnp.concatenate(
        [jnp.concatenate(firsts, axis=1), jnp.concatenate(seconds, axis=1)], axis=0
    )
    msg_ref[...] = sums


def mid_norm(
    place,
    sums_refs,
    affine_ref,
):
    sums = summed_over(sums_refs)
    center, scale = moments(sums[0:1], sums[1:2], place.total() * PIXELS)
    gain = affine_ref[0:1, :] * scale
    return center, scale, gain, affine_ref[1:2, :] - center * gain


def pool(
    counts_ref,
    mid_ref,
    sums_refs,
    affine_ref,
    squeeze_ref,
    pooled_ref,
    msg_ref,
):
    place = Place(counts_ref)
    images = mid_ref.shape[0] // PADDED
    width = mid_ref.shape[1] // 2
    lanes = msg_ref.shape[1]
    center, scale, gain, shift = mid_norm(place, sums_refs, affine_ref)
    keep = columns_real(CHUNK)
    inclines = [[], []]
    for image in range(images):

        def gather(step, carry, image=image):
            active, rise, lean = carry
            at = pl.multiple_of(image * PADDED + step * CHUNK, CHUNK)
            before = mid_ref[pl.ds(at, CHUNK), :]
            value = before * gain + shift
            share = logistic(value) * keep
            active = active + fold(value * share)
            inclined = share + value * (share * (1.0 - share))
            return active, rise + fold(inclined), lean + fold(inclined * before)

        nothing = jnp.zeros((8, 2 * width), F32)
        active, rise, lean = lax.fori_loop(
            0, SIDE, gather, (nothing, nothing, nothing), unroll=SIDE
        )
        active = total_of(active)
        pooled_ref[image : image + 1, :] = (active[:, :width] + active[:, width:]) / PIXELS
        rise = total_of(rise)
        inclines[0].append(rise)
        inclines[1].append(scale * (total_of(lean) - center * rise))
    inclined = jnp.concatenate(inclines[0] + inclines[1], axis=0)
    msg_ref[...] = jnp.zeros_like(msg_ref)
    for q in range(2 * width // lanes):
        row = 8 + q * 2 * images
        msg_ref[row : row + 2 * images, :] = inclined[:, q * lanes : (q + 1) * lanes]
    msg_ref[0:images, :] = exact_dot(dot_nn, pooled_ref[...], squeeze_ref[...])[:images]
    real = [place.real(image) * pooled_ref[image : image + 1, :] for image in range(images)]
    real = functools.reduce(jnp.add, real)
    for q in range(width // lanes):
        msg_ref[images + q : images + q + 1, :] = real[:, q * lanes : (q + 1) * lanes]


def gate_norm(
    place,
    rows,
    wall,
):
    return moments(total_of(wall * rows), total_of(wall * rows * rows), place.total())


def attend(
    counts_ref,
    gathered_refs,
    wall_ref,
    gate_affine_ref,
    excite_ref,
    bias_ref,
    mid_ref,
    mid_sums_refs,
    mid_affine_ref,
    w_out_ref,
    gate_ref,
    attention_ref,
    weighted_ref,
    out_ref,
    msg_ref,
    wide_ref,
    flat_ref,
):
    place = Place(counts_ref)
    images = mid_ref.shape[0] // PADDED
    width = mid_ref.shape[1] // 2
    rows = slot_rows(gathered_refs, GATHERED, 0, images)
    center, scale = gate_norm(place, rows, wall_ref[...])
    normed = (rows[0:images] - center) * scale
    gate_pre = normed * gate_affine_ref[0:1, :] + gate_affine_ref[1:2, :]
    gate = silu(gate_pre)
    gate_ref[0] = gate
    gate_ref[1] = slope(gate_pre)
    logits = (
        exact_dot(dot_nt, gate, excite_ref[...])[:images] + bias_ref[...]
    )
    lean = 0.5 * jnp.tanh(0.5 * (logits[:, :width] - logits[:, width:]))
    attention_ref[:, :width] = 0.5 + lean
    attention_ref[:, width:] = 0.5 - lean
    center, scale, gain, shift = mid_norm(place, mid_sums_refs, mid_affine_ref)
    for image in range(images):
        share = attention_ref[image : image + 1, :]

        def weigh(step, carry, image=image, share=share):
            at = pl.multiple_of(image * PADDED + step * CHUNK, CHUNK)
            value = share * silu(mid_ref[pl.ds(at, CHUNK), :] * gain + shift)
            wide_ref[pl.ds(at, CHUNK), :] = value[:, :width] + value[:, width:]
            return carry

        lax.fori_loop(0, SIDE, weigh, 0, unroll=SIDE)
    pack_map_rows(wide_ref, flat_ref)
    weighted_ref[...] = flat_ref[...].astype(BF16)
    spot = lax.broadcasted_iota(jnp.int32, (flat_ref.shape[0], 1), 0)
    real = (spot < place.images(place.depth, place.core) * PIXELS).astype(F32)
    blocks = w_out_ref.shape[0]
    for k in range(blocks):
        value = dot_nn(weighted_ref[...], w_out_ref[place.batch ^ k])
        out_ref[k] = value
        held = value * real
        for t, row in enumerate((total_of(held), total_of(held * value))):
            msg_ref[t * blocks + k : t * blocks + k + 1, :] = row


def finish(
    counts_ref,
    out_ref,
    sums_refs,
    affine_ref,
    weighted_ref,
    x_refs,
    cot_near_ref,
    cot_odd_ref,
    cot_across_ref,
    shared_ref,
    grad_ref,
    msg_ref,
    map_ref,
):
    place = Place(counts_ref)
    cot_refs = slot_refs(cot_near_ref, cot_odd_ref, cot_across_ref)
    blocks, rows, lanes = out_ref.shape
    sums = summed_over(sums_refs)
    center, scale = moments(sums[:blocks], sums[blocks:], place.total() * PIXELS)
    limit = place.images(place.depth, place.core) * PIXELS
    for k in range(blocks):
        mu, r = center[k : k + 1], scale[k : k + 1]
        block = place.batch ^ k
        gain = affine_ref[0, block] * r
        shift = affine_ref[1, block] - mu * gain
        map_ref[block] = gain
        map_ref[blocks + block] = shift
        x_ref, upstream_ref = x_refs[k], cot_refs[k]

        def chunk(
            step, carry, k=k, gain=gain, shift=shift, x_ref=x_ref, upstream_ref=upstream_ref
        ):
            first, second = carry
            at = pl.multiple_of(step * CHUNK, CHUNK)
            here = pl.ds(at, CHUNK)
            spot = lax.broadcasted_iota(jnp.int32, (CHUNK, 1), 0) + at
            real = (spot < limit).astype(F32)
            before = out_ref[k, here, :]
            summed = x_ref[here, :].astype(F32) + (before * gain + shift)
            share = logistic(summed)
            grad = upstream_ref[here, :].astype(F32) * real
            grad = grad * (share * (1.0 + summed * (1.0 - share)))
            grad_ref[k, here, :] = grad
            return first + fold(grad), second + fold(grad * before)

        nothing = jnp.zeros((8, lanes), F32)
        first, second = lax.fori_loop(
            0, rows // CHUNK, chunk, (nothing, nothing), unroll=UNROLL
        )
        first = total_of(first)
        for t, row in enumerate((first, r * (total_of(second) - mu * first))):
            msg_ref[t * blocks + k : t * blocks + k + 1, :] = row
    shared_ref[0:rows, :] = weighted_ref[...]
    exact = jnp.concatenate([map_ref[n] for n in range(2 * blocks)], axis=0)
    high = exact.astype(BF16).astype(F32)
    middle = (exact - high).astype(BF16).astype(F32)
    shared_ref[rows : rows + 16, :] = jnp.concatenate([high, middle], axis=0).astype(BF16)
    rest = jnp.concatenate([exact - high - middle, jnp.zeros_like(exact)], axis=0)
    shared_ref[rows + 16 : rows + 32, :] = rest.astype(BF16)


def finish_owned(
    counts_ref, near_ref, swapped_ref, far_ref, w_ref, x_ref, cot_ref, result_ref, grad_ref, out_ref
):
    chan, group = lax.axis_index("chan"), lax.axis_index("dp")
    rows = cot_ref.shape[1]
    blocks = len(SLOTS)
    for s, piece in enumerate((near_ref, swapped_ref.at[0], far_ref, swapped_ref.at[1])):
        batch = chan ^ s
        limit = counts_ref[batch, group] * PIXELS
        out_ref[...] = dot_nn(piece[0:rows, :], w_ref[chan])
        exact = piece[rows : rows + 32, :].astype(F32)
        exact = exact[0:8] + exact[8:16] + exact[16:24]
        gain, shift = exact[0:1], exact[blocks : blocks + 1]
        for k in range(1, blocks):
            gain = jnp.where(chan == k, exact[k : k + 1], gain)
            shift = jnp.where(chan == k, exact[blocks + k : blocks + k + 1], shift)

        def chunk(step, carry, batch=batch, limit=limit, gain=gain, shift=shift):
            at = pl.multiple_of(step * CHUNK, CHUNK)
            here = pl.ds(at, CHUNK)
            spot = lax.broadcasted_iota(jnp.int32, (CHUNK, 1), 0) + at
            real = (spot < limit).astype(F32)
            summed = x_ref[batch, here, :].astype(F32) + (out_ref[here, :] * gain + shift)
            share = logistic(summed)
            held = share * real
            result_ref[batch, here, :] = (summed * held).astype(BF16)
            grad = cot_ref[batch, here, :].astype(F32) * (held * (1.0 + summed * (1.0 - share)))
            grad_ref[batch, here, :] = grad.astype(BF16)
            return carry

        lax.fori_loop(0, rows // CHUNK, chunk, 0, unroll=UNROLL)


def back_out(
    counts_ref,
    grad_ref,
    out_ref,
    sums_refs,
    back_refs,
    affine_ref,
    w_out_ref,
    mid_ref,
    mid_sums_refs,
    mid_affine_ref,
    attention_ref,
    gate_ref,
    excite_ref,
    low_ref,
    gw_ref,
    logits_ref,
    msg_ref,
    flat_ref,
):
    place = Place(counts_ref)
    blocks, rows, lanes = out_ref.shape
    images = attention_ref.shape[0]
    width = attention_ref.shape[1] // 2
    total = place.total() * PIXELS
    sums = summed_over(sums_refs)
    center, scale = moments(sums[:blocks], sums[blocks:], total)
    back = summed_over(back_refs) / total
    limit = place.images(place.depth, place.core) * PIXELS
    for k in range(blocks):
        mu, r = center[k : k + 1], scale[k : k + 1]
        gain = affine_ref[0, place.batch ^ k] * r
        second = gain * r * back[blocks + k : blocks + k + 1]
        first = gain * back[k : k + 1] - mu * second

        def chunk(step, carry, k=k, gain=gain, first=first, second=second):
            at = pl.multiple_of(step * CHUNK, CHUNK)
            here = pl.ds(at, CHUNK)
            spot = lax.broadcasted_iota(jnp.int32, (CHUNK, 1), 0) + at
            real = (spot < limit).astype(F32)
            value = gain * grad_ref[k, here, :] - real * (first + out_ref[k, here, :] * second)
            low_ref[k, here, :] = value.astype(BF16)
            return carry

        lax.fori_loop(0, rows // CHUNK, chunk, 0, unroll=UNROLL)
    parts = [dot_nt(low_ref[k], w_out_ref[place.batch ^ k]) for k in range(blocks)]
    flat_ref[...] = functools.reduce(jnp.add, parts)
    spread_map_rows(flat_ref, gw_ref)
    center, scale, gain, shift = mid_norm(place, mid_sums_refs, mid_affine_ref)
    rises, leans, attended = [], [], []
    for image in range(images):

        def gather(step, carry, image=image):
            attended, rise, lean = carry
            at = pl.multiple_of(image * PADDED + step * CHUNK, CHUNK)
            before = mid_ref[pl.ds(at, CHUNK), :]
            value = before * gain + shift
            share = logistic(value)
            grad = gw_ref[pl.ds(at, CHUNK), :]
            grad = jnp.concatenate([grad, grad], axis=1)
            active = grad * share
            attended = attended + fold(active * value)
            inclined = active * (1.0 + value * (1.0 - share))
            return attended, rise + fold(inclined), lean + fold(inclined * before)

        nothing = jnp.zeros((8, 2 * width), F32)
        parts = lax.fori_loop(
            0, SIDE, gather, (nothing, nothing, nothing), unroll=SIDE
        )
        share = attention_ref[image : image + 1, :]
        attended.append(total_of(parts[0]))
        rise = total_of(parts[1])
        rises.append(share * rise)
        leans.append(share * (scale * (total_of(parts[2]) - center * rise)))
    grad = jnp.concatenate(attended, axis=0)
    attention = attention_ref[...]
    inner = attention * grad
    inner = inner[:, :width] + inner[:, width:]
    logits = attention * (grad - jnp.concatenate([inner, inner], axis=1))
    logits_ref[...] = logits
    gate = exact_dot(dot_nn, logits, excite_ref[...])[:images] * gate_ref[1]
    pack = msg_ref.shape[1]
    pieces = 2 * width // pack
    for t, row in enumerate((functools.reduce(jnp.add, rises), functools.reduce(jnp.add, leans))):
        for q in range(pieces):
            msg_ref[t * pieces + q : t * pieces + q + 1, :] = row[:, q * pack : (q + 1) * pack]
    msg_ref[2 * pieces : 2 * pieces + images, :] = gate


def back_mid(
    counts_ref,
    back_refs,
    gathered_refs,
    wall_ref,
    gate_affine_ref,
    squeeze_ref,
    attention_ref,
    gw_ref,
    mid_ref,
    mid_sums_refs,
    mid_affine_ref,
    pre_ref,
    sums_refs,
    affine_ref,
    w_ref,
    low_ref,
    grad_ref,
    gate_ref,
    vector_ref,
    msg_ref,
    taps_ref,
):
    place = Place(counts_ref)
    images = attention_ref.shape[0]
    width = attention_ref.shape[1] // 2
    lanes = wall_ref.shape[1]
    pieces = 2 * width // lanes
    total = place.total() * PIXELS
    wall = wall_ref[...]
    rows = slot_rows(gathered_refs, GATHERED, 0, images)
    center, scale = gate_norm(place, rows, wall)
    gain = gate_affine_ref[0:1, :] * scale
    normed = (rows - center) * scale
    grads = slot_rows(back_refs, images, 0, images, 2 * pieces)
    first, second = total_of(wall * grads), total_of(wall * grads * normed)
    vector_ref[0:1, 0:lanes] = second
    vector_ref[0:1, lanes : 2 * lanes] = first
    squeezed = gain * (grads - wall * (first + normed * second) / place.total())
    gate_ref[...] = squeezed[0:images]
    pooled_grad = exact_dot(dot_nt, squeezed, squeeze_ref[...]) / PIXELS
    pooled_grad = jnp.concatenate([pooled_grad, pooled_grad], axis=1)
    slot = 0
    terms = jnp.zeros((2 * images, 2 * width), F32)
    for ref in gathered_refs:
        for at in range(8, ref.shape[0], GATHERED):
            inclines = [
                ref[at + q * 2 * images : at + (q + 1) * 2 * images, :] for q in range(pieces)
            ]
            grad = pooled_grad[slot * images : (slot + 1) * images, :]
            grad = jnp.concatenate([grad, grad], axis=0)
            terms = terms + jnp.concatenate(inclines, axis=1) * grad
            slot += 1
    sums = functools.reduce(jnp.add, [ref[0 : 2 * pieces, :] for ref in back_refs])
    back = []
    for t in range(2):
        row = [sums[t * pieces + q : t * pieces + q + 1, :] for q in range(pieces)]
        back.append(
            jnp.concatenate(row, axis=1) + total_of(terms[t * images : (t + 1) * images])
        )
    vector_ref[1:2, :] = back[1]
    vector_ref[2:3, :] = back[0]
    own = pooled_grad[0:images]
    center, scale, gain, shift = mid_norm(place, mid_sums_refs, mid_affine_ref)
    second = gain * scale * back[1] / total
    first = gain * back[0] / total - center * second
    clear_gaps(taps_ref, images)
    keep = columns_real(WIDE)
    for image in range(images):
        share = gain * attention_ref[image : image + 1, :]
        offset = gain * own[image : image + 1, :]
        real = place.real(image)
        lead, lag = real * first, real * second

        def chunk(step, carry, image=image, share=share, offset=offset, lead=lead, lag=lag):
            rows = pl.multiple_of(step * WIDE, WIDE)
            here = pl.ds(image * PADDED + rows, WIDE)
            before = mid_ref[here, :]
            grad = gw_ref[here, :]
            grad = jnp.concatenate([grad, grad], axis=1)
            grad = (share * grad + offset) * slope(before * gain + shift)
            value = (grad - (lead + before * lag)) * keep
            store_taps(taps_ref, image * STRIDE + WIDE + rows, value)
            return carry

        lax.fori_loop(0, SIDE, chunk, 0, unroll=SIDE)
    low_ref[...] = taps_ref[1]
    sums = summed_over(sums_refs)
    center, scale = moments(sums[0:1], sums[1:2], total)
    gain = affine_ref[0:1, :] * scale
    shift = affine_ref[1:2, :] - center * gain
    half = width // 2
    keep = columns_real(PADDED)
    firsts = [jnp.zeros((1, half), F32) for _ in range(2)]
    seconds = [jnp.zeros((1, half), F32) for _ in range(2)]
    for image in range(images):
        real = place.real(image)
        here = slice(image * PADDED, (image + 1) * PADDED)
        for r in range(2):
            left = jnp.concatenate(
                [
                    taps_ref[
                        2 - b,
                        image * STRIDE + (2 - a) * WIDE : image * STRIDE + (2 - a) * WIDE + PADDED,
                        r * width : (r + 1) * width,
                    ]
                    for a in range(3)
                    for b in range(3)
                ],
                axis=1,
            )
            lane = slice(r * half, (r + 1) * half)
            before = pre_ref[here, lane]
            value = dot_nn(left, w_ref[r]) * slope(before * gain[:, lane] + shift[:, lane])
            value = value * (keep * real)
            grad_ref[here, lane] = value
            firsts[r] = firsts[r] + total_of(value)
            seconds[r] = seconds[r] + total_of(value * before)
    first = jnp.concatenate(firsts, axis=1)
    second = scale * (jnp.concatenate(seconds, axis=1) - center * first)
    sums = jnp.concatenate([first, second], axis=0)
    msg_ref[...] = sums


def sort_pieces(
    place,
    source_ref,
    keep_ref,
    send_ref,
    row,
):
    for turn, s in enumerate(ORDER):
        target = keep_ref if turn < 2 else send_ref
        rows = source_ref.shape[1]
        target[turn % 2, row : row + rows, :] = source_ref[place.chan ^ s].astype(BF16)


def weight_out_term(
    counts_ref,
    weighted_ref,
    low_ref,
    gate_ref,
    logits_ref,
    affine_ref,
    keep_ref,
    send_ref,
    wide_ref,
    small_ref,
):
    place = Place(counts_ref)
    width = weighted_ref.shape[1]
    lanes = keep_ref.shape[2]
    own = width // len(SLOTS)
    center = expected(affine_ref[0:1, :], affine_ref[1:2, :])
    center = 0.5 * (center[:, :width] + center[:, width:])
    for turn, s in enumerate(ORDER):
        target = keep_ref if turn < 2 else send_ref
        held = place.batch ^ place.chan ^ s
        term = centred_dot(weighted_ref[...], center, low_ref[held]).astype(BF16)
        target[turn % 2, 0:width, :] = term[:, :lanes]
        target[turn % 2, width : 2 * width, :] = term[:, lanes:]
    wide_ref[...] = dot_tn(logits_ref[...], gate_ref[0], HIGHEST)
    for turn, s in enumerate(ORDER):
        target = keep_ref if turn < 2 else send_ref
        for r in range(2):
            at = pl.multiple_of(r * width + (place.chan ^ s) * own, own)
            row = 2 * width + r * own
            target[turn % 2, row : row + own, :] = wide_ref[pl.ds(at, own), :].astype(BF16)
    small_ref[...] = jnp.zeros_like(small_ref)
    bias = total_of(logits_ref[...])
    for k in range(len(SLOTS)):
        small_ref[k, 0:1, :own] = bias[:, k * own : (k + 1) * own]
        small_ref[k, 0:1, own:] = bias[:, width + k * own : width + (k + 1) * own]
    sort_pieces(place, small_ref, keep_ref, send_ref, 2 * width + 2 * own)


def weight_mid_term(
    counts_ref,
    taps_ref,
    low_ref,
    affine_ref,
    keep_ref,
    send_ref,
    wide_ref,
):
    place = Place(counts_ref)
    center = expected(affine_ref[0:1, :], affine_ref[1:2, :])
    half = taps_ref.shape[2] // 2
    width = low_ref.shape[1] // 2
    own = width // len(SLOTS)
    rows = low_ref.shape[0] - 2 * WIDE
    for r in range(2):
        right = jnp.concatenate(
            [
                taps_ref[b, a * WIDE : a * WIDE + rows, r * half : (r + 1) * half]
                for a in range(3)
                for b in range(3)
            ],
            axis=1,
        )
        low = low_ref[WIDE : WIDE + rows, r * width : (r + 1) * width]
        offset = jnp.concatenate([center[:, r * half : (r + 1) * half]] * 9, axis=1)
        wide_ref[...] = dot_centred(low, right, offset)
        for turn, s in enumerate(ORDER):
            target = keep_ref if turn < 2 else send_ref
            here = pl.ds(pl.multiple_of((place.chan ^ s) * own, own), own)
            for tap in range(9):
                row = (2 * tap + r) * own
                target[turn % 2, row : row + own, :] = wide_ref[
                    here, tap * half : (tap + 1) * half
                ].astype(BF16)


def back_in(
    share,
    counts_ref,
    grad_ref,
    pre_ref,
    sums_refs,
    back_refs,
    affine_ref,
    x0,
    x1,
    x2,
    x3,
    vector_ref,
    out_back_refs,
    pooled_ref,
    gathered_refs,
    squeezed_ref,
    low_ref,
    keep_ref,
    send_ref,
    flat_ref,
    wide_ref,
    narrow_ref,
    small_ref,
):
    place = Place(counts_ref)
    images = pre_ref.shape[0] // PADDED
    width = pre_ref.shape[1]
    own = width // len(SLOTS)
    chan, batch = place.chan, place.batch
    total = place.total() * PIXELS
    sums = summed_over(sums_refs)
    center, scale = moments(sums[0:1], sums[1:2], total)
    back = summed_over(back_refs)
    gain = affine_ref[0:1, :] * scale
    second = gain * scale * back[1:2] / total
    first = gain * back[0:1] / total - center * second
    for image in range(images):
        real = place.real(image)
        lead, lag = real * first, real * second
        for line in range(SIDE):
            at = image * PADDED + line * WIDE
            before = pre_ref[at : at + WIDE, :]
            value = gain * grad_ref[at : at + WIDE, :] - (lead + before * lag)
            at = image * PIXELS + line * SIDE
            flat_ref[at : at + SIDE, :] = value[:SIDE]
    low_ref[...] = flat_ref[...].astype(BF16)
    lanes = keep_ref.shape[2]
    low = jnp.concatenate([low_ref[...], sum_rows(low_ref[...])], axis=0)
    for k, x in enumerate((x0, x1, x2, x3)):
        center = same_rows(-sums[2 + k : 3 + k] / total)
        wide_ref[...] = dot_tn(low, jnp.concatenate([x[...], center], axis=0))
        for turn, s in enumerate(ORDER):
            target = keep_ref if turn < 2 else send_ref
            here = pl.ds(pl.multiple_of((chan ^ s) * own, own), own)
            for part in range(wide_ref.shape[1] // lanes):
                at = pl.multiple_of(((batch ^ k) * (wide_ref.shape[1] // lanes) + part) * own, own)
                target[turn % 2, pl.ds(at, own), :] = wide_ref[
                    here, part * lanes : (part + 1) * lanes
                ].astype(BF16)
    mean = [
        total_of(slot_rows(gathered_refs, GATHERED, images + q, 1)) for q in range(width // lanes)
    ]
    mean = jnp.concatenate(mean, axis=1) / place.total()
    narrow_ref[...] = dot_tn(pooled_ref[...] - mean, squeezed_ref[...], HIGHEST)
    row = keep_ref.shape[1] - small_ref.shape[1] - own
    for turn, s in enumerate(ORDER):
        target = keep_ref if turn < 2 else send_ref
        here = pl.ds(pl.multiple_of((chan ^ s) * own, own), own)
        target[turn % 2, row : row + own, :] = narrow_ref[here, :].astype(BF16)
    small_ref[...] = jnp.zeros_like(small_ref)
    outs = summed_over(out_back_refs)
    for k in range(len(SLOTS)):
        here = slice(k * own, (k + 1) * own)
        there = slice(width + k * own, width + (k + 1) * own)
        small_ref[k, 0:1, :own] = back[1:2, here]
        small_ref[k, 0:1, own:] = back[0:1, here]
        for t in range(2):
            small_ref[k, 1 + t : 2 + t, :own] = vector_ref[1 + t : 2 + t, here]
            small_ref[k, 1 + t : 2 + t, own:] = vector_ref[1 + t : 2 + t, there]
        small_ref[k, 3:4, :] = vector_ref[0:1, 0:lanes]
        small_ref[k, 4:5, :] = vector_ref[0:1, lanes : 2 * lanes]
    for s in SLOTS:
        for t in range(2):
            row = outs[(1 - t) * len(SLOTS) + s : (1 - t) * len(SLOTS) + s + 1, :]
            small_ref[batch ^ s, 5 + 2 * t : 6 + 2 * t, :] = row[:, :lanes]
            small_ref[batch ^ s, 6 + 2 * t : 7 + 2 * t, :] = row[:, lanes:]
    small_ref[...] = small_ref[...] * share
    sort_pieces(place, small_ref, keep_ref, send_ref, keep_ref.shape[1] - small_ref.shape[1])


def grad_owned(low_refs, w_ref, summed_ref, result_ref):
    chan = lax.axis_index("chan")
    for s, low_ref in enumerate(low_refs):
        value = dot_nn(low_ref[...], w_ref[chan]) + summed_ref[chan ^ s].astype(F32)
        result_ref[chan ^ s] = value.astype(BF16)


def add_groups(terms_ref, sum_ref):
    value = jnp.sum(terms_ref[...].astype(F32), axis=0).astype(BF16)
    sum_ref[...] = jnp.broadcast_to(value[None], sum_ref.shape)


def added(left_ref, right_ref):
    return left_ref[...].astype(F32) + right_ref[...].astype(F32)


def add_core(keep_refs, arrived_refs, kept_ref, send_ref):
    at = 0
    for keep_ref, arrived_ref in zip(keep_refs, arrived_refs):
        value = added(keep_ref, arrived_ref).astype(BF16)
        rows = keep_ref.shape[1]
        kept_ref[at : at + rows, :] = value[0]
        send_ref[at : at + rows, :] = value[1]
        at += rows
    if at < kept_ref.shape[0]:
        for ref in (kept_ref, send_ref):
            ref[at:, :] = jnp.zeros((kept_ref.shape[0] - at, ref.shape[1]), BF16)


def split_rows(parity, keep_ref, arrived_ref, kept_ref, send_ref):
    rows = kept_ref.shape[-2]
    for own, target in ((parity, kept_ref), (1 - parity, send_ref)):
        here = pl.ds(pl.multiple_of(own * rows, 16), rows)
        if target.ndim == 2:
            value = added(keep_ref.at[here, :], arrived_ref.at[here, :])
        else:
            value = added(keep_ref.at[:, here, :], arrived_ref.at[:, here, :])
        target[...] = value.astype(target.dtype)


def add_core_first(counts_ref, keep_ref, arrived_ref, kept_ref, send_ref):
    split_rows(Place(counts_ref).parity, keep_ref, arrived_ref, kept_ref, send_ref)


def add_parity_first(keep_ref, arrived_ref, kept_ref, send_ref):
    kept_ref[...] = added(keep_ref.at[0], arrived_ref.at[0])
    send_ref[...] = added(keep_ref.at[1], arrived_ref.at[1]).astype(BF16)


def add_chip(counts_ref, keep_ref, arrived_ref, kept_ref, send_ref):
    split_rows(Place(counts_ref).parity, keep_ref, arrived_ref, kept_ref, send_ref)


def add_last(counts_ref, keep_refs, arrived_refs, kept_ref, s1, s2, s3):
    place = Place(counts_ref)
    at = 0
    for keep_ref, arrived_ref in zip(keep_refs, arrived_refs):
        rows = keep_ref.shape[0] // len(SLOTS)
        for t, target in enumerate((kept_ref, s1, s2, s3)):
            here = pl.ds(pl.multiple_of((place.depth ^ t) * rows, 16), rows)
            value = added(keep_ref.at[here, :], arrived_ref.at[here, :])
            target[at : at + rows, :] = value.astype(target.dtype)
        at += rows


def add_depth(keep_ref, arrived_refs, sum_ref):
    value = keep_ref[...]
    for ref in arrived_refs:
        value = value + ref[...].astype(F32)
    sum_ref[...] = value.astype(BF16)


def unpack(
    joined,
    counts_ref,
    term_refs,
    in_ref,
    gain_in_ref,
    shift_in_ref,
    mid_ref,
    gain_mid_ref,
    shift_mid_ref,
    squeeze_ref,
    gain_gate_ref,
    shift_gate_ref,
    excite_ref,
    bias_ref,
    out_ref,
    gain_out_ref,
    shift_out_ref,
    second_ref,
):
    own, lanes = squeeze_ref.shape
    width = out_ref.shape[0]
    places = [(out_ref, 0, 0, width), (out_ref, 0, 1, width), (excite_ref, 0, 0, 2 * own)]
    places += [(second_ref, 0, 0, 16)]
    places += [(in_ref, 0, block, own) for block in range(in_ref.shape[1] // lanes)]
    places += [(squeeze_ref, 0, 0, own), (second_ref, 16, 0, 16)]

    def write(value, row):
        start = 0
        for target, at, block, rows in places:
            first, last = max(row, start), min(row + value.shape[0], start + rows)
            if first < last:
                there = slice(at + first - start, at + last - start)
                target[there, block * lanes : (block + 1) * lanes] = value[first - row : last - row]
            start += rows

    if joined:
        mid_ref[...] = term_refs[0][...].astype(F32)
        write(term_refs[1][...].astype(F32), 0)
    else:
        place = Place(counts_ref)
        even = place.parity == 0
        piece = term_refs[0].shape[0] // len(SLOTS)
        rows = mid_ref.shape[0] // 2 // len(SLOTS)
        for half in range(2):
            mine, other = term_refs[half], term_refs[1 - half]
            for z in range(len(SLOTS)):
                here = pl.ds(pl.multiple_of((place.depth ^ z) * piece, 16), piece)
                value = jnp.where(even, mine[here, :].astype(F32), other[here, :].astype(F32))
                at = (half * len(SLOTS) + z) * rows
                mid_ref[at : at + rows, :] = value[:rows]
                write(value[rows:], (half * len(SLOTS) + z) * (piece - rows))

    def halves(target, row):
        target[0:1, :] = second_ref[row : row + 1, :own]
        target[1:2, :] = second_ref[row : row + 1, own:]

    halves(bias_ref, 0)
    row = 16
    gain_in_ref[...] = second_ref[row : row + 1, :own]
    shift_in_ref[...] = second_ref[row : row + 1, own:]
    halves(gain_mid_ref, row + 1)
    halves(shift_mid_ref, row + 2)
    gain_gate_ref[...] = second_ref[row + 3 : row + 4, :]
    shift_gate_ref[...] = second_ref[row + 4 : row + 5, :]
    for t, target in enumerate((gain_out_ref, shift_out_ref)):
        target[:, :lanes] = second_ref[row + 5 + 2 * t : row + 6 + 2 * t, :]
        target[:, lanes:] = second_ref[row + 6 + 2 * t : row + 7 + 2 * t, :]


def per_device(
    activations,
    counts,
    weight_in,
    gain_in,
    shift_in,
    weight_mid,
    gain_mid,
    shift_mid,
    weight_squeeze,
    gain_gate,
    shift_gate,
    weight_excite,
    shift_excite,
    weight_out,
    gain_out,
    shift_out,
    cotangent,
    *,
    groups,
    parts,
):
    batches, rows, lanes = activations.shape
    images = rows // PIXELS
    own = weight_in.shape[1]
    width = own * parts
    inter = gain_gate.shape[0]
    wide_rows = images * PADDED
    gap_rows = WIDE + images * STRIDE
    chan, group = lax.axis_index("chan"), lax.axis_index("dp")
    depth = groups // 2

    def permute(tensor, to):
        pairs = []
        for index in range(groups * parts):
            z, x, y, c = index // parts // 2, index // parts % 2, index % parts // 2, index % 2
            z, x, y, c = to(z, x, y, c)
            pairs.append((index, (2 * z + x) * parts + 2 * y + c))
        return lax.ppermute(tensor, ("dp", "chan"), pairs)

    def home(tensor, s):
        return permute(tensor, lambda z, x, y, c: (z, c ^ (s & 1), y ^ (s >> 1), x))

    def away_plane(tensor):
        return permute(tensor, lambda z, x, y, c: (z, c, y, x))

    def cross(even, odd):
        return even, odd, across(jnp.stack([even[1], odd[1]]))

    def core(tensor):
        return permute(tensor, lambda z, x, y, c: (z, x, y, c ^ 1))

    def across(tensor):
        return permute(tensor, lambda z, x, y, c: (z, x, y ^ 1, c))

    def parity(tensor):
        return permute(tensor, lambda z, x, y, c: (z, x ^ 1, y, c))

    def along(tensor, t):
        return permute(tensor, lambda z, x, y, c: (z ^ t, x, y, c))

    def after(tensor, *others):
        return lax.optimization_barrier((tensor,) + others)[0]

    def after_all(tensors, *others):
        return lax.optimization_barrier(tuple(tensors) + others)[: len(tensors)]

    def exchange(total, gather):
        def merge(mine, other):
            cut = 0 if total is None else total
            joined = [mine[:cut] + other[:cut]] if cut else []
            if gather:
                joined += [mine[cut : cut + gather], other[cut : cut + gather]]
            return jnp.concatenate(joined) if len(joined) > 1 else joined[0]

        def run(mine):
            nonlocal gather
            mine = merge(mine, core(mine))
            gather = 2 * gather
            if depth <= 4:
                return (mine,) + tuple(along(mine, t) for t in range(1, depth))
            step = 1
            while step < depth:
                mine = merge(mine, along(mine, step))
                gather, step = 2 * gather, 2 * step
            return (mine,)

        return run

    def padded(rows):
        return -(-rows // (16 * groups)) * 16 * groups

    def kernel(body, outs, *args, smem=1):
        return call(body, outs, [], 0, *args, smem=smem)

    def add_over_all(first, second, low, shared, finish_own):
        first_rows, second_rows = first[0].shape[1], sum(k.shape[1] for k in second[0])
        if groups != 8:
            rows = padded(first_rows + second_rows)
            keep, send = kernel(
                add_core,
                [shape((rows, 2 * own), BF16)] * 2,
                (first[0],) + second[0],
                (first[1],) + second[1],
                smem=0,
            )
            terms = (keep.astype(F32) + across(send).astype(F32)).astype(BF16)
            terms = lax.all_to_all(terms.reshape(groups, rows // groups, -1), "dp", 0, 0)
            (terms,) = kernel(add_groups, [shape(terms.shape, BF16)], terms, smem=0)
            terms = lax.all_to_all(terms, "dp", 0, 0).reshape(rows, -1)
            terms = terms[:first_rows], terms[first_rows : first_rows + second_rows]
            low = away_plane(low)
            near, far = shared
            owned = finish_own(near, core(jnp.stack([near, far])), far)
            return (terms, low, across(low)) + tuple(owned)
        second_rows = padded(second_rows)
        halves = (first_rows // 2, second_rows // 2)
        pieces = (first_rows // groups, second_rows // groups)

        def rows(number, kind=F32):
            return shape((number, 2 * own), kind)

        keep, second_send = kernel(add_core, [rows(second_rows, BF16)] * 2, *second, smem=0)
        arrived = across(second_send)
        pair = (2, halves[0], 2 * own)
        first_keep, send = call(
            add_core_first,
            [shape(pair), shape(pair, BF16)],
            [],
            0,
            counts,
            *first,
        )
        first_arrived = parity(send)
        near, far = after_all(shared, send, second_send)
        swapped = core(jnp.stack([near, far]))
        arrived = after(arrived, swapped)
        low = away_plane(after(low, send))
        keep, send = call(
            add_chip,
            [rows(halves[1]), rows(halves[1], BF16)],
            [],
            0,
            counts,
            keep,
            arrived,
        )
        arrived = parity(send)
        first_keep, send = kernel(
            add_parity_first,
            [rows(halves[0]), rows(halves[0], BF16)],
            first_keep,
            first_arrived,
            smem=0,
        )
        first_arrived = across(send)
        arrived = after(arrived, first_arrived, low)
        keep, *send = call(
            add_last,
            [rows(sum(pieces))] + [rows(sum(pieces), BF16)] * (depth - 1),
            [],
            0,
            counts,
            (first_keep, keep),
            (first_arrived, arrived),
        )
        result, grad_summed = finish_own(*after_all((near, swapped, far), keep))
        arrived = tuple(along(send[t - 1], t) for t in range(1, depth))
        arrived = after_all(arrived, result)
        low_other = across(after(low, *arrived))
        (mine,) = kernel(add_depth, [rows(sum(pieces), BF16)], keep, arrived, smem=0)
        mine = (mine,) + tuple(along(mine, t) for t in range(1, depth))
        low, low_other = after_all((low, low_other), *mine)
        mine = jnp.concatenate(mine)
        return (mine, parity(mine)), low, low_other, result, grad_summed

    def slots_of(tensor, *which):
        return [lax.dynamic_index_in_dim(tensor, chan ^ s, 0, keepdims=False) for s in which]

    first = weight_in.T
    other, near = across(first), core(first)
    far = slots_of(activations, 2, 3)
    x = slots_of(after(activations, near), 0, 1) + far
    x = tuple(home(piece, s) for s, piece in enumerate(x))

    (weights,) = call(
        pack,
        [shape((19 * own + 16 + inter + 2 * width, 2 * own), BF16)],
        [pltpu.VMEM((16, 2 * own), F32)],
        0,
        weight_mid.transpose(0, 1, 3, 4, 2).reshape(-1, 2 * own),
        weight_squeeze,
        gain_in.reshape(1, -1),
        shift_in.reshape(1, -1),
        gain_mid,
        shift_mid,
        shift_excite,
        gain_out.reshape(1, -1),
        shift_out.reshape(1, -1),
        weight_excite.transpose(1, 2, 0).reshape(-1, inter),
        weight_out,
        smem=0,
    )
    other = after(other, weights)
    first = (first, near, other, core(other))
    near = core(weights)
    cot = slots_of(after(cotangent, x[0], x[1]), *SLOTS)
    even, odd = jnp.stack([cot[0], cot[2]]), jnp.stack([cot[1], cot[3]])
    other = across(after(weights, x[2], x[3], first[3]))
    even = home(after(even, x[2], x[3]), 0)
    gate_affine = jnp.stack([gain_gate, shift_gate]).astype(F32)

    product = 2 * rows * lanes * parts * width
    pre_in, msg, w_in, wall = call(
        reduce_in,
        [
            shape((wide_rows, width)),
            shape((2 + parts, lanes)),
            shape((parts, width, lanes), BF16),
            shape((groups * images, inter)),
        ],
        [pltpu.VMEM((rows, width), F32)],
        product,
        counts,
        *x,
        *first,
    )
    in_sums = exchange(2 + parts, 0)(after(msg, near, odd))
    other = after(other, *in_sums)
    odd = home(after(odd, *in_sums), 1)
    weights = (weights, near, other, core(other))
    w_mid, w_mid_back, squeeze, in_affine, mid_affine, bias, out_affine = call(
        place_mid,
        [
            shape((2, width, 9 * inter), BF16),
            shape((2, 9 * width, inter), BF16),
            shape((width, inter), BF16),
            shape((2, width)),
            shape((2, 2 * width)),
            shape((1, 2 * width)),
            shape((2, parts, 1, lanes)),
        ],
        [pltpu.VMEM((parts, 16, 2 * own), F32)],
        0,
        counts,
        *weights,
    )
    conv = 2 * wide_rows * 9 * width * width
    taps, mid, msg = call(
        conv_mid,
        [
            shape((3, gap_rows, width), BF16),
            shape((wide_rows, 2 * width)),
            shape((2, 2 * width)),
        ],
        [],
        conv,
        counts,
        pre_in,
        in_sums,
        in_affine,
        w_mid,
    )
    mid_sums = exchange(2, 0)(msg)
    excite, w_out = call(
        place_rest,
        [
            shape((2 * width, inter), BF16),
            shape((parts, width, lanes), BF16),
        ],
        [],
        0,
        counts,
        *weights,
    )
    pooled, msg = call(
        pool,
        [shape((images, width)), shape((GATHERED, inter))],
        [],
        0,
        counts,
        mid,
        mid_sums,
        mid_affine,
        squeeze,
    )
    cot = cross(*after_all((even, odd), msg))
    gathered = exchange(None, GATHERED)(msg)
    gate, attention, weighted, out, msg = call(
        attend,
        [
            shape((2, images, inter)),
            shape((images, 2 * width)),
            shape((rows, width), BF16),
            shape((parts, rows, lanes)),
            shape((2 * parts, lanes)),
        ],
        [pltpu.VMEM((wide_rows, width), F32), pltpu.VMEM((rows, width), F32)],
        product,
        counts,
        gathered,
        wall,
        gate_affine,
        excite,
        bias,
        mid,
        mid_sums,
        mid_affine,
        w_out,
    )
    out_sums = exchange(2 * parts, 0)(msg)
    shared, grad, msg = call(
        finish,
        [
            shape((rows + 32, width), BF16),
            shape((parts, rows, lanes)),
            shape((2 * parts, lanes)),
        ],
        [pltpu.VMEM((2 * parts, 1, lanes), F32)],
        0,
        counts,
        out,
        out_sums,
        out_affine,
        weighted,
        x,
        *cot,
    )
    out_back = exchange(2 * parts, 0)(msg)

    shared = away_plane(shared)

    sums_rows = 2 * 2 * width // inter
    low_out, grad_weighted, grad_logits, msg = call(
        back_out,
        [
            shape((parts, rows, lanes), BF16),
            shape((wide_rows, width)),
            shape((images, 2 * width)),
            shape((sums_rows + images, inter)),
        ],
        [pltpu.VMEM((rows, width), F32)],
        product,
        counts,
        grad,
        out,
        out_sums,
        out_back,
        out_affine,
        w_out,
        mid,
        mid_sums,
        mid_affine,
        attention,
        gate,
        excite,
    )
    mid_back = exchange(sums_rows, images)(msg)
    term_rows = 2 * width + 2 * own + 16
    keep, send = call(
        weight_out_term,
        [shape((2, term_rows, 2 * own), BF16)] * 2,
        [pltpu.VMEM((2 * width, inter), F32), pltpu.VMEM((parts, 16, 2 * own), F32)],
        product,
        counts,
        after(weighted, mid_back[0]),
        low_out,
        gate,
        grad_logits,
        mid_affine,
    )
    mid_back = after_all(mid_back, keep, shared)
    shared = after(shared, mid_back[0])
    shared = (shared, across(shared))
    out_keep, out_send = keep, send
    low_mid, grad_hidden, grad_squeeze, vectors, msg = call(
        back_mid,
        [
            shape((gap_rows, 2 * width), BF16),
            shape((wide_rows, width)),
            shape((images, inter)),
            shape((8, 2 * width)),
            shape((2, width)),
        ],
        [pltpu.VMEM((3, gap_rows, 2 * width), BF16)],
        conv,
        counts,
        mid_back,
        gathered,
        wall,
        gate_affine,
        squeeze,
        attention,
        grad_weighted,
        mid,
        mid_sums,
        mid_affine,
        pre_in,
        in_sums,
        in_affine,
        w_mid_back,
    )
    out_arrived = core(after(out_send, msg))
    in_back = exchange(2, 0)(msg)
    keep, send = call(
        weight_mid_term,
        [shape((2, 18 * own, 2 * own), BF16)] * 2,
        [pltpu.VMEM((width, 9 * inter), F32)],
        conv,
        counts,
        after(taps, in_back[0]),
        low_mid,
        in_affine,
    )
    in_back = after_all(in_back, keep, shared[1])
    in_rows = parts * lanes // (2 * own) * own
    low_in, in_keep, in_send = call(
        functools.partial(back_in, 1.0 / groups),
        [shape((rows, width), BF16)] + [shape((2, in_rows + own + 16, 2 * own), BF16)] * 2,
        [
            pltpu.VMEM((rows, width), F32),
            pltpu.VMEM((width, lanes), F32),
            pltpu.VMEM((width, inter), F32),
            pltpu.VMEM((parts, 16, 2 * own), F32),
        ],
        product,
        counts,
        grad_hidden,
        pre_in,
        in_sums,
        in_back,
        in_affine,
        *x,
        vectors,
        out_back,
        pooled,
        gathered,
        grad_squeeze,
    )
    owned = shape((batches, rows, lanes), BF16)

    def finish_own(near, swapped, far):
        return call(
            finish_owned,
            [owned, owned],
            [pltpu.VMEM((rows, lanes), F32)],
            product,
            counts,
            near,
            swapped,
            far,
            w_out,
            activations,
            cotangent,
        )

    send = after(send, low_in)
    terms, low_in, low_other, result, grad_summed = add_over_all(
        (keep, core(send)),
        ((out_keep, in_keep), (out_arrived, core(in_send))),
        low_in,
        shared,
        finish_own,
    )
    lows = (low_in, core(low_in), low_other, core(low_other))
    (grad_x,) = call(grad_owned, [owned], [], product, lows, w_in, grad_summed, smem=0)
    terms = after_all(terms, grad_x)
    (
        g_in,
        g_gain_in,
        g_shift_in,
        g_mid,
        g_gain_mid,
        g_shift_mid,
        g_squeeze,
        g_gain_gate,
        g_shift_gate,
        g_excite,
        g_bias,
        g_out,
        g_gain_out,
        g_shift_out,
    ) = call(
        functools.partial(unpack, groups != 8),
        [
            shape((own, parts * lanes)),
            shape((1, own)),
            shape((1, own)),
            shape((18 * own, inter)),
            shape((2, own)),
            shape((2, own)),
            shape((own, inter)),
            shape((1, inter)),
            shape((1, inter)),
            shape((2 * own, inter)),
            shape((2, own)),
            shape((width, lanes)),
            shape((1, lanes)),
            shape((1, lanes)),
        ],
        [pltpu.VMEM((32, 2 * own), F32)],
        0,
        counts,
        terms,
    )
    return (
        result,
        grad_x,
        g_in.T,
        g_gain_in.reshape(-1),
        g_shift_in.reshape(-1),
        g_mid.reshape(3, 3, 2, own, inter).transpose(0, 1, 4, 2, 3),
        g_gain_mid,
        g_shift_mid,
        g_squeeze,
        g_gain_gate.reshape(-1),
        g_shift_gate.reshape(-1),
        g_excite.reshape(2, own, inter).transpose(2, 0, 1),
        g_bias,
        g_out,
        g_gain_out.reshape(-1),
        g_shift_out.reshape(-1),
    )


def solution(mesh):
    placed = (
        P(None, "dp", "chan"),
        P(),
        P(None, "chan"),
        P("chan"),
        P("chan"),
        P(None, None, None, None, "chan"),
        P(None, "chan"),
        P(None, "chan"),
        P("chan", None),
        P(),
        P(),
        P(None, None, "chan"),
        P(None, "chan"),
        P(None, "chan"),
        P("chan"),
        P("chan"),
        P(None, "dp", "chan"),
    )
    return jax.shard_map(
        functools.partial(per_device, groups=mesh.shape["dp"], parts=mesh.shape["chan"]),
        mesh=mesh,
        in_specs=placed,
        out_specs=placed[:1] + placed[:1] + placed[2:16],
        check_vma=False,
    )
```
